32 devices in a mesh: groups: 2 (over y), dp: 4 (over z), seq: 4 (over x, core).
Axes of the slice: x: 2, y: 2, z: 4, core: 2. Of those that a mesh axis runs over, the one named last changes fastest.
Arguments:
- query_rows: bfloat16 [8, 1024, 8192], P(('groups', 'dp'), 'seq'), parts along dimension 0, may hold values from -60 to 60
- key_rows: bfloat16 [8, 1024, 1024], P(('groups', 'dp'), 'seq'), parts along dimension 0, may hold values from -4 to 4
- placed_value_rows: bfloat16 [8, 1024, 1024], P(('groups', 'dp'), 'seq'), parts along dimension 0, may hold values from -4 to 4
- doc_lengths: int32 [8, 8], P(('groups', 'dp')), parts along dimension 0, may hold values from 1 to 512, 1024 in all within a row
- span_order: int32 [8, 8], P(('groups', 'dp')), parts along dimension 0, may hold values from 0 to 7, each once within a row
- out_weight: bfloat16 [8192, 8192], P('dp', 'seq'), may hold values from -0.25 to 0.25
Outputs:
- whitened: float32 [32, 512, 8192], P(('groups', 'seq'), None, 'dp'), parts along dimension 0
The draws below stay inside these ranges and needn't reach their ends.
There are 2 independent parts, one for each index of `groups`. The reference program is written for one: setup_inputs(seed, part) draws one part's arguments, and reference() takes and returns one part's arrays. A program takes and returns all parts, laid end to end along the dimension named above; an argument that names none is the same for every part. Nothing has to cross between parts.
All inputs are finite; a program needn't handle non-finite values.
Results may differ from the reference program's by a relative error of at most 0.00073.
Values may be sent and summed in bfloat16 or wider, within the bound.
No kernel may reach another device: no remote copies, remote signals or barrier semaphores. Data moves between devices by JAX's collectives and lax.ppermute only.
A program may use at most 128 MiB of HBM per device.

```python
import math
import jax
import jax.numpy as jnp
import numpy as np
from jax import lax

D_OUT = 8192
QUERY_HEADS = 64
KEY_VALUE_HEADS = 8
HEAD_SIZE = 128
BLOCK_W = 512
NDOCS = 8
SPAN = 128
NCHUNK = 8
SEQUENCE_LENGTH = 1024
SEQUENCE_COUNT = 4
NB = 16


def draw_pair(key):
    base = jax.random.fold_in(key, 7)
    first_key, second_key = jax.random.split(base, 2)
    head_group = QUERY_HEADS // KEY_VALUE_HEADS
    key_dimensions = (SEQUENCE_COUNT, SEQUENCE_LENGTH, KEY_VALUE_HEADS, HEAD_SIZE)
    query_dimensions = (SEQUENCE_COUNT, SEQUENCE_LENGTH, KEY_VALUE_HEADS, head_group, HEAD_SIZE)
    key_portion = jnp.clip(jax.random.normal(first_key, key_dimensions, jnp.float32), -4.0, 4.0)
    query_portion = jnp.clip(jax.random.normal(second_key, query_dimensions, jnp.float32), -4.0, 4.0)
    return (query_portion.reshape(SEQUENCE_COUNT, SEQUENCE_LENGTH, QUERY_HEADS * HEAD_SIZE), key_portion.reshape(SEQUENCE_COUNT, SEQUENCE_LENGTH, KEY_VALUE_HEADS * HEAD_SIZE))


def draw_query_rows(key, part):
    query_portion, key_portion = draw_pair(key)
    return query_portion.astype(jnp.bfloat16)


def draw_key_rows(key, part):
    query_portion, key_portion = draw_pair(key)
    return key_portion.astype(jnp.bfloat16)


def steps_of(stream_key, dims, cuts, low, high):
    gain, own = 1.0, jax.random.fold_in(stream_key, 6)
    for position, blocks in cuts:
        draws = jnp.exp(jax.random.uniform(jax.random.fold_in(own, position), (blocks,), jnp.float32, low / len(cuts), high / len(cuts)))
        gain = gain * jnp.repeat(draws, dims[position] // blocks).reshape([-1 if axis == position else 1 for axis in range(len(dims))])
    return gain


def split_up(amount, total, most, skew):
    weights = [(1 << 20) // math.isqrt(grade ** skew) + 1 for grade in range(2, amount + 1)]
    rest, given = total - most - (amount - 1), [1] * (amount - 1)
    while rest > 0:
        candidates = [i for i in range(amount - 1) if given[i] < most]
        mass, budget = sum([weights[i] for i in candidates]), rest
        for i in candidates:
            more = min(most - given[i], max(1, budget * weights[i] // mass), rest)
            given[i] = given[i] + more
            rest = rest - more
    return np.array([most] + given)


def ragged_sizes(own_key, amount, total, most, slope):
    if amount == 2:
        one = jax.random.randint(own_key, (), max(1, total - most), min(most, total - 1) + 1)
        return jnp.stack([one, total - one])
    sizes = jnp.asarray(split_up(amount, total, most, slope), jnp.int32)
    couples = (amount - 1) // 2
    donor, receiver = sizes[1:1 + 2 * couples:2], sizes[2:2 + 2 * couples:2]
    room = jnp.minimum(donor - 1, most - receiver)
    shifted = jax.random.randint(jax.random.fold_in(own_key, 1), (couples,), 0, 1 << 20) % (room + 1)
    sizes = sizes.at[1:1 + 2 * couples:2].set(donor - shifted).at[2:2 + 2 * couples:2].set(receiver + shifted)
    return sizes[jax.random.permutation(jax.random.fold_in(own_key, 2), amount)]


def gaussian(own_key, dims, deviation, bound, shards=(), kind=jnp.bfloat16):
    factor_of = steps_of(own_key, dims, shards, -0.22, 0.18) if shards else 1.0
    drawn = jax.random.normal(own_key, dims, jnp.float32) * deviation * factor_of
    return jnp.minimum(jnp.maximum(drawn, -bound), bound).astype(kind)


def setup_inputs(seed: int = 0, part: int = 0) -> dict:
    splits = jax.random.split(jax.random.key(seed), 7)
    own_keys = jax.random.split(jax.random.fold_in(splits[6], part), 7)
    return {
        "query_rows": draw_query_rows(jax.random.fold_in(jax.random.fold_in(splits[6], part), 71), part),
        "key_rows": draw_key_rows(jax.random.fold_in(jax.random.fold_in(splits[6], part), 71), part),
        "placed_value_rows": gaussian(own_keys[2], (SEQUENCE_COUNT, SEQUENCE_LENGTH, KEY_VALUE_HEADS * HEAD_SIZE), 1.0, 4.0, ((0, 4), (1, 4))),
        "doc_lengths": jax.vmap(lambda own: ragged_sizes(own, NDOCS, SEQUENCE_LENGTH, SEQUENCE_LENGTH // 2, 2))(jax.random.split(own_keys[3], SEQUENCE_COUNT)).reshape((SEQUENCE_COUNT, NDOCS)).astype(jnp.int32),
        "span_order": jax.vmap(lambda own: jax.random.permutation(own, NCHUNK))(jax.random.split(own_keys[4], SEQUENCE_COUNT)).reshape((SEQUENCE_COUNT, NCHUNK)).astype(jnp.int32),
        "out_weight": gaussian(splits[5], (D_OUT, QUERY_HEADS * HEAD_SIZE), BLOCK_W ** -0.5, 0.25, ((0, 4), (1, 4))),
    }


def doc_numbers(positions, lengths):
    starts = jnp.cumsum(lengths) - lengths
    return jnp.sum((positions[:, None] >= starts[None, :]).astype(jnp.int32), axis=1).astype(jnp.int32)

def sequence_grams(query_seq, key_seq, value_seq, length_seq, order_seq):
    row_ids = jnp.arange(SEQUENCE_LENGTH, dtype=jnp.int32)
    positions = (order_seq[row_ids // SPAN] * SPAN + row_ids % SPAN).astype(jnp.int32)
    doc_ids = doc_numbers(positions, length_seq)
    visible = (doc_ids[:, None] == doc_ids[None, :]) & (positions[None, :] <= positions[:, None])
    head_group = QUERY_HEADS // KEY_VALUE_HEADS

    def one_head(head_index):
        query_head = lax.dynamic_slice_in_dim(query_seq, head_index * HEAD_SIZE, HEAD_SIZE, 1)
        key_head = lax.dynamic_slice_in_dim(key_seq, head_index // head_group * HEAD_SIZE, HEAD_SIZE, 1)
        value_head = lax.dynamic_slice_in_dim(value_seq, head_index // head_group * HEAD_SIZE, HEAD_SIZE, 1)
        scores = lax.dot_general(query_head.astype(jnp.float32), key_head.astype(jnp.float32), (((1,), (1,)), ((), ())), preferred_element_type=jnp.float32) * HEAD_SIZE ** (-0.5)
        scores = jnp.where(visible, scores, -1e+30)
        largest = jnp.max(scores, axis=1, keepdims=True)
        lifted = jnp.exp(scores - largest)
        weights = (lifted / jnp.sum(lifted, axis=1, keepdims=True)).astype(jnp.bfloat16)
        return jnp.dot(weights.astype(jnp.float32), value_head.astype(jnp.float32), preferred_element_type=jnp.float32)
    per_head = lax.map(one_head, jnp.arange(QUERY_HEADS, dtype=jnp.int32))
    outputs = jnp.transpose(per_head, (1, 0, 2)).reshape(SEQUENCE_LENGTH, NB, BLOCK_W)
    return jnp.einsum('rbi,rbj->bij', outputs, outputs, precision=lax.Precision.HIGHEST)

def reference(query_rows, key_rows, placed_value_rows, doc_lengths, span_order, out_weight):

    def accumulate(carry, items):
        query_seq, key_seq, value_seq, length_seq, order_seq = items
        return (carry + sequence_grams(query_seq, key_seq, value_seq, length_seq, order_seq), None)
    begin = jnp.zeros((NB, BLOCK_W, BLOCK_W), jnp.float32)
    grams, ignored = lax.scan(accumulate, begin, (query_rows, key_rows, placed_value_rows, doc_lengths, span_order))
    traces = jnp.trace(grams, axis1=1, axis2=2)
    identity = jnp.eye(BLOCK_W, dtype=jnp.float32)
    damped = grams + (0.1 * traces / BLOCK_W)[:, None, None] * identity
    upper = jnp.swapaxes(jnp.linalg.cholesky(damped), 1, 2)
    weight_blocks = out_weight.astype(jnp.float32).reshape(D_OUT, NB, BLOCK_W)
    return jnp.einsum('bij,obj->bio', upper, weight_blocks, precision=lax.Precision.HIGHEST)
```

```python
import functools
import math

import jax
import jax.numpy as jnp
from jax import lax
from jax.experimental import pallas as pl
from jax.experimental.pallas import tpu as pltpu
from jax.sharding import PartitionSpec as P

QUERY_HEADS = 64
KEY_VALUE_HEADS = 8
HEAD_SIZE = 128
BLOCK_W = 512
NB = 16
SPAN = 128
GROUP = QUERY_HEADS // KEY_VALUE_HEADS
BLOCK_HEADS = BLOCK_W // HEAD_SIZE
KV_BLOCKS = GROUP // BLOCK_HEADS
PANELS = BLOCK_W // SPAN
STARTS = [sum(BLOCK_W - SPAN * j for j in range(k)) for k in range(PANELS)]
PACKED = sum(BLOCK_W - SPAN * j for j in range(PANELS))
VMEM_BYTES = 50 * 1024 * 1024
F32 = jnp.float32
BF16 = jnp.bfloat16
NT = (((1,), (1,)), ((), ()))
TN = (((0,), (0,)), ((), ()))


def params(limit=VMEM_BYTES):
    return pltpu.CompilerParams(vmem_limit_bytes=limit)


def cost(flops, moved, trans=0):
    return pl.CostEstimate(flops=int(flops), bytes_accessed=int(moved), transcendentals=int(trans))


def encode(value, exponent):
    scaled = value * jnp.exp2(15.0 - exponent)
    power = scaled * scaled
    power = power * power
    power = power * power
    return jnp.where(scaled < 0.0, -power, power)


def decode(code, exponent):
    code = code.astype(F32)
    root = jnp.exp2(jnp.log(jnp.maximum(jnp.abs(code), 1e-37)) * (0.125 / math.log(2.0)) + (exponent - 15.0))
    return jnp.where(code < 0.0, -root, root)


def marker():
    rows = lax.broadcasted_iota(jnp.int32, (SPAN, SPAN), 0)
    columns = lax.broadcasted_iota(jnp.int32, (SPAN, SPAN), 1)
    return (rows == SPAN - 1) & (columns == 0)


def exponent_of(largest):
    return jnp.ceil(jnp.log(jnp.maximum(largest, 1e-30)) * (1.0 / math.log(2.0)) + 0.001)


def write_coded(panels, out, largest):
    exponent = exponent_of(largest)
    at = 0
    for k, panel in enumerate(panels):
        coded = encode(panel, exponent)
        if k == 0:
            first = jnp.where(marker(), jnp.broadcast_to(exponent, (SPAN, SPAN)), coded[:, :SPAN])
            coded = jnp.concatenate([first, coded[:, SPAN:]], axis=1)
        out[:, at : at + panel.shape[1]] = coded.astype(BF16)
        at += panel.shape[1]


def read_coded(ref):
    exponent = ref[SPAN - 16 : SPAN, :SPAN].astype(F32)[15:16, 0:1]
    return decode(ref[...], exponent)


def split(value):
    high = value.astype(BF16)
    return high, (value - high.astype(F32)).astype(BF16)


def cut_kernel(meta, query_ref, key_ref, value_ref, *refs, chips, blocks, per, with_kv):
    outs, sems = refs[:-1], refs[-1]
    own, block, kv = meta[0], meta[1], meta[2]
    chip, core = own // 2, lax.rem(own, 2)
    copies = []
    for number, out in enumerate(outs):
        distance, cross = (number + 1) // 2, (number + 1) % 2
        target = lax.rem(chip + distance, chips) * 2 + lax.rem(core + cross, 2)
        columns = pl.ds(pl.multiple_of((target * blocks + block) * BLOCK_W, BLOCK_W), BLOCK_W)
        moves = [(query_ref.at[:, columns], out.at[:, :BLOCK_W])]
        if with_kv:
            head = pl.ds(pl.multiple_of((target * per + kv) * HEAD_SIZE, HEAD_SIZE), HEAD_SIZE)
            moves.append((key_ref.at[:, head], out.at[:, BLOCK_W : BLOCK_W + HEAD_SIZE]))
            moves.append((value_ref.at[:, head], out.at[:, BLOCK_W + HEAD_SIZE :]))
        for source, target_ref in moves:
            copies.append(pltpu.make_async_copy(source, target_ref, sems.at[len(copies)]))
    for copy in copies:
        copy.start()
    for copy in copies:
        copy.wait()


def turn_kernel(w_ref, out):
    out[...] = w_ref[...].T


def attention_kernel(meta, *refs, chips, spans, all_spans, documents, most, sets):
    sources = 2 * chips
    query_refs = refs[:sources]
    own_key, own_value = refs[sources : sources + 2]
    kv_refs = refs[sources + 2 : sources + 2 + sets * (sources - 1)]
    out, queries, keys, values, slots, limits, left, right = refs[sources + 2 + sets * (sources - 1) :]
    own = meta[0]
    chip, core = own // 2, lax.rem(own, 2)
    lengths = 4
    order = lengths + documents

    for r in range(all_spans):
        device = r // spans
        distance = lax.rem(chip - device // 2 + chips, chips)
        cross = lax.rem(core + device % 2, 2)
        slots[meta[order + r]] = (distance * 2 + cross) * spans + r % spans

    for t in range(spans):
        rows = slice(t * SPAN, (t + 1) * SPAN)
        keys[t] = own_key[rows]
        values[t] = own_value[rows].astype(F32).T.astype(BF16)
    for which in range(sets):

        @pl.when(meta[3] == which)
        def _(which=which):
            for source in range(1, sources):
                ref = kv_refs[which * (sources - 1) + source - 1]
                for t in range(spans):
                    rows = slice(t * SPAN, (t + 1) * SPAN)
                    keys[source * spans + t] = ref[rows, :HEAD_SIZE]
                    values[source * spans + t] = ref[rows, HEAD_SIZE:].astype(F32).T.astype(BF16)

    for source in range(sources):
        for t in range(spans):
            for h in range(BLOCK_HEADS):
                queries[source * spans + t, h * SPAN : (h + 1) * SPAN] = query_refs[source][
                    t * SPAN : (t + 1) * SPAN, h * HEAD_SIZE : (h + 1) * HEAD_SIZE
                ]

    factor = HEAD_SIZE ** (-0.5) / math.log(2.0)

    def one_span(q, carry):
        source = q // spans
        distance, cross = source // 2, lax.rem(source, 2)
        device = lax.rem(chip - distance + chips, chips) * 2 + lax.rem(core + cross, 2)
        position = meta[order + device * spans + lax.rem(q, spans)]
        first_row = position * SPAN
        begin = jnp.int32(0)
        at = jnp.int32(0)
        query_pos = lax.broadcasted_iota(jnp.int32, (SPAN, SPAN), 1) + first_row
        query_begin = jnp.zeros((SPAN, SPAN), jnp.int32)
        for d in range(documents):
            begin = jnp.where(at <= first_row, at, begin)
            query_begin = jnp.where(query_pos >= at, at, query_begin)
            at = at + meta[lengths + d]
        count = position - begin // SPAN + 1

        for n in range(1, most + 1):

            @pl.when(count == n)
            def _(n=n):
                held = [slots[position - n + 1 + i] for i in range(n)]
                for i in range(n):
                    key_pos = lax.broadcasted_iota(jnp.int32, (SPAN, SPAN), 0) + (position - n + 1 + i) * SPAN
                    seen = (key_pos <= query_pos) & (key_pos >= query_begin)
                    limits[i * SPAN : (i + 1) * SPAN] = jnp.where(seen, 3e38, -1e30)
                key_part = jnp.concatenate([keys[slot] for slot in held], axis=0)
                value_part = jnp.concatenate([values[slot] for slot in held], axis=1)
                for pair in range(BLOCK_HEADS // 2):
                    query_part = queries[q, pair * 2 * SPAN : (pair + 1) * 2 * SPAN]
                    scores = lax.dot_general(key_part, query_part, NT, preferred_element_type=F32)
                    limit = limits[: n * SPAN]
                    scores = jnp.minimum(scores, jnp.concatenate([limit, limit], axis=1))
                    largest = jnp.max(scores, axis=0, keepdims=True)
                    lifted = jnp.exp2((scores - largest) * factor)
                    total = jnp.sum(lifted, axis=0, keepdims=True)
                    weights = (lifted * (1.0 / total)).astype(BF16)
                    mixed = jnp.dot(value_part, weights, preferred_element_type=F32)
                    for j in range(2):
                        one_head = mixed[:, j * SPAN : (j + 1) * SPAN]
                        columns = slice((pair * 2 + j) * HEAD_SIZE, (pair * 2 + j + 1) * HEAD_SIZE)
                        high, low = split(one_head)
                        for place, part in enumerate((high, low, high)):
                            left[columns, pl.ds(pl.multiple_of((place * all_spans + q) * SPAN, SPAN), SPAN)] = part
                        high, low = split(one_head.T)
                        for place, part in enumerate((high, high, low)):
                            right[pl.ds(pl.multiple_of((place * all_spans + q) * SPAN, SPAN), SPAN), columns] = part

        return carry

    lax.fori_loop(0, all_spans, one_span, 0)

    half = BLOCK_W // 2
    for part in range(2):
        gram = jnp.dot(left[part * half : (part + 1) * half], right[:, part * half :], preferred_element_type=F32)
        for k, panel in ((2 * part, gram[:SPAN]), (2 * part + 1, gram[SPAN:, SPAN:])):
            out[:, STARTS[k] : STARTS[k] + BLOCK_W - SPAN * k] = panel


def factor_kernel(*refs, start, stop):
    width = BLOCK_W - start
    panels = width // SPAN
    step = 32
    groups = step // 8
    per_tile = SPAN // step
    last = stop == BLOCK_W
    if start == 0:
        given, refs = refs[:2], refs[2:]
    else:
        given, refs = refs[:1], refs[1:]
    out, refs = refs[0], refs[1:]
    if not last:
        rest, refs = refs[0], refs[1:]
    work, previous, upper = refs
    if start == 0:
        total = given[0][...] if given[1] is None else given[0][...] + given[1][...]
        rows = lax.broadcasted_iota(jnp.int32, (SPAN, SPAN), 0)
        columns = lax.broadcasted_iota(jnp.int32, (SPAN, SPAN), 1)
        diagonal = rows == columns
        trace = jnp.zeros((1, 1), F32)
        for k in range(PANELS):
            square = total[:, STARTS[k] : STARTS[k] + SPAN]
            trace = trace + jnp.sum(jnp.where(diagonal, square, 0.0), axis=(0, 1), keepdims=True)
        damping = trace * (0.1 / BLOCK_W)
        work[...] = jnp.zeros_like(work)
        for k in range(PANELS):
            panel = total[:, STARTS[k] : STARTS[k] + BLOCK_W - SPAN * k]
            square = jnp.where(diagonal, panel[:, :SPAN] + damping, panel[:, :SPAN])
            work[k * SPAN : (k + 1) * SPAN, k * SPAN : (k + 1) * SPAN] = square
            if k < PANELS - 1:
                work[k * SPAN : (k + 1) * SPAN, (k + 1) * SPAN :] = panel[:, SPAN:]
    else:
        work[...] = given[0][...]
    previous[...] = jnp.zeros_like(previous)

    def triple(value, first):
        high, low = split(value)
        return jnp.concatenate((high, low, high) if first else (high, high, low), axis=0)

    def superpanel(g, carry):
        row = pl.multiple_of(g * step, step)
        tile_index = g // per_tile
        tile = pl.ds(pl.multiple_of(tile_index * SPAN, SPAN), SPAN)
        turn = lax.rem(SPAN - lax.rem(g, per_tile) * step, SPAN)
        before = previous[...]
        right = triple(before, False)
        near = pltpu.roll(previous[:, tile], turn, 1)
        fresh = lax.dot_general(triple(near, True), right, TN, preferred_element_type=F32)[:step]
        current = work[pl.ds(row, step), :] - fresh
        work[...] = work[...] - lax.dot_general(triple(before, True), right, TN, preferred_element_type=F32)

        square = current[:, :SPAN]
        for k in range(1, panels):
            square = jnp.where(tile_index == k, current[:, k * SPAN : (k + 1) * SPAN], square)
        square = pltpu.roll(square, turn, 1)
        line = lax.broadcasted_iota(jnp.int32, (8, SPAN), 0)
        held = [
            {q: jnp.broadcast_to(square[8 * q : 8 * q + 8, j : j + 1], (8, SPAN)) for q in range(j // 8, groups)}
            for j in range(step)
        ]
        body = [[current[8 * q : 8 * q + 8, k * SPAN : (k + 1) * SPAN] for k in range(panels)] for q in range(groups)]
        scales = [jnp.zeros((8, SPAN), F32) for _ in range(groups)]

        def spread(value, i):
            return jnp.broadcast_to(value[i % 8 : i % 8 + 1], (8, SPAN))

        for i in range(step):
            at = i // 8
            root = lax.rsqrt(spread(held[i][at], i))
            inverse = root * root
            scales[at] = jnp.where(line == i % 8, root, scales[at])
            ratio = {q: held[i][q] * inverse for q in range(at, groups)}
            ratio[at] = jnp.where(line > i % 8, ratio[at], 0.0)
            for j in range(i + 1, step):
                entry = spread(held[i][j // 8], j)
                for q in range(j // 8, groups):
                    held[j][q] = held[j][q] - ratio[q] * entry
            for k in range(panels):
                pivot_row = spread(body[at][k], i)
                for q in range(at, groups):
                    body[q][k] = body[q][k] - ratio[q] * pivot_row
        result = jnp.concatenate(
            [jnp.concatenate([body[q][k] * scales[q] for k in range(panels)], axis=1) for q in range(groups)], axis=0
        )
        across = lax.broadcasted_iota(jnp.int32, (step, width), 1)
        down = lax.broadcasted_iota(jnp.int32, (step, width), 0)
        result = jnp.where(across >= down + row, result, 0.0)
        previous[...] = result
        upper[pl.ds(row, step), :] = result
        return carry

    lax.fori_loop(0, (stop - start) // step, superpanel, 0)
    if not last:
        done = stop - start
        before = previous[...]
        final = lax.dot_general(
            triple(before[:, done:], True), triple(before[:, done:], False), TN, preferred_element_type=F32
        )
        rest[...] = work[done:, done:] - final
    ready = [upper[k * SPAN : (k + 1) * SPAN, k * SPAN :] for k in range((stop - start) // SPAN)]
    largest = functools.reduce(jnp.maximum, [jnp.max(jnp.abs(p), axis=(0, 1), keepdims=True) for p in ready])
    write_coded(ready, out, largest)


def whiten_kernel(order, *refs, blocks, start):
    u_refs, refs = refs[:blocks], refs[blocks:]
    w_ref, out, left = refs[0], refs[-2], refs[-1]
    width = BLOCK_W - start
    half = BLOCK_W // 2
    for which in range(blocks):

        @pl.when((pl.program_id(0) == which) & (pl.program_id(1) == 0))
        def _(which=which):
            upper = read_coded(u_refs[which])
            rows = lax.broadcasted_iota(jnp.int32, (SPAN, SPAN), 0)
            columns = lax.broadcasted_iota(jnp.int32, (SPAN, SPAN), 1)
            at = 0
            for k in range(half // SPAN):
                panel = upper[:, at : at + width - SPAN * k]
                at += width - SPAN * k
                pieces = [jnp.zeros((SPAN, SPAN * k), F32)] if k else []
                pieces += [jnp.where(rows > columns, 0.0, panel[:, :SPAN]), panel[:, SPAN:]]
                high, low = split(jnp.concatenate([p for p in pieces if p.shape[1]], axis=1))
                left[k * SPAN : (k + 1) * SPAN] = high
                left[half + k * SPAN : half + (k + 1) * SPAN] = low

    product = jnp.dot(left[...], w_ref[...], preferred_element_type=F32)
    out[0] = product[:half] + product[half:]


def shards(query_rows, key_rows, placed_value_rows, doc_lengths, span_order, out_weight):
    tokens = query_rows.shape[1]
    features = out_weight.shape[0]
    seq = lax.axis_size("seq")
    ring = lax.axis_size("dp")
    chips = seq // 2
    spans = tokens // SPAN
    all_spans = spans * seq
    documents = doc_lengths.shape[1]
    per = KEY_VALUE_HEADS // seq
    blocks = NB // seq
    own = lax.axis_index("seq").astype(jnp.int32)
    place = lax.axis_index("dp").astype(jnp.int32)
    query, key, value = query_rows[0], key_rows[0], placed_value_rows[0]
    vmem = pl.BlockSpec(memory_space=pltpu.VMEM)
    smem = pl.BlockSpec(memory_space=pltpu.SMEM)
    anywhere = pl.BlockSpec(memory_space=pl.ANY)
    in_ring = blocks == ring

    if in_ring:
        turns = [lax.rem(place + 2 * ring - 1 - t, ring) for t in range(blocks)]
    else:
        turns = [jnp.int32(t) for t in range(blocks)]
    first_kv = turns[0] // KV_BLOCKS

    def moved(distance, cross):
        return [
            (x * 2 + c, (x + distance) % chips * 2 + (1 - c if cross else c)) for x in range(chips) for c in range(2)
        ]

    pieces = []
    for t in range(blocks):
        with_kv = t < per
        kv = first_kv if t == 0 else per - 1 - first_kv
        width = BLOCK_W + (2 * HEAD_SIZE if with_kv else 0)
        cut = pl.pallas_call(
            functools.partial(cut_kernel, chips=chips, blocks=blocks, per=per, with_kv=with_kv),
            out_shape=[jax.ShapeDtypeStruct((tokens, width), BF16)] * (seq - 1),
            in_specs=[smem, anywhere, anywhere, anywhere],
            out_specs=[anywhere] * (seq - 1),
            scratch_shapes=[pltpu.SemaphoreType.DMA((3 * (seq - 1),))],
            cost_estimate=cost(0, 2**20),
            name="cut_piece",
        )(jnp.stack([own, turns[t], kv]), query, key, value)
        pieces.append([lax.ppermute(cut[i], "seq", moved((i + 1) // 2, (i + 1) % 2)) for i in range(seq - 1)])

    tile = 512
    turned = pl.pallas_call(
        turn_kernel,
        out_shape=jax.ShapeDtypeStruct((blocks * BLOCK_W, features), BF16),
        grid=(blocks, features // tile),
        in_specs=[pl.BlockSpec((tile, BLOCK_W), lambda b, o: (o, b))],
        out_specs=pl.BlockSpec((BLOCK_W, tile), lambda b, o: (b, o)),
        compiler_params=params(),
        cost_estimate=cost(0, 2**20),
        name="turn_weight",
    )(out_weight)

    most = all_spans // 2 + 1

    def grams_of(t):
        kv = turns[t] // KV_BLOCKS
        carriers = pieces[: min(t + 1, per)]
        which = jnp.where(kv == first_kv, 0, 1).astype(jnp.int32)
        meta = jnp.concatenate([jnp.stack([own, turns[t], kv, which]), doc_lengths[0], span_order[0]])
        return pl.pallas_call(
            functools.partial(
                attention_kernel,
                chips=chips, spans=spans, all_spans=all_spans, documents=documents, most=most, sets=len(carriers),
            ),
            out_shape=jax.ShapeDtypeStruct((SPAN, PACKED), F32),
            grid_spec=pltpu.PrefetchScalarGridSpec(
                num_scalar_prefetch=1,
                grid=(1,),
                in_specs=[pl.BlockSpec((tokens, BLOCK_W), lambda i, meta: (0, meta[0] * blocks + meta[1]))]
                + [pl.BlockSpec((tokens, BLOCK_W), lambda i, meta: (0, 0))] * (seq - 1)
                + [pl.BlockSpec((tokens, HEAD_SIZE), lambda i, meta: (0, meta[0] * per + meta[2]))] * 2
                + [pl.BlockSpec((tokens, 2 * HEAD_SIZE), lambda i, meta: (0, BLOCK_W // (2 * HEAD_SIZE)))]
                * (len(carriers) * (seq - 1)),
                out_specs=pl.BlockSpec((SPAN, PACKED), lambda i, meta: (0, 0)),
                scratch_shapes=[
                    pltpu.VMEM((all_spans, BLOCK_HEADS * SPAN, HEAD_SIZE), BF16),
                    pltpu.VMEM((all_spans, SPAN, HEAD_SIZE), BF16),
                    pltpu.VMEM((all_spans, HEAD_SIZE, SPAN), BF16),
                    pltpu.SMEM((all_spans,), jnp.int32),
                    pltpu.VMEM((most * SPAN, SPAN), F32),
                    pltpu.VMEM((BLOCK_W, 3 * all_spans * SPAN), BF16),
                    pltpu.VMEM((3 * all_spans * SPAN, BLOCK_W), BF16),
                ],
            ),
            compiler_params=params(),
            cost_estimate=cost(0, 2**20),
            name="attention_outer_products",
        )(meta, query, *pieces[t], key, value, *[array for carrier in carriers for array in carrier])

    half = BLOCK_W // 2
    top_width, bottom_width = STARTS[2], PACKED - STARTS[2]
    scratch = lambda width: [pltpu.VMEM((width, width), F32), pltpu.VMEM((32, width), F32), pltpu.VMEM((half, width), F32)]

    def factor_top(*given):
        body = functools.partial(factor_kernel, start=0, stop=half)
        if len(given) == 1:
            body = lambda first, *refs: factor_kernel(first, None, *refs, start=0, stop=half)
        return pl.pallas_call(
            body,
            out_shape=[
                jax.ShapeDtypeStruct((SPAN, top_width), BF16),
                jax.ShapeDtypeStruct((half, half), F32),
            ],
            in_specs=[vmem] * len(given),
            out_specs=[vmem] * 2,
            scratch_shapes=scratch(BLOCK_W),
            compiler_params=params(),
            cost_estimate=cost(0, 2**20),
            name="factor_top",
        )(*given)

    def factor_bottom(rest):
        return pl.pallas_call(
            functools.partial(factor_kernel, start=half, stop=BLOCK_W),
            out_shape=jax.ShapeDtypeStruct((SPAN, bottom_width), BF16),
            in_specs=[vmem],
            out_specs=vmem,
            scratch_shapes=scratch(half),
            compiler_params=params(),
            cost_estimate=cost(0, 2**20),
            name="factor_bottom",
        )(rest)

    if in_ring:
        carried = None
        for t in range(ring - 1):
            partial = grams_of(t)
            if carried is not None:
                partial = partial + carried
            carried = lax.ppermute(partial, "dp", [(z, (z + 1) % ring) for z in range(ring)])
        top, rest = factor_top(grams_of(ring - 1), carried)

        def shared(array):
            return [array] + [
                lax.ppermute(array, "dp", [(z, (z + d) % ring) for z in range(ring)]) for d in range(1, ring)
            ]

        tops = shared(top)
        bottoms = shared(factor_bottom(rest))
        order = jnp.stack([lax.rem(place - d + ring, ring) for d in range(ring)])
    else:
        summed = lax.psum(jnp.stack([grams_of(t) for t in range(blocks)]), "dp")
        halves = [factor_top(summed[t]) for t in range(blocks)]
        tops = [top for top, _ in halves]
        bottoms = [factor_bottom(rest) for _, rest in halves]
        order = jnp.arange(blocks, dtype=jnp.int32)

    wide = 1024

    def whiten(uppers, start, result):
        more = [] if result is None else [result]
        depth = BLOCK_W - start
        return pl.pallas_call(
            functools.partial(whiten_kernel, blocks=blocks, start=start),
            out_shape=jax.ShapeDtypeStruct((blocks, BLOCK_W, features), F32),
            grid_spec=pltpu.PrefetchScalarGridSpec(
                num_scalar_prefetch=1,
                grid=(blocks, features // wide),
                in_specs=[vmem] * blocks
                + [pl.BlockSpec((depth, wide), lambda b, o, order: (order[b] * (BLOCK_W // depth) + start // depth, o))]
                + [anywhere] * len(more),
                out_specs=pl.BlockSpec((1, half, wide), lambda b, o, order: (order[b], start // half, o)),
                scratch_shapes=[pltpu.VMEM((2 * half, depth), BF16)],
            ),
            input_output_aliases={blocks + 2: 0} if more else {},
            compiler_params=params(),
            cost_estimate=cost(0, 2**20),
            name="whiten_bottom" if start else "whiten_top",
        )(order, *uppers, turned, *more)

    return whiten(bottoms, half, whiten(tops, 0, None))


def solution(mesh):
    in_specs = (
        P(("groups", "dp"), "seq", None),
        P(("groups", "dp"), "seq", None),
        P(("groups", "dp"), "seq", None),
        P(("groups", "dp"), None),
        P(("groups", "dp"), None),
        P("dp", "seq"),
    )
    out_specs = P(("groups", "seq"), None, "dp")
    return jax.shard_map(shards, mesh=mesh, in_specs=in_specs, out_specs=out_specs, check_vma=False)
```

```python
import functools
import math

import jax
import jax.numpy as jnp
from jax import lax
from jax.experimental import pallas as pl
from jax.experimental.pallas import tpu as pltpu
from jax.sharding import PartitionSpec as P

QUERY_HEADS = 64
KEY_VALUE_HEADS = 8
HEAD_SIZE = 128
BLOCK_W = 512
NB = 16
SPAN = 128
GROUP = QUERY_HEADS // KEY_VALUE_HEADS
BLOCK_HEADS = BLOCK_W // HEAD_SIZE
KV_BLOCKS = GROUP // BLOCK_HEADS
PANELS = BLOCK_W // SPAN
STARTS = [sum(BLOCK_W - SPAN * j for j in range(k)) for k in range(PANELS)]
PACKED = sum(BLOCK_W - SPAN * j for j in range(PANELS))
VMEM_BYTES = 50 * 1024 * 1024
F32 = jnp.float32
BF16 = jnp.bfloat16
NT = (((1,), (1,)), ((), ()))
TN = (((0,), (0,)), ((), ()))


def params(limit=VMEM_BYTES):
    return pltpu.CompilerParams(vmem_limit_bytes=limit)


def cost(flops, moved, trans=0):
    return pl.CostEstimate(flops=int(flops), bytes_accessed=int(moved), transcendentals=int(trans))


def encode(value, exponent):
    scaled = value * jnp.exp2(15.0 - exponent)
    power = scaled * scaled
    power = power * power
    power = power * power
    return jnp.where(scaled < 0.0, -power, power)


def decode(code, exponent):
    code = code.astype(F32)
    root = jnp.exp2(jnp.log(jnp.maximum(jnp.abs(code), 1e-37)) * (0.125 / math.log(2.0)) + (exponent - 15.0))
    return jnp.where(code < 0.0, -root, root)


def marker():
    rows = lax.broadcasted_iota(jnp.int32, (SPAN, SPAN), 0)
    columns = lax.broadcasted_iota(jnp.int32, (SPAN, SPAN), 1)
    return (rows == SPAN - 1) & (columns == 0)


def exponent_of(largest):
    return jnp.ceil(jnp.log(jnp.maximum(largest, 1e-30)) * (1.0 / math.log(2.0)) + 0.001)


def write_coded(panels, out, largest):
    exponent = exponent_of(largest)
    at = 0
    for k, panel in enumerate(panels):
        coded = encode(panel, exponent)
        if k == 0:
            first = jnp.where(marker(), jnp.broadcast_to(exponent, (SPAN, SPAN)), coded[:, :SPAN])
            coded = jnp.concatenate([first, coded[:, SPAN:]], axis=1)
        out[:, at : at + panel.shape[1]] = coded.astype(BF16)
        at += panel.shape[1]


def read_coded(ref):
    exponent = ref[SPAN - 16 : SPAN, :SPAN].astype(F32)[15:16, 0:1]
    return decode(ref[...], exponent)


def split(value):
    high = value.astype(BF16)
    return high, (value - high.astype(F32)).astype(BF16)


def cut_kernel(meta, *refs, given):
    out = refs[-1]
    at = 0
    for ref in refs[:given]:
        out[:, at : at + ref.shape[1]] = ref[...]
        at += ref.shape[1]


def turn_kernel(w_ref, out):
    out[...] = w_ref[...].T


def attention_kernel(meta, *refs, chips, spans, all_spans, documents, most, sets):
    sources = 2 * chips
    near = sources + 4
    query_refs, near_refs = refs[:sources], refs[sources:near]
    far_refs = refs[near : near + sets * (sources - 2)]
    out_top, out_bottom, queries, keys, values, slots, limits, left, right, total = refs[near + sets * (sources - 2) :]
    own = meta[0]
    chip, core = own // 2, lax.rem(own, 2)
    lengths = 4
    order = lengths + documents

    for r in range(all_spans):
        device = r // spans
        distance = lax.rem(chip - device // 2 + chips, chips)
        cross = lax.rem(core + device % 2, 2)
        slots[meta[order + r]] = (distance * 2 + cross) * spans + r % spans

    def place_kv(source, key_part, value_part):
        for t in range(spans):
            rows = slice(t * SPAN, (t + 1) * SPAN)
            keys[source * spans + t] = key_part[rows]
            values[source * spans + t] = value_part[rows].astype(F32).T.astype(BF16)

    place_kv(0, near_refs[0], near_refs[1])
    place_kv(1, near_refs[2], near_refs[3])
    for which in range(sets):

        @pl.when(meta[3] == which)
        def _(which=which):
            for source in range(2, sources):
                ref = far_refs[which * (sources - 2) + source - 2]
                place_kv(source, ref[:, :HEAD_SIZE], ref[:, HEAD_SIZE:])

    for source in range(sources):
        for t in range(spans):
            for h in range(BLOCK_HEADS):
                queries[source * spans + t, h * SPAN : (h + 1) * SPAN] = query_refs[source][
                    t * SPAN : (t + 1) * SPAN, h * HEAD_SIZE : (h + 1) * HEAD_SIZE
                ]

    factor = HEAD_SIZE ** (-0.5) / math.log(2.0)

    def one_span(q, carry):
        source = q // spans
        distance, cross = source // 2, lax.rem(source, 2)
        device = lax.rem(chip - distance + chips, chips) * 2 + lax.rem(core + cross, 2)
        position = meta[order + device * spans + lax.rem(q, spans)]
        first_row = position * SPAN
        begin = jnp.int32(0)
        at = jnp.int32(0)
        query_pos = lax.broadcasted_iota(jnp.int32, (1, SPAN), 1) + first_row
        query_begin = jnp.zeros((1, SPAN), jnp.int32)
        for d in range(documents):
            begin = jnp.where(at <= first_row, at, begin)
            query_begin = jnp.where(query_pos >= at, at, query_begin)
            at = at + meta[lengths + d]
        count = position - begin // SPAN + 1
        lanes = pl.ds(pl.multiple_of(q * SPAN, SPAN), SPAN)

        for n in range(1, most + 1):

            @pl.when(count == n)
            def _(n=n):
                held = [slots[position - n + 1 + i] for i in range(n)]
                for i in range(n):
                    key_pos = lax.broadcasted_iota(jnp.int32, (SPAN, SPAN), 0) + (position - n + 1 + i) * SPAN
                    seen = (key_pos <= query_pos) & (key_pos >= query_begin)
                    limits[i * SPAN : (i + 1) * SPAN] = jnp.where(seen, 3e38, -1e30)
                key_part = jnp.concatenate([keys[slot] for slot in held], axis=0)
                value_part = jnp.concatenate([values[slot] for slot in held], axis=1)
                scores = lax.dot_general(key_part, queries[q], NT, preferred_element_type=F32)
                limit = limits[: n * SPAN]
                scores = jnp.minimum(scores, jnp.concatenate([limit] * BLOCK_HEADS, axis=1))
                largest = jnp.max(scores, axis=0, keepdims=True)
                lifted = jnp.exp2((scores - largest) * factor)
                summed = jnp.sum(lifted, axis=0, keepdims=True)
                weights = (lifted * (1.0 / summed)).astype(BF16)
                mixed = jnp.dot(value_part, weights, preferred_element_type=F32)
                for h in range(BLOCK_HEADS):
                    one_head = mixed[:, h * SPAN : (h + 1) * SPAN]
                    columns = slice(h * HEAD_SIZE, (h + 1) * HEAD_SIZE)
                    high, low = split(one_head)
                    left[0, columns, lanes] = high
                    left[1, columns, lanes] = low
                    high, low = split(one_head.T)
                    right[0, lanes, columns] = high
                    right[1, lanes, columns] = low

        return carry

    lax.fori_loop(0, all_spans, one_span, 0)

    half = BLOCK_W // 2
    total[...] = jnp.zeros_like(total)

    def one_pass(i, carry):
        a, b = lax.rem(i, 2), i // 2
        total[:half] += jnp.dot(left[a, :half], right[b], preferred_element_type=F32)
        total[half:, half:] += jnp.dot(left[a, half:], right[b, :, half:], preferred_element_type=F32)
        return carry

    lax.fori_loop(0, 3, one_pass, 0)
    for out, packed in zip((out_top, out_bottom), fold(total)):
        out[...] = packed


def tile_of(ref, i, j):
    return ref[i * SPAN : (i + 1) * SPAN, j * SPAN : (j + 1) * SPAN]


def diagonal_masks():
    rows = lax.broadcasted_iota(jnp.int32, (SPAN, SPAN), 0)
    columns = lax.broadcasted_iota(jnp.int32, (SPAN, SPAN), 1)
    return rows <= columns, rows == columns


def fold(ref):
    upper, equal = diagonal_masks()
    for off, (a, b) in ((((0, 1), (0, 2), (0, 3)), (0, 1)), (((1, 2), (1, 3), (2, 3)), (2, 3))):
        second = tile_of(ref, b, b)
        square = jnp.where(upper, tile_of(ref, a, a), second)
        line = jnp.sum(jnp.where(equal, second, 0.0), axis=0, keepdims=True)
        body = jnp.concatenate([tile_of(ref, *where) for where in off] + [square], axis=1)
        tail = jnp.concatenate([jnp.zeros((8, 3 * SPAN), F32), jnp.broadcast_to(line, (8, SPAN))], axis=1)
        yield jnp.concatenate([body, tail], axis=0)


def unfold(packs, work):
    upper, equal = diagonal_masks()
    trace = jnp.zeros((1, 1), F32)
    squares = []
    for pack, off, (a, b) in zip(
        packs, (((0, 1), (0, 2), (0, 3)), ((1, 2), (1, 3), (2, 3))), ((0, 1), (2, 3))
    ):
        for i, (row, column) in enumerate(off):
            work[row * SPAN : (row + 1) * SPAN, column * SPAN : (column + 1) * SPAN] = pack[:SPAN, i * SPAN : (i + 1) * SPAN]
        square = pack[:SPAN, 3 * SPAN :]
        turned = square.T
        line = jnp.broadcast_to(pack[SPAN : SPAN + 1, 3 * SPAN :], (SPAN, SPAN))
        squares.append((a, jnp.where(upper, square, turned)))
        squares.append((b, jnp.where(equal, line, jnp.where(upper, turned, square))))
    for _, square in squares:
        trace = trace + jnp.sum(jnp.where(equal, square, 0.0), axis=(0, 1), keepdims=True)
    damping = trace * (0.1 / BLOCK_W)
    for a, square in squares:
        work[a * SPAN : (a + 1) * SPAN, a * SPAN : (a + 1) * SPAN] = jnp.where(equal, square + damping, square)


def factor_kernel(*refs, start, stop, received):
    width = BLOCK_W - start
    panels = width // SPAN
    step = 32
    groups = step // 8
    per_tile = SPAN // step
    last = stop == BLOCK_W
    given, refs = (refs[:received], refs[received:])
    out, refs = refs[0], refs[1:]
    if not last:
        rest, refs = refs[0], refs[1:]
    work, previous, upper = refs
    if start == 0:
        work[...] = jnp.zeros_like(work)
        packs = [given[0][...], given[1][...]]
        if received == 4:
            packs = [packs[0] + given[2][...], packs[1] + given[3][...]]
        unfold(packs, work)
    else:
        work[...] = given[0][...]
    previous[...] = jnp.zeros_like(previous)

    def triple(value, first):
        high, low = split(value)
        return jnp.concatenate((high, low, high) if first else (high, high, low), axis=0)

    def superpanel(g, carry):
        row = pl.multiple_of(g * step, step)
        tile_index = g // per_tile
        tile = pl.ds(pl.multiple_of(tile_index * SPAN, SPAN), SPAN)
        turn = lax.rem(SPAN - lax.rem(g, per_tile) * step, SPAN)
        before = previous[...]
        right = triple(before, False)
        near = pltpu.roll(previous[:, tile], turn, 1)
        fresh = lax.dot_general(triple(near, True), right, TN, preferred_element_type=F32)[:step]
        current = work[pl.ds(row, step), :] - fresh
        work[...] = work[...] - lax.dot_general(triple(before, True), right, TN, preferred_element_type=F32)

        square = current[:, :SPAN]
        for k in range(1, panels):
            square = jnp.where(tile_index == k, current[:, k * SPAN : (k + 1) * SPAN], square)
        square = pltpu.roll(square, turn, 1)
        line = lax.broadcasted_iota(jnp.int32, (8, SPAN), 0)
        held = [
            {q: jnp.broadcast_to(square[8 * q : 8 * q + 8, j : j + 1], (8, SPAN)) for q in range(j // 8, groups)}
            for j in range(step)
        ]
        body = [[current[8 * q : 8 * q + 8, k * SPAN : (k + 1) * SPAN] for k in range(panels)] for q in range(groups)]
        scales = [jnp.zeros((8, SPAN), F32) for _ in range(groups)]

        def spread(value, i):
            return jnp.broadcast_to(value[i % 8 : i % 8 + 1], (8, SPAN))

        for i in range(step):
            at = i // 8
            root = lax.rsqrt(spread(held[i][at], i))
            inverse = root * root
            scales[at] = jnp.where(line == i % 8, root, scales[at])
            ratio = {q: held[i][q] * inverse for q in range(at, groups)}
            ratio[at] = jnp.where(line > i % 8, ratio[at], 0.0)
            for j in range(i + 1, step):
                entry = spread(held[i][j // 8], j)
                for q in range(j // 8, groups):
                    held[j][q] = held[j][q] - ratio[q] * entry
            for k in range(panels):
                pivot_row = spread(body[at][k], i)
                for q in range(at, groups):
                    body[q][k] = body[q][k] - ratio[q] * pivot_row
        result = jnp.concatenate(
            [jnp.concatenate([body[q][k] * scales[q] for k in range(panels)], axis=1) for q in range(groups)], axis=0
        )
        across = lax.broadcasted_iota(jnp.int32, (step, width), 1)
        down = lax.broadcasted_iota(jnp.int32, (step, width), 0)
        result = jnp.where(across >= down + row, result, 0.0)
        previous[...] = result
        upper[pl.ds(row, step), :] = result
        return carry

    lax.fori_loop(0, (stop - start) // step, superpanel, 0)
    if not last:
        done = stop - start
        before = previous[...]
        final = lax.dot_general(
            triple(before[:, done:], True), triple(before[:, done:], False), TN, preferred_element_type=F32
        )
        rest[...] = work[done:, done:] - final
    ready = [upper[k * SPAN : (k + 1) * SPAN, k * SPAN :] for k in range((stop - start) // SPAN)]
    largest = functools.reduce(jnp.maximum, [jnp.max(jnp.abs(p), axis=(0, 1), keepdims=True) for p in ready])
    write_coded(ready, out, largest)


def whiten_kernel(order, *refs, blocks, start):
    u_refs, refs = refs[:blocks], refs[blocks:]
    w_ref, out, left = refs[0], refs[-2], refs[-1]
    width = BLOCK_W - start
    half = BLOCK_W // 2
    for which in range(blocks):

        @pl.when((pl.program_id(0) == which) & (pl.program_id(1) == 0))
        def _(which=which):
            upper = read_coded(u_refs[which])
            rows = lax.broadcasted_iota(jnp.int32, (SPAN, SPAN), 0)
            columns = lax.broadcasted_iota(jnp.int32, (SPAN, SPAN), 1)
            at = 0
            for k in range(half // SPAN):
                panel = upper[:, at : at + width - SPAN * k]
                at += width - SPAN * k
                pieces = [jnp.zeros((SPAN, SPAN * k), F32)] if k else []
                pieces += [jnp.where(rows > columns, 0.0, panel[:, :SPAN]), panel[:, SPAN:]]
                high, low = split(jnp.concatenate([p for p in pieces if p.shape[1]], axis=1))
                left[k * SPAN : (k + 1) * SPAN] = high
                left[half + k * SPAN : half + (k + 1) * SPAN] = low

    product = jnp.dot(left[...], w_ref[...], preferred_element_type=F32)
    out[0] = product[:half] + product[half:]


def shards(query_rows, key_rows, placed_value_rows, doc_lengths, span_order, out_weight):
    tokens = query_rows.shape[1]
    features = out_weight.shape[0]
    seq = lax.axis_size("seq")
    ring = lax.axis_size("dp")
    chips = seq // 2
    spans = tokens // SPAN
    all_spans = spans * seq
    documents = doc_lengths.shape[1]
    per = KEY_VALUE_HEADS // seq
    blocks = NB // seq
    own = lax.axis_index("seq").astype(jnp.int32)
    place = lax.axis_index("dp").astype(jnp.int32)
    query, key, value = query_rows[0], key_rows[0], placed_value_rows[0]
    vmem = pl.BlockSpec(memory_space=pltpu.VMEM)
    anywhere = pl.BlockSpec(memory_space=pl.ANY)
    in_ring = blocks == ring

    if in_ring:
        turns = [lax.rem(place + 2 * ring - 1 - t, ring) for t in range(blocks)]
    else:
        turns = [jnp.int32(t) for t in range(blocks)]
    first_kv = turns[0] // KV_BLOCKS

    def moved(distance, cross):
        return [
            (x * 2 + c, (x + distance) % chips * 2 + (1 - c if cross else c)) for x in range(chips) for c in range(2)
        ]

    def cut(target, columns, scalars, name, after=()):
        specs = [
            pl.BlockSpec((tokens, size), lambda i, meta, index=index: (0, index(target(meta), meta)))
            for _, size, index in columns
        ]
        arrays = [array for array, _, _ in columns]
        width = sum(size for _, size, _ in columns)
        return pl.pallas_call(
            functools.partial(cut_kernel, given=len(columns)),
            out_shape=jax.ShapeDtypeStruct((tokens, width), BF16),
            grid_spec=pltpu.PrefetchScalarGridSpec(
                num_scalar_prefetch=1,
                grid=(1,),
                in_specs=specs + [anywhere] * len(after),
                out_specs=pl.BlockSpec((tokens, width), lambda i, meta: (0, 0)),
            ),
            compiler_params=params(),
            cost_estimate=cost(0, 2**21),
            name=name,
        )(scalars, *arrays, *after)

    def target_at(distance, cross):
        return lambda meta: lax.rem(meta[0] // 2 + distance, chips) * 2 + lax.rem(lax.rem(meta[0], 2) + cross, 2)

    far = [(distance, cross) for distance in range(1, chips) for cross in range(2)]
    pieces = []

    most = all_spans // 2 + 1

    def grams_of(t, peer):
        kv = turns[t] // KV_BLOCKS
        carriers = pieces[: min(t + 1, per)]
        which = jnp.where(kv == first_kv, 0, 1).astype(jnp.int32)
        meta = jnp.concatenate([jnp.stack([own, turns[t], kv, which]), doc_lengths[0], span_order[0]])
        folded = jax.ShapeDtypeStruct((SPAN + 8, BLOCK_W), F32)
        peer_kv = blocks * BLOCK_W // HEAD_SIZE
        return pl.pallas_call(
            functools.partial(
                attention_kernel,
                chips=chips, spans=spans, all_spans=all_spans, documents=documents, most=most, sets=len(carriers),
            ),
            out_shape=[folded] * 2,
            grid_spec=pltpu.PrefetchScalarGridSpec(
                num_scalar_prefetch=1,
                grid=(1,),
                in_specs=[
                    pl.BlockSpec((tokens, BLOCK_W), lambda i, meta: (0, meta[0] * blocks + meta[1])),
                    pl.BlockSpec((tokens, BLOCK_W), lambda i, meta: (0, meta[1])),
                ]
                + [pl.BlockSpec((tokens, BLOCK_W), lambda i, meta: (0, 0))] * len(far)
                + [pl.BlockSpec((tokens, HEAD_SIZE), lambda i, meta: (0, meta[0] * per + meta[2]))] * 2
                + [
                    pl.BlockSpec((tokens, HEAD_SIZE), lambda i, meta: (0, peer_kv + meta[2])),
                    pl.BlockSpec((tokens, HEAD_SIZE), lambda i, meta: (0, peer_kv + per + meta[2])),
                ]
                + [pl.BlockSpec((tokens, 2 * HEAD_SIZE), lambda i, meta: (0, BLOCK_W // (2 * HEAD_SIZE)))]
                * (len(carriers) * len(far)),
                out_specs=[pl.BlockSpec((SPAN + 8, BLOCK_W), lambda i, meta: (0, 0))] * 2,
                scratch_shapes=[
                    pltpu.VMEM((all_spans, BLOCK_HEADS * SPAN, HEAD_SIZE), BF16),
                    pltpu.VMEM((all_spans, SPAN, HEAD_SIZE), BF16),
                    pltpu.VMEM((all_spans, HEAD_SIZE, SPAN), BF16),
                    pltpu.SMEM((all_spans,), jnp.int32),
                    pltpu.VMEM((most * SPAN, SPAN), F32),
                    pltpu.VMEM((2, BLOCK_W, all_spans * SPAN), BF16),
                    pltpu.VMEM((2, all_spans * SPAN, BLOCK_W), BF16),
                    pltpu.VMEM((BLOCK_W, BLOCK_W), F32),
                ],
            ),
            compiler_params=params(),
            cost_estimate=cost(1.4e10, 2**20),
            name="attention_outer_products",
        )(meta, query, peer, *pieces[t], key, value, peer, peer, *[array for carrier in carriers for array in carrier])

    grams = []
    for t in range(blocks):
        kv = first_kv if t == 0 else per - 1 - first_kv
        columns = [(query, BLOCK_W, lambda target, meta: target * blocks + meta[1])]
        if t < per:
            columns += [(array, HEAD_SIZE, lambda target, meta: target * per + meta[2]) for array in (key, value)]
        scalars = jnp.stack([own, turns[t], kv])
        piece = []
        for i, where in enumerate(far):
            after = ([pieces[-1][i]] if t else []) + ([grams[t - 2][0]] if t > 1 else [])
            part = cut(target_at(*where), columns, scalars, "cut_piece", after)
            piece.append(lax.ppermute(part, "seq", moved(*where)))
        pieces.append(piece)
        if t == 0:
            columns = [(query, blocks * BLOCK_W, lambda target, meta: target)]
            columns += [(array, per * HEAD_SIZE, lambda target, meta: target) for array in (key, value)]
            peer = lax.ppermute(cut(target_at(0, 1), columns, own[None], "cut_peer"), "seq", moved(0, 1))
        grams.append(grams_of(t, peer))

    tile = 512
    turned = pl.pallas_call(
        turn_kernel,
        out_shape=jax.ShapeDtypeStruct((blocks * BLOCK_W, features), BF16),
        grid=(blocks, features // tile),
        in_specs=[pl.BlockSpec((tile, BLOCK_W), lambda b, o: (o, b))],
        out_specs=pl.BlockSpec((BLOCK_W, tile), lambda b, o: (b, o)),
        compiler_params=params(),
        cost_estimate=cost(1.4e10, 2**20),
        name="turn_weight",
    )(out_weight)

    half = BLOCK_W // 2
    top_width, bottom_width = STARTS[2], PACKED - STARTS[2]
    scratch = lambda width: [pltpu.VMEM((width, width), F32), pltpu.VMEM((32, width), F32), pltpu.VMEM((half, width), F32)]

    def factor_top(*given):
        return pl.pallas_call(
            functools.partial(factor_kernel, start=0, stop=half, received=len(given)),
            out_shape=[
                jax.ShapeDtypeStruct((SPAN, top_width), BF16),
                jax.ShapeDtypeStruct((half, half), F32),
            ],
            in_specs=[vmem] * len(given),
            out_specs=[vmem] * 2,
            scratch_shapes=scratch(BLOCK_W),
            compiler_params=params(),
            cost_estimate=cost(1.0e10, 2**20),
            name="factor_top",
        )(*given)

    def factor_bottom(rest):
        return pl.pallas_call(
            functools.partial(factor_kernel, start=half, stop=BLOCK_W, received=1),
            out_shape=jax.ShapeDtypeStruct((SPAN, bottom_width), BF16),
            in_specs=[vmem],
            out_specs=vmem,
            scratch_shapes=scratch(half),
            compiler_params=params(),
            cost_estimate=cost(0.9e10, 2**20),
            name="factor_bottom",
        )(rest)

    if in_ring:
        carried = []
        for t in range(ring - 1):
            partial = grams[t]
            if carried:
                partial = [mine + theirs for mine, theirs in zip(partial, carried)]
            carried = [lax.ppermute(part, "dp", [(z, (z + 1) % ring) for z in range(ring)]) for part in partial]
        top, rest = factor_top(*grams[ring - 1], *carried)

        def shared(array):
            return [array] + [
                lax.ppermute(array, "dp", [(z, (z + d) % ring) for z in range(ring)]) for d in range(1, ring)
            ]

        tops = shared(top)
        bottoms = shared(factor_bottom(rest))
        order = jnp.stack([lax.rem(place - d + ring, ring) for d in range(ring)])
    else:
        halves = [factor_top(*[lax.psum(part, "dp") for part in grams[t]]) for t in range(blocks)]
        tops = [top for top, _ in halves]
        bottoms = [factor_bottom(rest) for _, rest in halves]
        order = jnp.arange(blocks, dtype=jnp.int32)

    wide = min(2048, features)

    def whiten(uppers, start, result):
        more = [] if result is None else [result]
        depth = BLOCK_W - start
        return pl.pallas_call(
            functools.partial(whiten_kernel, blocks=blocks, start=start),
            out_shape=jax.ShapeDtypeStruct((blocks, BLOCK_W, features), F32),
            grid_spec=pltpu.PrefetchScalarGridSpec(
                num_scalar_prefetch=1,
                grid=(blocks, features // wide),
                in_specs=[vmem] * blocks
                + [pl.BlockSpec((depth, wide), lambda b, o, order: (order[b] * (BLOCK_W // depth) + start // depth, o))]
                + [anywhere] * len(more),
                out_specs=pl.BlockSpec((1, half, wide), lambda b, o, order: (order[b], start // half, o)),
                scratch_shapes=[pltpu.VMEM((2 * half, depth), BF16)],
            ),
            input_output_aliases={blocks + 2: 0} if more else {},
            compiler_params=params(),
            cost_estimate=cost(1.0e10, 2**20),
            name="whiten_bottom" if start else "whiten_top",
        )(order, *uppers, turned, *more)

    return whiten(bottoms, half, whiten(tops, 0, None))


def solution(mesh):
    in_specs = (
        P(("groups", "dp"), "seq", None),
        P(("groups", "dp"), "seq", None),
        P(("groups", "dp"), "seq", None),
        P(("groups", "dp"), None),
        P(("groups", "dp"), None),
        P("dp", "seq"),
    )
    out_specs = P(("groups", "seq"), None, "dp")
    return jax.shard_map(shards, mesh=mesh, in_specs=in_specs, out_specs=out_specs, check_vma=False)
```

```python
import functools
import math

import jax
import jax.numpy as jnp
from jax import lax
from jax.experimental import pallas as pl
from jax.experimental.pallas import tpu as pltpu
from jax.sharding import PartitionSpec as P

QUERY_HEADS = 64
KEY_VALUE_HEADS = 8
HEAD_SIZE = 128
BLOCK_W = 512
NB = 16
SPAN = 128
GROUP = QUERY_HEADS // KEY_VALUE_HEADS
BLOCK_HEADS = BLOCK_W // HEAD_SIZE
KV_BLOCKS = GROUP // BLOCK_HEADS
PANELS = BLOCK_W // SPAN
STARTS = [sum(BLOCK_W - SPAN * j for j in range(k)) for k in range(PANELS)]
PACKED = sum(BLOCK_W - SPAN * j for j in range(PANELS))
VMEM_BYTES = 50 * 1024 * 1024
F32 = jnp.float32
BF16 = jnp.bfloat16
NT = (((1,), (1,)), ((), ()))
TN = (((0,), (0,)), ((), ()))


def params(limit=VMEM_BYTES):
    return pltpu.CompilerParams(vmem_limit_bytes=limit)


def cost(flops, moved, trans=0):
    return pl.CostEstimate(flops=int(flops), bytes_accessed=int(moved), transcendentals=int(trans))


def encode(value, exponent):
    scaled = value * jnp.exp2(15.0 - exponent)
    power = scaled * scaled
    power = power * power
    power = power * power
    return jnp.where(scaled < 0.0, -power, power)


def decode(code, exponent):
    code = code.astype(F32)
    root = jnp.exp2(jnp.log(jnp.maximum(jnp.abs(code), 1e-37)) * (0.125 / math.log(2.0)) + (exponent - 15.0))
    return jnp.where(code < 0.0, -root, root)


def marker():
    rows = lax.broadcasted_iota(jnp.int32, (SPAN, SPAN), 0)
    columns = lax.broadcasted_iota(jnp.int32, (SPAN, SPAN), 1)
    return (rows == SPAN - 1) & (columns == 0)


def exponent_of(largest):
    return jnp.ceil(jnp.log(jnp.maximum(largest, 1e-30)) * (1.0 / math.log(2.0)) + 0.001)


def write_coded(panels, out, largest):
    exponent = exponent_of(largest)
    at = 0
    for k, panel in enumerate(panels):
        coded = encode(panel, exponent)
        if k == 0:
            first = jnp.where(marker(), jnp.broadcast_to(exponent, (SPAN, SPAN)), coded[:, :SPAN])
            coded = jnp.concatenate([first, coded[:, SPAN:]], axis=1)
        out[:, at : at + panel.shape[1]] = coded.astype(BF16)
        at += panel.shape[1]


def read_coded(ref):
    exponent = ref[SPAN - 16 : SPAN, :SPAN].astype(F32)[15:16, 0:1]
    return decode(ref[...], exponent)


def split(value):
    high = value.astype(BF16)
    return high, (value - high.astype(F32)).astype(BF16)


def cut_kernel(meta, *refs, targets, given):
    outs = refs[-targets:]
    for number, out in enumerate(outs):
        at = 0
        for ref in refs[number * given : (number + 1) * given]:
            out[:, at : at + ref.shape[1]] = ref[...]
            at += ref.shape[1]


def turn_kernel(w_ref, *refs):
    refs[-1][...] = w_ref[...].T


def attention_kernel(meta, *refs, chips, spans, all_spans, documents, most, sets):
    sources = 2 * chips
    near = sources + 4
    query_refs, near_refs = refs[:sources], refs[sources:near]
    far_refs = refs[near : near + sets * (sources - 2)]
    out, queries, keys, values, slots, limits, left, right, total = refs[near + sets * (sources - 2) :]
    own = meta[0]
    chip, core = own // 2, lax.rem(own, 2)
    lengths = 4
    order = lengths + documents

    for r in range(all_spans):
        device = r // spans
        distance = lax.rem(chip - device // 2 + chips, chips)
        cross = lax.rem(core + device % 2, 2)
        slots[meta[order + r]] = (distance * 2 + cross) * spans + r % spans

    def place_kv(source, key_part, value_part):
        for t in range(spans):
            rows = slice(t * SPAN, (t + 1) * SPAN)
            keys[source * spans + t] = key_part[rows]
            values[source * spans + t] = value_part[rows].astype(F32).T.astype(BF16)

    place_kv(0, near_refs[0], near_refs[1])
    place_kv(1, near_refs[2], near_refs[3])
    for which in range(sets):

        @pl.when(meta[3] == which)
        def _(which=which):
            for source in range(2, sources):
                ref = far_refs[which * (sources - 2) + source - 2]
                place_kv(source, ref[:, :HEAD_SIZE], ref[:, HEAD_SIZE:])

    for source in range(sources):
        for t in range(spans):
            for h in range(BLOCK_HEADS):
                queries[source * spans + t, h * SPAN : (h + 1) * SPAN] = query_refs[source][
                    t * SPAN : (t + 1) * SPAN, h * HEAD_SIZE : (h + 1) * HEAD_SIZE
                ]

    factor = HEAD_SIZE ** (-0.5) / math.log(2.0)

    def one_span(q, carry):
        source = q // spans
        distance, cross = source // 2, lax.rem(source, 2)
        device = lax.rem(chip - distance + chips, chips) * 2 + lax.rem(core + cross, 2)
        position = meta[order + device * spans + lax.rem(q, spans)]
        first_row = position * SPAN
        begin = jnp.int32(0)
        at = jnp.int32(0)
        query_pos = lax.broadcasted_iota(jnp.int32, (1, SPAN), 1) + first_row
        query_begin = jnp.zeros((1, SPAN), jnp.int32)
        for d in range(documents):
            begin = jnp.where(at <= first_row, at, begin)
            query_begin = jnp.where(query_pos >= at, at, query_begin)
            at = at + meta[lengths + d]
        count = position - begin // SPAN + 1
        lanes = pl.ds(pl.multiple_of(q * SPAN, SPAN), SPAN)

        for n in range(1, most + 1):

            @pl.when(count == n)
            def _(n=n):
                held = [slots[position - n + 1 + i] for i in range(n)]
                for i in range(n):
                    key_pos = lax.broadcasted_iota(jnp.int32, (SPAN, SPAN), 0) + (position - n + 1 + i) * SPAN
                    seen = (key_pos <= query_pos) & (key_pos >= query_begin)
                    limits[i * SPAN : (i + 1) * SPAN] = jnp.where(seen, 3e38, -1e30)
                key_part = jnp.concatenate([keys[slot] for slot in held], axis=0)
                value_part = jnp.concatenate([values[slot] for slot in held], axis=1)
                scores = lax.dot_general(key_part, queries[q], NT, preferred_element_type=F32)
                limit = limits[: n * SPAN]
                scores = jnp.minimum(scores, jnp.concatenate([limit] * BLOCK_HEADS, axis=1))
                largest = jnp.max(scores, axis=0, keepdims=True)
                lifted = jnp.exp2((scores - largest) * factor)
                summed = jnp.sum(lifted, axis=0, keepdims=True)
                weights = (lifted * (1.0 / summed)).astype(BF16)
                mixed = jnp.dot(value_part, weights, preferred_element_type=F32)
                for h in range(BLOCK_HEADS):
                    one_head = mixed[:, h * SPAN : (h + 1) * SPAN]
                    columns = slice(h * HEAD_SIZE, (h + 1) * HEAD_SIZE)
                    high, low = split(one_head)
                    left[0, columns, lanes] = high
                    left[1, columns, lanes] = low
                    high, low = split(one_head.T)
                    right[0, lanes, columns] = high
                    right[1, lanes, columns] = low

        return carry

    lax.fori_loop(0, all_spans, one_span, 0)

    half = BLOCK_W // 2
    total[...] = jnp.zeros_like(total)

    def one_pass(i, carry):
        a, b = lax.rem(i, 2), i // 2
        total[:half] += jnp.dot(left[a, :half], right[b], preferred_element_type=F32)
        total[half:, half:] += jnp.dot(left[a, half:], right[b, :, half:], preferred_element_type=F32)
        return carry

    lax.fori_loop(0, 3, one_pass, 0)
    for i, packed in enumerate(fold(total)):
        out[:, i * BLOCK_W : (i + 1) * BLOCK_W] = packed


def tile_of(ref, i, j):
    return ref[i * SPAN : (i + 1) * SPAN, j * SPAN : (j + 1) * SPAN]


def diagonal_masks():
    rows = lax.broadcasted_iota(jnp.int32, (SPAN, SPAN), 0)
    columns = lax.broadcasted_iota(jnp.int32, (SPAN, SPAN), 1)
    return rows <= columns, rows == columns


def fold(ref):
    upper, equal = diagonal_masks()
    for off, (a, b) in ((((0, 1), (0, 2), (0, 3)), (0, 1)), (((1, 2), (1, 3), (2, 3)), (2, 3))):
        second = tile_of(ref, b, b)
        square = jnp.where(upper, tile_of(ref, a, a), second)
        line = jnp.sum(jnp.where(equal, second, 0.0), axis=0, keepdims=True)
        body = jnp.concatenate([tile_of(ref, *where) for where in off] + [square], axis=1)
        tail = jnp.concatenate([jnp.zeros((8, 3 * SPAN), F32), jnp.broadcast_to(line, (8, SPAN))], axis=1)
        yield jnp.concatenate([body, tail], axis=0)


def unfold(packs, work):
    upper, equal = diagonal_masks()
    trace = jnp.zeros((1, 1), F32)
    squares = []
    for pack, off, (a, b) in zip(
        packs, (((0, 1), (0, 2), (0, 3)), ((1, 2), (1, 3), (2, 3))), ((0, 1), (2, 3))
    ):
        for i, (row, column) in enumerate(off):
            work[row * SPAN : (row + 1) * SPAN, column * SPAN : (column + 1) * SPAN] = pack[:SPAN, i * SPAN : (i + 1) * SPAN]
        square = pack[:SPAN, 3 * SPAN :]
        turned = square.T
        line = jnp.broadcast_to(pack[SPAN : SPAN + 1, 3 * SPAN :], (SPAN, SPAN))
        squares.append((a, jnp.where(upper, square, turned)))
        squares.append((b, jnp.where(equal, line, jnp.where(upper, turned, square))))
    for _, square in squares:
        trace = trace + jnp.sum(jnp.where(equal, square, 0.0), axis=(0, 1), keepdims=True)
    damping = trace * (0.1 / BLOCK_W)
    for a, square in squares:
        work[a * SPAN : (a + 1) * SPAN, a * SPAN : (a + 1) * SPAN] = jnp.where(equal, square + damping, square)


def factor_kernel(*refs, start, stop, received):
    width = BLOCK_W - start
    panels = width // SPAN
    step = 32
    groups = step // 8
    per_tile = SPAN // step
    last = stop == BLOCK_W
    given, refs = (refs[:received], refs[received:])
    out, refs = refs[0], refs[1:]
    if not last:
        rest, refs = refs[0], refs[1:]
    work, previous, upper = refs
    if start == 0:
        work[...] = jnp.zeros_like(work)
        total = given[0][...] + given[1][...] if received == 2 else given[0][...]
        unfold((total[:, :BLOCK_W], total[:, BLOCK_W:]), work)
    else:
        work[...] = given[0][...]
    previous[...] = jnp.zeros_like(previous)

    def triple(value, first):
        high, low = split(value)
        return jnp.concatenate((high, low, high) if first else (high, high, low), axis=0)

    def superpanel(g, carry):
        row = pl.multiple_of(g * step, step)
        tile_index = g // per_tile
        tile = pl.ds(pl.multiple_of(tile_index * SPAN, SPAN), SPAN)
        turn = lax.rem(SPAN - lax.rem(g, per_tile) * step, SPAN)
        before = previous[...]
        right = triple(before, False)
        near = pltpu.roll(previous[:, tile], turn, 1)
        fresh = lax.dot_general(triple(near, True), right, TN, preferred_element_type=F32)[:step]
        current = work[pl.ds(row, step), :] - fresh
        work[...] = work[...] - lax.dot_general(triple(before, True), right, TN, preferred_element_type=F32)

        square = current[:, :SPAN]
        for k in range(1, panels):
            square = jnp.where(tile_index == k, current[:, k * SPAN : (k + 1) * SPAN], square)
        square = pltpu.roll(square, turn, 1)
        line = lax.broadcasted_iota(jnp.int32, (8, SPAN), 0)
        held = [
            {q: jnp.broadcast_to(square[8 * q : 8 * q + 8, j : j + 1], (8, SPAN)) for q in range(j // 8, groups)}
            for j in range(step)
        ]
        body = [[current[8 * q : 8 * q + 8, k * SPAN : (k + 1) * SPAN] for k in range(panels)] for q in range(groups)]
        scales = [jnp.zeros((8, SPAN), F32) for _ in range(groups)]

        def spread(value, i):
            return jnp.broadcast_to(value[i % 8 : i % 8 + 1], (8, SPAN))

        for i in range(step):
            at = i // 8
            root = lax.rsqrt(spread(held[i][at], i))
            inverse = root * root
            scales[at] = jnp.where(line == i % 8, root, scales[at])
            ratio = {q: held[i][q] * inverse for q in range(at, groups)}
            ratio[at] = jnp.where(line > i % 8, ratio[at], 0.0)
            for j in range(i + 1, step):
                entry = spread(held[i][j // 8], j)
                for q in range(j // 8, groups):
                    held[j][q] = held[j][q] - ratio[q] * entry
            for k in range(panels):
                pivot_row = spread(body[at][k], i)
                for q in range(at, groups):
                    body[q][k] = body[q][k] - ratio[q] * pivot_row
        result = jnp.concatenate(
            [jnp.concatenate([body[q][k] * scales[q] for k in range(panels)], axis=1) for q in range(groups)], axis=0
        )
        across = lax.broadcasted_iota(jnp.int32, (step, width), 1)
        down = lax.broadcasted_iota(jnp.int32, (step, width), 0)
        result = jnp.where(across >= down + row, result, 0.0)
        previous[...] = result
        upper[pl.ds(row, step), :] = result
        return carry

    lax.fori_loop(0, (stop - start) // step, superpanel, 0)
    if not last:
        done = stop - start
        before = previous[...]
        final = lax.dot_general(
            triple(before[:, done:], True), triple(before[:, done:], False), TN, preferred_element_type=F32
        )
        rest[...] = work[done:, done:] - final
    ready = [upper[k * SPAN : (k + 1) * SPAN, k * SPAN :] for k in range((stop - start) // SPAN)]
    largest = functools.reduce(jnp.maximum, [jnp.max(jnp.abs(p), axis=(0, 1), keepdims=True) for p in ready])
    write_coded(ready, out, largest)


def whiten_kernel(order, *refs, blocks, start):
    u_refs, refs = refs[:blocks], refs[blocks:]
    w_ref, out, left = refs[0], refs[-2], refs[-1]
    width = BLOCK_W - start
    half = BLOCK_W // 2
    for which in range(blocks):

        @pl.when((pl.program_id(0) == which) & (pl.program_id(1) == 0))
        def _(which=which):
            upper = read_coded(u_refs[which])
            rows = lax.broadcasted_iota(jnp.int32, (SPAN, SPAN), 0)
            columns = lax.broadcasted_iota(jnp.int32, (SPAN, SPAN), 1)
            at = 0
            for k in range(half // SPAN):
                panel = upper[:, at : at + width - SPAN * k]
                at += width - SPAN * k
                pieces = [jnp.zeros((SPAN, SPAN * k), F32)] if k else []
                pieces += [jnp.where(rows > columns, 0.0, panel[:, :SPAN]), panel[:, SPAN:]]
                high, low = split(jnp.concatenate([p for p in pieces if p.shape[1]], axis=1))
                left[k * SPAN : (k + 1) * SPAN] = high
                left[half + k * SPAN : half + (k + 1) * SPAN] = low

    product = jnp.dot(left[...], w_ref[...], preferred_element_type=F32)
    out[0] = product[:half] + product[half:]


def shards(query_rows, key_rows, placed_value_rows, doc_lengths, span_order, out_weight):
    tokens = query_rows.shape[1]
    features = out_weight.shape[0]
    seq = lax.axis_size("seq")
    ring = lax.axis_size("dp")
    chips = seq // 2
    spans = tokens // SPAN
    all_spans = spans * seq
    documents = doc_lengths.shape[1]
    per = KEY_VALUE_HEADS // seq
    blocks = NB // seq
    own = lax.axis_index("seq").astype(jnp.int32)
    place = lax.axis_index("dp").astype(jnp.int32)
    query, key, value = query_rows[0], key_rows[0], placed_value_rows[0]
    vmem = pl.BlockSpec(memory_space=pltpu.VMEM)
    anywhere = pl.BlockSpec(memory_space=pl.ANY)
    in_ring = blocks == ring

    if in_ring:
        turns = [lax.rem(place + 2 * ring - 1 - t, ring) for t in range(blocks)]
    else:
        turns = [jnp.int32(t) for t in range(blocks)]
    first_kv = turns[0] // KV_BLOCKS

    def moved(distance, cross):
        return [
            (x * 2 + c, (x + distance) % chips * 2 + (1 - c if cross else c)) for x in range(chips) for c in range(2)
        ]

    def cut(targets, columns, scalars, name, after=()):
        specs, arrays = [], []
        for target in targets:
            for array, size, index in columns:
                specs.append(
                    pl.BlockSpec((tokens, size), lambda i, meta, target=target, index=index: (0, index(target(meta), meta)))
                )
                arrays.append(array)
        width = sum(size for _, size, _ in columns)
        return pl.pallas_call(
            functools.partial(cut_kernel, targets=len(targets), given=len(columns)),
            out_shape=[jax.ShapeDtypeStruct((tokens, width), BF16)] * len(targets),
            grid_spec=pltpu.PrefetchScalarGridSpec(
                num_scalar_prefetch=1,
                grid=(1,),
                in_specs=specs + [anywhere] * len(after),
                out_specs=[pl.BlockSpec((tokens, width), lambda i, meta: (0, 0))] * len(targets),
            ),
            compiler_params=params(),
            cost_estimate=cost(0, 2**21),
            name=name,
        )(scalars, *arrays, *after)

    tile = 512

    def turn(first, count, *before):
        return pl.pallas_call(
            turn_kernel,
            out_shape=jax.ShapeDtypeStruct((blocks * BLOCK_W, features), BF16),
            grid=(count, features // tile),
            in_specs=[pl.BlockSpec((tile, BLOCK_W), lambda b, o: (o, first + b))] + [anywhere] * len(before),
            out_specs=pl.BlockSpec((BLOCK_W, tile), lambda b, o: (first + b, o)),
            input_output_aliases={1: 0} if before else {},
            compiler_params=params(),
            cost_estimate=cost(3.5e9 * count, 2**20),
            name="turn_weight",
        )(out_weight, *before)

    def target_at(distance, cross):
        return lambda meta: lax.rem(meta[0] // 2 + distance, chips) * 2 + lax.rem(lax.rem(meta[0], 2) + cross, 2)

    far = [(distance, cross) for distance in range(1, chips) for cross in range(2)]
    pieces = []

    most = all_spans // 2 + 1

    def grams_of(t, peer):
        kv = turns[t] // KV_BLOCKS
        carriers = pieces[: min(t + 1, per)]
        which = jnp.where(kv == first_kv, 0, 1).astype(jnp.int32)
        meta = jnp.concatenate([jnp.stack([own, turns[t], kv, which]), doc_lengths[0], span_order[0]])
        folded = jax.ShapeDtypeStruct((SPAN + 8, 2 * BLOCK_W), F32)
        peer_kv = blocks * BLOCK_W // HEAD_SIZE
        return pl.pallas_call(
            functools.partial(
                attention_kernel,
                chips=chips, spans=spans, all_spans=all_spans, documents=documents, most=most, sets=len(carriers),
            ),
            out_shape=folded,
            grid_spec=pltpu.PrefetchScalarGridSpec(
                num_scalar_prefetch=1,
                grid=(1,),
                in_specs=[
                    pl.BlockSpec((tokens, BLOCK_W), lambda i, meta: (0, meta[0] * blocks + meta[1])),
                    pl.BlockSpec((tokens, BLOCK_W), lambda i, meta: (0, meta[1])),
                ]
                + [pl.BlockSpec((tokens, BLOCK_W), lambda i, meta: (0, 0))] * len(far)
                + [pl.BlockSpec((tokens, HEAD_SIZE), lambda i, meta: (0, meta[0] * per + meta[2]))] * 2
                + [
                    pl.BlockSpec((tokens, HEAD_SIZE), lambda i, meta: (0, peer_kv + meta[2])),
                    pl.BlockSpec((tokens, HEAD_SIZE), lambda i, meta: (0, peer_kv + per + meta[2])),
                ]
                + [pl.BlockSpec((tokens, 2 * HEAD_SIZE), lambda i, meta: (0, BLOCK_W // (2 * HEAD_SIZE)))]
                * (len(carriers) * len(far)),
                out_specs=pl.BlockSpec((SPAN + 8, 2 * BLOCK_W), lambda i, meta: (0, 0)),
                scratch_shapes=[
                    pltpu.VMEM((all_spans, BLOCK_HEADS * SPAN, HEAD_SIZE), BF16),
                    pltpu.VMEM((all_spans, SPAN, HEAD_SIZE), BF16),
                    pltpu.VMEM((all_spans, HEAD_SIZE, SPAN), BF16),
                    pltpu.SMEM((all_spans,), jnp.int32),
                    pltpu.VMEM((most * SPAN, SPAN), F32),
                    pltpu.VMEM((2, BLOCK_W, all_spans * SPAN), BF16),
                    pltpu.VMEM((2, all_spans * SPAN, BLOCK_W), BF16),
                    pltpu.VMEM((BLOCK_W, BLOCK_W), F32),
                ],
            ),
            compiler_params=params(),
            cost_estimate=cost(1.4e10, 2**20),
            name="attention_outer_products",
        )(meta, query, peer, *pieces[t], key, value, peer, peer, *[array for carrier in carriers for array in carrier])

    grams = []
    for t in range(blocks):
        kv = first_kv if t == 0 else per - 1 - first_kv
        columns = [(query, BLOCK_W, lambda target, meta: target * blocks + meta[1])]
        if t < per:
            columns += [(array, HEAD_SIZE, lambda target, meta: target * per + meta[2]) for array in (key, value)]
        scalars = jnp.stack([own, turns[t], kv])
        after = [] if t == 0 else [peer, turned] if t == 1 else [grams[t - 2]]
        parts = cut([target_at(*where) for where in far], columns, scalars, "cut_piece", after)
        pieces.append([lax.ppermute(part, "seq", moved(*where)) for part, where in zip(parts, far)])
        if t == 0:
            columns = [(query, blocks * BLOCK_W, lambda target, meta: target)]
            columns += [(array, per * HEAD_SIZE, lambda target, meta: target) for array in (key, value)]
            peer = lax.ppermute(cut([target_at(0, 1)], columns, own[None], "cut_peer", parts)[0], "seq", moved(0, 1))
            turned = turn(0, blocks // 2)
        if t == 1:
            turned = turn(blocks // 2, blocks - blocks // 2, turned, parts[0])
        grams.append(grams_of(t, peer))

    half = BLOCK_W // 2
    top_width, bottom_width = STARTS[2], PACKED - STARTS[2]
    scratch = lambda width: [pltpu.VMEM((width, width), F32), pltpu.VMEM((32, width), F32), pltpu.VMEM((half, width), F32)]

    def factor_top(*given):
        return pl.pallas_call(
            functools.partial(factor_kernel, start=0, stop=half, received=len(given)),
            out_shape=[
                jax.ShapeDtypeStruct((SPAN, top_width), BF16),
                jax.ShapeDtypeStruct((half, half), F32),
            ],
            in_specs=[vmem] * len(given),
            out_specs=[vmem] * 2,
            scratch_shapes=scratch(BLOCK_W),
            compiler_params=params(),
            cost_estimate=cost(1.0e10, 2**20),
            name="factor_top",
        )(*given)

    def factor_bottom(rest):
        return pl.pallas_call(
            functools.partial(factor_kernel, start=half, stop=BLOCK_W, received=1),
            out_shape=jax.ShapeDtypeStruct((SPAN, bottom_width), BF16),
            in_specs=[vmem],
            out_specs=vmem,
            scratch_shapes=scratch(half),
            compiler_params=params(),
            cost_estimate=cost(0.9e10, 2**20),
            name="factor_bottom",
        )(rest)

    if in_ring:
        carried = None
        for t in range(ring - 1):
            partial = grams[t] if carried is None else grams[t] + carried
            carried = lax.ppermute(partial, "dp", [(z, (z + 1) % ring) for z in range(ring)])
        top, rest = factor_top(grams[ring - 1], carried)

        def shared(array):
            return [array] + [
                lax.ppermute(array, "dp", [(z, (z + d) % ring) for z in range(ring)]) for d in range(1, ring)
            ]

        tops = shared(top)
        bottoms = shared(factor_bottom(rest))
        order = jnp.stack([lax.rem(place - d + ring, ring) for d in range(ring)])
    else:
        halves = [factor_top(lax.psum(grams[t], "dp")) for t in range(blocks)]
        tops = [top for top, _ in halves]
        bottoms = [factor_bottom(rest) for _, rest in halves]
        order = jnp.arange(blocks, dtype=jnp.int32)

    wide = min(2048, features)

    def whiten(uppers, first, start, result):
        more = [] if result is None else [result]
        depth = BLOCK_W - start
        return pl.pallas_call(
            functools.partial(whiten_kernel, blocks=len(uppers), start=start),
            out_shape=jax.ShapeDtypeStruct((blocks, BLOCK_W, features), F32),
            grid_spec=pltpu.PrefetchScalarGridSpec(
                num_scalar_prefetch=1,
                grid=(len(uppers), features // wide),
                in_specs=[vmem] * len(uppers)
                + [
                    pl.BlockSpec(
                        (depth, wide),
                        lambda b, o, order: (order[first + b] * (BLOCK_W // depth) + start // depth, o),
                    )
                ]
                + [anywhere] * len(more),
                out_specs=pl.BlockSpec((1, half, wide), lambda b, o, order: (order[first + b], start // half, o)),
                scratch_shapes=[pltpu.VMEM((2 * half, depth), BF16)],
            ),
            input_output_aliases={len(uppers) + 2: 0} if more else {},
            compiler_params=params(),
            cost_estimate=cost(2.0e9 * len(uppers), 2**20),
            name="whiten_bottom" if start else "whiten_top",
        )(order, *uppers, turned, *more)

    result = whiten(tops[:1], 0, 0, None)
    result = whiten(bottoms[:1], 0, half, result)
    result = whiten(tops[1:], 1, 0, result)
    return whiten(bottoms[1:], 1, half, result)


def solution(mesh):
    in_specs = (
        P(("groups", "dp"), "seq", None),
        P(("groups", "dp"), "seq", None),
        P(("groups", "dp"), "seq", None),
        P(("groups", "dp"), None),
        P(("groups", "dp"), None),
        P("dp", "seq"),
    )
    out_specs = P(("groups", "seq"), None, "dp")
    return jax.shard_map(shards, mesh=mesh, in_specs=in_specs, out_specs=out_specs, check_vma=False)
```

```python
import functools
import math

import jax
import jax.numpy as jnp
from jax import lax
from jax.experimental import pallas as pl
from jax.experimental.pallas import tpu as pltpu
from jax.sharding import PartitionSpec as P

QUERY_HEADS = 64
KEY_VALUE_HEADS = 8
HEAD_SIZE = 128
BLOCK_W = 512
NB = 16
SPAN = 128
GROUP = QUERY_HEADS // KEY_VALUE_HEADS
BLOCK_HEADS = BLOCK_W // HEAD_SIZE
KV_BLOCKS = GROUP // BLOCK_HEADS
PANELS = BLOCK_W // SPAN
STARTS = [sum(BLOCK_W - SPAN * j for j in range(k)) for k in range(PANELS)]
PACKED = sum(BLOCK_W - SPAN * j for j in range(PANELS))
VMEM_BYTES = 50 * 1024 * 1024
F32 = jnp.float32
BF16 = jnp.bfloat16
NT = (((1,), (1,)), ((), ()))
TN = (((0,), (0,)), ((), ()))


def params(limit=VMEM_BYTES):
    return pltpu.CompilerParams(vmem_limit_bytes=limit)


def cost(flops, moved, trans=0):
    return pl.CostEstimate(flops=int(flops), bytes_accessed=int(moved), transcendentals=int(trans))


def encode(value, exponent):
    scaled = value * jnp.exp2(15.0 - exponent)
    power = scaled * scaled
    power = power * power
    power = power * power
    return jnp.where(scaled < 0.0, -power, power)


def decode(code, exponent):
    code = code.astype(F32)
    root = jnp.exp2(jnp.log(jnp.maximum(jnp.abs(code), 1e-37)) * (0.125 / math.log(2.0)) + (exponent - 15.0))
    return jnp.where(code < 0.0, -root, root)


def marker():
    rows = lax.broadcasted_iota(jnp.int32, (SPAN, SPAN), 0)
    columns = lax.broadcasted_iota(jnp.int32, (SPAN, SPAN), 1)
    return (rows == SPAN - 1) & (columns == 0)


def exponent_of(largest):
    return jnp.ceil(jnp.log(jnp.maximum(largest, 1e-30)) * (1.0 / math.log(2.0)) + 0.001)


def write_coded(panels, out, largest):
    exponent = exponent_of(largest)
    at = 0
    for k, panel in enumerate(panels):
        coded = encode(panel, exponent)
        if k == 0:
            first = jnp.where(marker(), jnp.broadcast_to(exponent, (SPAN, SPAN)), coded[:, :SPAN])
            coded = jnp.concatenate([first, coded[:, SPAN:]], axis=1)
        out[:, at : at + panel.shape[1]] = coded.astype(BF16)
        at += panel.shape[1]


def read_coded(ref):
    exponent = ref[SPAN - 16 : SPAN, :SPAN].astype(F32)[15:16, 0:1]
    return decode(ref[...], exponent)


def split(value):
    high = value.astype(BF16)
    return high, (value - high.astype(F32)).astype(BF16)


def cut_kernel(meta, *refs, targets, given):
    outs = refs[-targets:]
    for number, out in enumerate(outs):
        at = 0
        for ref in refs[number * given : (number + 1) * given]:
            out[:, at : at + ref.shape[1]] = ref[...]
            at += ref.shape[1]


def turn_kernel(w_ref, *refs):
    refs[-1][...] = w_ref[...].T


def attention_kernel(meta, *refs, chips, spans, all_spans, documents, most, sets):
    sources = 2 * chips
    near = sources + 4
    query_refs, near_refs = refs[:sources], refs[sources:near]
    far_refs = refs[near : near + sets * (sources - 2)]
    out, queries, keys, values, slots, limits, left, right, total = refs[near + sets * (sources - 2) :]
    own = meta[0]
    chip, core = own // 2, lax.rem(own, 2)
    lengths = 4
    order = lengths + documents

    for r in range(all_spans):
        device = r // spans
        distance = lax.rem(chip - device // 2 + chips, chips)
        cross = lax.rem(core + device % 2, 2)
        slots[meta[order + r]] = (distance * 2 + cross) * spans + r % spans

    def place_kv(source, key_part, value_part):
        for t in range(spans):
            rows = slice(t * SPAN, (t + 1) * SPAN)
            keys[source * spans + t] = key_part[rows]
            values[source * spans + t] = value_part[rows].astype(F32).T.astype(BF16)

    place_kv(0, near_refs[0], near_refs[1])
    place_kv(1, near_refs[2], near_refs[3])
    for which in range(sets):

        @pl.when(meta[3] == which)
        def _(which=which):
            for source in range(2, sources):
                ref = far_refs[which * (sources - 2) + source - 2]
                place_kv(source, ref[:, :HEAD_SIZE], ref[:, HEAD_SIZE:])

    for source in range(sources):
        for t in range(spans):
            for h in range(BLOCK_HEADS):
                queries[source * spans + t, h * SPAN : (h + 1) * SPAN] = query_refs[source][
                    t * SPAN : (t + 1) * SPAN, h * HEAD_SIZE : (h + 1) * HEAD_SIZE
                ]

    factor = HEAD_SIZE ** (-0.5) / math.log(2.0)

    def one_span(q, carry):
        source = q // spans
        distance, cross = source // 2, lax.rem(source, 2)
        device = lax.rem(chip - distance + chips, chips) * 2 + lax.rem(core + cross, 2)
        position = meta[order + device * spans + lax.rem(q, spans)]
        first_row = position * SPAN
        begin = jnp.int32(0)
        at = jnp.int32(0)
        query_pos = lax.broadcasted_iota(jnp.int32, (1, SPAN), 1) + first_row
        query_begin = jnp.zeros((1, SPAN), jnp.int32)
        for d in range(documents):
            begin = jnp.where(at <= first_row, at, begin)
            query_begin = jnp.where(query_pos >= at, at, query_begin)
            at = at + meta[lengths + d]
        count = position - begin // SPAN + 1
        lanes = pl.ds(pl.multiple_of(q * SPAN, SPAN), SPAN)

        for n in range(1, most + 1):

            @pl.when(count == n)
            def _(n=n):
                held = [slots[position - n + 1 + i] for i in range(n)]
                for i in range(n):
                    key_pos = lax.broadcasted_iota(jnp.int32, (SPAN, SPAN), 0) + (position - n + 1 + i) * SPAN
                    seen = (key_pos <= query_pos) & (key_pos >= query_begin)
                    limits[i * SPAN : (i + 1) * SPAN] = jnp.where(seen, 3e38, -1e30)
                key_part = jnp.concatenate([keys[slot] for slot in held], axis=0)
                value_part = jnp.concatenate([values[slot] for slot in held], axis=1)
                scores = lax.dot_general(key_part, queries[q], NT, preferred_element_type=F32)
                limit = limits[: n * SPAN]
                scores = jnp.minimum(scores, jnp.concatenate([limit] * BLOCK_HEADS, axis=1))
                largest = jnp.max(scores, axis=0, keepdims=True)
                lifted = jnp.exp2((scores - largest) * factor)
                summed = jnp.sum(lifted, axis=0, keepdims=True)
                weights = (lifted * (1.0 / summed)).astype(BF16)
                mixed = jnp.dot(value_part, weights, preferred_element_type=F32)
                for h in range(BLOCK_HEADS):
                    one_head = mixed[:, h * SPAN : (h + 1) * SPAN]
                    columns = slice(h * HEAD_SIZE, (h + 1) * HEAD_SIZE)
                    high, low = split(one_head)
                    left[0, columns, lanes] = high
                    left[1, columns, lanes] = low
                    high, low = split(one_head.T)
                    right[0, lanes, columns] = high
                    right[1, lanes, columns] = low

        return carry

    lax.fori_loop(0, all_spans, one_span, 0)

    half = BLOCK_W // 2
    total[...] = jnp.zeros_like(total)

    def one_pass(i, carry):
        a, b = lax.rem(i, 2), i // 2
        total[:half] += jnp.dot(left[a, :half], right[b], preferred_element_type=F32)
        total[half:, half:] += jnp.dot(left[a, half:], right[b, :, half:], preferred_element_type=F32)
        return carry

    lax.fori_loop(0, 3, one_pass, 0)
    for i, packed in enumerate(fold(total)):
        out[:, i * BLOCK_W : (i + 1) * BLOCK_W] = packed


def tile_of(ref, i, j):
    return ref[i * SPAN : (i + 1) * SPAN, j * SPAN : (j + 1) * SPAN]


def diagonal_masks():
    rows = lax.broadcasted_iota(jnp.int32, (SPAN, SPAN), 0)
    columns = lax.broadcasted_iota(jnp.int32, (SPAN, SPAN), 1)
    return rows <= columns, rows == columns


def fold(ref):
    upper, equal = diagonal_masks()
    for off, (a, b) in ((((0, 1), (0, 2), (0, 3)), (0, 1)), (((1, 2), (1, 3), (2, 3)), (2, 3))):
        second = tile_of(ref, b, b)
        square = jnp.where(upper, tile_of(ref, a, a), second)
        line = jnp.sum(jnp.where(equal, second, 0.0), axis=0, keepdims=True)
        body = jnp.concatenate([tile_of(ref, *where) for where in off] + [square], axis=1)
        tail = jnp.concatenate([jnp.zeros((8, 3 * SPAN), F32), jnp.broadcast_to(line, (8, SPAN))], axis=1)
        yield jnp.concatenate([body, tail], axis=0)


def unfold(packs, work):
    upper, equal = diagonal_masks()
    trace = jnp.zeros((1, 1), F32)
    squares = []
    for pack, off, (a, b) in zip(
        packs, (((0, 1), (0, 2), (0, 3)), ((1, 2), (1, 3), (2, 3))), ((0, 1), (2, 3))
    ):
        for i, (row, column) in enumerate(off):
            work[row * SPAN : (row + 1) * SPAN, column * SPAN : (column + 1) * SPAN] = pack[:SPAN, i * SPAN : (i + 1) * SPAN]
        square = pack[:SPAN, 3 * SPAN :]
        turned = square.T
        line = jnp.broadcast_to(pack[SPAN : SPAN + 1, 3 * SPAN :], (SPAN, SPAN))
        squares.append((a, jnp.where(upper, square, turned)))
        squares.append((b, jnp.where(equal, line, jnp.where(upper, turned, square))))
    for _, square in squares:
        trace = trace + jnp.sum(jnp.where(equal, square, 0.0), axis=(0, 1), keepdims=True)
    damping = trace * (0.1 / BLOCK_W)
    for a, square in squares:
        work[a * SPAN : (a + 1) * SPAN, a * SPAN : (a + 1) * SPAN] = jnp.where(equal, square + damping, square)


def factor_kernel(*refs, start, stop, received):
    width = BLOCK_W - start
    panels = width // SPAN
    step = 32
    groups = step // 8
    per_tile = SPAN // step
    last = stop == BLOCK_W
    given, refs = (refs[:received], refs[received:])
    out, refs = refs[0], refs[1:]
    if not last:
        rest, refs = refs[0], refs[1:]
    work, previous, upper = refs
    if start == 0:
        work[...] = jnp.zeros_like(work)
        total = given[0][...] + given[1][...] if received == 2 else given[0][...]
        unfold((total[:, :BLOCK_W], total[:, BLOCK_W:]), work)
    else:
        work[...] = given[0][...]
    previous[...] = jnp.zeros_like(previous)

    def triple(value, first):
        high, low = split(value)
        return jnp.concatenate((high, low, high) if first else (high, high, low), axis=0)

    def superpanel(g, carry):
        row = pl.multiple_of(g * step, step)
        tile_index = g // per_tile
        tile = pl.ds(pl.multiple_of(tile_index * SPAN, SPAN), SPAN)
        turn = lax.rem(SPAN - lax.rem(g, per_tile) * step, SPAN)
        before = previous[...]
        right = triple(before, False)
        near = pltpu.roll(previous[:, tile], turn, 1)
        fresh = lax.dot_general(triple(near, True), right, TN, preferred_element_type=F32)[:step]
        current = work[pl.ds(row, step), :] - fresh
        work[...] = work[...] - lax.dot_general(triple(before, True), right, TN, preferred_element_type=F32)

        square = current[:, :SPAN]
        for k in range(1, panels):
            square = jnp.where(tile_index == k, current[:, k * SPAN : (k + 1) * SPAN], square)
        square = pltpu.roll(square, turn, 1)
        line = lax.broadcasted_iota(jnp.int32, (8, SPAN), 0)
        held = [
            {q: jnp.broadcast_to(square[8 * q : 8 * q + 8, j : j + 1], (8, SPAN)) for q in range(j // 8, groups)}
            for j in range(step)
        ]
        body = [[current[8 * q : 8 * q + 8, k * SPAN : (k + 1) * SPAN] for k in range(panels)] for q in range(groups)]
        scales = [jnp.zeros((8, SPAN), F32) for _ in range(groups)]

        def spread(value, i):
            return jnp.broadcast_to(value[i % 8 : i % 8 + 1], (8, SPAN))

        for i in range(0, step, 2):
            at = i // 8
            first, cross, second = spread(held[i][at], i), spread(held[i][at], i + 1), spread(held[i + 1][at], i + 1)
            determinant = first * second - cross * cross
            inverse = 1.0 / determinant
            first_root = lax.rsqrt(first)
            first_inverse = first_root * first_root
            scales[at] = jnp.where(line == i % 8, first_root, scales[at])
            scales[at] = jnp.where(line == i % 8 + 1, lax.rsqrt(determinant * first_inverse), scales[at])
            ratios = {}
            for q in range(at, groups):
                x, y = held[i][q], held[i + 1][q]
                ratios[q] = ((x * second - y * cross) * inverse, (y * first - x * cross) * inverse)
            ratios[at] = tuple(jnp.where(line > i % 8 + 1, ratio, 0.0) for ratio in ratios[at])
            for j in range(i + 2, step):
                x, y = spread(held[i][j // 8], j), spread(held[i + 1][j // 8], j)
                for q in range(j // 8, groups):
                    held[j][q] = held[j][q] - (ratios[q][0] * x + ratios[q][1] * y)
            between = jnp.where(line == i % 8 + 1, cross * first_inverse, 0.0)
            for k in range(panels):
                x, y = spread(body[at][k], i), spread(body[at][k], i + 1)
                for q in range(at, groups):
                    body[q][k] = body[q][k] - (ratios[q][0] * x + ratios[q][1] * y)
                body[at][k] = body[at][k] - between * x
        result = jnp.concatenate(
            [jnp.concatenate([body[q][k] * scales[q] for k in range(panels)], axis=1) for q in range(groups)], axis=0
        )
        across = lax.broadcasted_iota(jnp.int32, (step, width), 1)
        down = lax.broadcasted_iota(jnp.int32, (step, width), 0)
        result = jnp.where(across >= down + row, result, 0.0)
        previous[...] = result
        upper[pl.ds(row, step), :] = result
        return carry

    lax.fori_loop(0, (stop - start) // step, superpanel, 0)
    if not last:
        done = stop - start
        before = previous[...]
        final = lax.dot_general(
            triple(before[:, done:], True), triple(before[:, done:], False), TN, preferred_element_type=F32
        )
        rest[...] = work[done:, done:] - final
    ready = [upper[k * SPAN : (k + 1) * SPAN, k * SPAN :] for k in range((stop - start) // SPAN)]
    largest = functools.reduce(jnp.maximum, [jnp.max(jnp.abs(p), axis=(0, 1), keepdims=True) for p in ready])
    write_coded(ready, out, largest)


def whiten_kernel(order, *refs, blocks, start, first, chunks, aliased):
    u_refs, w_refs, refs = refs[:blocks], refs[blocks : blocks + chunks], refs[blocks + chunks + aliased :]
    out, left, ready, sems = refs
    width = BLOCK_W - start
    half = BLOCK_W // 2
    chunk = ready.shape[2] // chunks
    step = pl.program_id(0)
    for which in range(blocks):

        @pl.when(step == which)
        def _(which=which):
            upper = read_coded(u_refs[which])
            rows = lax.broadcasted_iota(jnp.int32, (SPAN, SPAN), 0)
            columns = lax.broadcasted_iota(jnp.int32, (SPAN, SPAN), 1)
            at = 0
            for k in range(half // SPAN):
                panel = upper[:, at : at + width - SPAN * k]
                at += width - SPAN * k
                pieces = [jnp.zeros((SPAN, SPAN * k), F32)] if k else []
                pieces += [jnp.where(rows > columns, 0.0, panel[:, :SPAN]), panel[:, SPAN:]]
                high, low = split(jnp.concatenate([p for p in pieces if p.shape[1]], axis=1))
                left[k * SPAN : (k + 1) * SPAN] = high
                left[half + k * SPAN : half + (k + 1) * SPAN] = low

    def copy(number, c):
        slot = lax.rem(number, 2)
        columns = pl.ds(c * chunk, chunk)
        return pltpu.make_async_copy(
            ready.at[slot, :, columns],
            out.at[order[first + number], pl.ds(start, half), columns],
            sems.at[slot, c],
        )

    for c in range(chunks):

        @pl.when(step >= 2)
        def _(c=c):
            copy(step - 2, c).wait()

        product = jnp.dot(left[...], w_refs[c][...], preferred_element_type=F32)
        ready[lax.rem(step, 2), :, c * chunk : (c + 1) * chunk] = product[:half] + product[half:]
        copy(step, c).start()

    @pl.when(step == blocks - 1)
    def _():
        for c in range(chunks):
            if blocks > 1:
                copy(step - 1, c).wait()
            copy(step, c).wait()


def shards(query_rows, key_rows, placed_value_rows, doc_lengths, span_order, out_weight):
    tokens = query_rows.shape[1]
    features = out_weight.shape[0]
    seq = lax.axis_size("seq")
    ring = lax.axis_size("dp")
    chips = seq // 2
    spans = tokens // SPAN
    all_spans = spans * seq
    documents = doc_lengths.shape[1]
    per = KEY_VALUE_HEADS // seq
    blocks = NB // seq
    own = lax.axis_index("seq").astype(jnp.int32)
    place = lax.axis_index("dp").astype(jnp.int32)
    query, key, value = query_rows[0], key_rows[0], placed_value_rows[0]
    vmem = pl.BlockSpec(memory_space=pltpu.VMEM)
    anywhere = pl.BlockSpec(memory_space=pl.ANY)
    in_ring = blocks == ring

    if in_ring:
        turns = [lax.rem(place + 2 * ring - 1 - t, ring) for t in range(blocks)]
    else:
        turns = [jnp.int32(t) for t in range(blocks)]
    first_kv = turns[0] // KV_BLOCKS

    def moved(distance, cross):
        return [
            (x * 2 + c, (x + distance) % chips * 2 + (1 - c if cross else c)) for x in range(chips) for c in range(2)
        ]

    def cut(targets, columns, scalars, name, after=()):
        specs, arrays = [], []
        for target in targets:
            for array, size, index in columns:
                specs.append(
                    pl.BlockSpec((tokens, size), lambda i, meta, target=target, index=index: (0, index(target(meta), meta)))
                )
                arrays.append(array)
        width = sum(size for _, size, _ in columns)
        return pl.pallas_call(
            functools.partial(cut_kernel, targets=len(targets), given=len(columns)),
            out_shape=[jax.ShapeDtypeStruct((tokens, width), BF16)] * len(targets),
            grid_spec=pltpu.PrefetchScalarGridSpec(
                num_scalar_prefetch=1,
                grid=(1,),
                in_specs=specs + [anywhere] * len(after),
                out_specs=[pl.BlockSpec((tokens, width), lambda i, meta: (0, 0))] * len(targets),
            ),
            compiler_params=params(),
            cost_estimate=cost(0, 2**21),
            name=name,
        )(scalars, *arrays, *after)

    tile = 512

    def turn(first, count, *before):
        return pl.pallas_call(
            turn_kernel,
            out_shape=jax.ShapeDtypeStruct((blocks * BLOCK_W, features), BF16),
            grid=(count, features // tile),
            in_specs=[pl.BlockSpec((tile, BLOCK_W), lambda b, o: (o, first + b))] + [anywhere] * len(before),
            out_specs=pl.BlockSpec((BLOCK_W, tile), lambda b, o: (first + b, o)),
            input_output_aliases={1: 0} if before else {},
            compiler_params=params(),
            cost_estimate=cost(3.5e9 * count, 2**20),
            name="turn_weight",
        )(out_weight, *before)

    def target_at(distance, cross):
        return lambda meta: lax.rem(meta[0] // 2 + distance, chips) * 2 + lax.rem(lax.rem(meta[0], 2) + cross, 2)

    far = [(distance, cross) for distance in range(1, chips) for cross in range(2)]
    pieces = []

    most = all_spans // 2 + 1

    def grams_of(t, peer):
        kv = turns[t] // KV_BLOCKS
        carriers = pieces[: min(t + 1, per)]
        which = jnp.where(kv == first_kv, 0, 1).astype(jnp.int32)
        meta = jnp.concatenate([jnp.stack([own, turns[t], kv, which]), doc_lengths[0], span_order[0]])
        folded = jax.ShapeDtypeStruct((SPAN + 8, 2 * BLOCK_W), F32)
        peer_kv = blocks * BLOCK_W // HEAD_SIZE
        return pl.pallas_call(
            functools.partial(
                attention_kernel,
                chips=chips, spans=spans, all_spans=all_spans, documents=documents, most=most, sets=len(carriers),
            ),
            out_shape=folded,
            grid_spec=pltpu.PrefetchScalarGridSpec(
                num_scalar_prefetch=1,
                grid=(1,),
                in_specs=[
                    pl.BlockSpec((tokens, BLOCK_W), lambda i, meta: (0, meta[0] * blocks + meta[1])),
                    pl.BlockSpec((tokens, BLOCK_W), lambda i, meta: (0, meta[1])),
                ]
                + [pl.BlockSpec((tokens, BLOCK_W), lambda i, meta: (0, 0))] * len(far)
                + [pl.BlockSpec((tokens, HEAD_SIZE), lambda i, meta: (0, meta[0] * per + meta[2]))] * 2
                + [
                    pl.BlockSpec((tokens, HEAD_SIZE), lambda i, meta: (0, peer_kv + meta[2])),
                    pl.BlockSpec((tokens, HEAD_SIZE), lambda i, meta: (0, peer_kv + per + meta[2])),
                ]
                + [pl.BlockSpec((tokens, 2 * HEAD_SIZE), lambda i, meta: (0, BLOCK_W // (2 * HEAD_SIZE)))]
                * (len(carriers) * len(far)),
                out_specs=pl.BlockSpec((SPAN + 8, 2 * BLOCK_W), lambda i, meta: (0, 0)),
                scratch_shapes=[
                    pltpu.VMEM((all_spans, BLOCK_HEADS * SPAN, HEAD_SIZE), BF16),
                    pltpu.VMEM((all_spans, SPAN, HEAD_SIZE), BF16),
                    pltpu.VMEM((all_spans, HEAD_SIZE, SPAN), BF16),
                    pltpu.SMEM((all_spans,), jnp.int32),
                    pltpu.VMEM((most * SPAN, SPAN), F32),
                    pltpu.VMEM((2, BLOCK_W, all_spans * SPAN), BF16),
                    pltpu.VMEM((2, all_spans * SPAN, BLOCK_W), BF16),
                    pltpu.VMEM((BLOCK_W, BLOCK_W), F32),
                ],
            ),
            compiler_params=params(),
            cost_estimate=cost(1.4e10, 2**20),
            name="attention_outer_products",
        )(meta, query, peer, *pieces[t], key, value, peer, peer, *[array for carrier in carriers for array in carrier])

    grams = []
    for t in range(blocks):
        kv = first_kv if t == 0 else per - 1 - first_kv
        columns = [(query, BLOCK_W, lambda target, meta: target * blocks + meta[1])]
        if t < per:
            columns += [(array, HEAD_SIZE, lambda target, meta: target * per + meta[2]) for array in (key, value)]
        scalars = jnp.stack([own, turns[t], kv])
        after = [] if t == 0 else [peer, turned] if t == 1 else [grams[t - 2]]
        parts = cut([target_at(*where) for where in far], columns, scalars, "cut_piece", after)
        pieces.append([lax.ppermute(part, "seq", moved(*where)) for part, where in zip(parts, far)])
        if t == 0:
            columns = [(query, blocks * BLOCK_W, lambda target, meta: target)]
            columns += [(array, per * HEAD_SIZE, lambda target, meta: target) for array in (key, value)]
            peer = lax.ppermute(cut([target_at(0, 1)], columns, own[None], "cut_peer", parts)[0], "seq", moved(0, 1))
            turned = turn(0, blocks // 2)
        grams.append(grams_of(t, peer))

    half = BLOCK_W // 2
    top_width, bottom_width = STARTS[2], PACKED - STARTS[2]
    scratch = lambda width: [pltpu.VMEM((width, width), F32), pltpu.VMEM((32, width), F32), pltpu.VMEM((half, width), F32)]

    def factor_top(*given):
        return pl.pallas_call(
            functools.partial(factor_kernel, start=0, stop=half, received=len(given)),
            out_shape=[
                jax.ShapeDtypeStruct((SPAN, top_width), BF16),
                jax.ShapeDtypeStruct((half, half), F32),
            ],
            in_specs=[vmem] * len(given),
            out_specs=[vmem] * 2,
            scratch_shapes=scratch(BLOCK_W),
            compiler_params=params(),
            cost_estimate=cost(1.0e10, 2**20),
            name="factor_top",
        )(*given)

    def factor_bottom(rest):
        return pl.pallas_call(
            functools.partial(factor_kernel, start=half, stop=BLOCK_W, received=1),
            out_shape=jax.ShapeDtypeStruct((SPAN, bottom_width), BF16),
            in_specs=[vmem],
            out_specs=vmem,
            scratch_shapes=scratch(half),
            compiler_params=params(),
            cost_estimate=cost(0.9e10, 2**20),
            name="factor_bottom",
        )(rest)

    if in_ring:
        carried = None
        for t in range(ring - 1):
            partial = grams[t] if carried is None else grams[t] + carried
            carried = lax.ppermute(partial, "dp", [(z, (z + 1) % ring) for z in range(ring)])
        top, rest = factor_top(grams[ring - 1], carried)

        def shared(array):
            return [array] + [
                lax.ppermute(array, "dp", [(z, (z + d) % ring) for z in range(ring)]) for d in range(1, ring)
            ]

        tops = shared(top)
        bottom = factor_bottom(rest)
        bottoms = shared(bottom)
        order = jnp.stack([lax.rem(place - d + ring, ring) for d in range(ring)])
    else:
        halves = [factor_top(lax.psum(grams[t], "dp")) for t in range(blocks)]
        tops = [top for top, _ in halves]
        bottoms = [factor_bottom(rest) for _, rest in halves]
        bottom = bottoms[0]
        order = jnp.arange(blocks, dtype=jnp.int32)

    turned = turn(blocks // 2, blocks - blocks // 2, turned, bottom)

    def whiten(uppers, first, start, result):
        more = [] if result is None else [result]
        depth = BLOCK_W - start
        chunks = features // tile
        weights = [
            pl.BlockSpec(
                (depth, tile),
                lambda b, order, c=c: (order[first + b] * (BLOCK_W // depth) + start // depth, c),
            )
            for c in range(chunks)
        ]
        return pl.pallas_call(
            functools.partial(
                whiten_kernel, blocks=len(uppers), start=start, first=first, chunks=chunks, aliased=len(more)
            ),
            out_shape=jax.ShapeDtypeStruct((blocks, BLOCK_W, features), F32),
            grid_spec=pltpu.PrefetchScalarGridSpec(
                num_scalar_prefetch=1,
                grid=(len(uppers),),
                in_specs=[vmem] * len(uppers) + weights + [anywhere] * len(more),
                out_specs=anywhere,
                scratch_shapes=[
                    pltpu.VMEM((2 * half, depth), BF16),
                    pltpu.VMEM((2, half, features), F32),
                    pltpu.SemaphoreType.DMA((2, chunks)),
                ],
            ),
            input_output_aliases={1 + len(uppers) + chunks: 0} if more else {},
            compiler_params=params(),
            cost_estimate=cost(2.0e9 * len(uppers), 2**20),
            name="whiten_bottom" if start else "whiten_top",
        )(order, *uppers, *[turned] * chunks, *more)

    result = whiten(tops[:1], 0, 0, None)
    result = whiten(bottoms[:1], 0, half, result)
    result = whiten(tops[1:], 1, 0, result)
    return whiten(bottoms[1:], 1, half, result)


def solution(mesh):
    in_specs = (
        P(("groups", "dp"), "seq", None),
        P(("groups", "dp"), "seq", None),
        P(("groups", "dp"), "seq", None),
        P(("groups", "dp"), None),
        P(("groups", "dp"), None),
        P("dp", "seq"),
    )
    out_specs = P(("groups", "seq"), None, "dp")
    return jax.shard_map(shards, mesh=mesh, in_specs=in_specs, out_specs=out_specs, check_vma=False)
```

```python
import functools
import math

import jax
import jax.numpy as jnp
from jax import lax
from jax.experimental import pallas as pl
from jax.experimental.pallas import tpu as pltpu
from jax.sharding import PartitionSpec as P

QUERY_HEADS = 64
KEY_VALUE_HEADS = 8
HEAD_SIZE = 128
BLOCK_W = 512
NB = 16
SPAN = 128
GROUP = QUERY_HEADS // KEY_VALUE_HEADS
BLOCK_HEADS = BLOCK_W // HEAD_SIZE
KV_BLOCKS = GROUP // BLOCK_HEADS
PANELS = BLOCK_W // SPAN
STARTS = [sum(BLOCK_W - SPAN * j for j in range(k)) for k in range(PANELS)]
PACKED = sum(BLOCK_W - SPAN * j for j in range(PANELS))
VMEM_BYTES = 50 * 1024 * 1024
F32 = jnp.float32
BF16 = jnp.bfloat16
NT = (((1,), (1,)), ((), ()))
TN = (((0,), (0,)), ((), ()))


def params(limit=VMEM_BYTES):
    return pltpu.CompilerParams(vmem_limit_bytes=limit)


def cost(flops, moved, trans=0):
    return pl.CostEstimate(flops=int(flops), bytes_accessed=int(moved), transcendentals=int(trans))


def encode(value, exponent):
    scaled = value * jnp.exp2(15.0 - exponent)
    power = scaled * scaled
    power = power * power
    power = power * power
    return jnp.where(scaled < 0.0, -power, power)


def decode(code, exponent):
    code = code.astype(F32)
    root = jnp.exp2(jnp.log(jnp.maximum(jnp.abs(code), 1e-37)) * (0.125 / math.log(2.0)) + (exponent - 15.0))
    return jnp.where(code < 0.0, -root, root)


def marker():
    rows = lax.broadcasted_iota(jnp.int32, (SPAN, SPAN), 0)
    columns = lax.broadcasted_iota(jnp.int32, (SPAN, SPAN), 1)
    return (rows == SPAN - 1) & (columns == 0)


def exponent_of(largest):
    return jnp.ceil(jnp.log(jnp.maximum(largest, 1e-30)) * (1.0 / math.log(2.0)) + 0.001)


def write_coded(panels, out, largest):
    exponent = exponent_of(largest)
    at = 0
    for k, panel in enumerate(panels):
        coded = encode(panel, exponent)
        if k == 0:
            first = jnp.where(marker(), jnp.broadcast_to(exponent, (SPAN, SPAN)), coded[:, :SPAN])
            coded = jnp.concatenate([first, coded[:, SPAN:]], axis=1)
        out[:, at : at + panel.shape[1]] = coded.astype(BF16)
        at += panel.shape[1]


def read_coded(ref):
    exponent = ref[SPAN - 16 : SPAN, :SPAN].astype(F32)[15:16, 0:1]
    return decode(ref[...], exponent)


def split(value):
    high = value.astype(BF16)
    return high, (value - high.astype(F32)).astype(BF16)


def cut_kernel(meta, *refs, targets, given):
    outs = refs[-targets:]
    for number, out in enumerate(outs):
        at = 0
        for ref in refs[number * given : (number + 1) * given]:
            out[:, at : at + ref.shape[1]] = ref[...]
            at += ref.shape[1]


def turn_kernel(w_ref, *refs):
    refs[-1][...] = w_ref[...].T


def attention_kernel(meta, *refs, chips, spans, all_spans, documents, most, sets, waited):
    sources = 2 * chips
    near = sources + 4
    query_refs, near_refs = refs[:sources], refs[sources:near]
    far_refs = refs[near : near + sets * (sources - 2)]
    out, queries, keys, values, slots, limits, left, right, total = refs[near + sets * (sources - 2) + waited :]
    own = meta[0]
    chip, core = own // 2, lax.rem(own, 2)
    lengths = 4
    order = lengths + documents

    for r in range(all_spans):
        device = r // spans
        distance = lax.rem(chip - device // 2 + chips, chips)
        cross = lax.rem(core + device % 2, 2)
        slots[meta[order + r]] = (distance * 2 + cross) * spans + r % spans

    def place_kv(source, key_part, value_part):
        for t in range(spans):
            rows = slice(t * SPAN, (t + 1) * SPAN)
            keys[source * spans + t] = key_part[rows]
            values[source * spans + t] = value_part[rows].astype(F32).T.astype(BF16)

    place_kv(0, near_refs[0], near_refs[1])
    place_kv(1, near_refs[2], near_refs[3])
    for which in range(sets):

        @pl.when(meta[3] == which)
        def _(which=which):
            for source in range(2, sources):
                ref = far_refs[which * (sources - 2) + source - 2]
                place_kv(source, ref[:, :HEAD_SIZE], ref[:, HEAD_SIZE:])

    for source in range(sources):
        for t in range(spans):
            for h in range(BLOCK_HEADS):
                queries[source * spans + t, h * SPAN : (h + 1) * SPAN] = query_refs[source][
                    t * SPAN : (t + 1) * SPAN, h * HEAD_SIZE : (h + 1) * HEAD_SIZE
                ]

    factor = HEAD_SIZE ** (-0.5) / math.log(2.0)

    def one_span(q, carry):
        source = q // spans
        distance, cross = source // 2, lax.rem(source, 2)
        device = lax.rem(chip - distance + chips, chips) * 2 + lax.rem(core + cross, 2)
        position = meta[order + device * spans + lax.rem(q, spans)]
        first_row = position * SPAN
        begin = jnp.int32(0)
        at = jnp.int32(0)
        query_pos = lax.broadcasted_iota(jnp.int32, (1, SPAN), 1) + first_row
        query_begin = jnp.zeros((1, SPAN), jnp.int32)
        for d in range(documents):
            begin = jnp.where(at <= first_row, at, begin)
            query_begin = jnp.where(query_pos >= at, at, query_begin)
            at = at + meta[lengths + d]
        count = position - begin // SPAN + 1
        lanes = pl.ds(pl.multiple_of(q * SPAN, SPAN), SPAN)

        for n in range(1, most + 1):

            @pl.when(count == n)
            def _(n=n):
                held = [slots[position - n + 1 + i] for i in range(n)]
                for i in range(n):
                    key_pos = lax.broadcasted_iota(jnp.int32, (SPAN, SPAN), 0) + (position - n + 1 + i) * SPAN
                    seen = (key_pos <= query_pos) & (key_pos >= query_begin)
                    limits[i * SPAN : (i + 1) * SPAN] = jnp.where(seen, 3e38, -1e30)
                key_part = jnp.concatenate([keys[slot] for slot in held], axis=0)
                value_part = jnp.concatenate([values[slot] for slot in held], axis=1)
                scores = lax.dot_general(key_part, queries[q], NT, preferred_element_type=F32)
                limit = limits[: n * SPAN]
                scores = jnp.minimum(scores, jnp.concatenate([limit] * BLOCK_HEADS, axis=1))
                largest = jnp.max(scores, axis=0, keepdims=True)
                lifted = jnp.exp2((scores - largest) * factor)
                summed = jnp.sum(lifted, axis=0, keepdims=True)
                weights = (lifted * (1.0 / summed)).astype(BF16)
                mixed = jnp.dot(value_part, weights, preferred_element_type=F32)
                for h in range(BLOCK_HEADS):
                    one_head = mixed[:, h * SPAN : (h + 1) * SPAN]
                    columns = slice(h * HEAD_SIZE, (h + 1) * HEAD_SIZE)
                    high, low = split(one_head)
                    left[0, columns, lanes] = high
                    left[1, columns, lanes] = low
                    high, low = split(one_head.T)
                    right[0, lanes, columns] = high
                    right[1, lanes, columns] = low

        return carry

    lax.fori_loop(0, all_spans, one_span, 0)

    half = BLOCK_W // 2
    total[...] = jnp.zeros_like(total)

    def one_pass(i, carry):
        a, b = lax.rem(i, 2), i // 2
        total[:half] += jnp.dot(left[a, :half], right[b], preferred_element_type=F32)
        total[half:, half:] += jnp.dot(left[a, half:], right[b, :, half:], preferred_element_type=F32)
        return carry

    lax.fori_loop(0, 3, one_pass, 0)
    for i, packed in enumerate(fold(total)):
        out[:, i * BLOCK_W : (i + 1) * BLOCK_W] = packed


def tile_of(ref, i, j):
    return ref[i * SPAN : (i + 1) * SPAN, j * SPAN : (j + 1) * SPAN]


def diagonal_masks():
    rows = lax.broadcasted_iota(jnp.int32, (SPAN, SPAN), 0)
    columns = lax.broadcasted_iota(jnp.int32, (SPAN, SPAN), 1)
    return rows <= columns, rows == columns


def fold(ref):
    upper, equal = diagonal_masks()
    for off, (a, b) in ((((0, 1), (0, 2), (0, 3)), (0, 1)), (((1, 2), (1, 3), (2, 3)), (2, 3))):
        second = tile_of(ref, b, b)
        square = jnp.where(upper, tile_of(ref, a, a), second)
        line = jnp.sum(jnp.where(equal, second, 0.0), axis=0, keepdims=True)
        body = jnp.concatenate([tile_of(ref, *where) for where in off] + [square], axis=1)
        tail = jnp.concatenate([jnp.zeros((8, 3 * SPAN), F32), jnp.broadcast_to(line, (8, SPAN))], axis=1)
        yield jnp.concatenate([body, tail], axis=0)


def unfold(packs, work):
    upper, equal = diagonal_masks()
    trace = jnp.zeros((1, 1), F32)
    squares = []
    for pack, off, (a, b) in zip(
        packs, (((0, 1), (0, 2), (0, 3)), ((1, 2), (1, 3), (2, 3))), ((0, 1), (2, 3))
    ):
        for i, (row, column) in enumerate(off):
            work[row * SPAN : (row + 1) * SPAN, column * SPAN : (column + 1) * SPAN] = pack[:SPAN, i * SPAN : (i + 1) * SPAN]
        square = pack[:SPAN, 3 * SPAN :]
        turned = square.T
        line = jnp.broadcast_to(pack[SPAN : SPAN + 1, 3 * SPAN :], (SPAN, SPAN))
        squares.append((a, jnp.where(upper, square, turned)))
        squares.append((b, jnp.where(equal, line, jnp.where(upper, turned, square))))
    for _, square in squares:
        trace = trace + jnp.sum(jnp.where(equal, square, 0.0), axis=(0, 1), keepdims=True)
    damping = trace * (0.1 / BLOCK_W)
    for a, square in squares:
        work[a * SPAN : (a + 1) * SPAN, a * SPAN : (a + 1) * SPAN] = jnp.where(equal, square + damping, square)


def factor_kernel(*refs, start, stop, received):
    width = BLOCK_W - start
    panels = width // SPAN
    step = 32
    groups = step // 8
    per_tile = SPAN // step
    last = stop == BLOCK_W
    given, refs = (refs[:received], refs[received:])
    out, refs = refs[0], refs[1:]
    if not last:
        rest, refs = refs[0], refs[1:]
    work, previous, upper = refs
    if start == 0:
        work[...] = jnp.zeros_like(work)
        total = given[0][...] + given[1][...] if received == 2 else given[0][...]
        unfold((total[:, :BLOCK_W], total[:, BLOCK_W:]), work)
    else:
        work[...] = given[0][...]
    previous[...] = jnp.zeros_like(previous)

    def triple(value, first):
        high, low = split(value)
        return jnp.concatenate((high, low, high) if first else (high, high, low), axis=0)

    def superpanel(g, carry):
        row = pl.multiple_of(g * step, step)
        tile_index = g // per_tile
        tile = pl.ds(pl.multiple_of(tile_index * SPAN, SPAN), SPAN)
        turn = lax.rem(SPAN - lax.rem(g, per_tile) * step, SPAN)
        before = previous[...]
        right = triple(before, False)
        near = pltpu.roll(previous[:, tile], turn, 1)
        fresh = lax.dot_general(triple(near, True), right, TN, preferred_element_type=F32)[:step]
        current = work[pl.ds(row, step), :] - fresh
        work[...] = work[...] - lax.dot_general(triple(before, True), right, TN, preferred_element_type=F32)

        square = current[:, :SPAN]
        for k in range(1, panels):
            square = jnp.where(tile_index == k, current[:, k * SPAN : (k + 1) * SPAN], square)
        square = pltpu.roll(square, turn, 1)
        line = lax.broadcasted_iota(jnp.int32, (8, SPAN), 0)
        held = [
            {q: jnp.broadcast_to(square[8 * q : 8 * q + 8, j : j + 1], (8, SPAN)) for q in range(j // 8, groups)}
            for j in range(step)
        ]
        body = [[current[8 * q : 8 * q + 8, k * SPAN : (k + 1) * SPAN] for k in range(panels)] for q in range(groups)]
        scales = [jnp.zeros((8, SPAN), F32) for _ in range(groups)]

        def spread(value, i):
            return jnp.broadcast_to(value[i % 8 : i % 8 + 1], (8, SPAN))

        for i in range(step):
            at = i // 8
            root = lax.rsqrt(spread(held[i][at], i))
            inverse = root * root
            scales[at] = jnp.where(line == i % 8, root, scales[at])
            ratio = {q: held[i][q] * inverse for q in range(at, groups)}
            ratio[at] = jnp.where(line > i % 8, ratio[at], 0.0)
            for j in range(i + 1, step):
                entry = spread(held[i][j // 8], j)
                for q in range(j // 8, groups):
                    held[j][q] = held[j][q] - ratio[q] * entry
            for k in range(panels):
                pivot_row = spread(body[at][k], i)
                for q in range(at, groups):
                    body[q][k] = body[q][k] - ratio[q] * pivot_row
        result = jnp.concatenate(
            [jnp.concatenate([body[q][k] * scales[q] for k in range(panels)], axis=1) for q in range(groups)], axis=0
        )
        across = lax.broadcasted_iota(jnp.int32, (step, width), 1)
        down = lax.broadcasted_iota(jnp.int32, (step, width), 0)
        result = jnp.where(across >= down + row, result, 0.0)
        previous[...] = result
        upper[pl.ds(row, step), :] = result
        return carry

    lax.fori_loop(0, (stop - start) // step, superpanel, 0)
    if not last:
        done = stop - start
        before = previous[...]
        final = lax.dot_general(
            triple(before[:, done:], True), triple(before[:, done:], False), TN, preferred_element_type=F32
        )
        rest[...] = work[done:, done:] - final
    ready = [upper[k * SPAN : (k + 1) * SPAN, k * SPAN :] for k in range((stop - start) // SPAN)]
    largest = functools.reduce(jnp.maximum, [jnp.max(jnp.abs(p), axis=(0, 1), keepdims=True) for p in ready])
    write_coded(ready, out, largest)


def whiten_kernel(order, *refs, blocks, starts, first, chunks, aliased):
    count = len(starts)
    u_refs, refs = refs[: blocks * count], refs[blocks * count :]
    w_refs, refs = refs[:chunks], refs[chunks + aliased :]
    out, left, ready, sems = refs
    half = BLOCK_W // 2
    chunk = ready.shape[2] // chunks
    step = pl.program_id(0)
    lowest = starts[0]

    def copy(number, which, c):
        slot = lax.rem(number * count + which, 2)
        columns = pl.ds(c * chunk, chunk)
        return pltpu.make_async_copy(
            ready.at[slot, :, columns],
            out.at[order[first + number], pl.ds(starts[which], half), columns],
            sems.at[slot, c],
        )

    for which, start in enumerate(starts):
        width = BLOCK_W - start
        for b in range(blocks):

            @pl.when(step == b)
            def _(b=b):
                upper = read_coded(u_refs[b * count + which])
                rows = lax.broadcasted_iota(jnp.int32, (SPAN, SPAN), 0)
                columns = lax.broadcasted_iota(jnp.int32, (SPAN, SPAN), 1)
                at = 0
                for k in range(half // SPAN):
                    panel = upper[:, at : at + width - SPAN * k]
                    at += width - SPAN * k
                    pieces = [jnp.zeros((SPAN, SPAN * k), F32)] if k else []
                    pieces += [jnp.where(rows > columns, 0.0, panel[:, :SPAN]), panel[:, SPAN:]]
                    high, low = split(jnp.concatenate([p for p in pieces if p.shape[1]], axis=1))
                    left[k * SPAN : (k + 1) * SPAN, :width] = high
                    left[k * SPAN : (k + 1) * SPAN, width : 2 * width] = low

        for c in range(chunks):
            if count == 1:

                @pl.when(step >= 2)
                def _(c=c):
                    copy(step - 2, which, c).wait()

            elif blocks > 1:

                @pl.when(step >= 1)
                def _(c=c):
                    copy(step - 1, which, c).wait()

            weight = w_refs[c][start - lowest :]
            product = jnp.dot(
                left[:, : 2 * width], jnp.concatenate([weight, weight], axis=0), preferred_element_type=F32
            )
            ready[lax.rem(step * count + which, 2), :, c * chunk : (c + 1) * chunk] = product
            copy(step, which, c).start()

    @pl.when(step == blocks - 1)
    def _():
        for c in range(chunks):
            if count > 1:
                copy(step, 0, c).wait()
            elif blocks > 1:
                copy(step - 1, 0, c).wait()
            copy(step, count - 1, c).wait()


def shards(query_rows, key_rows, placed_value_rows, doc_lengths, span_order, out_weight):
    tokens = query_rows.shape[1]
    features = out_weight.shape[0]
    seq = lax.axis_size("seq")
    ring = lax.axis_size("dp")
    chips = seq // 2
    spans = tokens // SPAN
    all_spans = spans * seq
    documents = doc_lengths.shape[1]
    per = KEY_VALUE_HEADS // seq
    blocks = NB // seq
    own = lax.axis_index("seq").astype(jnp.int32)
    place = lax.axis_index("dp").astype(jnp.int32)
    query, key, value = query_rows[0], key_rows[0], placed_value_rows[0]
    vmem = pl.BlockSpec(memory_space=pltpu.VMEM)
    anywhere = pl.BlockSpec(memory_space=pl.ANY)
    in_ring = blocks == ring

    if in_ring:
        turns = [lax.rem(place + 2 * ring - 1 - t, ring) for t in range(blocks)]
    else:
        turns = [jnp.int32(t) for t in range(blocks)]
    first_kv = turns[0] // KV_BLOCKS

    def moved(distance, cross):
        return [
            (x * 2 + c, (x + distance) % chips * 2 + (1 - c if cross else c)) for x in range(chips) for c in range(2)
        ]

    def cut(targets, columns, scalars, name, after=(), limit=VMEM_BYTES):
        specs, arrays = [], []
        for target in targets:
            for array, size, index in columns:
                specs.append(
                    pl.BlockSpec((tokens, size), lambda i, meta, target=target, index=index: (0, index(target(meta), meta)))
                )
                arrays.append(array)
        width = sum(size for _, size, _ in columns)
        return pl.pallas_call(
            functools.partial(cut_kernel, targets=len(targets), given=len(columns)),
            out_shape=[jax.ShapeDtypeStruct((tokens, width), BF16)] * len(targets),
            grid_spec=pltpu.PrefetchScalarGridSpec(
                num_scalar_prefetch=1,
                grid=(1,),
                in_specs=specs + [anywhere] * len(after),
                out_specs=[pl.BlockSpec((tokens, width), lambda i, meta: (0, 0))] * len(targets),
            ),
            compiler_params=params(limit),
            cost_estimate=cost(0, 2**21),
            name=name,
        )(scalars, *arrays, *after)

    tile = 512

    def turn(first, count, *before):
        return pl.pallas_call(
            turn_kernel,
            out_shape=jax.ShapeDtypeStruct((blocks * BLOCK_W, features), BF16),
            grid=(count, features // tile),
            in_specs=[pl.BlockSpec((tile, BLOCK_W), lambda b, o: (o, first + b))] + [anywhere] * len(before),
            out_specs=pl.BlockSpec((BLOCK_W, tile), lambda b, o: (first + b, o)),
            input_output_aliases={1: 0} if first else {},
            compiler_params=params(),
            cost_estimate=cost(1.0e9 * count, 2**20),
            name="turn_weight",
        )(out_weight, *before)

    def target_at(distance, cross):
        return lambda meta: lax.rem(meta[0] // 2 + distance, chips) * 2 + lax.rem(lax.rem(meta[0], 2) + cross, 2)

    far = [(distance, cross) for distance in range(1, chips) for cross in range(2)]
    pieces = []

    most = all_spans // 2 + 1

    def grams_of(t, peer, after):
        kv = turns[t] // KV_BLOCKS
        carriers = pieces[: min(t + 1, per)]
        which = jnp.where(kv == first_kv, 0, 1).astype(jnp.int32)
        meta = jnp.concatenate([jnp.stack([own, turns[t], kv, which]), doc_lengths[0], span_order[0]])
        folded = jax.ShapeDtypeStruct((SPAN + 8, 2 * BLOCK_W), F32)
        peer_kv = blocks * BLOCK_W // HEAD_SIZE
        return pl.pallas_call(
            functools.partial(
                attention_kernel,
                chips=chips, spans=spans, all_spans=all_spans, documents=documents, most=most, sets=len(carriers),
                waited=len(after),
            ),
            out_shape=folded,
            grid_spec=pltpu.PrefetchScalarGridSpec(
                num_scalar_prefetch=1,
                grid=(1,),
                in_specs=[
                    pl.BlockSpec((tokens, BLOCK_W), lambda i, meta: (0, meta[0] * blocks + meta[1])),
                    pl.BlockSpec((tokens, BLOCK_W), lambda i, meta: (0, meta[1])),
                ]
                + [pl.BlockSpec((tokens, BLOCK_W), lambda i, meta: (0, 0))] * len(far)
                + [pl.BlockSpec((tokens, HEAD_SIZE), lambda i, meta: (0, meta[0] * per + meta[2]))] * 2
                + [
                    pl.BlockSpec((tokens, HEAD_SIZE), lambda i, meta: (0, peer_kv + meta[2])),
                    pl.BlockSpec((tokens, HEAD_SIZE), lambda i, meta: (0, peer_kv + per + meta[2])),
                ]
                + [pl.BlockSpec((tokens, 2 * HEAD_SIZE), lambda i, meta: (0, BLOCK_W // (2 * HEAD_SIZE)))]
                * (len(carriers) * len(far))
                + [anywhere] * len(after),
                out_specs=pl.BlockSpec((SPAN + 8, 2 * BLOCK_W), lambda i, meta: (0, 0)),
                scratch_shapes=[
                    pltpu.VMEM((all_spans, BLOCK_HEADS * SPAN, HEAD_SIZE), BF16),
                    pltpu.VMEM((all_spans, SPAN, HEAD_SIZE), BF16),
                    pltpu.VMEM((all_spans, HEAD_SIZE, SPAN), BF16),
                    pltpu.SMEM((all_spans,), jnp.int32),
                    pltpu.VMEM((most * SPAN, SPAN), F32),
                    pltpu.VMEM((2, BLOCK_W, all_spans * SPAN), BF16),
                    pltpu.VMEM((2, all_spans * SPAN, BLOCK_W), BF16),
                    pltpu.VMEM((BLOCK_W, BLOCK_W), F32),
                ],
            ),
            compiler_params=params(),
            cost_estimate=cost(1.4e10, 2**20),
            name="attention_outer_products",
        )(meta, query, peer, *pieces[t], key, value, peer, peer, *[array for carrier in carriers for array in carrier], *after)

    grams = []
    held = []
    for t in range(blocks + 1):
        if t < blocks:
            kv = first_kv if t == 0 else per - 1 - first_kv
            columns = [(query, BLOCK_W, lambda target, meta: target * blocks + meta[1])]
            if t < per:
                columns += [(array, HEAD_SIZE, lambda target, meta: target * per + meta[2]) for array in (key, value)]
            scalars = jnp.stack([own, turns[t], kv])
            after = [] if t == 0 else [peer, turned] if t == 1 else [held[t - 2]]
            parts = cut(
                [target_at(*where) for where in far], columns, scalars, "cut_piece", after,
                VMEM_BYTES if t else 63 * 2**20,
            )
            pieces.append([lax.ppermute(part, "seq", moved(*where)) for part, where in zip(parts, far)])
        if t == 0:
            columns = [(query, blocks * BLOCK_W, lambda target, meta: target)]
            columns += [(array, per * HEAD_SIZE, lambda target, meta: target) for array in (key, value)]
            peer = cut([target_at(0, 1)], columns, own[None], "cut_peer", parts)[0]
            turned = turn(0, 1, peer)
            peer = lax.ppermute(peer, "seq", moved(0, 1))
            turned = turn(1, 1, turned)
            continue
        if t == 1:
            for b in range(2, blocks - 1):
                turned = turn(b, 1, turned, parts[0])
        done = t - 1
        grams.append(grams_of(done, peer, [turned] if t == 1 else []))
        if done == 0 or not in_ring:
            held.append(grams[done])
        else:
            held.append(grams[done] + carried if done < ring - 1 else None)
        if in_ring and done < ring - 1:
            carried = lax.ppermute(held[done], "dp", [(z, (z + 1) % ring) for z in range(ring)])
    if blocks > 2:
        turned = turn(blocks - 1, 1, turned, grams[-1])

    half = BLOCK_W // 2
    top_width, bottom_width = STARTS[2], PACKED - STARTS[2]
    scratch = lambda width: [pltpu.VMEM((width, width), F32), pltpu.VMEM((32, width), F32), pltpu.VMEM((half, width), F32)]

    def factor_top(*given):
        return pl.pallas_call(
            functools.partial(factor_kernel, start=0, stop=half, received=len(given)),
            out_shape=[
                jax.ShapeDtypeStruct((SPAN, top_width), BF16),
                jax.ShapeDtypeStruct((half, half), F32),
            ],
            in_specs=[vmem] * len(given),
            out_specs=[vmem] * 2,
            scratch_shapes=scratch(BLOCK_W),
            compiler_params=params(),
            cost_estimate=cost(1.0e10, 2**20),
            name="factor_top",
        )(*given)

    def factor_bottom(rest):
        return pl.pallas_call(
            functools.partial(factor_kernel, start=half, stop=BLOCK_W, received=1),
            out_shape=jax.ShapeDtypeStruct((SPAN, bottom_width), BF16),
            in_specs=[vmem],
            out_specs=vmem,
            scratch_shapes=scratch(half),
            compiler_params=params(),
            cost_estimate=cost(0.9e10, 2**20),
            name="factor_bottom",
        )(rest)

    if in_ring:
        top, rest = factor_top(grams[ring - 1], carried)

        def shared(array):
            return [array] + [
                lax.ppermute(array, "dp", [(z, (z + d) % ring) for z in range(ring)]) for d in range(1, ring)
            ]

        tops = shared(top)
        bottom = factor_bottom(rest)
        bottoms = shared(bottom)
        order = jnp.stack([lax.rem(place - d + ring, ring) for d in range(ring)])
    else:
        halves = [factor_top(lax.psum(grams[t], "dp")) for t in range(blocks)]
        tops = [top for top, _ in halves]
        bottoms = [factor_bottom(rest) for _, rest in halves]
        bottom = bottoms[0]
        order = jnp.arange(blocks, dtype=jnp.int32)


    def whiten(uppers, first, starts, result):
        more = [] if result is None else [result]
        depth = BLOCK_W - starts[0]
        chunks = features // tile
        count = len(uppers) // len(starts)
        weights = [
            pl.BlockSpec(
                (depth, tile),
                lambda b, order, c=c: (order[first + b] * (BLOCK_W // depth) + starts[0] // depth, c),
            )
            for c in range(chunks)
        ]
        return pl.pallas_call(
            functools.partial(
                whiten_kernel, blocks=count, starts=starts, first=first, chunks=chunks, aliased=len(more)
            ),
            out_shape=jax.ShapeDtypeStruct((blocks, BLOCK_W, features), F32),
            grid_spec=pltpu.PrefetchScalarGridSpec(
                num_scalar_prefetch=1,
                grid=(count,),
                in_specs=[vmem] * len(uppers) + weights + [anywhere] * len(more),
                out_specs=anywhere,
                scratch_shapes=[
                    pltpu.VMEM((half, 2 * depth), BF16),
                    pltpu.VMEM((2, half, features), F32),
                    pltpu.SemaphoreType.DMA((2, chunks)),
                ],
            ),
            input_output_aliases={1 + len(uppers) + chunks: 0} if more else {},
            compiler_params=params(),
            cost_estimate=cost(2.0e9 * len(uppers), 2**20),
            name="whiten_bottom" if starts[0] else "whiten_top",
        )(order, *uppers, *[turned] * chunks, *more)

    result = whiten([tops[0], bottoms[0]], 0, (0, half), None)
    result = whiten(tops[1:], 1, (0,), result)
    return whiten(bottoms[1:], 1, (half,), result)


def solution(mesh):
    in_specs = (
        P(("groups", "dp"), "seq", None),
        P(("groups", "dp"), "seq", None),
        P(("groups", "dp"), "seq", None),
        P(("groups", "dp"), None),
        P(("groups", "dp"), None),
        P("dp", "seq"),
    )
    out_specs = P(("groups", "seq"), None, "dp")
    return jax.shard_map(shards, mesh=mesh, in_specs=in_specs, out_specs=out_specs, check_vma=False)
```

```python
import functools
import math

import jax
import jax.numpy as jnp
from jax import lax
from jax.experimental import pallas as pl
from jax.experimental.pallas import tpu as pltpu
from jax.sharding import PartitionSpec as P

QUERY_HEADS = 64
KEY_VALUE_HEADS = 8
HEAD_SIZE = 128
BLOCK_W = 512
NB = 16
SPAN = 128
GROUP = QUERY_HEADS // KEY_VALUE_HEADS
BLOCK_HEADS = BLOCK_W // HEAD_SIZE
KV_BLOCKS = GROUP // BLOCK_HEADS
PANELS = BLOCK_W // SPAN
SUM_ROWS = SPAN * (PANELS * (PANELS - 1) // 2 + PANELS // 2) + 8
VMEM_BYTES = 50 * 2**20
FULL_VMEM = 63 * 2**20
TURN_VMEM = 50 * 2**20
ATTENTION_VMEM = 44 * 2**20
WHITEN_VMEM = 44 * 2**20
OTHER_VMEM = 44 * 2**20
F32 = jnp.float32
BF16 = jnp.bfloat16
NT = (((1,), (1,)), ((), ()))
TN = (((0,), (0,)), ((), ()))


def params(limit=OTHER_VMEM):
    return pltpu.CompilerParams(vmem_limit_bytes=limit)


def cost(flops, moved, trans=0):
    return pl.CostEstimate(flops=int(flops), bytes_accessed=int(moved), transcendentals=int(trans))


def encode(value, exponent):
    scaled = value * jnp.exp2(15.0 - exponent)
    power = scaled * scaled
    power = power * power
    power = power * power
    return jnp.where(scaled < 0.0, -power, power)


def decode(code, exponent):
    code = code.astype(F32)
    root = jnp.exp2(jnp.log(jnp.maximum(jnp.abs(code), 1e-37)) * (0.125 / math.log(2.0)) + (exponent - 15.0))
    return jnp.where(code < 0.0, -root, root)


def exponent_of(largest):
    return jnp.ceil(jnp.log(jnp.maximum(largest, 1e-30)) * (1.0 / math.log(2.0)) + 0.001)


def write_coded(tiles, out):
    off, pairs = tile_order(tiles.rows, tiles.columns)
    places = off + [(i, i) for i in range(tiles.rows)]
    largest = functools.reduce(jnp.maximum, [jnp.max(jnp.abs(tiles(*p)), axis=(0, 1), keepdims=True) for p in places])
    exponent = exponent_of(largest)
    (line,) = fold(tiles, out, lambda value: encode(value, exponent))
    row = lax.broadcasted_iota(jnp.int32, (16, SPAN), 0)
    out[(len(off) + len(pairs)) * SPAN :] = jnp.where(row < 8, line, exponent).astype(BF16)


def read_coded(ref, columns):
    upper, equal = diagonal_masks()
    off, pairs = tile_order(2, columns)
    at = (len(off) + len(pairs)) * SPAN
    tail = ref[at:].astype(F32)
    exponent = tail[15:16, 0:1]
    tiles = {place: decode(ref[i * SPAN : (i + 1) * SPAN], exponent) for i, place in enumerate(off)}
    square = decode(ref[at - SPAN : at], exponent)
    line = decode(tail[0:1], exponent)
    tiles[0, 0] = jnp.where(upper, square, 0.0)
    tiles[1, 1] = jnp.where(equal, line, jnp.where(upper, square.T, 0.0))
    return tiles


def split(value):
    high = value.astype(BF16)
    return high, (value - high.astype(F32)).astype(BF16)


def cut_kernel(meta, *refs, targets, given):
    outs = refs[-targets:]
    for number, out in enumerate(outs):
        at = 0
        for ref in refs[number * given : (number + 1) * given]:
            out[:, at : at + ref.shape[1]] = ref[...]
            at += ref.shape[1]


def turn_kernel(w_ref, *refs):
    refs[-1][...] = w_ref[...].T


def attention_kernel(meta, *refs, chips, spans, all_spans, documents, most, sets, waited):
    sources = 2 * chips
    near = sources + 4
    query_refs, near_refs = refs[:sources], refs[sources:near]
    far_refs = refs[near : near + sets * (sources - 2)]
    out, queries, keys, values, slots, limits, left, right, total = refs[near + sets * (sources - 2) + waited :]
    own = meta[0]
    chip, core = own // 2, lax.rem(own, 2)
    lengths = 4
    order = lengths + documents

    for r in range(all_spans):
        device = r // spans
        distance = lax.rem(chip - device // 2 + chips, chips)
        cross = lax.rem(core + device % 2, 2)
        slots[meta[order + r]] = (distance * 2 + cross) * spans + r % spans

    def place_kv(source, key_part, value_part):
        for t in range(spans):
            rows = slice(t * SPAN, (t + 1) * SPAN)
            keys[source * spans + t] = key_part[rows]
            values[source * spans + t] = value_part[rows].astype(F32).T.astype(BF16)

    place_kv(0, near_refs[0], near_refs[1])
    place_kv(1, near_refs[2], near_refs[3])
    for which in range(sets):

        @pl.when(meta[3] == which)
        def _(which=which):
            for source in range(2, sources):
                ref = far_refs[which * (sources - 2) + source - 2]
                place_kv(source, ref[:, :HEAD_SIZE], ref[:, HEAD_SIZE:])

    for source in range(sources):
        for t in range(spans):
            for h in range(BLOCK_HEADS):
                queries[source * spans + t, h * SPAN : (h + 1) * SPAN] = query_refs[source][
                    t * SPAN : (t + 1) * SPAN, h * HEAD_SIZE : (h + 1) * HEAD_SIZE
                ]

    factor = HEAD_SIZE ** (-0.5) / math.log(2.0)

    def one_span(q, carry):
        source = q // spans
        distance, cross = source // 2, lax.rem(source, 2)
        device = lax.rem(chip - distance + chips, chips) * 2 + lax.rem(core + cross, 2)
        position = meta[order + device * spans + lax.rem(q, spans)]
        first_row = position * SPAN
        begin = jnp.int32(0)
        at = jnp.int32(0)
        query_pos = lax.broadcasted_iota(jnp.int32, (1, SPAN), 1) + first_row
        query_begin = jnp.zeros((1, SPAN), jnp.int32)
        for d in range(documents):
            begin = jnp.where(at <= first_row, at, begin)
            query_begin = jnp.where(query_pos >= at, at, query_begin)
            at = at + meta[lengths + d]
        count = position - begin // SPAN + 1
        lanes = pl.ds(pl.multiple_of(q * SPAN, SPAN), SPAN)

        for n in range(1, most + 1):

            @pl.when(count == n)
            def _(n=n):
                held = [slots[position - n + 1 + i] for i in range(n)]
                for i in range(n):
                    key_pos = lax.broadcasted_iota(jnp.int32, (SPAN, SPAN), 0) + (position - n + 1 + i) * SPAN
                    seen = (key_pos <= query_pos) & (key_pos >= query_begin)
                    limits[i * SPAN : (i + 1) * SPAN] = jnp.where(seen, 3e38, -1e30)
                key_part = jnp.concatenate([keys[slot] for slot in held], axis=0)
                value_part = jnp.concatenate([values[slot] for slot in held], axis=1)
                scores = lax.dot_general(key_part, queries[q], NT, preferred_element_type=F32)
                limit = limits[: n * SPAN]
                scores = jnp.minimum(scores, jnp.concatenate([limit] * BLOCK_HEADS, axis=1))
                largest = jnp.max(scores, axis=0, keepdims=True)
                lifted = jnp.exp2((scores - largest) * factor)
                summed = jnp.sum(lifted, axis=0, keepdims=True)
                weights = (lifted * (1.0 / summed)).astype(BF16)
                mixed = jnp.dot(value_part, weights, preferred_element_type=F32)
                for h in range(BLOCK_HEADS):
                    one_head = mixed[:, h * SPAN : (h + 1) * SPAN]
                    columns = slice(h * HEAD_SIZE, (h + 1) * HEAD_SIZE)
                    high, low = split(one_head)
                    left[0, columns, lanes] = high
                    left[1, columns, lanes] = low
                    high, low = split(one_head.T)
                    right[0, lanes, columns] = high
                    right[1, lanes, columns] = low

        return carry

    lax.fori_loop(0, all_spans, one_span, 0)

    half = BLOCK_W // 2
    total[...] = jnp.zeros_like(total)

    def one_pass(i, carry):
        a, b = lax.rem(i, 2), i // 2
        total[:half] += jnp.dot(left[a, :half], right[b], preferred_element_type=F32)
        total[half:, half:] += jnp.dot(left[a, half:], right[b, :, half:], preferred_element_type=F32)
        return carry

    lax.fori_loop(0, 3, one_pass, 0)
    lines = fold(Tiles(total, PANELS, PANELS, False), out)
    row = lax.broadcasted_iota(jnp.int32, (8, SPAN), 0)
    out[SUM_ROWS - 8 :] = jnp.where(row == 0, lines[0], lines[1])


def diagonal_masks():
    rows = lax.broadcasted_iota(jnp.int32, (SPAN, SPAN), 0)
    columns = lax.broadcasted_iota(jnp.int32, (SPAN, SPAN), 1)
    return rows <= columns, rows == columns


def tile_order(rows, columns):
    off = [(i, j) for i in range(rows) for j in range(i + 1, columns)]
    return off, [(i, i + 1) for i in range(0, rows, 2)]


def fold(tiles, out, change=lambda value: value):
    upper, equal = diagonal_masks()
    off, pairs = tile_order(tiles.rows, tiles.columns)
    for i, place in enumerate(off):
        out[i * SPAN : (i + 1) * SPAN] = change(tiles(*place)).astype(out.dtype)
    lines = []
    for i, (a, b) in enumerate(pairs):
        second = tiles(b, b)
        at = (len(off) + i) * SPAN
        lower = second.T if tiles.turn else second
        out[at : at + SPAN] = change(jnp.where(upper, tiles(a, a), lower)).astype(out.dtype)
        lines.append(change(jnp.sum(jnp.where(equal, second, 0.0), axis=0, keepdims=True)))
    return lines


class Tiles:
    def __init__(self, ref, rows, columns, turn):
        self.ref, self.rows, self.columns, self.turn = ref, rows, columns, turn

    def __call__(self, i, j):
        return self.ref[i * SPAN : (i + 1) * SPAN, j * SPAN : (j + 1) * SPAN]


def unfold(total, work):
    upper, equal = diagonal_masks()
    off, pairs = tile_order(PANELS, PANELS)
    for i, (row, column) in enumerate(off):
        work[row * SPAN : (row + 1) * SPAN, column * SPAN : (column + 1) * SPAN] = total[i * SPAN : (i + 1) * SPAN]
    trace = jnp.zeros((1, 1), F32)
    squares = []
    for i, (a, b) in enumerate(pairs):
        at = (len(off) + i) * SPAN
        square = total[at : at + SPAN]
        turned = square.T
        at = (len(off) + len(pairs)) * SPAN + i
        line = jnp.broadcast_to(total[at : at + 1], (SPAN, SPAN))
        squares.append((a, jnp.where(upper, square, turned)))
        squares.append((b, jnp.where(equal, line, jnp.where(upper, turned, square))))
    for _, square in squares:
        trace = trace + jnp.sum(jnp.where(equal, square, 0.0), axis=(0, 1), keepdims=True)
    damping = trace * (0.1 / BLOCK_W)
    for a, square in squares:
        work[a * SPAN : (a + 1) * SPAN, a * SPAN : (a + 1) * SPAN] = jnp.where(equal, square + damping, square)


def factor_kernel(*refs, start, stop, received):
    width = BLOCK_W - start
    panels = width // SPAN
    step = 32
    groups = step // 8
    per_tile = SPAN // step
    last = stop == BLOCK_W
    given, refs = (refs[:received], refs[received:])
    out, refs = refs[0], refs[1:]
    if not last:
        rest, refs = refs[0], refs[1:]
    work, previous, upper = refs
    if start == 0:
        work[...] = jnp.zeros_like(work)
        total = given[0][...] + given[1][...] if received == 2 else given[0][...]
        unfold(total, work)
    else:
        work[...] = given[0][...]
    previous[...] = jnp.zeros_like(previous)

    def triple(value, first):
        high, low = split(value)
        return jnp.concatenate((high, low, high) if first else (high, high, low), axis=0)

    def superpanel(g, carry):
        row = pl.multiple_of(g * step, step)
        tile_index = g // per_tile
        tile = pl.ds(pl.multiple_of(tile_index * SPAN, SPAN), SPAN)
        turn = lax.rem(SPAN - lax.rem(g, per_tile) * step, SPAN)
        before = previous[...]
        right = triple(before, False)
        near = pltpu.roll(previous[:, tile], turn, 1)
        fresh = lax.dot_general(triple(near, True), right, TN, preferred_element_type=F32)[:step]
        current = work[pl.ds(row, step), :] - fresh
        work[...] = work[...] - lax.dot_general(triple(before, True), right, TN, preferred_element_type=F32)

        square = current[:, :SPAN]
        for k in range(1, panels):
            square = jnp.where(tile_index == k, current[:, k * SPAN : (k + 1) * SPAN], square)
        square = pltpu.roll(square, turn, 1)
        line = lax.broadcasted_iota(jnp.int32, (8, SPAN), 0)
        held = [
            {q: jnp.broadcast_to(square[8 * q : 8 * q + 8, j : j + 1], (8, SPAN)) for q in range(j // 8, groups)}
            for j in range(step)
        ]
        body = [[current[8 * q : 8 * q + 8, k * SPAN : (k + 1) * SPAN] for k in range(panels)] for q in range(groups)]
        scales = [jnp.zeros((8, SPAN), F32) for _ in range(groups)]

        def spread(value, i):
            return jnp.broadcast_to(value[i % 8 : i % 8 + 1], (8, SPAN))

        for i in range(step):
            at = i // 8
            root = lax.rsqrt(spread(held[i][at], i))
            inverse = root * root
            scales[at] = jnp.where(line == i % 8, root, scales[at])
            ratio = {q: held[i][q] * inverse for q in range(at, groups)}
            ratio[at] = jnp.where(line > i % 8, ratio[at], 0.0)
            for j in range(i + 1, step):
                entry = spread(held[i][j // 8], j)
                for q in range(j // 8, groups):
                    held[j][q] = held[j][q] - ratio[q] * entry
            for k in range(panels):
                pivot_row = spread(body[at][k], i)
                for q in range(at, groups):
                    body[q][k] = body[q][k] - ratio[q] * pivot_row
        result = jnp.concatenate(
            [jnp.concatenate([body[q][k] * scales[q] for k in range(panels)], axis=1) for q in range(groups)], axis=0
        )
        across = lax.broadcasted_iota(jnp.int32, (step, width), 1)
        down = lax.broadcasted_iota(jnp.int32, (step, width), 0)
        result = jnp.where(across >= down + row, result, 0.0)
        previous[...] = result
        upper[pl.ds(row, step), :] = result
        return carry

    lax.fori_loop(0, (stop - start) // step, superpanel, 0)
    if not last:
        done = stop - start
        before = previous[...]
        final = lax.dot_general(
            triple(before[:, done:], True), triple(before[:, done:], False), TN, preferred_element_type=F32
        )
        rest[...] = work[done:, done:] - final
    write_coded(Tiles(upper, (stop - start) // SPAN, panels, True), out)


def whiten_kernel(order, *refs, blocks, starts, first, chunks, aliased):
    count = len(starts)
    u_refs, refs = refs[: blocks * count], refs[blocks * count :]
    w_refs, refs = refs[:chunks], refs[chunks + aliased :]
    out, left, ready, sems = refs
    half = BLOCK_W // 2
    chunk = ready.shape[2] // chunks
    step = pl.program_id(0)
    lowest = starts[0]

    def copy(number, which, c):
        slot = lax.rem(number * count + which, 2)
        columns = pl.ds(c * chunk, chunk)
        return pltpu.make_async_copy(
            ready.at[slot, :, columns],
            out.at[order[first + number], pl.ds(starts[which], half), columns],
            sems.at[slot, c],
        )

    for which, start in enumerate(starts):
        width = BLOCK_W - start
        for b in range(blocks):

            @pl.when(step == b)
            def _(b=b):
                tiles = read_coded(u_refs[b * count + which], width // SPAN)
                for row in range(half // SPAN):
                    rows = slice(row * SPAN, (row + 1) * SPAN)
                    for column in range(width // SPAN):
                        value = tiles[row, column] if column >= row else jnp.zeros((SPAN, SPAN), F32)
                        high, low = split(value)
                        left[rows, column * SPAN : (column + 1) * SPAN] = high
                        left[rows, width + column * SPAN : width + (column + 1) * SPAN] = low

        for c in range(chunks):
            if count == 1:

                @pl.when(step >= 2)
                def _(c=c):
                    copy(step - 2, which, c).wait()

            elif blocks > 1:

                @pl.when(step >= 1)
                def _(c=c):
                    copy(step - 1, which, c).wait()

            weight = w_refs[c][start - lowest :]
            product = jnp.dot(
                left[:, : 2 * width], jnp.concatenate([weight, weight], axis=0), preferred_element_type=F32
            )
            ready[lax.rem(step * count + which, 2), :, c * chunk : (c + 1) * chunk] = product
            copy(step, which, c).start()

    @pl.when(step == blocks - 1)
    def _():
        for c in range(chunks):
            if count > 1:
                copy(step, 0, c).wait()
            elif blocks > 1:
                copy(step - 1, 0, c).wait()
            copy(step, count - 1, c).wait()


def shards(query_rows, key_rows, placed_value_rows, doc_lengths, span_order, out_weight):
    tokens = query_rows.shape[1]
    features = out_weight.shape[0]
    seq = lax.axis_size("seq")
    ring = lax.axis_size("dp")
    chips = seq // 2
    spans = tokens // SPAN
    all_spans = spans * seq
    documents = doc_lengths.shape[1]
    per = KEY_VALUE_HEADS // seq
    blocks = NB // seq
    own = lax.axis_index("seq").astype(jnp.int32)
    place = lax.axis_index("dp").astype(jnp.int32)
    query, key, value = query_rows[0], key_rows[0], placed_value_rows[0]
    vmem = pl.BlockSpec(memory_space=pltpu.VMEM)
    anywhere = pl.BlockSpec(memory_space=pl.ANY)
    in_ring = blocks == ring

    if in_ring:
        turns = [lax.rem(place + 2 * ring - 1 - t, ring) for t in range(blocks)]
    else:
        turns = [jnp.int32(t) for t in range(blocks)]
    first_kv = turns[0] // KV_BLOCKS

    def moved(distance, cross):
        return [
            (x * 2 + c, (x + distance) % chips * 2 + (1 - c if cross else c)) for x in range(chips) for c in range(2)
        ]

    def cut(targets, columns, scalars, name, after=(), limit=OTHER_VMEM):
        specs, arrays = [], []
        for target in targets:
            for array, size, index in columns:
                specs.append(
                    pl.BlockSpec((tokens, size), lambda i, meta, target=target, index=index: (0, index(target(meta), meta)))
                )
                arrays.append(array)
        width = sum(size for _, size, _ in columns)
        return pl.pallas_call(
            functools.partial(cut_kernel, targets=len(targets), given=len(columns)),
            out_shape=[jax.ShapeDtypeStruct((tokens, width), BF16)] * len(targets),
            grid_spec=pltpu.PrefetchScalarGridSpec(
                num_scalar_prefetch=1,
                grid=(1,),
                in_specs=specs + [anywhere] * len(after),
                out_specs=[pl.BlockSpec((tokens, width), lambda i, meta: (0, 0))] * len(targets),
            ),
            compiler_params=params(limit),
            cost_estimate=cost(0, 2**21),
            name=name,
        )(scalars, *arrays, *after)

    tile = 512

    def turn(first, count, *before):
        return pl.pallas_call(
            turn_kernel,
            out_shape=jax.ShapeDtypeStruct((blocks * BLOCK_W, features), BF16),
            grid=(count, features // tile),
            in_specs=[pl.BlockSpec((tile, BLOCK_W), lambda b, o: (o, first + b))] + [anywhere] * len(before),
            out_specs=pl.BlockSpec((BLOCK_W, tile), lambda b, o: (first + b, o)),
            input_output_aliases={1: 0} if first else {},
            compiler_params=params(TURN_VMEM),
            cost_estimate=cost(1.0e9 * count, 2**20),
            name="turn_weight",
        )(out_weight, *before)

    def target_at(distance, cross):
        return lambda meta: lax.rem(meta[0] // 2 + distance, chips) * 2 + lax.rem(lax.rem(meta[0], 2) + cross, 2)

    far = [(distance, cross) for distance in range(1, chips) for cross in range(2)]
    pieces = []

    most = all_spans // 2 + 1

    def grams_of(t, peer, after):
        kv = turns[t] // KV_BLOCKS
        carriers = pieces[: min(t + 1, per)]
        which = jnp.where(kv == first_kv, 0, 1).astype(jnp.int32)
        meta = jnp.concatenate([jnp.stack([own, turns[t], kv, which]), doc_lengths[0], span_order[0]])
        folded = jax.ShapeDtypeStruct((SUM_ROWS, SPAN), F32)
        peer_kv = blocks * BLOCK_W // HEAD_SIZE
        return pl.pallas_call(
            functools.partial(
                attention_kernel,
                chips=chips, spans=spans, all_spans=all_spans, documents=documents, most=most, sets=len(carriers),
                waited=len(after),
            ),
            out_shape=folded,
            grid_spec=pltpu.PrefetchScalarGridSpec(
                num_scalar_prefetch=1,
                grid=(1,),
                in_specs=[
                    pl.BlockSpec((tokens, BLOCK_W), lambda i, meta: (0, meta[0] * blocks + meta[1])),
                    pl.BlockSpec((tokens, BLOCK_W), lambda i, meta: (0, meta[1])),
                ]
                + [pl.BlockSpec((tokens, BLOCK_W), lambda i, meta: (0, 0))] * len(far)
                + [pl.BlockSpec((tokens, HEAD_SIZE), lambda i, meta: (0, meta[0] * per + meta[2]))] * 2
                + [
                    pl.BlockSpec((tokens, HEAD_SIZE), lambda i, meta: (0, peer_kv + meta[2])),
                    pl.BlockSpec((tokens, HEAD_SIZE), lambda i, meta: (0, peer_kv + per + meta[2])),
                ]
                + [pl.BlockSpec((tokens, 2 * HEAD_SIZE), lambda i, meta: (0, BLOCK_W // (2 * HEAD_SIZE)))]
                * (len(carriers) * len(far))
                + [anywhere] * len(after),
                out_specs=pl.BlockSpec((SUM_ROWS, SPAN), lambda i, meta: (0, 0)),
                scratch_shapes=[
                    pltpu.VMEM((all_spans, BLOCK_HEADS * SPAN, HEAD_SIZE), BF16),
                    pltpu.VMEM((all_spans, SPAN, HEAD_SIZE), BF16),
                    pltpu.VMEM((all_spans, HEAD_SIZE, SPAN), BF16),
                    pltpu.SMEM((all_spans,), jnp.int32),
                    pltpu.VMEM((most * SPAN, SPAN), F32),
                    pltpu.VMEM((2, BLOCK_W, all_spans * SPAN), BF16),
                    pltpu.VMEM((2, all_spans * SPAN, BLOCK_W), BF16),
                    pltpu.VMEM((BLOCK_W, BLOCK_W), F32),
                ],
            ),
            compiler_params=params(ATTENTION_VMEM),
            cost_estimate=cost(1.4e10, 2**20),
            name="attention_outer_products",
        )(meta, query, peer, *pieces[t], key, value, peer, peer, *[array for carrier in carriers for array in carrier], *after)

    grams = []
    held = []
    for t in range(blocks + 1):
        if t < blocks:
            kv = first_kv if t == 0 else per - 1 - first_kv
            columns = [(query, BLOCK_W, lambda target, meta: target * blocks + meta[1])]
            if t < per:
                columns += [(array, HEAD_SIZE, lambda target, meta: target * per + meta[2]) for array in (key, value)]
            scalars = jnp.stack([own, turns[t], kv])
            after = [] if t == 0 else [peer, turned] if t == 1 else [peer, turned]
            parts = cut(
                [target_at(*where) for where in far], columns, scalars, "cut_piece", after,
                OTHER_VMEM if t else FULL_VMEM,
            )
            if t > 1:
                *parts, held[t - 2] = lax.optimization_barrier((*parts, held[t - 2]))
            pieces.append([lax.ppermute(part, "seq", moved(*where)) for part, where in zip(parts, far)])
        if t == 0:
            columns = [(query, blocks * BLOCK_W, lambda target, meta: target)]
            columns += [(array, per * HEAD_SIZE, lambda target, meta: target) for array in (key, value)]
            peer = cut([target_at(0, 1)], columns, own[None], "cut_peer", parts, FULL_VMEM)[0]
            turned = turn(0, 1, peer)
            peer = lax.ppermute(peer, "seq", moved(0, 1))
            turned = turn(1, 1, turned)
            continue
        if t == 1:
            for b in range(2, blocks - 1):
                turned = turn(b, 1, turned, parts[0])
        done = t - 1
        grams.append(grams_of(done, peer, [turned] if t == 1 else []))
        if done == 0 or not in_ring:
            held.append(grams[done])
        else:
            held.append(grams[done] + carried if done < ring - 1 else None)
        if in_ring and done < ring - 1:
            carried = lax.ppermute(held[done], "dp", [(z, (z + 1) % ring) for z in range(ring)])
    if blocks > 2:
        turned = turn(blocks - 1, 1, turned, grams[-1])

    half = BLOCK_W // 2
    top_rows, bottom_rows = [
        SPAN * (sum(len(part) for part in tile_order(2, columns))) + 16 for columns in (PANELS, PANELS // 2)
    ]
    scratch = lambda width: [pltpu.VMEM((width, width), F32), pltpu.VMEM((32, width), F32), pltpu.VMEM((half, width), F32)]

    def factor_top(*given):
        return pl.pallas_call(
            functools.partial(factor_kernel, start=0, stop=half, received=len(given)),
            out_shape=[
                jax.ShapeDtypeStruct((top_rows, SPAN), BF16),
                jax.ShapeDtypeStruct((half, half), F32),
            ],
            in_specs=[vmem] * len(given),
            out_specs=[vmem] * 2,
            scratch_shapes=scratch(BLOCK_W),
            compiler_params=params(OTHER_VMEM),
            cost_estimate=cost(1.0e10, 2**20),
            name="factor_top",
        )(*given)

    def factor_bottom(rest):
        return pl.pallas_call(
            functools.partial(factor_kernel, start=half, stop=BLOCK_W, received=1),
            out_shape=jax.ShapeDtypeStruct((bottom_rows, SPAN), BF16),
            in_specs=[vmem],
            out_specs=vmem,
            scratch_shapes=scratch(half),
            compiler_params=params(OTHER_VMEM),
            cost_estimate=cost(0.9e10, 2**20),
            name="factor_bottom",
        )(rest)

    if in_ring:
        top, rest = factor_top(grams[ring - 1], carried)

        def shared(array):
            return [array] + [
                lax.ppermute(array, "dp", [(z, (z + d) % ring) for z in range(ring)]) for d in range(1, ring)
            ]

        tops = shared(top)
        bottom = factor_bottom(rest)
        bottoms = shared(bottom)
        order = jnp.stack([lax.rem(place - d + ring, ring) for d in range(ring)])
    else:
        halves = [factor_top(lax.psum(grams[t], "dp")) for t in range(blocks)]
        tops = [top for top, _ in halves]
        bottoms = [factor_bottom(rest) for _, rest in halves]
        bottom = bottoms[0]
        order = jnp.arange(blocks, dtype=jnp.int32)


    def whiten(uppers, first, starts, result):
        more = [] if result is None else [result]
        depth = BLOCK_W - starts[0]
        chunks = features // tile
        count = len(uppers) // len(starts)
        weights = [
            pl.BlockSpec(
                (depth, tile),
                lambda b, order, c=c: (order[first + b] * (BLOCK_W // depth) + starts[0] // depth, c),
            )
            for c in range(chunks)
        ]
        return pl.pallas_call(
            functools.partial(
                whiten_kernel, blocks=count, starts=starts, first=first, chunks=chunks, aliased=len(more)
            ),
            out_shape=jax.ShapeDtypeStruct((blocks, BLOCK_W, features), F32),
            grid_spec=pltpu.PrefetchScalarGridSpec(
                num_scalar_prefetch=1,
                grid=(count,),
                in_specs=[vmem] * len(uppers) + weights + [anywhere] * len(more),
                out_specs=anywhere,
                scratch_shapes=[
                    pltpu.VMEM((half, 2 * depth), BF16),
                    pltpu.VMEM((2, half, features), F32),
                    pltpu.SemaphoreType.DMA((2, chunks)),
                ],
            ),
            input_output_aliases={1 + len(uppers) + chunks: 0} if more else {},
            compiler_params=params(WHITEN_VMEM),
            cost_estimate=cost(2.0e9 * len(uppers), 2**20),
            name="whiten_bottom" if starts[0] else "whiten_top",
        )(order, *uppers, *[turned] * chunks, *more)

    result = whiten([tops[0], bottoms[0]], 0, (0, half), None)
    result = whiten(tops[1:], 1, (0,), result)
    return whiten(bottoms[1:], 1, (half,), result)


def solution(mesh):
    in_specs = (
        P(("groups", "dp"), "seq", None),
        P(("groups", "dp"), "seq", None),
        P(("groups", "dp"), "seq", None),
        P(("groups", "dp"), None),
        P(("groups", "dp"), None),
        P("dp", "seq"),
    )
    out_specs = P(("groups", "seq"), None, "dp")
    return jax.shard_map(shards, mesh=mesh, in_specs=in_specs, out_specs=out_specs, check_vma=False)
```

```python
import functools
import math

import jax
import jax.numpy as jnp
from jax import lax
from jax.experimental import pallas as pl
from jax.experimental.pallas import tpu as pltpu
from jax.sharding import PartitionSpec as P

QUERY_HEADS = 64
KEY_VALUE_HEADS = 8
HEAD_SIZE = 128
BLOCK_W = 512
NB = 16
SPAN = 128
GROUP = QUERY_HEADS // KEY_VALUE_HEADS
BLOCK_HEADS = BLOCK_W // HEAD_SIZE
KV_BLOCKS = GROUP // BLOCK_HEADS
PANELS = BLOCK_W // SPAN
SUM_ROWS = SPAN * (PANELS * (PANELS - 1) // 2 + PANELS // 2) + 8
VMEM_BYTES = 50 * 2**20
FULL_VMEM = 63 * 2**20
TURN_VMEM = 50 * 2**20
ATTENTION_VMEM = 44 * 2**20
WHITEN_VMEM = 44 * 2**20
OTHER_VMEM = 44 * 2**20
F32 = jnp.float32
BF16 = jnp.bfloat16
NT = (((1,), (1,)), ((), ()))
TN = (((0,), (0,)), ((), ()))


def params(limit=OTHER_VMEM):
    return pltpu.CompilerParams(vmem_limit_bytes=limit)


def cost(flops, moved, trans=0):
    return pl.CostEstimate(flops=int(flops), bytes_accessed=int(moved), transcendentals=int(trans))


def encode(value, exponent):
    scaled = value * jnp.exp2(15.0 - exponent)
    power = scaled * scaled
    power = power * power
    power = power * power
    return jnp.where(scaled < 0.0, -power, power)


def decode(code, exponent):
    code = code.astype(F32)
    quarter = lax.rsqrt(lax.rsqrt(jnp.maximum(jnp.abs(code), 1e-37)))
    root = quarter * lax.rsqrt(quarter) * jnp.exp2(exponent - 15.0)
    return jnp.where(code < 0.0, -root, root)


def exponent_of(largest):
    return jnp.ceil(jnp.log(jnp.maximum(largest, 1e-30)) * (1.0 / math.log(2.0)) + 0.001)


def write_coded(tiles, out):
    off, pairs = tile_order(tiles.rows, tiles.columns)
    places = off + [(i, i) for i in range(tiles.rows)]
    largest = functools.reduce(jnp.maximum, [jnp.max(jnp.abs(tiles(*p)), axis=(0, 1), keepdims=True) for p in places])
    exponent = exponent_of(largest)
    (line,) = fold(tiles, out, lambda value: encode(value, exponent))
    row = lax.broadcasted_iota(jnp.int32, (16, SPAN), 0)
    out[(len(off) + len(pairs)) * SPAN :] = jnp.where(row < 8, line, exponent).astype(BF16)


def read_coded(ref, columns):
    upper, equal = diagonal_masks()
    off, pairs = tile_order(2, columns)
    at = (len(off) + len(pairs)) * SPAN
    tail = ref[at:].astype(F32)
    exponent = tail[15:16, 0:1]
    tiles = {place: decode(ref[i * SPAN : (i + 1) * SPAN], exponent) for i, place in enumerate(off)}
    square = decode(ref[at - SPAN : at], exponent)
    line = decode(tail[0:1], exponent)
    tiles[0, 0] = jnp.where(upper, square, 0.0)
    tiles[1, 1] = jnp.where(equal, line, jnp.where(upper, square.T, 0.0))
    return tiles


def split(value):
    high = value.astype(BF16)
    return high, (value - high.astype(F32)).astype(BF16)


def cut_kernel(meta, *refs, targets, given):
    outs = refs[-targets:]
    for number, out in enumerate(outs):
        at = 0
        for ref in refs[number * given : (number + 1) * given]:
            out[:, at : at + ref.shape[1]] = ref[...]
            at += ref.shape[1]


def turn_kernel(w_ref, *refs):
    refs[-1][...] = w_ref[...].T


def attention_kernel(meta, *refs, chips, spans, all_spans, documents, most, sets, waited):
    sources = 2 * chips
    near = sources + 4
    query_refs, near_refs = refs[:sources], refs[sources:near]
    far_refs = refs[near : near + sets * (sources - 2)]
    out, queries, keys, values, slots, limits, left, right, total = refs[near + sets * (sources - 2) + waited :]
    own = meta[0]
    chip, core = own // 2, lax.rem(own, 2)
    lengths = 4
    order = lengths + documents

    for r in range(all_spans):
        device = r // spans
        distance = lax.rem(chip - device // 2 + chips, chips)
        cross = lax.rem(core + device % 2, 2)
        slots[meta[order + r]] = (distance * 2 + cross) * spans + r % spans

    def place_kv(source, key_part, value_part):
        for t in range(spans):
            rows = slice(t * SPAN, (t + 1) * SPAN)
            keys[source * spans + t] = key_part[rows]
            values[source * spans + t] = value_part[rows].astype(F32).T.astype(BF16)

    place_kv(0, near_refs[0], near_refs[1])
    place_kv(1, near_refs[2], near_refs[3])
    for which in range(sets):

        @pl.when(meta[3] == which)
        def _(which=which):
            for source in range(2, sources):
                ref = far_refs[which * (sources - 2) + source - 2]
                place_kv(source, ref[:, :HEAD_SIZE], ref[:, HEAD_SIZE:])

    for source in range(sources):
        for t in range(spans):
            for h in range(BLOCK_HEADS):
                queries[source * spans + t, h * SPAN : (h + 1) * SPAN] = query_refs[source][
                    t * SPAN : (t + 1) * SPAN, h * HEAD_SIZE : (h + 1) * HEAD_SIZE
                ]

    factor = HEAD_SIZE ** (-0.5) / math.log(2.0)

    def place_of(q):
        source = q // spans
        distance, cross = source // 2, lax.rem(source, 2)
        device = lax.rem(chip - distance + chips, chips) * 2 + lax.rem(core + cross, 2)
        position = meta[order + device * spans + lax.rem(q, spans)]
        first_row = position * SPAN
        begin = jnp.int32(0)
        at = jnp.int32(0)
        query_pos = lax.broadcasted_iota(jnp.int32, (1, SPAN), 1) + first_row
        query_begin = jnp.zeros((1, SPAN), jnp.int32)
        for d in range(documents):
            begin = jnp.where(at <= first_row, at, begin)
            query_begin = jnp.where(query_pos >= at, at, query_begin)
            at = at + meta[lengths + d]
        return position, query_pos, query_begin, position - begin // SPAN + 1

    def one_pair(p, carry):
        pair = [(which, 2 * p + which, place_of(2 * p + which)) for which in range(2)]
        count = jnp.maximum(pair[0][2][3], pair[1][2][3])

        for n in range(1, most + 1):

            @pl.when(count == n)
            def _(n=n):
                for which, q, (position, query_pos, query_begin, _) in pair:
                    lanes = pl.ds(pl.multiple_of(q * SPAN, SPAN), SPAN)
                    held = [slots[jnp.maximum(position - n + 1 + i, 0)] for i in range(n)]
                    for i in range(n):
                        key_pos = lax.broadcasted_iota(jnp.int32, (SPAN, SPAN), 0) + (position - n + 1 + i) * SPAN
                        seen = (key_pos <= query_pos) & (key_pos >= query_begin)
                        limits[which, i * SPAN : (i + 1) * SPAN] = jnp.where(seen, 3e38, -1e30)
                    key_part = jnp.concatenate([keys[slot] for slot in held], axis=0)
                    value_part = jnp.concatenate([values[slot] for slot in held], axis=1)
                    scores = lax.dot_general(key_part, queries[q], NT, preferred_element_type=F32)
                    limit = limits[which, : n * SPAN]
                    scores = jnp.minimum(scores, jnp.concatenate([limit] * BLOCK_HEADS, axis=1))
                    largest = jnp.max(scores, axis=0, keepdims=True)
                    lifted = jnp.exp2((scores - largest) * factor)
                    summed = jnp.sum(lifted, axis=0, keepdims=True)
                    weights = (lifted * (1.0 / summed)).astype(BF16)
                    mixed = jnp.dot(value_part, weights, preferred_element_type=F32)
                    for h in range(BLOCK_HEADS):
                        one_head = mixed[:, h * SPAN : (h + 1) * SPAN]
                        columns = slice(h * HEAD_SIZE, (h + 1) * HEAD_SIZE)
                        high, low = split(one_head)
                        left[0, columns, lanes] = high
                        left[1, columns, lanes] = low
                        high, low = split(one_head.T)
                        right[0, lanes, columns] = high
                        right[1, lanes, columns] = low

        return carry

    lax.fori_loop(0, all_spans // 2, one_pair, 0)

    half = BLOCK_W // 2
    total[...] = jnp.zeros_like(total)

    def one_pass(i, carry):
        a, b = lax.rem(i, 2), i // 2
        total[:half] += jnp.dot(left[a, :half], right[b], preferred_element_type=F32)
        total[half:, half:] += jnp.dot(left[a, half:], right[b, :, half:], preferred_element_type=F32)
        return carry

    lax.fori_loop(0, 3, one_pass, 0)
    lines = fold(Tiles(total, PANELS, PANELS, False), out)
    row = lax.broadcasted_iota(jnp.int32, (8, SPAN), 0)
    out[SUM_ROWS - 8 :] = jnp.where(row == 0, lines[0], lines[1])


def diagonal_masks():
    rows = lax.broadcasted_iota(jnp.int32, (SPAN, SPAN), 0)
    columns = lax.broadcasted_iota(jnp.int32, (SPAN, SPAN), 1)
    return rows <= columns, rows == columns


def tile_order(rows, columns):
    off = [(i, j) for i in range(rows) for j in range(i + 1, columns)]
    return off, [(i, i + 1) for i in range(0, rows, 2)]


def fold(tiles, out, change=lambda value: value):
    upper, equal = diagonal_masks()
    off, pairs = tile_order(tiles.rows, tiles.columns)
    for i, place in enumerate(off):
        out[i * SPAN : (i + 1) * SPAN] = change(tiles(*place)).astype(out.dtype)
    lines = []
    for i, (a, b) in enumerate(pairs):
        second = tiles(b, b)
        at = (len(off) + i) * SPAN
        lower = second.T if tiles.turn else second
        out[at : at + SPAN] = change(jnp.where(upper, tiles(a, a), lower)).astype(out.dtype)
        lines.append(change(jnp.sum(jnp.where(equal, second, 0.0), axis=0, keepdims=True)))
    return lines


class Tiles:
    def __init__(self, ref, rows, columns, turn):
        self.ref, self.rows, self.columns, self.turn = ref, rows, columns, turn

    def __call__(self, i, j):
        return self.ref[i * SPAN : (i + 1) * SPAN, j * SPAN : (j + 1) * SPAN]


def unfold(total, work):
    upper, equal = diagonal_masks()
    off, pairs = tile_order(PANELS, PANELS)
    for i, (row, column) in enumerate(off):
        work[row * SPAN : (row + 1) * SPAN, column * SPAN : (column + 1) * SPAN] = total[i * SPAN : (i + 1) * SPAN]
    trace = jnp.zeros((1, 1), F32)
    squares = []
    for i, (a, b) in enumerate(pairs):
        at = (len(off) + i) * SPAN
        square = total[at : at + SPAN]
        turned = square.T
        at = (len(off) + len(pairs)) * SPAN + i
        line = jnp.broadcast_to(total[at : at + 1], (SPAN, SPAN))
        squares.append((a, jnp.where(upper, square, turned)))
        squares.append((b, jnp.where(equal, line, jnp.where(upper, turned, square))))
    for _, square in squares:
        trace = trace + jnp.sum(jnp.where(equal, square, 0.0), axis=(0, 1), keepdims=True)
    damping = trace * (0.1 / BLOCK_W)
    for a, square in squares:
        work[a * SPAN : (a + 1) * SPAN, a * SPAN : (a + 1) * SPAN] = jnp.where(equal, square + damping, square)


def factor_kernel(*refs, start, stop, received):
    width = BLOCK_W - start
    panels = width // SPAN
    step = 32
    groups = step // 8
    per_tile = SPAN // step
    last = stop == BLOCK_W
    given, refs = (refs[:received], refs[received:])
    out, refs = refs[0], refs[1:]
    if not last:
        rest, refs = refs[0], refs[1:]
    work, previous, upper = refs
    if start == 0:
        work[...] = jnp.zeros_like(work)
        total = given[0][...] + given[1][...] if received == 2 else given[0][...]
        unfold(total, work)
    else:
        work[...] = given[0][...]
    previous[...] = jnp.zeros_like(previous)

    def triple(value, first):
        high, low = split(value)
        return jnp.concatenate((high, low, high) if first else (high, high, low), axis=0)

    def superpanel(g, carry):
        row = pl.multiple_of(g * step, step)
        tile_index = g // per_tile
        tile = pl.ds(pl.multiple_of(tile_index * SPAN, SPAN), SPAN)
        turn = lax.rem(SPAN - lax.rem(g, per_tile) * step, SPAN)
        before = previous[...]
        right = triple(before, False)
        near = pltpu.roll(previous[:, tile], turn, 1)
        fresh = lax.dot_general(triple(near, True), right, TN, preferred_element_type=F32)[:step]
        current = work[pl.ds(row, step), :] - fresh
        work[...] = work[...] - lax.dot_general(triple(before, True), right, TN, preferred_element_type=F32)

        square = current[:, :SPAN]
        for k in range(1, panels):
            square = jnp.where(tile_index == k, current[:, k * SPAN : (k + 1) * SPAN], square)
        square = pltpu.roll(square, turn, 1)
        line = lax.broadcasted_iota(jnp.int32, (8, SPAN), 0)
        square = [square[8 * q : 8 * q + 8] for q in range(groups)]
        body = [[current[8 * q : 8 * q + 8, k * SPAN : (k + 1) * SPAN] for k in range(panels)] for q in range(groups)]
        scales = [jnp.zeros((8, SPAN), F32) for _ in range(groups)]

        def spread(value, i):
            return jnp.broadcast_to(value[i % 8 : i % 8 + 1], (8, SPAN))

        def column(j):
            return {q: jnp.broadcast_to(square[q][:, j : j + 1], (8, SPAN)) for q in range(j // 8, groups)}

        ahead = 4
        held = {j: column(j) for j in range(ahead)}
        for i in range(step):
            at = i // 8
            pivots = held.pop(i)
            root = lax.rsqrt(spread(pivots[at], i))
            inverse = root * root
            scales[at] = jnp.where(line == i % 8, root, scales[at])
            ratio = {q: pivots[q] * inverse for q in range(at, groups)}
            ratio[at] = jnp.where(line > i % 8, ratio[at], 0.0)
            for j in held:
                entry = spread(pivots[j // 8], j)
                for q in range(j // 8, groups):
                    held[j][q] = held[j][q] - ratio[q] * entry
            pivot_row = spread(square[at], i)
            for q in range(at, groups):
                square[q] = square[q] - ratio[q] * pivot_row
            if i + ahead < step:
                held[i + ahead] = column(i + ahead)
            for k in range(panels):
                pivot_row = spread(body[at][k], i)
                for q in range(at, groups):
                    body[q][k] = body[q][k] - ratio[q] * pivot_row
        result = jnp.concatenate(
            [jnp.concatenate([body[q][k] * scales[q] for k in range(panels)], axis=1) for q in range(groups)], axis=0
        )
        across = lax.broadcasted_iota(jnp.int32, (step, width), 1)
        down = lax.broadcasted_iota(jnp.int32, (step, width), 0)
        result = jnp.where(across >= down + row, result, 0.0)
        previous[...] = result
        upper[pl.ds(row, step), :] = result
        return carry

    lax.fori_loop(0, (stop - start) // step, superpanel, 0)
    if not last:
        done = stop - start
        before = previous[...]
        final = lax.dot_general(
            triple(before[:, done:], True), triple(before[:, done:], False), TN, preferred_element_type=F32
        )
        rest[...] = work[done:, done:] - final
    write_coded(Tiles(upper, (stop - start) // SPAN, panels, True), out)


def whiten_kernel(order, *refs, blocks, starts, first, chunks, aliased):
    count = len(starts)
    u_refs, refs = refs[: blocks * count], refs[blocks * count :]
    w_ref, refs = refs[0], refs[1 + aliased :]
    out, left, ready, sems = refs
    half = BLOCK_W // 2
    chunk = ready.shape[2] // chunks
    step = pl.program_id(0)

    def copy(number, which, c):
        slot = lax.rem(number * count + which, 2)
        columns = pl.ds(c * chunk, chunk)
        return pltpu.make_async_copy(
            ready.at[slot, :, columns],
            out.at[order[first + number], pl.ds(starts[which], half), columns],
            sems.at[slot, c],
        )

    for which, start in enumerate(starts):
        width = BLOCK_W - start
        for b in range(blocks):

            @pl.when(step == b)
            def _(b=b):
                tiles = read_coded(u_refs[b * count + which], width // SPAN)
                for row in range(half // SPAN):
                    rows = slice(row * SPAN, (row + 1) * SPAN)
                    for column in range(width // SPAN):
                        value = tiles[row, column] if column >= row else jnp.zeros((SPAN, SPAN), F32)
                        high, low = split(value)
                        left[rows, column * SPAN : (column + 1) * SPAN] = high
                        left[rows, width + column * SPAN : width + (column + 1) * SPAN] = low

        above = 0 if blocks == 1 else order[first + step] * BLOCK_W
        depths = pl.ds(pl.multiple_of(above + start, SPAN), width)
        for c in range(chunks):
            if count == 1:

                @pl.when(step >= 2)
                def _(c=c):
                    copy(step - 2, which, c).wait()

            elif blocks > 1:

                @pl.when(step >= 1)
                def _(c=c):
                    copy(step - 1, which, c).wait()

            weight = w_ref[depths, c * chunk : (c + 1) * chunk]
            product = jnp.dot(
                left[:, : 2 * width], jnp.concatenate([weight, weight], axis=0), preferred_element_type=F32
            )
            ready[lax.rem(step * count + which, 2), :, c * chunk : (c + 1) * chunk] = product
            copy(step, which, c).start()

    @pl.when(step == blocks - 1)
    def _():
        for c in range(chunks):
            if count > 1:
                copy(step, 0, c).wait()
            elif blocks > 1:
                copy(step - 1, 0, c).wait()
            copy(step, count - 1, c).wait()


def shards(query_rows, key_rows, placed_value_rows, doc_lengths, span_order, out_weight):
    tokens = query_rows.shape[1]
    features = out_weight.shape[0]
    seq = lax.axis_size("seq")
    ring = lax.axis_size("dp")
    chips = seq // 2
    spans = tokens // SPAN
    all_spans = spans * seq
    documents = doc_lengths.shape[1]
    per = KEY_VALUE_HEADS // seq
    blocks = NB // seq
    own = lax.axis_index("seq").astype(jnp.int32)
    place = lax.axis_index("dp").astype(jnp.int32)
    query, key, value = query_rows[0], key_rows[0], placed_value_rows[0]
    vmem = pl.BlockSpec(memory_space=pltpu.VMEM)
    anywhere = pl.BlockSpec(memory_space=pl.ANY)
    in_ring = blocks == ring

    if in_ring:
        turns = [lax.rem(place + 2 * ring - 1 - t, ring) for t in range(blocks)]
    else:
        turns = [jnp.int32(t) for t in range(blocks)]
    first_kv = turns[0] // KV_BLOCKS

    def moved(distance, cross):
        return [
            (x * 2 + c, (x + distance) % chips * 2 + (1 - c if cross else c)) for x in range(chips) for c in range(2)
        ]

    def cut(targets, columns, scalars, name, after=(), limit=OTHER_VMEM):
        specs, arrays = [], []
        for target in targets:
            for array, size, index in columns:
                specs.append(
                    pl.BlockSpec((tokens, size), lambda i, meta, target=target, index=index: (0, index(target(meta), meta)))
                )
                arrays.append(array)
        width = sum(size for _, size, _ in columns)
        return pl.pallas_call(
            functools.partial(cut_kernel, targets=len(targets), given=len(columns)),
            out_shape=[jax.ShapeDtypeStruct((tokens, width), BF16)] * len(targets),
            grid_spec=pltpu.PrefetchScalarGridSpec(
                num_scalar_prefetch=1,
                grid=(1,),
                in_specs=specs + [anywhere] * len(after),
                out_specs=[pl.BlockSpec((tokens, width), lambda i, meta: (0, 0))] * len(targets),
            ),
            compiler_params=params(limit),
            cost_estimate=cost(0, 2**21),
            name=name,
        )(scalars, *arrays, *after)

    tile = 512

    def turn(first, count, *before):
        return pl.pallas_call(
            turn_kernel,
            out_shape=jax.ShapeDtypeStruct((blocks * BLOCK_W, features), BF16),
            grid=(count, features // tile),
            in_specs=[pl.BlockSpec((tile, BLOCK_W), lambda b, o: (o, first + b))] + [anywhere] * len(before),
            out_specs=pl.BlockSpec((BLOCK_W, tile), lambda b, o: (first + b, o)),
            input_output_aliases={1: 0} if first else {},
            compiler_params=params(TURN_VMEM),
            cost_estimate=cost(1.0e9 * count, 2**20),
            name="turn_weight",
        )(out_weight, *before)

    def target_at(distance, cross):
        return lambda meta: lax.rem(meta[0] // 2 + distance, chips) * 2 + lax.rem(lax.rem(meta[0], 2) + cross, 2)

    far = [(distance, cross) for distance in range(1, chips) for cross in range(2)]
    pieces = []

    most = all_spans // 2 + 1

    def grams_of(t, peer, after):
        kv = turns[t] // KV_BLOCKS
        carriers = pieces[: min(t + 1, per)]
        which = jnp.where(kv == first_kv, 0, 1).astype(jnp.int32)
        meta = jnp.concatenate([jnp.stack([own, turns[t], kv, which]), doc_lengths[0], span_order[0]])
        folded = jax.ShapeDtypeStruct((SUM_ROWS, SPAN), F32)
        peer_kv = blocks * BLOCK_W // HEAD_SIZE
        return pl.pallas_call(
            functools.partial(
                attention_kernel,
                chips=chips, spans=spans, all_spans=all_spans, documents=documents, most=most, sets=len(carriers),
                waited=len(after),
            ),
            out_shape=folded,
            grid_spec=pltpu.PrefetchScalarGridSpec(
                num_scalar_prefetch=1,
                grid=(1,),
                in_specs=[
                    pl.BlockSpec((tokens, BLOCK_W), lambda i, meta: (0, meta[0] * blocks + meta[1])),
                    pl.BlockSpec((tokens, BLOCK_W), lambda i, meta: (0, meta[1])),
                ]
                + [pl.BlockSpec((tokens, BLOCK_W), lambda i, meta: (0, 0))] * len(far)
                + [pl.BlockSpec((tokens, HEAD_SIZE), lambda i, meta: (0, meta[0] * per + meta[2]))] * 2
                + [
                    pl.BlockSpec((tokens, HEAD_SIZE), lambda i, meta: (0, peer_kv + meta[2])),
                    pl.BlockSpec((tokens, HEAD_SIZE), lambda i, meta: (0, peer_kv + per + meta[2])),
                ]
                + [pl.BlockSpec((tokens, 2 * HEAD_SIZE), lambda i, meta: (0, BLOCK_W // (2 * HEAD_SIZE)))]
                * (len(carriers) * len(far))
                + [anywhere] * len(after),
                out_specs=pl.BlockSpec((SUM_ROWS, SPAN), lambda i, meta: (0, 0)),
                scratch_shapes=[
                    pltpu.VMEM((all_spans, BLOCK_HEADS * SPAN, HEAD_SIZE), BF16),
                    pltpu.VMEM((all_spans, SPAN, HEAD_SIZE), BF16),
                    pltpu.VMEM((all_spans, HEAD_SIZE, SPAN), BF16),
                    pltpu.SMEM((all_spans,), jnp.int32),
                    pltpu.VMEM((2, most * SPAN, SPAN), F32),
                    pltpu.VMEM((2, BLOCK_W, all_spans * SPAN), BF16),
                    pltpu.VMEM((2, all_spans * SPAN, BLOCK_W), BF16),
                    pltpu.VMEM((BLOCK_W, BLOCK_W), F32),
                ],
            ),
            compiler_params=params(ATTENTION_VMEM),
            cost_estimate=cost(1.4e10, 2**20),
            name="attention_outer_products",
        )(meta, query, peer, *pieces[t], key, value, peer, peer, *[array for carrier in carriers for array in carrier], *after)

    grams = []
    held = []
    for t in range(blocks + 1):
        if t < blocks:
            kv = first_kv if t == 0 else per - 1 - first_kv
            columns = [(query, BLOCK_W, lambda target, meta: target * blocks + meta[1])]
            if t < per:
                columns += [(array, HEAD_SIZE, lambda target, meta: target * per + meta[2]) for array in (key, value)]
            scalars = jnp.stack([own, turns[t], kv])
            after = [] if t == 0 else [peer, turned] if t == 1 else [peer, turned]
            parts = cut(
                [target_at(*where) for where in far], columns, scalars, "cut_piece", after,
                OTHER_VMEM if t else FULL_VMEM,
            )
            if t > 1:
                *parts, held[t - 2] = lax.optimization_barrier((*parts, held[t - 2]))
            pieces.append([lax.ppermute(part, "seq", moved(*where)) for part, where in zip(parts, far)])
        if t == 0:
            columns = [(query, blocks * BLOCK_W, lambda target, meta: target)]
            columns += [(array, per * HEAD_SIZE, lambda target, meta: target) for array in (key, value)]
            peer = cut([target_at(0, 1)], columns, own[None], "cut_peer", parts, FULL_VMEM)[0]
            turned = turn(0, 1, peer)
            peer = lax.ppermute(peer, "seq", moved(0, 1))
            turned = turn(1, 1, turned)
            continue
        if t == 1:
            for b in range(2, blocks - 1):
                turned = turn(b, 1, turned, parts[0])
        done = t - 1
        grams.append(grams_of(done, peer, [turned] if t == 1 else []))
        if done == 0 or not in_ring:
            held.append(grams[done])
        else:
            held.append(grams[done] + carried if done < ring - 1 else None)
        if in_ring and done < ring - 1:
            carried = lax.ppermute(held[done], "dp", [(z, (z + 1) % ring) for z in range(ring)])
    if blocks > 2:
        turned = turn(blocks - 1, 1, turned, grams[-1])

    half = BLOCK_W // 2
    top_rows, bottom_rows = [
        SPAN * (sum(len(part) for part in tile_order(2, columns))) + 16 for columns in (PANELS, PANELS // 2)
    ]
    scratch = lambda width: [pltpu.VMEM((width, width), F32), pltpu.VMEM((32, width), F32), pltpu.VMEM((half, width), F32)]

    def factor_top(*given):
        return pl.pallas_call(
            functools.partial(factor_kernel, start=0, stop=half, received=len(given)),
            out_shape=[
                jax.ShapeDtypeStruct((top_rows, SPAN), BF16),
                jax.ShapeDtypeStruct((half, half), F32),
            ],
            in_specs=[vmem] * len(given),
            out_specs=[vmem] * 2,
            scratch_shapes=scratch(BLOCK_W),
            compiler_params=params(OTHER_VMEM),
            cost_estimate=cost(1.0e10, 2**20),
            name="factor_top",
        )(*given)

    def factor_bottom(rest):
        return pl.pallas_call(
            functools.partial(factor_kernel, start=half, stop=BLOCK_W, received=1),
            out_shape=jax.ShapeDtypeStruct((bottom_rows, SPAN), BF16),
            in_specs=[vmem],
            out_specs=vmem,
            scratch_shapes=scratch(half),
            compiler_params=params(OTHER_VMEM),
            cost_estimate=cost(0.9e10, 2**20),
            name="factor_bottom",
        )(rest)

    if in_ring:
        top, rest = factor_top(grams[ring - 1], carried)

        def shared(array):
            return [array] + [
                lax.ppermute(array, "dp", [(z, (z + d) % ring) for z in range(ring)]) for d in range(1, ring)
            ]

        tops = shared(top)
        bottom = factor_bottom(rest)
        bottoms = shared(bottom)
        order = jnp.stack([lax.rem(place - d + ring, ring) for d in range(ring)])
    else:
        halves = [factor_top(lax.psum(grams[t], "dp")) for t in range(blocks)]
        tops = [top for top, _ in halves]
        bottoms = [factor_bottom(rest) for _, rest in halves]
        bottom = bottoms[0]
        order = jnp.arange(blocks, dtype=jnp.int32)


    def whiten(uppers, first, starts, result):
        more = [] if result is None else [result]
        depth = BLOCK_W - starts[0]
        weights = vmem if len(uppers) > len(starts) else pl.BlockSpec(
            (BLOCK_W, features), lambda b, order: (order[first + b], 0)
        )
        chunks = features // tile
        count = len(uppers) // len(starts)
        return pl.pallas_call(
            functools.partial(
                whiten_kernel, blocks=count, starts=starts, first=first, chunks=chunks, aliased=len(more)
            ),
            out_shape=jax.ShapeDtypeStruct((blocks, BLOCK_W, features), F32),
            grid_spec=pltpu.PrefetchScalarGridSpec(
                num_scalar_prefetch=1,
                grid=(count,),
                in_specs=[vmem] * len(uppers) + [weights] + [anywhere] * len(more),
                out_specs=anywhere,
                scratch_shapes=[
                    pltpu.VMEM((half, 2 * depth), BF16),
                    pltpu.VMEM((2, half, features), F32),
                    pltpu.SemaphoreType.DMA((2, chunks)),
                ],
            ),
            input_output_aliases={2 + len(uppers): 0} if more else {},
            compiler_params=params(WHITEN_VMEM),
            cost_estimate=cost(2.0e9 * len(uppers), 2**20),
            name="whiten_bottom" if starts[0] else "whiten_top",
        )(order, *uppers, turned, *more)

    result = whiten([tops[0], bottoms[0]], 0, (0, half), None)
    result = whiten(tops[1:], 1, (0,), result)
    return whiten(bottoms[1:], 1, (half,), result)


def solution(mesh):
    in_specs = (
        P(("groups", "dp"), "seq", None),
        P(("groups", "dp"), "seq", None),
        P(("groups", "dp"), "seq", None),
        P(("groups", "dp"), None),
        P(("groups", "dp"), None),
        P("dp", "seq"),
    )
    out_specs = P(("groups", "seq"), None, "dp")
    return jax.shard_map(shards, mesh=mesh, in_specs=in_specs, out_specs=out_specs, check_vma=False)
```

```python
import functools
import math

import jax
import jax.numpy as jnp
from jax import lax
from jax.experimental import pallas as pl
from jax.experimental.pallas import tpu as pltpu
from jax.sharding import PartitionSpec as P

QUERY_HEADS = 64
KEY_VALUE_HEADS = 8
HEAD_SIZE = 128
BLOCK_W = 512
NB = 16
SPAN = 128
GROUP = QUERY_HEADS // KEY_VALUE_HEADS
BLOCK_HEADS = BLOCK_W // HEAD_SIZE
KV_BLOCKS = GROUP // BLOCK_HEADS
PANELS = BLOCK_W // SPAN
SUM_ROWS = SPAN * PANELS + 8
VMEM_BYTES = 50 * 2**20
FULL_VMEM = 63 * 2**20
TURN_VMEM = 50 * 2**20
ATTENTION_VMEM = 44 * 2**20
WHITEN_VMEM = 44 * 2**20
OTHER_VMEM = 44 * 2**20
F32 = jnp.float32
BF16 = jnp.bfloat16
NT = (((1,), (1,)), ((), ()))
TN = (((0,), (0,)), ((), ()))


def params(limit=OTHER_VMEM):
    return pltpu.CompilerParams(vmem_limit_bytes=limit)


def cost(flops, moved, trans=0):
    return pl.CostEstimate(flops=int(flops), bytes_accessed=int(moved), transcendentals=int(trans))


def encode(value, exponent):
    scaled = value * jnp.exp2(15.0 - exponent)
    power = scaled * scaled
    power = power * power
    power = power * power
    return jnp.where(scaled < 0.0, -power, power)


def decode(code, exponent):
    code = code.astype(F32)
    quarter = lax.rsqrt(lax.rsqrt(jnp.maximum(jnp.abs(code), 1e-37)))
    root = quarter * lax.rsqrt(quarter) * jnp.exp2(exponent - 15.0)
    return jnp.where(code < 0.0, -root, root)


def exponent_of(largest):
    return jnp.ceil(jnp.log(jnp.maximum(largest, 1e-30)) * (1.0 / math.log(2.0)) + 0.001)


def write_coded(tiles, out):
    off, pairs = tile_order(tiles.rows, tiles.columns)
    places = off + [(i, i) for i in range(tiles.rows)]
    largest = functools.reduce(jnp.maximum, [jnp.max(jnp.abs(tiles(*p)), axis=(0, 1), keepdims=True) for p in places])
    exponent = exponent_of(largest)
    (line,) = fold(tiles, out, lambda value: encode(value, exponent))
    row = lax.broadcasted_iota(jnp.int32, (16, SPAN), 0)
    out[(len(off) + len(pairs)) * SPAN :] = jnp.where(row < 8, line, exponent).astype(BF16)


def read_coded(ref, columns):
    upper, equal = diagonal_masks()
    off, pairs = tile_order(2, columns)
    at = (len(off) + len(pairs)) * SPAN
    tail = ref[at:].astype(F32)
    exponent = tail[15:16, 0:1]
    tiles = {place: decode(ref[i * SPAN : (i + 1) * SPAN], exponent) for i, place in enumerate(off)}
    square = decode(ref[at - SPAN : at], exponent)
    line = decode(tail[0:1], exponent)
    tiles[0, 0] = jnp.where(upper, square, 0.0)
    tiles[1, 1] = jnp.where(equal, line, jnp.where(upper, square.T, 0.0))
    return tiles


def split(value):
    high = value.astype(BF16)
    return high, (value - high.astype(F32)).astype(BF16)


def cut_kernel(meta, *refs, targets, given):
    outs = refs[-targets:]
    for number, out in enumerate(outs):
        at = 0
        for ref in refs[number * given : (number + 1) * given]:
            out[:, at : at + ref.shape[1]] = ref[...]
            at += ref.shape[1]


def turn_kernel(w_ref, *refs):
    refs[-1][...] = w_ref[...].T


def attention_kernel(meta, *refs, chips, spans, all_spans, documents, most, sets, waited):
    sources = 2 * chips
    near = sources + 4
    query_refs, near_refs = refs[:sources], refs[sources:near]
    far_refs = refs[near : near + sets * (sources - 2)]
    top, bottom, queries, keys, values, slots, limits, left, right, total = refs[near + sets * (sources - 2) + waited :]
    own = meta[0]
    chip, core = own // 2, lax.rem(own, 2)
    lengths = 4
    order = lengths + documents

    for r in range(all_spans):
        device = r // spans
        distance = lax.rem(chip - device // 2 + chips, chips)
        cross = lax.rem(core + device % 2, 2)
        slots[meta[order + r]] = (distance * 2 + cross) * spans + r % spans

    def place_kv(source, key_part, value_part):
        for t in range(spans):
            rows = slice(t * SPAN, (t + 1) * SPAN)
            keys[source * spans + t] = key_part[rows]
            values[source * spans + t] = value_part[rows].astype(F32).T.astype(BF16)

    place_kv(0, near_refs[0], near_refs[1])
    place_kv(1, near_refs[2], near_refs[3])
    for which in range(sets):

        @pl.when(meta[3] == which)
        def _(which=which):
            for source in range(2, sources):
                ref = far_refs[which * (sources - 2) + source - 2]
                place_kv(source, ref[:, :HEAD_SIZE], ref[:, HEAD_SIZE:])

    for source in range(sources):
        for t in range(spans):
            for h in range(BLOCK_HEADS):
                queries[source * spans + t, h * SPAN : (h + 1) * SPAN] = query_refs[source][
                    t * SPAN : (t + 1) * SPAN, h * HEAD_SIZE : (h + 1) * HEAD_SIZE
                ]

    factor = HEAD_SIZE ** (-0.5) / math.log(2.0)

    def place_of(q):
        source = q // spans
        distance, cross = source // 2, lax.rem(source, 2)
        device = lax.rem(chip - distance + chips, chips) * 2 + lax.rem(core + cross, 2)
        position = meta[order + device * spans + lax.rem(q, spans)]
        first_row = position * SPAN
        begin = jnp.int32(0)
        at = jnp.int32(0)
        query_pos = lax.broadcasted_iota(jnp.int32, (1, SPAN), 1) + first_row
        query_begin = jnp.zeros((1, SPAN), jnp.int32)
        for d in range(documents):
            begin = jnp.where(at <= first_row, at, begin)
            query_begin = jnp.where(query_pos >= at, at, query_begin)
            at = at + meta[lengths + d]
        return position, query_pos, query_begin, position - begin // SPAN + 1

    def one_pair(p, carry):
        pair = [(which, 2 * p + which, place_of(2 * p + which)) for which in range(2)]
        count = jnp.maximum(pair[0][2][3], pair[1][2][3])

        for n in range(1, most + 1):

            @pl.when(count == n)
            def _(n=n):
                for which, q, (position, query_pos, query_begin, _) in pair:
                    lanes = pl.ds(pl.multiple_of(q * SPAN, SPAN), SPAN)
                    held = [slots[jnp.maximum(position - n + 1 + i, 0)] for i in range(n)]
                    for i in range(n):
                        key_pos = lax.broadcasted_iota(jnp.int32, (SPAN, SPAN), 0) + (position - n + 1 + i) * SPAN
                        seen = (key_pos <= query_pos) & (key_pos >= query_begin)
                        limits[which, i * SPAN : (i + 1) * SPAN] = jnp.where(seen, 3e38, -1e30)
                    key_part = jnp.concatenate([keys[slot] for slot in held], axis=0)
                    value_part = jnp.concatenate([values[slot] for slot in held], axis=1)
                    scores = lax.dot_general(key_part, queries[q], NT, preferred_element_type=F32)
                    limit = limits[which, : n * SPAN]
                    scores = jnp.minimum(scores, jnp.concatenate([limit] * BLOCK_HEADS, axis=1))
                    largest = jnp.max(scores, axis=0, keepdims=True)
                    lifted = jnp.exp2((scores - largest) * factor)
                    summed = jnp.sum(lifted, axis=0, keepdims=True)
                    weights = (lifted * (1.0 / summed)).astype(BF16)
                    mixed = jnp.dot(value_part, weights, preferred_element_type=F32)
                    for h in range(BLOCK_HEADS):
                        one_head = mixed[:, h * SPAN : (h + 1) * SPAN]
                        columns = slice(h * HEAD_SIZE, (h + 1) * HEAD_SIZE)
                        high, low = split(one_head)
                        left[0, columns, lanes] = high
                        left[1, columns, lanes] = low
                        high, low = split(one_head.T)
                        right[0, lanes, columns] = high
                        right[1, lanes, columns] = low

        return carry

    lax.fori_loop(0, all_spans // 2, one_pair, 0)

    half = BLOCK_W // 2
    total[...] = jnp.zeros_like(total)

    def one_pass(i, carry):
        a, b = lax.rem(i, 2), i // 2
        total[:half] += jnp.dot(left[a, :half], right[b], preferred_element_type=F32)
        total[half:, half:] += jnp.dot(left[a, half:], right[b, :, half:], preferred_element_type=F32)
        return carry

    lax.fori_loop(0, 3, one_pass, 0)
    for out, where in zip((top, bottom), sum_tiles()):
        off, pair = where
        (line,) = fold(Tiles(total, PANELS, PANELS, False), out, where=(off, [pair]))
        out[SUM_ROWS - 8 :] = jnp.broadcast_to(line, (8, SPAN))


def diagonal_masks():
    rows = lax.broadcasted_iota(jnp.int32, (SPAN, SPAN), 0)
    columns = lax.broadcasted_iota(jnp.int32, (SPAN, SPAN), 1)
    return rows <= columns, rows == columns


def tile_order(rows, columns):
    off = [(i, j) for i in range(rows) for j in range(i + 1, columns)]
    return off, [(i, i + 1) for i in range(0, rows, 2)]


def sum_tiles():
    off, pairs = tile_order(PANELS, PANELS)
    half = len(off) // 2
    return [(off[:half], pairs[0]), (off[half:], pairs[1])]


def fold(tiles, out, change=lambda value: value, where=None):
    upper, equal = diagonal_masks()
    off, pairs = tile_order(tiles.rows, tiles.columns) if where is None else where
    for i, place in enumerate(off):
        out[i * SPAN : (i + 1) * SPAN] = change(tiles(*place)).astype(out.dtype)
    lines = []
    for i, (a, b) in enumerate(pairs):
        second = tiles(b, b)
        at = (len(off) + i) * SPAN
        lower = second.T if tiles.turn else second
        out[at : at + SPAN] = change(jnp.where(upper, tiles(a, a), lower)).astype(out.dtype)
        lines.append(change(jnp.sum(jnp.where(equal, second, 0.0), axis=0, keepdims=True)))
    return lines


class Tiles:
    def __init__(self, ref, rows, columns, turn):
        self.ref, self.rows, self.columns, self.turn = ref, rows, columns, turn

    def __call__(self, i, j):
        return self.ref[i * SPAN : (i + 1) * SPAN, j * SPAN : (j + 1) * SPAN]


def unfold(halves, work):
    upper, equal = diagonal_masks()
    trace = jnp.zeros((1, 1), F32)
    squares = []
    for total, (off, (a, b)) in zip(halves, sum_tiles()):
        for i, (row, column) in enumerate(off):
            work[row * SPAN : (row + 1) * SPAN, column * SPAN : (column + 1) * SPAN] = total[i * SPAN : (i + 1) * SPAN]
        at = len(off) * SPAN
        square = total[at : at + SPAN]
        turned = square.T
        line = jnp.broadcast_to(total[at + SPAN : at + SPAN + 1], (SPAN, SPAN))
        squares.append((a, jnp.where(upper, square, turned)))
        squares.append((b, jnp.where(equal, line, jnp.where(upper, turned, square))))
    for _, square in squares:
        trace = trace + jnp.sum(jnp.where(equal, square, 0.0), axis=(0, 1), keepdims=True)
    damping = trace * (0.1 / BLOCK_W)
    for a, square in squares:
        work[a * SPAN : (a + 1) * SPAN, a * SPAN : (a + 1) * SPAN] = jnp.where(equal, square + damping, square)


def factor_kernel(*refs, start, stop, received):
    width = BLOCK_W - start
    panels = width // SPAN
    step = 32
    groups = step // 8
    per_tile = SPAN // step
    last = stop == BLOCK_W
    given, refs = (refs[:received], refs[received:])
    out, refs = refs[0], refs[1:]
    if not last:
        rest, refs = refs[0], refs[1:]
    work, previous, upper = refs
    if start == 0:
        work[...] = jnp.zeros_like(work)
        halves = [ref[...] for ref in given[:2]]
        if received == 4:
            halves = [mine + ref[...] for mine, ref in zip(halves, given[2:])]
        unfold(halves, work)
    else:
        work[...] = given[0][...]
    previous[...] = jnp.zeros_like(previous)

    def triple(value, first):
        high, low = split(value)
        return jnp.concatenate((high, low, high) if first else (high, high, low), axis=0)

    def superpanel(g, carry):
        row = pl.multiple_of(g * step, step)
        tile_index = g // per_tile
        tile = pl.ds(pl.multiple_of(tile_index * SPAN, SPAN), SPAN)
        turn = lax.rem(SPAN - lax.rem(g, per_tile) * step, SPAN)
        before = previous[...]
        right = triple(before, False)
        near = pltpu.roll(previous[:, tile], turn, 1)
        fresh = lax.dot_general(triple(near, True), right, TN, preferred_element_type=F32)[:step]
        current = work[pl.ds(row, step), :] - fresh
        work[...] = work[...] - lax.dot_general(triple(before, True), right, TN, preferred_element_type=F32)

        square = current[:, :SPAN]
        for k in range(1, panels):
            square = jnp.where(tile_index == k, current[:, k * SPAN : (k + 1) * SPAN], square)
        square = pltpu.roll(square, turn, 1)
        line = lax.broadcasted_iota(jnp.int32, (8, SPAN), 0)
        square = [square[8 * q : 8 * q + 8] for q in range(groups)]
        body = [[current[8 * q : 8 * q + 8, k * SPAN : (k + 1) * SPAN] for k in range(panels)] for q in range(groups)]
        scales = [jnp.zeros((8, SPAN), F32) for _ in range(groups)]

        def spread(value, i):
            return jnp.broadcast_to(value[i % 8 : i % 8 + 1], (8, SPAN))

        def column(j):
            return {q: jnp.broadcast_to(square[q][:, j : j + 1], (8, SPAN)) for q in range(j // 8, groups)}

        ahead = 4
        held = {j: column(j) for j in range(ahead)}
        pivot = spread(held[0][0], 0)
        for i in range(step):
            at = i // 8
            pivots = held.pop(i)
            root = lax.rsqrt(pivot)
            inverse = root * root
            if i + 1 < step:
                entry = spread(pivots[(i + 1) // 8], i + 1)
                pivot = spread(held[i + 1][(i + 1) // 8], i + 1) - (entry * entry) * inverse
            for j in held:
                entry = spread(pivots[j // 8], j)
                for q in range(j // 8, groups):
                    held[j][q] = held[j][q] - (pivots[q] * entry) * inverse
            scales[at] = jnp.where(line == i % 8, root, scales[at])
            ratio = {q: pivots[q] * inverse for q in range(at, groups)}
            ratio[at] = jnp.where(line > i % 8, ratio[at], 0.0)
            pivot_row = spread(square[at], i)
            for q in range(at, groups):
                square[q] = square[q] - ratio[q] * pivot_row
            if i + ahead < step:
                held[i + ahead] = column(i + ahead)
            for k in range(panels):
                pivot_row = spread(body[at][k], i)
                for q in range(at, groups):
                    body[q][k] = body[q][k] - ratio[q] * pivot_row
        result = jnp.concatenate(
            [jnp.concatenate([body[q][k] * scales[q] for k in range(panels)], axis=1) for q in range(groups)], axis=0
        )
        across = lax.broadcasted_iota(jnp.int32, (step, width), 1)
        down = lax.broadcasted_iota(jnp.int32, (step, width), 0)
        result = jnp.where(across >= down + row, result, 0.0)
        previous[...] = result
        upper[pl.ds(row, step), :] = result
        return carry

    lax.fori_loop(0, (stop - start) // step, superpanel, 0)
    if not last:
        done = stop - start
        before = previous[...]
        final = lax.dot_general(
            triple(before[:, done:], True), triple(before[:, done:], False), TN, preferred_element_type=F32
        )
        rest[...] = work[done:, done:] - final
    write_coded(Tiles(upper, (stop - start) // SPAN, panels, True), out)


def whiten_kernel(order, *refs, blocks, starts, first, chunks, aliased):
    count = len(starts)
    u_refs, refs = refs[: blocks * count], refs[blocks * count :]
    w_refs, refs = refs[:chunks], refs[chunks + aliased :]
    lowest = starts[0]
    out, left, ready, sems = refs
    half = BLOCK_W // 2
    chunk = ready.shape[2] // chunks
    step = pl.program_id(0)

    def copy(number, which, c):
        slot = lax.rem(number * count + which, 2)
        columns = pl.ds(c * chunk, chunk)
        return pltpu.make_async_copy(
            ready.at[slot, :, columns],
            out.at[order[first + number], pl.ds(starts[which], half), columns],
            sems.at[slot, c],
        )

    for which, start in enumerate(starts):
        width = BLOCK_W - start
        for b in range(blocks):

            @pl.when(step == b)
            def _(b=b):
                tiles = read_coded(u_refs[b * count + which], width // SPAN)
                for row in range(half // SPAN):
                    rows = slice(row * SPAN, (row + 1) * SPAN)
                    for column in range(width // SPAN):
                        value = tiles[row, column] if column >= row else jnp.zeros((SPAN, SPAN), F32)
                        high, low = split(value)
                        left[rows, column * SPAN : (column + 1) * SPAN] = high
                        left[rows, width + column * SPAN : width + (column + 1) * SPAN] = low

        for c in range(chunks):
            if count == 1:

                @pl.when(step >= 2)
                def _(c=c):
                    copy(step - 2, which, c).wait()

            elif blocks > 1:

                @pl.when(step >= 1)
                def _(c=c):
                    copy(step - 1, which, c).wait()

            weight = w_refs[c][start - lowest :]
            product = jnp.dot(
                left[:, : 2 * width], jnp.concatenate([weight, weight], axis=0), preferred_element_type=F32
            )
            ready[lax.rem(step * count + which, 2), :, c * chunk : (c + 1) * chunk] = product
            copy(step, which, c).start()

    @pl.when(step == blocks - 1)
    def _():
        for c in range(chunks):
            if count > 1:
                copy(step, 0, c).wait()
            elif blocks > 1:
                copy(step - 1, 0, c).wait()
            copy(step, count - 1, c).wait()


def shards(query_rows, key_rows, placed_value_rows, doc_lengths, span_order, out_weight):
    tokens = query_rows.shape[1]
    features = out_weight.shape[0]
    seq = lax.axis_size("seq")
    ring = lax.axis_size("dp")
    chips = seq // 2
    spans = tokens // SPAN
    all_spans = spans * seq
    documents = doc_lengths.shape[1]
    per = KEY_VALUE_HEADS // seq
    blocks = NB // seq
    own = lax.axis_index("seq").astype(jnp.int32)
    place = lax.axis_index("dp").astype(jnp.int32)
    query, key, value = query_rows[0], key_rows[0], placed_value_rows[0]
    vmem = pl.BlockSpec(memory_space=pltpu.VMEM)
    anywhere = pl.BlockSpec(memory_space=pl.ANY)
    in_ring = blocks == ring

    if in_ring:
        turns = [lax.rem(place + 2 * ring - 1 - t, ring) for t in range(blocks)]
    else:
        turns = [jnp.int32(t) for t in range(blocks)]
    first_kv = turns[0] // KV_BLOCKS

    def moved(distance, cross):
        return [
            (x * 2 + c, (x + distance) % chips * 2 + (1 - c if cross else c)) for x in range(chips) for c in range(2)
        ]

    def cut(targets, columns, scalars, name, after=(), limit=OTHER_VMEM):
        specs, arrays = [], []
        for target in targets:
            for array, size, index in columns:
                specs.append(
                    pl.BlockSpec((tokens, size), lambda i, meta, target=target, index=index: (0, index(target(meta), meta)))
                )
                arrays.append(array)
        width = sum(size for _, size, _ in columns)
        return pl.pallas_call(
            functools.partial(cut_kernel, targets=len(targets), given=len(columns)),
            out_shape=[jax.ShapeDtypeStruct((tokens, width), BF16)] * len(targets),
            grid_spec=pltpu.PrefetchScalarGridSpec(
                num_scalar_prefetch=1,
                grid=(1,),
                in_specs=specs + [anywhere] * len(after),
                out_specs=[pl.BlockSpec((tokens, width), lambda i, meta: (0, 0))] * len(targets),
            ),
            compiler_params=params(limit),
            cost_estimate=cost(0, 2**21),
            name=name,
        )(scalars, *arrays, *after)

    tile = 512

    def turn(first, count, *before):
        return pl.pallas_call(
            turn_kernel,
            out_shape=jax.ShapeDtypeStruct((blocks * BLOCK_W, features), BF16),
            grid=(count, features // tile),
            in_specs=[pl.BlockSpec((tile, BLOCK_W), lambda b, o: (o, first + b))] + [anywhere] * len(before),
            out_specs=pl.BlockSpec((BLOCK_W, tile), lambda b, o: (first + b, o)),
            input_output_aliases={1: 0} if first else {},
            compiler_params=params(TURN_VMEM),
            cost_estimate=cost(1.0e9 * count, 2**20),
            name="turn_weight",
        )(out_weight, *before)

    def target_at(distance, cross):
        return lambda meta: lax.rem(meta[0] // 2 + distance, chips) * 2 + lax.rem(lax.rem(meta[0], 2) + cross, 2)

    far = [(distance, cross) for distance in range(1, chips) for cross in range(2)]
    pieces = []

    most = all_spans // 2 + 1

    def grams_of(t, peer, after):
        kv = turns[t] // KV_BLOCKS
        carriers = pieces[: min(t + 1, per)]
        which = jnp.where(kv == first_kv, 0, 1).astype(jnp.int32)
        meta = jnp.concatenate([jnp.stack([own, turns[t], kv, which]), doc_lengths[0], span_order[0]])
        folded = jax.ShapeDtypeStruct((SUM_ROWS, SPAN), F32)
        peer_kv = blocks * BLOCK_W // HEAD_SIZE
        return pl.pallas_call(
            functools.partial(
                attention_kernel,
                chips=chips, spans=spans, all_spans=all_spans, documents=documents, most=most, sets=len(carriers),
                waited=len(after),
            ),
            out_shape=[folded] * 2,
            grid_spec=pltpu.PrefetchScalarGridSpec(
                num_scalar_prefetch=1,
                grid=(1,),
                in_specs=[
                    pl.BlockSpec((tokens, BLOCK_W), lambda i, meta: (0, meta[0] * blocks + meta[1])),
                    pl.BlockSpec((tokens, BLOCK_W), lambda i, meta: (0, meta[1])),
                ]
                + [pl.BlockSpec((tokens, BLOCK_W), lambda i, meta: (0, 0))] * len(far)
                + [pl.BlockSpec((tokens, HEAD_SIZE), lambda i, meta: (0, meta[0] * per + meta[2]))] * 2
                + [
                    pl.BlockSpec((tokens, HEAD_SIZE), lambda i, meta: (0, peer_kv + meta[2])),
                    pl.BlockSpec((tokens, HEAD_SIZE), lambda i, meta: (0, peer_kv + per + meta[2])),
                ]
                + [pl.BlockSpec((tokens, 2 * HEAD_SIZE), lambda i, meta: (0, BLOCK_W // (2 * HEAD_SIZE)))]
                * (len(carriers) * len(far))
                + [anywhere] * len(after),
                out_specs=[pl.BlockSpec((SUM_ROWS, SPAN), lambda i, meta: (0, 0))] * 2,
                scratch_shapes=[
                    pltpu.VMEM((all_spans, BLOCK_HEADS * SPAN, HEAD_SIZE), BF16),
                    pltpu.VMEM((all_spans, SPAN, HEAD_SIZE), BF16),
                    pltpu.VMEM((all_spans, HEAD_SIZE, SPAN), BF16),
                    pltpu.SMEM((all_spans,), jnp.int32),
                    pltpu.VMEM((2, most * SPAN, SPAN), F32),
                    pltpu.VMEM((2, BLOCK_W, all_spans * SPAN), BF16),
                    pltpu.VMEM((2, all_spans * SPAN, BLOCK_W), BF16),
                    pltpu.VMEM((BLOCK_W, BLOCK_W), F32),
                ],
            ),
            compiler_params=params(ATTENTION_VMEM),
            cost_estimate=cost(1.4e10, 2**20),
            name="attention_outer_products",
        )(meta, query, peer, *pieces[t], key, value, peer, peer, *[array for carrier in carriers for array in carrier], *after)

    grams = []
    held = []
    for t in range(blocks + 1):
        if t < blocks:
            kv = first_kv if t == 0 else per - 1 - first_kv
            columns = [(query, BLOCK_W, lambda target, meta: target * blocks + meta[1])]
            if t < per:
                columns += [(array, HEAD_SIZE, lambda target, meta: target * per + meta[2]) for array in (key, value)]
            scalars = jnp.stack([own, turns[t], kv])
            after = [] if t == 0 else [peer, turned] if t == 1 else [peer, turned]
            parts = cut(
                [target_at(*where) for where in far], columns, scalars, "cut_piece", after,
                OTHER_VMEM if t else FULL_VMEM,
            )
            if t > 1:
                *parts, held[t - 2] = lax.optimization_barrier((*parts, held[t - 2]))
            pieces.append([lax.ppermute(part, "seq", moved(*where)) for part, where in zip(parts, far)])
        if t == 0:
            columns = [(query, blocks * BLOCK_W, lambda target, meta: target)]
            columns += [(array, per * HEAD_SIZE, lambda target, meta: target) for array in (key, value)]
            peer = cut([target_at(0, 1)], columns, own[None], "cut_peer", parts, FULL_VMEM)[0]
            turned = turn(0, 1, peer)
            peer = lax.ppermute(peer, "seq", moved(0, 1))
            turned = turn(1, 1, turned)
            continue
        if t == 1:
            for b in range(2, blocks - 1):
                turned = turn(b, 1, turned, parts[0])
        done = t - 1
        grams.append(grams_of(done, peer, [turned] if t == 1 else []))
        if done == 0 or not in_ring:
            held.append(grams[done])
        else:
            held.append([mine + theirs for mine, theirs in zip(grams[done], carried)] if done < ring - 1 else None)
        if in_ring and done < ring - 1:
            carried = [lax.ppermute(part, "dp", [(z, (z + 1) % ring) for z in range(ring)]) for part in held[done]]
    if blocks > 2:
        turned = turn(blocks - 1, 1, turned, *grams[-1])

    half = BLOCK_W // 2
    top_rows, bottom_rows = [
        SPAN * (sum(len(part) for part in tile_order(2, columns))) + 16 for columns in (PANELS, PANELS // 2)
    ]
    scratch = lambda width: [pltpu.VMEM((width, width), F32), pltpu.VMEM((32, width), F32), pltpu.VMEM((half, width), F32)]

    def factor_top(*given):
        return pl.pallas_call(
            functools.partial(factor_kernel, start=0, stop=half, received=len(given)),
            out_shape=[
                jax.ShapeDtypeStruct((top_rows, SPAN), BF16),
                jax.ShapeDtypeStruct((half, half), F32),
            ],
            in_specs=[vmem] * len(given),
            out_specs=[vmem] * 2,
            scratch_shapes=scratch(BLOCK_W),
            compiler_params=params(OTHER_VMEM),
            cost_estimate=cost(1.0e10, 2**20),
            name="factor_top",
        )(*given)

    def factor_bottom(rest):
        return pl.pallas_call(
            functools.partial(factor_kernel, start=half, stop=BLOCK_W, received=1),
            out_shape=jax.ShapeDtypeStruct((bottom_rows, SPAN), BF16),
            in_specs=[vmem],
            out_specs=vmem,
            scratch_shapes=scratch(half),
            compiler_params=params(OTHER_VMEM),
            cost_estimate=cost(0.9e10, 2**20),
            name="factor_bottom",
        )(rest)

    if in_ring:
        top, rest = factor_top(*grams[ring - 1], *carried)

        def shared(array):
            return [array] + [
                lax.ppermute(array, "dp", [(z, (z + d) % ring) for z in range(ring)]) for d in range(1, ring)
            ]

        tops = shared(top)
        bottom = factor_bottom(rest)
        bottoms = shared(bottom)
        order = jnp.stack([lax.rem(place - d + ring, ring) for d in range(ring)])
    else:
        halves = [factor_top(*[lax.psum(part, "dp") for part in grams[t]]) for t in range(blocks)]
        tops = [top for top, _ in halves]
        bottoms = [factor_bottom(rest) for _, rest in halves]
        bottom = bottoms[0]
        order = jnp.arange(blocks, dtype=jnp.int32)


    def whiten(uppers, first, starts, result):
        more = [] if result is None else [result]
        depth = BLOCK_W - starts[0]
        chunks = features // tile
        weights = [
            pl.BlockSpec(
                (depth, tile),
                lambda b, order, c=c: (order[first + b] * (BLOCK_W // depth) + starts[0] // depth, c),
            )
            for c in range(chunks)
        ]
        count = len(uppers) // len(starts)
        return pl.pallas_call(
            functools.partial(
                whiten_kernel, blocks=count, starts=starts, first=first, chunks=chunks, aliased=len(more)
            ),
            out_shape=jax.ShapeDtypeStruct((blocks, BLOCK_W, features), F32),
            grid_spec=pltpu.PrefetchScalarGridSpec(
                num_scalar_prefetch=1,
                grid=(count,),
                in_specs=[vmem] * len(uppers) + weights + [anywhere] * len(more),
                out_specs=anywhere,
                scratch_shapes=[
                    pltpu.VMEM((half, 2 * depth), BF16),
                    pltpu.VMEM((2, half, features), F32),
                    pltpu.SemaphoreType.DMA((2, chunks)),
                ],
            ),
            input_output_aliases={1 + len(uppers) + chunks: 0} if more else {},
            compiler_params=params(WHITEN_VMEM),
            cost_estimate=cost(2.0e9 * len(uppers), 2**20),
            name="whiten_bottom" if starts[0] else "whiten_top",
        )(order, *uppers, *[turned] * chunks, *more)

    result = whiten([tops[0], bottoms[0]], 0, (0, half), None)
    result = whiten(tops[1:], 1, (0,), result)
    return whiten(bottoms[1:], 1, (half,), result)


def solution(mesh):
    in_specs = (
        P(("groups", "dp"), "seq", None),
        P(("groups", "dp"), "seq", None),
        P(("groups", "dp"), "seq", None),
        P(("groups", "dp"), None),
        P(("groups", "dp"), None),
        P("dp", "seq"),
    )
    out_specs = P(("groups", "seq"), None, "dp")
    return jax.shard_map(shards, mesh=mesh, in_specs=in_specs, out_specs=out_specs, check_vma=False)
```

```python
import functools
import math

import jax
import jax.numpy as jnp
from jax import lax
from jax.experimental import pallas as pl
from jax.experimental.pallas import tpu as pltpu
from jax.sharding import PartitionSpec as P

QUERY_HEADS = 64
KEY_VALUE_HEADS = 8
HEAD_SIZE = 128
BLOCK_W = 512
NB = 16
SPAN = 128
GROUP = QUERY_HEADS // KEY_VALUE_HEADS
BLOCK_HEADS = BLOCK_W // HEAD_SIZE
KV_BLOCKS = GROUP // BLOCK_HEADS
PANELS = BLOCK_W // SPAN
SUM_ROWS = SPAN * PANELS + 8
VMEM_BYTES = 50 * 2**20
FULL_VMEM = 63 * 2**20
ATTENTION_VMEM = 44 * 2**20
WHITEN_VMEM = 44 * 2**20
OTHER_VMEM = 44 * 2**20
F32 = jnp.float32
BF16 = jnp.bfloat16
NT = (((1,), (1,)), ((), ()))
TN = (((0,), (0,)), ((), ()))


def params(limit=OTHER_VMEM):
    return pltpu.CompilerParams(vmem_limit_bytes=limit)


def cost(flops, moved, trans=0):
    return pl.CostEstimate(flops=int(flops), bytes_accessed=int(moved), transcendentals=int(trans))


def encode(value, exponent):
    scaled = value * jnp.exp2(15.0 - exponent)
    power = scaled * scaled
    power = power * power
    power = power * power
    return jnp.where(scaled < 0.0, -power, power)


def decode(code, exponent):
    code = code.astype(F32)
    quarter = lax.rsqrt(lax.rsqrt(jnp.maximum(jnp.abs(code), 1e-37)))
    root = quarter * lax.rsqrt(quarter) * jnp.exp2(exponent - 15.0)
    return jnp.where(code < 0.0, -root, root)


def exponent_of(largest):
    return jnp.ceil(jnp.log(jnp.maximum(largest, 1e-30)) * (1.0 / math.log(2.0)) + 0.001)


def write_coded(tiles, out):
    off, pairs = tile_order(tiles.rows, tiles.columns)
    places = off + [(i, i) for i in range(tiles.rows)]
    largest = functools.reduce(jnp.maximum, [jnp.max(jnp.abs(tiles(*p)), axis=(0, 1), keepdims=True) for p in places])
    exponent = exponent_of(largest)
    (line,) = fold(tiles, out, lambda value: encode(value, exponent))
    row = lax.broadcasted_iota(jnp.int32, (16, SPAN), 0)
    out[(len(off) + len(pairs)) * SPAN :] = jnp.where(row < 8, line, exponent).astype(BF16)


def read_coded(ref, columns):
    upper, equal = diagonal_masks()
    off, pairs = tile_order(2, columns)
    at = (len(off) + len(pairs)) * SPAN
    tail = ref[at:].astype(F32)
    exponent = tail[15:16, 0:1]
    tiles = {place: decode(ref[i * SPAN : (i + 1) * SPAN], exponent) for i, place in enumerate(off)}
    square = decode(ref[at - SPAN : at], exponent)
    line = decode(tail[0:1], exponent)
    tiles[0, 0] = jnp.where(upper, square, 0.0)
    tiles[1, 1] = jnp.where(equal, line, jnp.where(upper, square.T, 0.0))
    return tiles


def split(value):
    high = value.astype(BF16)
    return high, (value - high.astype(F32)).astype(BF16)


def cut_kernel(meta, *refs, targets, given):
    outs = refs[-targets:]
    for number, out in enumerate(outs):
        at = 0
        for ref in refs[number * given : (number + 1) * given]:
            out[:, at : at + ref.shape[1]] = ref[...]
            at += ref.shape[1]


def attention_kernel(meta, *refs, chips, spans, all_spans, documents, most, sets):
    sources = 2 * chips
    near = sources + 4
    query_refs, near_refs = refs[:sources], refs[sources:near]
    far_refs = refs[near : near + sets * (sources - 2)]
    top, bottom, queries, keys, values, slots, limits, left, total = refs[near + sets * (sources - 2) :]
    own = meta[0]
    chip, core = own // 2, lax.rem(own, 2)
    lengths = 4
    order = lengths + documents

    for r in range(all_spans):
        device = r // spans
        distance = lax.rem(chip - device // 2 + chips, chips)
        cross = lax.rem(core + device % 2, 2)
        slots[meta[order + r]] = (distance * 2 + cross) * spans + r % spans

    def place_kv(source, key_part, value_part):
        for t in range(spans):
            rows = slice(t * SPAN, (t + 1) * SPAN)
            keys[source * spans + t] = key_part[rows]
            values[source * spans + t] = value_part[rows].astype(F32).T.astype(BF16)

    place_kv(0, near_refs[0], near_refs[1])
    place_kv(1, near_refs[2], near_refs[3])
    for which in range(sets):

        @pl.when(meta[3] == which)
        def _(which=which):
            for source in range(2, sources):
                ref = far_refs[which * (sources - 2) + source - 2]
                place_kv(source, ref[:, :HEAD_SIZE], ref[:, HEAD_SIZE:])

    for source in range(sources):
        for t in range(spans):
            for h in range(BLOCK_HEADS):
                queries[source * spans + t, h * SPAN : (h + 1) * SPAN] = query_refs[source][
                    t * SPAN : (t + 1) * SPAN, h * HEAD_SIZE : (h + 1) * HEAD_SIZE
                ]

    factor = HEAD_SIZE ** (-0.5) / math.log(2.0)

    def place_of(q):
        source = q // spans
        distance, cross = source // 2, lax.rem(source, 2)
        device = lax.rem(chip - distance + chips, chips) * 2 + lax.rem(core + cross, 2)
        position = meta[order + device * spans + lax.rem(q, spans)]
        first_row = position * SPAN
        begin = jnp.int32(0)
        at = jnp.int32(0)
        query_pos = lax.broadcasted_iota(jnp.int32, (1, SPAN), 1) + first_row
        query_begin = jnp.zeros((1, SPAN), jnp.int32)
        for d in range(documents):
            begin = jnp.where(at <= first_row, at, begin)
            query_begin = jnp.where(query_pos >= at, at, query_begin)
            at = at + meta[lengths + d]
        return position, query_pos, query_begin, position - begin // SPAN + 1

    def one_pair(p, carry):
        pair = [(which, 2 * p + which, place_of(2 * p + which)) for which in range(2)]
        count = jnp.maximum(pair[0][2][3], pair[1][2][3])

        for n in range(1, most + 1):

            @pl.when(count == n)
            def _(n=n):
                for which, q, (position, query_pos, query_begin, _) in pair:
                    lanes = pl.ds(pl.multiple_of(q * SPAN, SPAN), SPAN)
                    held = [slots[jnp.maximum(position - n + 1 + i, 0)] for i in range(n)]
                    for i in range(n):
                        key_pos = lax.broadcasted_iota(jnp.int32, (SPAN, SPAN), 0) + (position - n + 1 + i) * SPAN
                        seen = (key_pos <= query_pos) & (key_pos >= query_begin)
                        limits[which, i * SPAN : (i + 1) * SPAN] = jnp.where(seen, 3e38, -1e30)
                    key_part = jnp.concatenate([keys[slot] for slot in held], axis=0)
                    value_part = jnp.concatenate([values[slot] for slot in held], axis=1)
                    scores = lax.dot_general(key_part, queries[q], NT, preferred_element_type=F32)
                    limit = limits[which, : n * SPAN]
                    scores = jnp.minimum(scores, jnp.concatenate([limit] * BLOCK_HEADS, axis=1))
                    largest = jnp.max(scores, axis=0, keepdims=True)
                    lifted = jnp.exp2((scores - largest) * factor)
                    summed = jnp.sum(lifted, axis=0, keepdims=True)
                    weights = (lifted * (1.0 / summed)).astype(BF16)
                    mixed = jnp.dot(value_part, weights, preferred_element_type=F32)
                    for h in range(BLOCK_HEADS):
                        one_head = mixed[:, h * SPAN : (h + 1) * SPAN]
                        columns = slice(h * HEAD_SIZE, (h + 1) * HEAD_SIZE)
                        high, low = split(one_head)
                        left[0, columns, lanes] = high
                        left[1, columns, lanes] = low

        return carry

    lax.fori_loop(0, all_spans // 2, one_pair, 0)

    half = BLOCK_W // 2
    total[...] = jnp.zeros_like(total)

    def one_pass(i, carry):
        a, b = lax.rem(i, 2), i // 2
        total[:half] += lax.dot_general(left[a, :half], left[b], NT, preferred_element_type=F32)
        total[half:, half:] += lax.dot_general(left[a, half:], left[b, half:], NT, preferred_element_type=F32)
        return carry

    lax.fori_loop(0, 3, one_pass, 0)
    for out, where in zip((top, bottom), sum_tiles()):
        off, pair = where
        (line,) = fold(Tiles(total, PANELS, PANELS, False), out, where=(off, [pair]))
        out[SUM_ROWS - 8 :] = jnp.broadcast_to(line, (8, SPAN))


def diagonal_masks():
    rows = lax.broadcasted_iota(jnp.int32, (SPAN, SPAN), 0)
    columns = lax.broadcasted_iota(jnp.int32, (SPAN, SPAN), 1)
    return rows <= columns, rows == columns


def tile_order(rows, columns):
    off = [(i, j) for i in range(rows) for j in range(i + 1, columns)]
    return off, [(i, i + 1) for i in range(0, rows, 2)]


def sum_tiles():
    off, pairs = tile_order(PANELS, PANELS)
    half = len(off) // 2
    return [(off[:half], pairs[0]), (off[half:], pairs[1])]


def fold(tiles, out, change=lambda value: value, where=None):
    upper, equal = diagonal_masks()
    off, pairs = tile_order(tiles.rows, tiles.columns) if where is None else where
    for i, place in enumerate(off):
        out[i * SPAN : (i + 1) * SPAN] = change(tiles(*place)).astype(out.dtype)
    lines = []
    for i, (a, b) in enumerate(pairs):
        second = tiles(b, b)
        at = (len(off) + i) * SPAN
        lower = second.T if tiles.turn else second
        out[at : at + SPAN] = change(jnp.where(upper, tiles(a, a), lower)).astype(out.dtype)
        lines.append(change(jnp.sum(jnp.where(equal, second, 0.0), axis=0, keepdims=True)))
    return lines


class Tiles:
    def __init__(self, ref, rows, columns, turn):
        self.ref, self.rows, self.columns, self.turn = ref, rows, columns, turn

    def __call__(self, i, j):
        return self.ref[i * SPAN : (i + 1) * SPAN, j * SPAN : (j + 1) * SPAN]


def unfold(halves, work):
    upper, equal = diagonal_masks()
    trace = jnp.zeros((1, 1), F32)
    squares = []
    for total, (off, (a, b)) in zip(halves, sum_tiles()):
        for i, (row, column) in enumerate(off):
            work[row * SPAN : (row + 1) * SPAN, column * SPAN : (column + 1) * SPAN] = total[i * SPAN : (i + 1) * SPAN]
        at = len(off) * SPAN
        square = total[at : at + SPAN]
        turned = square.T
        line = jnp.broadcast_to(total[at + SPAN : at + SPAN + 1], (SPAN, SPAN))
        squares.append((a, jnp.where(upper, square, turned)))
        squares.append((b, jnp.where(equal, line, jnp.where(upper, turned, square))))
    for _, square in squares:
        trace = trace + jnp.sum(jnp.where(equal, square, 0.0), axis=(0, 1), keepdims=True)
    damping = trace * (0.1 / BLOCK_W)
    for a, square in squares:
        work[a * SPAN : (a + 1) * SPAN, a * SPAN : (a + 1) * SPAN] = jnp.where(equal, square + damping, square)


def factor_kernel(*refs, start, stop, received):
    width = BLOCK_W - start
    panels = width // SPAN
    step = 32
    groups = step // 8
    per_tile = SPAN // step
    last = stop == BLOCK_W
    given, refs = (refs[:received], refs[received:])
    out, refs = refs[0], refs[1:]
    if not last:
        rest, refs = refs[0], refs[1:]
    work, previous, upper = refs
    if start == 0:
        work[...] = jnp.zeros_like(work)
        halves = [ref[...] for ref in given[:2]]
        if received == 4:
            halves = [mine + ref[...] for mine, ref in zip(halves, given[2:])]
        unfold(halves, work)
    else:
        work[...] = given[0][...]
    previous[...] = jnp.zeros_like(previous)

    def triple(value, first):
        high, low = split(value)
        return jnp.concatenate((high, low, high) if first else (high, high, low), axis=0)

    def superpanel(g, carry):
        row = pl.multiple_of(g * step, step)
        tile_index = g // per_tile
        tile = pl.ds(pl.multiple_of(tile_index * SPAN, SPAN), SPAN)
        turn = lax.rem(SPAN - lax.rem(g, per_tile) * step, SPAN)
        before = previous[...]
        right = triple(before, False)
        near = pltpu.roll(previous[:, tile], turn, 1)
        fresh = lax.dot_general(triple(near, True), right, TN, preferred_element_type=F32)[:step]
        current = work[pl.ds(row, step), :] - fresh
        work[...] = work[...] - lax.dot_general(triple(before, True), right, TN, preferred_element_type=F32)

        square = current[:, :SPAN]
        for k in range(1, panels):
            square = jnp.where(tile_index == k, current[:, k * SPAN : (k + 1) * SPAN], square)
        square = pltpu.roll(square, turn, 1)
        line = lax.broadcasted_iota(jnp.int32, (8, SPAN), 0)
        held = [
            {q: jnp.broadcast_to(square[8 * q : 8 * q + 8, j : j + 1], (8, SPAN)) for q in range(j // 8, groups)}
            for j in range(step)
        ]
        body = [[current[8 * q : 8 * q + 8, k * SPAN : (k + 1) * SPAN] for k in range(panels)] for q in range(groups)]
        scales = [jnp.zeros((8, SPAN), F32) for _ in range(groups)]

        def spread(value, i):
            return jnp.broadcast_to(value[i % 8 : i % 8 + 1], (8, SPAN))

        for i in range(step):
            at = i // 8
            root = lax.rsqrt(spread(held[i][at], i))
            inverse = root * root
            scales[at] = jnp.where(line == i % 8, root, scales[at])
            ratio = {q: held[i][q] * inverse for q in range(at, groups)}
            ratio[at] = jnp.where(line > i % 8, ratio[at], 0.0)
            for j in range(i + 1, step):
                entry = spread(held[i][j // 8], j)
                for q in range(j // 8, groups):
                    held[j][q] = held[j][q] - ratio[q] * entry
            for k in range(panels):
                pivot_row = spread(body[at][k], i)
                for q in range(at, groups):
                    body[q][k] = body[q][k] - ratio[q] * pivot_row
        result = jnp.concatenate(
            [jnp.concatenate([body[q][k] * scales[q] for k in range(panels)], axis=1) for q in range(groups)], axis=0
        )
        across = lax.broadcasted_iota(jnp.int32, (step, width), 1)
        down = lax.broadcasted_iota(jnp.int32, (step, width), 0)
        result = jnp.where(across >= down + row, result, 0.0)
        previous[...] = result
        upper[pl.ds(row, step), :] = result
        return carry

    lax.fori_loop(0, (stop - start) // step, superpanel, 0)
    if not last:
        done = stop - start
        before = previous[...]
        final = lax.dot_general(
            triple(before[:, done:], True), triple(before[:, done:], False), TN, preferred_element_type=F32
        )
        rest[...] = work[done:, done:] - final
    write_coded(Tiles(upper, (stop - start) // SPAN, panels, True), out)


def whiten_kernel(order, *refs, blocks, starts, first, chunks, aliased):
    count = len(starts)
    u_refs, refs = refs[: blocks * count], refs[blocks * count :]
    w_refs, refs = refs[:chunks], refs[chunks + aliased :]
    lowest = starts[0]
    out, left, ready, sems = refs
    half = BLOCK_W // 2
    chunk = ready.shape[2] // chunks
    step = pl.program_id(0)

    def copy(number, which, c):
        slot = lax.rem(number * count + which, 2)
        columns = pl.ds(c * chunk, chunk)
        return pltpu.make_async_copy(
            ready.at[slot, :, columns],
            out.at[order[first + number], pl.ds(starts[which], half), columns],
            sems.at[slot, c],
        )

    for which, start in enumerate(starts):
        width = BLOCK_W - start
        for b in range(blocks):

            @pl.when(step == b)
            def _(b=b):
                tiles = read_coded(u_refs[b * count + which], width // SPAN)
                for row in range(half // SPAN):
                    rows = slice(row * SPAN, (row + 1) * SPAN)
                    for column in range(width // SPAN):
                        value = tiles[row, column] if column >= row else jnp.zeros((SPAN, SPAN), F32)
                        high, low = split(value)
                        columns = slice(column * SPAN, (column + 1) * SPAN)
                        left[rows, columns] = high
                        left[half + row * SPAN : half + (row + 1) * SPAN, columns] = low

        for c in range(chunks):
            if count == 1:

                @pl.when(step >= 2)
                def _(c=c):
                    copy(step - 2, which, c).wait()

            elif blocks > 1:

                @pl.when(step >= 1)
                def _(c=c):
                    copy(step - 1, which, c).wait()

            weight = w_refs[c][:, start - lowest :]
            product = lax.dot_general(left[:, :width], weight, NT, preferred_element_type=F32)
            ready[lax.rem(step * count + which, 2), :, c * chunk : (c + 1) * chunk] = product[:half] + product[half:]
            copy(step, which, c).start()

    @pl.when(step == blocks - 1)
    def _():
        for c in range(chunks):
            if count > 1:
                copy(step, 0, c).wait()
            elif blocks > 1:
                copy(step - 1, 0, c).wait()
            copy(step, count - 1, c).wait()


def shards(query_rows, key_rows, placed_value_rows, doc_lengths, span_order, out_weight):
    tokens = query_rows.shape[1]
    features = out_weight.shape[0]
    seq = lax.axis_size("seq")
    ring = lax.axis_size("dp")
    chips = seq // 2
    spans = tokens // SPAN
    all_spans = spans * seq
    documents = doc_lengths.shape[1]
    per = KEY_VALUE_HEADS // seq
    blocks = NB // seq
    own = lax.axis_index("seq").astype(jnp.int32)
    place = lax.axis_index("dp").astype(jnp.int32)
    query, key, value = query_rows[0], key_rows[0], placed_value_rows[0]
    vmem = pl.BlockSpec(memory_space=pltpu.VMEM)
    anywhere = pl.BlockSpec(memory_space=pl.ANY)
    in_ring = blocks == ring

    if in_ring:
        turns = [lax.rem(place + 2 * ring - 1 - t, ring) for t in range(blocks)]
    else:
        turns = [jnp.int32(t) for t in range(blocks)]
    first_kv = turns[0] // KV_BLOCKS

    def moved(distance, cross):
        return [
            (x * 2 + c, (x + distance) % chips * 2 + (1 - c if cross else c)) for x in range(chips) for c in range(2)
        ]

    def cut(targets, columns, scalars, name, after=(), limit=OTHER_VMEM):
        specs, arrays = [], []
        for target in targets:
            for array, size, index in columns:
                specs.append(
                    pl.BlockSpec((tokens, size), lambda i, meta, target=target, index=index: (0, index(target(meta), meta)))
                )
                arrays.append(array)
        width = sum(size for _, size, _ in columns)
        return pl.pallas_call(
            functools.partial(cut_kernel, targets=len(targets), given=len(columns)),
            out_shape=[jax.ShapeDtypeStruct((tokens, width), BF16)] * len(targets),
            grid_spec=pltpu.PrefetchScalarGridSpec(
                num_scalar_prefetch=1,
                grid=(1,),
                in_specs=specs + [anywhere] * len(after),
                out_specs=[pl.BlockSpec((tokens, width), lambda i, meta: (0, 0))] * len(targets),
            ),
            compiler_params=params(limit),
            cost_estimate=cost(0, 2**21),
            name=name,
        )(scalars, *arrays, *after)

    tile = 512

    def target_at(distance, cross):
        return lambda meta: lax.rem(meta[0] // 2 + distance, chips) * 2 + lax.rem(lax.rem(meta[0], 2) + cross, 2)

    far = [(distance, cross) for distance in range(1, chips) for cross in range(2)]
    pieces = []

    most = all_spans // 2 + 1

    def grams_of(t, peer):
        kv = turns[t] // KV_BLOCKS
        carriers = pieces[: min(t + 1, per)]
        which = jnp.where(kv == first_kv, 0, 1).astype(jnp.int32)
        meta = jnp.concatenate([jnp.stack([own, turns[t], kv, which]), doc_lengths[0], span_order[0]])
        folded = jax.ShapeDtypeStruct((SUM_ROWS, SPAN), F32)
        peer_kv = blocks * BLOCK_W // HEAD_SIZE
        return pl.pallas_call(
            functools.partial(
                attention_kernel,
                chips=chips, spans=spans, all_spans=all_spans, documents=documents, most=most, sets=len(carriers),
            ),
            out_shape=[folded] * 2,
            grid_spec=pltpu.PrefetchScalarGridSpec(
                num_scalar_prefetch=1,
                grid=(1,),
                in_specs=[
                    pl.BlockSpec((tokens, BLOCK_W), lambda i, meta: (0, meta[0] * blocks + meta[1])),
                    pl.BlockSpec((tokens, BLOCK_W), lambda i, meta: (0, meta[1])),
                ]
                + [pl.BlockSpec((tokens, BLOCK_W), lambda i, meta: (0, 0))] * len(far)
                + [pl.BlockSpec((tokens, HEAD_SIZE), lambda i, meta: (0, meta[0] * per + meta[2]))] * 2
                + [
                    pl.BlockSpec((tokens, HEAD_SIZE), lambda i, meta: (0, peer_kv + meta[2])),
                    pl.BlockSpec((tokens, HEAD_SIZE), lambda i, meta: (0, peer_kv + per + meta[2])),
                ]
                + [pl.BlockSpec((tokens, 2 * HEAD_SIZE), lambda i, meta: (0, BLOCK_W // (2 * HEAD_SIZE)))]
                * (len(carriers) * len(far)),
                out_specs=[pl.BlockSpec((SUM_ROWS, SPAN), lambda i, meta: (0, 0))] * 2,
                scratch_shapes=[
                    pltpu.VMEM((all_spans, BLOCK_HEADS * SPAN, HEAD_SIZE), BF16),
                    pltpu.VMEM((all_spans, SPAN, HEAD_SIZE), BF16),
                    pltpu.VMEM((all_spans, HEAD_SIZE, SPAN), BF16),
                    pltpu.SMEM((all_spans,), jnp.int32),
                    pltpu.VMEM((2, most * SPAN, SPAN), F32),
                    pltpu.VMEM((2, BLOCK_W, all_spans * SPAN), BF16),
                    pltpu.VMEM((BLOCK_W, BLOCK_W), F32),
                ],
            ),
            compiler_params=params(ATTENTION_VMEM),
            cost_estimate=cost(1.4e10, 2**20),
            name="attention_outer_products",
        )(meta, query, peer, *pieces[t], key, value, peer, peer, *[array for carrier in carriers for array in carrier])

    grams = []
    held = []
    for t in range(blocks + 1):
        if t < blocks:
            kv = first_kv if t == 0 else per - 1 - first_kv
            columns = [(query, BLOCK_W, lambda target, meta: target * blocks + meta[1])]
            if t < per:
                columns += [(array, HEAD_SIZE, lambda target, meta: target * per + meta[2]) for array in (key, value)]
            scalars = jnp.stack([own, turns[t], kv])
            after = [] if t == 0 else [peer]
            parts = cut(
                [target_at(*where) for where in far], columns, scalars, "cut_piece", after,
                OTHER_VMEM if t else FULL_VMEM,
            )
            if t > 1:
                *parts, held[t - 2] = lax.optimization_barrier((*parts, held[t - 2]))
            pieces.append([lax.ppermute(part, "seq", moved(*where)) for part, where in zip(parts, far)])
        if t == 0:
            columns = [(query, blocks * BLOCK_W, lambda target, meta: target)]
            columns += [(array, per * HEAD_SIZE, lambda target, meta: target) for array in (key, value)]
            peer = cut([target_at(0, 1)], columns, own[None], "cut_peer", parts, FULL_VMEM)[0]
            peer = lax.ppermute(peer, "seq", moved(0, 1))
            continue
        done = t - 1
        grams.append(grams_of(done, peer))
        if done == 0 or not in_ring:
            held.append(grams[done])
        else:
            held.append([mine + theirs for mine, theirs in zip(grams[done], carried)] if done < ring - 1 else None)
        if in_ring and done < ring - 1:
            carried = [lax.ppermute(part, "dp", [(z, (z + 1) % ring) for z in range(ring)]) for part in held[done]]

    half = BLOCK_W // 2
    top_rows, bottom_rows = [
        SPAN * (sum(len(part) for part in tile_order(2, columns))) + 16 for columns in (PANELS, PANELS // 2)
    ]
    scratch = lambda width: [pltpu.VMEM((width, width), F32), pltpu.VMEM((32, width), F32), pltpu.VMEM((half, width), F32)]

    def factor_top(*given):
        return pl.pallas_call(
            functools.partial(factor_kernel, start=0, stop=half, received=len(given)),
            out_shape=[
                jax.ShapeDtypeStruct((top_rows, SPAN), BF16),
                jax.ShapeDtypeStruct((half, half), F32),
            ],
            in_specs=[vmem] * len(given),
            out_specs=[vmem] * 2,
            scratch_shapes=scratch(BLOCK_W),
            compiler_params=params(OTHER_VMEM),
            cost_estimate=cost(1.0e10, 2**20),
            name="factor_top",
        )(*given)

    def factor_bottom(rest):
        return pl.pallas_call(
            functools.partial(factor_kernel, start=half, stop=BLOCK_W, received=1),
            out_shape=jax.ShapeDtypeStruct((bottom_rows, SPAN), BF16),
            in_specs=[vmem],
            out_specs=vmem,
            scratch_shapes=scratch(half),
            compiler_params=params(OTHER_VMEM),
            cost_estimate=cost(0.9e10, 2**20),
            name="factor_bottom",
        )(rest)

    if in_ring:
        top, rest = factor_top(*grams[ring - 1], *carried)

        def shared(array):
            return [array] + [
                lax.ppermute(array, "dp", [(z, (z + d) % ring) for z in range(ring)]) for d in range(1, ring)
            ]

        tops = shared(top)
        bottom = factor_bottom(rest)
        bottoms = shared(bottom)
        order = jnp.stack([lax.rem(place - d + ring, ring) for d in range(ring)])
    else:
        halves = [factor_top(*[lax.psum(part, "dp") for part in grams[t]]) for t in range(blocks)]
        tops = [top for top, _ in halves]
        bottoms = [factor_bottom(rest) for _, rest in halves]
        bottom = bottoms[0]
        order = jnp.arange(blocks, dtype=jnp.int32)


    def whiten(uppers, first, starts, result):
        more = [] if result is None else [result]
        depth = BLOCK_W - starts[0]
        chunks = features // tile
        weights = [
            pl.BlockSpec(
                (tile, depth),
                lambda b, order, c=c: (c, order[first + b] * (BLOCK_W // depth) + starts[0] // depth),
            )
            for c in range(chunks)
        ]
        count = len(uppers) // len(starts)
        return pl.pallas_call(
            functools.partial(
                whiten_kernel, blocks=count, starts=starts, first=first, chunks=chunks, aliased=len(more)
            ),
            out_shape=jax.ShapeDtypeStruct((blocks, BLOCK_W, features), F32),
            grid_spec=pltpu.PrefetchScalarGridSpec(
                num_scalar_prefetch=1,
                grid=(count,),
                in_specs=[vmem] * len(uppers) + weights + [anywhere] * len(more),
                out_specs=anywhere,
                scratch_shapes=[
                    pltpu.VMEM((2 * half, depth), BF16),
                    pltpu.VMEM((2, half, features), F32),
                    pltpu.SemaphoreType.DMA((2, chunks)),
                ],
            ),
            input_output_aliases={1 + len(uppers) + chunks: 0} if more else {},
            compiler_params=params(WHITEN_VMEM),
            cost_estimate=cost(2.0e9 * len(uppers), 2**20),
            name="whiten_bottom" if starts[0] else "whiten_top",
        )(order, *uppers, *[out_weight] * chunks, *more)

    result = whiten([tops[0], bottoms[0]], 0, (0, half), None)
    result = whiten(tops[1:], 1, (0,), result)
    return whiten(bottoms[1:], 1, (half,), result)


def solution(mesh):
    in_specs = (
        P(("groups", "dp"), "seq", None),
        P(("groups", "dp"), "seq", None),
        P(("groups", "dp"), "seq", None),
        P(("groups", "dp"), None),
        P(("groups", "dp"), None),
        P("dp", "seq"),
    )
    out_specs = P(("groups", "seq"), None, "dp")
    return jax.shard_map(shards, mesh=mesh, in_specs=in_specs, out_specs=out_specs, check_vma=False)
```

```python
import functools
import math

import jax
import jax.numpy as jnp
from jax import lax
from jax.experimental import pallas as pl
from jax.experimental.pallas import tpu as pltpu
from jax.sharding import PartitionSpec as P

QUERY_HEADS = 64
KEY_VALUE_HEADS = 8
HEAD_SIZE = 128
BLOCK_W = 512
NB = 16
SPAN = 128
GROUP = QUERY_HEADS // KEY_VALUE_HEADS
BLOCK_HEADS = BLOCK_W // HEAD_SIZE
KV_BLOCKS = GROUP // BLOCK_HEADS
PANELS = BLOCK_W // SPAN
SUM_ROWS = SPAN * PANELS + 8
VMEM_BYTES = 50 * 2**20
FULL_VMEM = 63 * 2**20
ATTENTION_VMEM = 44 * 2**20
WHITEN_VMEM = 44 * 2**20
OTHER_VMEM = 44 * 2**20
F32 = jnp.float32
BF16 = jnp.bfloat16
NT = (((1,), (1,)), ((), ()))
TN = (((0,), (0,)), ((), ()))


def params(limit=OTHER_VMEM):
    return pltpu.CompilerParams(vmem_limit_bytes=limit)


def cost(flops, moved, trans=0):
    return pl.CostEstimate(flops=int(flops), bytes_accessed=int(moved), transcendentals=int(trans))


def encode(value, exponent):
    scaled = value * jnp.exp2(15.0 - exponent)
    power = scaled * scaled
    power = power * power
    power = power * power
    return jnp.where(scaled < 0.0, -power, power)


def decode(code, exponent):
    code = code.astype(F32)
    quarter = lax.rsqrt(lax.rsqrt(jnp.maximum(jnp.abs(code), 1e-37)))
    root = quarter * lax.rsqrt(quarter) * jnp.exp2(exponent - 15.0)
    return jnp.where(code < 0.0, -root, root)


def exponent_of(largest):
    return jnp.ceil(jnp.log(jnp.maximum(largest, 1e-30)) * (1.0 / math.log(2.0)) + 0.001)


def write_coded(tiles, out):
    off, pairs = tile_order(tiles.rows, tiles.columns)
    places = off + [(i, i) for i in range(tiles.rows)]
    largest = functools.reduce(jnp.maximum, [jnp.max(jnp.abs(tiles(*p)), axis=(0, 1), keepdims=True) for p in places])
    exponent = exponent_of(largest)
    (line,) = fold(tiles, out, lambda value: encode(value, exponent))
    row = lax.broadcasted_iota(jnp.int32, (16, SPAN), 0)
    out[(len(off) + len(pairs)) * SPAN :] = jnp.where(row < 8, line, exponent).astype(BF16)


def read_coded(ref, columns):
    upper, equal = diagonal_masks()
    off, pairs = tile_order(2, columns)
    at = (len(off) + len(pairs)) * SPAN
    tail = ref[at:].astype(F32)
    exponent = tail[15:16, 0:1]
    tiles = {place: decode(ref[i * SPAN : (i + 1) * SPAN], exponent) for i, place in enumerate(off)}
    square = decode(ref[at - SPAN : at], exponent)
    line = decode(tail[0:1], exponent)
    tiles[0, 0] = jnp.where(upper, square, 0.0)
    tiles[1, 1] = jnp.where(equal, line, jnp.where(upper, square.T, 0.0))
    return tiles


def split(value):
    high = value.astype(BF16)
    return high, (value - high.astype(F32)).astype(BF16)


def cut_kernel(meta, *refs, targets, given):
    outs = refs[-targets:]
    for number, out in enumerate(outs):
        at = 0
        for ref in refs[number * given : (number + 1) * given]:
            out[:, at : at + ref.shape[1]] = ref[...]
            at += ref.shape[1]


def attention_kernel(meta, *refs, chips, spans, all_spans, documents, most, sets):
    sources = 2 * chips
    near = sources + 4
    query_refs, near_refs = refs[:sources], refs[sources:near]
    far_refs = refs[near : near + sets * (sources - 2)]
    top, bottom, queries, keys, values, slots, limits, left, total = refs[near + sets * (sources - 2) :]
    own = meta[0]
    chip, core = own // 2, lax.rem(own, 2)
    lengths = 4
    order = lengths + documents

    for r in range(all_spans):
        device = r // spans
        distance = lax.rem(chip - device // 2 + chips, chips)
        cross = lax.rem(core + device % 2, 2)
        slots[meta[order + r]] = (distance * 2 + cross) * spans + r % spans

    def place_kv(source, key_part, value_part):
        for t in range(spans):
            rows = slice(t * SPAN, (t + 1) * SPAN)
            keys[source * spans + t] = key_part[rows]
            values[source * spans + t] = value_part[rows].astype(F32).T.astype(BF16)

    place_kv(0, near_refs[0], near_refs[1])
    place_kv(1, near_refs[2], near_refs[3])
    for which in range(sets):

        @pl.when(meta[3] == which)
        def _(which=which):
            for source in range(2, sources):
                ref = far_refs[which * (sources - 2) + source - 2]
                place_kv(source, ref[:, :HEAD_SIZE], ref[:, HEAD_SIZE:])

    for source in range(sources):
        for t in range(spans):
            for h in range(BLOCK_HEADS):
                queries[source * spans + t, h * SPAN : (h + 1) * SPAN] = query_refs[source][
                    t * SPAN : (t + 1) * SPAN, h * HEAD_SIZE : (h + 1) * HEAD_SIZE
                ]

    factor = HEAD_SIZE ** (-0.5) / math.log(2.0)

    def place_of(q):
        source = q // spans
        distance, cross = source // 2, lax.rem(source, 2)
        device = lax.rem(chip - distance + chips, chips) * 2 + lax.rem(core + cross, 2)
        position = meta[order + device * spans + lax.rem(q, spans)]
        first_row = position * SPAN
        begin = jnp.int32(0)
        at = jnp.int32(0)
        query_pos = lax.broadcasted_iota(jnp.int32, (1, SPAN), 1) + first_row
        query_begin = jnp.zeros((1, SPAN), jnp.int32)
        for d in range(documents):
            begin = jnp.where(at <= first_row, at, begin)
            query_begin = jnp.where(query_pos >= at, at, query_begin)
            at = at + meta[lengths + d]
        return position, query_pos, query_begin, position - begin // SPAN + 1

    def one_pair(p, carry):
        pair = [(which, 2 * p + which, place_of(2 * p + which)) for which in range(2)]
        count = jnp.maximum(pair[0][2][3], pair[1][2][3])

        for n in range(1, most + 1):

            @pl.when(count == n)
            def _(n=n):
                for which, q, (position, query_pos, query_begin, _) in pair:
                    lanes = pl.ds(pl.multiple_of(q * SPAN, SPAN), SPAN)
                    held = [slots[jnp.maximum(position - n + 1 + i, 0)] for i in range(n)]
                    for i in range(n):
                        key_pos = lax.broadcasted_iota(jnp.int32, (SPAN, SPAN), 0) + (position - n + 1 + i) * SPAN
                        seen = (key_pos <= query_pos) & (key_pos >= query_begin)
                        limits[which, i * SPAN : (i + 1) * SPAN] = jnp.where(seen, 3e38, -1e30)
                    key_part = jnp.concatenate([keys[slot] for slot in held], axis=0)
                    value_part = jnp.concatenate([values[slot] for slot in held], axis=1)
                    scores = lax.dot_general(key_part, queries[q], NT, preferred_element_type=F32)
                    limit = limits[which, : n * SPAN]
                    scores = jnp.minimum(scores, jnp.concatenate([limit] * BLOCK_HEADS, axis=1))
                    largest = jnp.max(scores, axis=0, keepdims=True)
                    lifted = jnp.exp2((scores - largest) * factor)
                    summed = jnp.sum(lifted, axis=0, keepdims=True)
                    weights = (lifted * (1.0 / summed)).astype(BF16)
                    mixed = jnp.dot(value_part, weights, preferred_element_type=F32)
                    for h in range(BLOCK_HEADS):
                        one_head = mixed[:, h * SPAN : (h + 1) * SPAN]
                        columns = slice(h * HEAD_SIZE, (h + 1) * HEAD_SIZE)
                        high, low = split(one_head)
                        left[0, columns, lanes] = high
                        left[1, columns, lanes] = low

        return carry

    lax.fori_loop(0, all_spans // 2, one_pair, 0)

    half = BLOCK_W // 2
    total[...] = jnp.zeros_like(total)

    def one_pass(i, carry):
        a, b = lax.rem(i, 2), i // 2
        total[:half] += lax.dot_general(left[a, :half], left[b], NT, preferred_element_type=F32)
        total[half:, half:] += lax.dot_general(left[a, half:], left[b, half:], NT, preferred_element_type=F32)
        return carry

    lax.fori_loop(0, 3, one_pass, 0)
    for out, where in zip((top, bottom), sum_tiles()):
        off, pair = where
        (line,) = fold(Tiles(total, PANELS, PANELS, False), out, where=(off, [pair]))
        out[SUM_ROWS - 8 :] = jnp.broadcast_to(line, (8, SPAN))


def diagonal_masks():
    rows = lax.broadcasted_iota(jnp.int32, (SPAN, SPAN), 0)
    columns = lax.broadcasted_iota(jnp.int32, (SPAN, SPAN), 1)
    return rows <= columns, rows == columns


def tile_order(rows, columns):
    off = [(i, j) for i in range(rows) for j in range(i + 1, columns)]
    return off, [(i, i + 1) for i in range(0, rows, 2)]


def sum_tiles():
    off, pairs = tile_order(PANELS, PANELS)
    half = len(off) // 2
    return [(off[:half], pairs[0]), (off[half:], pairs[1])]


def fold(tiles, out, change=lambda value: value, where=None):
    upper, equal = diagonal_masks()
    off, pairs = tile_order(tiles.rows, tiles.columns) if where is None else where
    for i, place in enumerate(off):
        out[i * SPAN : (i + 1) * SPAN] = change(tiles(*place)).astype(out.dtype)
    lines = []
    for i, (a, b) in enumerate(pairs):
        second = tiles(b, b)
        at = (len(off) + i) * SPAN
        lower = second.T if tiles.turn else second
        out[at : at + SPAN] = change(jnp.where(upper, tiles(a, a), lower)).astype(out.dtype)
        lines.append(change(jnp.sum(jnp.where(equal, second, 0.0), axis=0, keepdims=True)))
    return lines


class Tiles:
    def __init__(self, ref, rows, columns, turn):
        self.ref, self.rows, self.columns, self.turn = ref, rows, columns, turn

    def __call__(self, i, j):
        return self.ref[i * SPAN : (i + 1) * SPAN, j * SPAN : (j + 1) * SPAN]


def unfold(halves, work):
    upper, equal = diagonal_masks()
    trace = jnp.zeros((1, 1), F32)
    squares = []
    for total, (off, (a, b)) in zip(halves, sum_tiles()):
        for i, (row, column) in enumerate(off):
            work[row * SPAN : (row + 1) * SPAN, column * SPAN : (column + 1) * SPAN] = total[i * SPAN : (i + 1) * SPAN]
        at = len(off) * SPAN
        square = total[at : at + SPAN]
        turned = square.T
        line = jnp.broadcast_to(total[at + SPAN : at + SPAN + 1], (SPAN, SPAN))
        squares.append((a, jnp.where(upper, square, turned)))
        squares.append((b, jnp.where(equal, line, jnp.where(upper, turned, square))))
    for _, square in squares:
        trace = trace + jnp.sum(jnp.where(equal, square, 0.0), axis=(0, 1), keepdims=True)
    damping = trace * (0.1 / BLOCK_W)
    for a, square in squares:
        work[a * SPAN : (a + 1) * SPAN, a * SPAN : (a + 1) * SPAN] = jnp.where(equal, square + damping, square)


def factor_kernel(*refs, start, stop, received):
    width = BLOCK_W - start
    panels = width // SPAN
    step = 32
    groups = step // 8
    per_tile = SPAN // step
    last = stop == BLOCK_W
    given, refs = (refs[:received], refs[received:])
    out, refs = refs[0], refs[1:]
    if not last:
        rest, refs = refs[0], refs[1:]
    work, previous, upper = refs
    if start == 0:
        work[...] = jnp.zeros_like(work)
        halves = [ref[...] for ref in given[:2]]
        if received == 4:
            halves = [mine + ref[...] for mine, ref in zip(halves, given[2:])]
        unfold(halves, work)
    else:
        work[...] = given[0][...]
    previous[...] = jnp.zeros_like(previous)

    def triple(value, first):
        high, low = split(value)
        return jnp.concatenate((high, low, high) if first else (high, high, low), axis=0)

    def superpanel(g, carry):
        row = pl.multiple_of(g * step, step)
        tile_index = g // per_tile
        tile = pl.ds(pl.multiple_of(tile_index * SPAN, SPAN), SPAN)
        turn = lax.rem(SPAN - lax.rem(g, per_tile) * step, SPAN)
        before = previous[...]
        right = triple(before, False)
        near = pltpu.roll(previous[:, tile], turn, 1)
        fresh = lax.dot_general(triple(near, True), right, TN, preferred_element_type=F32)[:step]
        current = work[pl.ds(row, step), :] - fresh
        work[...] = work[...] - lax.dot_general(triple(before, True), right, TN, preferred_element_type=F32)

        square = current[:, :SPAN]
        for k in range(1, panels):
            square = jnp.where(tile_index == k, current[:, k * SPAN : (k + 1) * SPAN], square)
        square = pltpu.roll(square, turn, 1)
        line = lax.broadcasted_iota(jnp.int32, (8, SPAN), 0)
        held = [
            {q: jnp.broadcast_to(square[8 * q : 8 * q + 8, j : j + 1], (8, SPAN)) for q in range(j // 8, groups)}
            for j in range(step)
        ]
        body = [[current[8 * q : 8 * q + 8, k * SPAN : (k + 1) * SPAN] for k in range(panels)] for q in range(groups)]
        scales = [jnp.zeros((8, SPAN), F32) for _ in range(groups)]

        def spread(value, i):
            return jnp.broadcast_to(value[i % 8 : i % 8 + 1], (8, SPAN))

        for i in range(step):
            at = i // 8
            root = lax.rsqrt(spread(held[i][at], i))
            inverse = root * root
            scales[at] = jnp.where(line == i % 8, root, scales[at])
            ratio = {q: held[i][q] * inverse for q in range(at, groups)}
            ratio[at] = jnp.where(line > i % 8, ratio[at], 0.0)
            for j in range(i + 1, step):
                entry = spread(held[i][j // 8], j)
                for q in range(j // 8, groups):
                    held[j][q] = held[j][q] - ratio[q] * entry
            for k in range(panels):
                pivot_row = spread(body[at][k], i)
                for q in range(at, groups):
                    body[q][k] = body[q][k] - ratio[q] * pivot_row
        result = jnp.concatenate(
            [jnp.concatenate([body[q][k] * scales[q] for k in range(panels)], axis=1) for q in range(groups)], axis=0
        )
        across = lax.broadcasted_iota(jnp.int32, (step, width), 1)
        down = lax.broadcasted_iota(jnp.int32, (step, width), 0)
        result = jnp.where(across >= down + row, result, 0.0)
        previous[...] = result
        upper[pl.ds(row, step), :] = result
        return carry

    lax.fori_loop(0, (stop - start) // step, superpanel, 0)
    if not last:
        done = stop - start
        before = previous[...]
        final = lax.dot_general(
            triple(before[:, done:], True), triple(before[:, done:], False), TN, preferred_element_type=F32
        )
        rest[...] = work[done:, done:] - final
    write_coded(Tiles(upper, (stop - start) // SPAN, panels, True), out)


def whiten_kernel(order, *refs, blocks, given, starts, first, chunks, aliased):
    count = len(starts)
    u_refs, refs = refs[:given], refs[given:]
    w_refs, refs = refs[:chunks], refs[chunks + aliased :]
    lowest = starts[0]
    out, left, ready, sems = refs
    half = BLOCK_W // 2
    chunk = ready.shape[2] // chunks
    step = pl.program_id(0)

    def copy(number, which, c):
        slot = lax.rem(number * count + which, 2)
        columns = pl.ds(c * chunk, chunk)
        return pltpu.make_async_copy(
            ready.at[slot, :, columns],
            out.at[order[first + number], pl.ds(starts[which], half), columns],
            sems.at[slot, c],
        )

    for which, start in enumerate(starts):
        width = BLOCK_W - start
        for b in range(given // count):

            @pl.when((step == b) | (given < blocks * count))
            def _(b=b):
                tiles = read_coded(u_refs[b * count + which], width // SPAN)
                for row in range(half // SPAN):
                    rows = slice(row * SPAN, (row + 1) * SPAN)
                    for column in range(width // SPAN):
                        value = tiles[row, column] if column >= row else jnp.zeros((SPAN, SPAN), F32)
                        high, low = split(value)
                        columns = slice(column * SPAN, (column + 1) * SPAN)
                        left[rows, columns] = high
                        left[half + row * SPAN : half + (row + 1) * SPAN, columns] = low

        for c in range(chunks):
            if count == 1:

                @pl.when(step >= 2)
                def _(c=c):
                    copy(step - 2, which, c).wait()

            elif blocks > 1:

                @pl.when(step >= 1)
                def _(c=c):
                    copy(step - 1, which, c).wait()

            weight = w_refs[c][:, start - lowest :]
            product = lax.dot_general(left[:, :width], weight, NT, preferred_element_type=F32)
            ready[lax.rem(step * count + which, 2), :, c * chunk : (c + 1) * chunk] = product[:half] + product[half:]
            copy(step, which, c).start()

    @pl.when(step == blocks - 1)
    def _():
        for c in range(chunks):
            if count > 1:
                copy(step, 0, c).wait()
            elif blocks > 1:
                copy(step - 1, 0, c).wait()
            copy(step, count - 1, c).wait()


def shards(query_rows, key_rows, placed_value_rows, doc_lengths, span_order, out_weight):
    tokens = query_rows.shape[1]
    features = out_weight.shape[0]
    seq = lax.axis_size("seq")
    ring = lax.axis_size("dp")
    chips = seq // 2
    spans = tokens // SPAN
    all_spans = spans * seq
    documents = doc_lengths.shape[1]
    per = KEY_VALUE_HEADS // seq
    blocks = NB // seq
    own = lax.axis_index("seq").astype(jnp.int32)
    place = lax.axis_index("dp").astype(jnp.int32)
    query, key, value = query_rows[0], key_rows[0], placed_value_rows[0]
    vmem = pl.BlockSpec(memory_space=pltpu.VMEM)
    anywhere = pl.BlockSpec(memory_space=pl.ANY)
    in_ring = blocks == ring

    if in_ring:
        turns = [lax.rem(place + 2 * ring - 1 - t, ring) for t in range(blocks)]
    else:
        turns = [jnp.int32(t) for t in range(blocks)]
    first_kv = turns[0] // KV_BLOCKS

    def moved(distance, cross):
        return [
            (x * 2 + c, (x + distance) % chips * 2 + (1 - c if cross else c)) for x in range(chips) for c in range(2)
        ]

    def cut(targets, columns, scalars, name, after=(), limit=OTHER_VMEM):
        specs, arrays = [], []
        for target in targets:
            for array, size, index in columns:
                specs.append(
                    pl.BlockSpec((tokens, size), lambda i, meta, target=target, index=index: (0, index(target(meta), meta)))
                )
                arrays.append(array)
        width = sum(size for _, size, _ in columns)
        return pl.pallas_call(
            functools.partial(cut_kernel, targets=len(targets), given=len(columns)),
            out_shape=[jax.ShapeDtypeStruct((tokens, width), BF16)] * len(targets),
            grid_spec=pltpu.PrefetchScalarGridSpec(
                num_scalar_prefetch=1,
                grid=(1,),
                in_specs=specs + [anywhere] * len(after),
                out_specs=[pl.BlockSpec((tokens, width), lambda i, meta: (0, 0))] * len(targets),
            ),
            compiler_params=params(limit),
            cost_estimate=cost(0, 2**21),
            name=name,
        )(scalars, *arrays, *after)

    tile = 512

    def target_at(distance, cross):
        return lambda meta: lax.rem(meta[0] // 2 + distance, chips) * 2 + lax.rem(lax.rem(meta[0], 2) + cross, 2)

    far = [(distance, cross) for distance in range(1, chips) for cross in range(2)]
    pieces = []

    most = all_spans // 2 + 1

    def grams_of(t):
        kv = turns[t] // KV_BLOCKS
        carriers = pieces[: min(t + 1, per)]
        which = jnp.where(kv == first_kv, 0, 1).astype(jnp.int32)
        meta = jnp.concatenate([jnp.stack([own, turns[t], kv, which]), doc_lengths[0], span_order[0]])
        folded = jax.ShapeDtypeStruct((SUM_ROWS, SPAN), F32)
        return pl.pallas_call(
            functools.partial(
                attention_kernel,
                chips=chips, spans=spans, all_spans=all_spans, documents=documents, most=most, sets=len(carriers),
            ),
            out_shape=[folded] * 2,
            grid_spec=pltpu.PrefetchScalarGridSpec(
                num_scalar_prefetch=1,
                grid=(1,),
                in_specs=[
                    pl.BlockSpec((tokens, BLOCK_W), lambda i, meta: (0, meta[0] * blocks + meta[1])),
                    pl.BlockSpec((tokens, BLOCK_W), lambda i, meta: (0, meta[0] * blocks + meta[1])),
                ]
                + [pl.BlockSpec((tokens, BLOCK_W), lambda i, meta: (0, 0))] * len(far)
                + [pl.BlockSpec((tokens, HEAD_SIZE), lambda i, meta: (0, meta[0] * per + meta[2]))] * 4
                + [pl.BlockSpec((tokens, 2 * HEAD_SIZE), lambda i, meta: (0, BLOCK_W // (2 * HEAD_SIZE)))]
                * (len(carriers) * len(far)),
                out_specs=[pl.BlockSpec((SUM_ROWS, SPAN), lambda i, meta: (0, 0))] * 2,
                scratch_shapes=[
                    pltpu.VMEM((all_spans, BLOCK_HEADS * SPAN, HEAD_SIZE), BF16),
                    pltpu.VMEM((all_spans, SPAN, HEAD_SIZE), BF16),
                    pltpu.VMEM((all_spans, HEAD_SIZE, SPAN), BF16),
                    pltpu.SMEM((all_spans,), jnp.int32),
                    pltpu.VMEM((2, most * SPAN, SPAN), F32),
                    pltpu.VMEM((2, BLOCK_W, all_spans * SPAN), BF16),
                    pltpu.VMEM((BLOCK_W, BLOCK_W), F32),
                ],
            ),
            compiler_params=params(ATTENTION_VMEM),
            cost_estimate=cost(1.4e10, 2**20),
            name="attention_outer_products",
        )(meta, query, peer[0], *pieces[t], key, value, *peer[1:], *[a for carrier in carriers for a in carrier])

    grams = []
    held = []
    peer = [lax.ppermute(array, "seq", moved(0, 1)) for array in (query, key, value)]
    for t in range(blocks + 1):
        if t < blocks:
            kv = first_kv if t == 0 else per - 1 - first_kv
            columns = [(query, BLOCK_W, lambda target, meta: target * blocks + meta[1])]
            if t < per:
                columns += [(array, HEAD_SIZE, lambda target, meta: target * per + meta[2]) for array in (key, value)]
            scalars = jnp.stack([own, turns[t], kv])
            after = [] if t == 0 else peer[1:2]
            parts = cut(
                [target_at(*where) for where in far], columns, scalars, "cut_piece", after,
                OTHER_VMEM if t else FULL_VMEM,
            )
            if t > 1:
                *parts, held[t - 2] = lax.optimization_barrier((*parts, held[t - 2]))
            pieces.append([lax.ppermute(part, "seq", moved(*where)) for part, where in zip(parts, far)])
        if t == 0:
            continue
        done = t - 1
        grams.append(grams_of(done))
        if done == 0 or not in_ring:
            held.append(grams[done])
        else:
            held.append([mine + theirs for mine, theirs in zip(grams[done], carried)] if done < ring - 1 else None)
        if in_ring and done < ring - 1:
            carried = [lax.ppermute(part, "dp", [(z, (z + 1) % ring) for z in range(ring)]) for part in held[done]]

    half = BLOCK_W // 2
    top_rows, bottom_rows = [
        SPAN * (sum(len(part) for part in tile_order(2, columns))) + 16 for columns in (PANELS, PANELS // 2)
    ]
    scratch = lambda width: [pltpu.VMEM((width, width), F32), pltpu.VMEM((32, width), F32), pltpu.VMEM((half, width), F32)]

    def factor_top(*given):
        return pl.pallas_call(
            functools.partial(factor_kernel, start=0, stop=half, received=len(given)),
            out_shape=[
                jax.ShapeDtypeStruct((top_rows, SPAN), BF16),
                jax.ShapeDtypeStruct((half, half), F32),
            ],
            in_specs=[vmem] * len(given),
            out_specs=[vmem] * 2,
            scratch_shapes=scratch(BLOCK_W),
            compiler_params=params(OTHER_VMEM),
            cost_estimate=cost(1.0e10, 2**20),
            name="factor_top",
        )(*given)

    def factor_bottom(rest):
        return pl.pallas_call(
            functools.partial(factor_kernel, start=half, stop=BLOCK_W, received=1),
            out_shape=jax.ShapeDtypeStruct((bottom_rows, SPAN), BF16),
            in_specs=[vmem],
            out_specs=vmem,
            scratch_shapes=scratch(half),
            compiler_params=params(OTHER_VMEM),
            cost_estimate=cost(0.9e10, 2**20),
            name="factor_bottom",
        )(rest)

    if in_ring:
        top, rest = factor_top(*grams[ring - 1], *carried)

        def shared(array):
            return [array] + [
                lax.ppermute(array, "dp", [(z, (z + d) % ring) for z in range(ring)]) for d in range(1, ring)
            ]

        tops = shared(top)
        bottom = factor_bottom(rest)
        bottoms = lax.all_gather(bottom, "dp", axis=0, tiled=True)
        order = jnp.stack([lax.rem(place - d + ring, ring) for d in range(ring)])
    else:
        halves = [factor_top(*[lax.psum(part, "dp") for part in grams[t]]) for t in range(blocks)]
        tops = [top for top, _ in halves]
        bottoms = jnp.concatenate([factor_bottom(rest) for _, rest in halves], axis=0)
        bottom = bottoms[:bottom_rows]
        order = jnp.arange(blocks, dtype=jnp.int32)


    def whiten(uppers, first, starts, result, gathered=0):
        more = [] if result is None else [result]
        depth = BLOCK_W - starts[0]
        chunks = features // tile
        triangles = [vmem] * len(uppers)
        if gathered:
            triangles = [pl.BlockSpec((bottom_rows, SPAN), lambda b, order: (order[first + b], 0))]
        weights = [
            pl.BlockSpec(
                (tile, depth),
                lambda b, order, c=c: (c, order[first + b] * (BLOCK_W // depth) + starts[0] // depth),
            )
            for c in range(chunks)
        ]
        count = gathered or len(uppers) // len(starts)
        return pl.pallas_call(
            functools.partial(
                whiten_kernel, blocks=count, given=len(uppers), starts=starts, first=first, chunks=chunks, aliased=len(more)
            ),
            out_shape=jax.ShapeDtypeStruct((blocks, BLOCK_W, features), F32),
            grid_spec=pltpu.PrefetchScalarGridSpec(
                num_scalar_prefetch=1,
                grid=(count,),
                in_specs=triangles + weights + [anywhere] * len(more),
                out_specs=anywhere,
                scratch_shapes=[
                    pltpu.VMEM((2 * half, depth), BF16),
                    pltpu.VMEM((2, half, features), F32),
                    pltpu.SemaphoreType.DMA((2, chunks)),
                ],
            ),
            input_output_aliases={1 + len(uppers) + chunks: 0} if more else {},
            compiler_params=params(WHITEN_VMEM),
            cost_estimate=cost(2.0e9 * len(uppers), 2**20),
            name="whiten_bottom" if starts[0] else "whiten_top",
        )(order, *uppers, *[out_weight] * chunks, *more)

    result = whiten([tops[0], bottom], 0, (0, half), None)
    result = whiten(tops[1:2], 1, (0,), result)
    if blocks > 2:
        result = whiten(tops[2:], 2, (0,), result)
    return whiten([bottoms], 1, (half,), result, blocks - 1)


def solution(mesh):
    in_specs = (
        P(("groups", "dp"), "seq", None),
        P(("groups", "dp"), "seq", None),
        P(("groups", "dp"), "seq", None),
        P(("groups", "dp"), None),
        P(("groups", "dp"), None),
        P("dp", "seq"),
    )
    out_specs = P(("groups", "seq"), None, "dp")
    return jax.shard_map(shards, mesh=mesh, in_specs=in_specs, out_specs=out_specs, check_vma=False)
```

```python
import functools
import math

import jax
import jax.numpy as jnp
from jax import lax
from jax.experimental import pallas as pl
from jax.experimental.pallas import tpu as pltpu
from jax.sharding import PartitionSpec as P

QUERY_HEADS = 64
KEY_VALUE_HEADS = 8
HEAD_SIZE = 128
BLOCK_W = 512
NB = 16
SPAN = 128
GROUP = QUERY_HEADS // KEY_VALUE_HEADS
BLOCK_HEADS = BLOCK_W // HEAD_SIZE
KV_BLOCKS = GROUP // BLOCK_HEADS
PANELS = BLOCK_W // SPAN
SUM_ROWS = SPAN * PANELS + 8
VMEM_BYTES = 50 * 2**20
FULL_VMEM = 63 * 2**20
ATTENTION_VMEM = 44 * 2**20
WHITEN_VMEM = 44 * 2**20
OTHER_VMEM = 44 * 2**20
F32 = jnp.float32
BF16 = jnp.bfloat16
NT = (((1,), (1,)), ((), ()))
TN = (((0,), (0,)), ((), ()))


def params(limit=OTHER_VMEM):
    return pltpu.CompilerParams(vmem_limit_bytes=limit)


def cost(flops, moved, trans=0):
    return pl.CostEstimate(flops=int(flops), bytes_accessed=int(moved), transcendentals=int(trans))


def encode(value, exponent):
    scaled = value * jnp.exp2(15.0 - exponent)
    power = scaled * scaled
    power = power * power
    power = power * power
    return jnp.where(scaled < 0.0, -power, power)


def decode(code, exponent):
    code = code.astype(F32)
    quarter = lax.rsqrt(lax.rsqrt(jnp.maximum(jnp.abs(code), 1e-37)))
    root = quarter * lax.rsqrt(quarter) * jnp.exp2(exponent - 15.0)
    return jnp.where(code < 0.0, -root, root)


def exponent_of(largest):
    return jnp.ceil(jnp.log(jnp.maximum(largest, 1e-30)) * (1.0 / math.log(2.0)) + 0.001)


def write_coded(tiles, out):
    off, pairs = tile_order(tiles.rows, tiles.columns)
    places = off + [(i, i) for i in range(tiles.rows)]
    largest = functools.reduce(jnp.maximum, [jnp.max(jnp.abs(tiles(*p)), axis=(0, 1), keepdims=True) for p in places])
    exponent = exponent_of(largest)
    (line,) = fold(tiles, out, lambda value: encode(value, exponent))
    row = lax.broadcasted_iota(jnp.int32, (16, SPAN), 0)
    out[(len(off) + len(pairs)) * SPAN :] = jnp.where(row < 8, line, exponent).astype(BF16)


def read_coded(ref, columns):
    upper, equal = diagonal_masks()
    off, pairs = tile_order(2, columns)
    at = (len(off) + len(pairs)) * SPAN
    tail = ref[at:].astype(F32)
    exponent = tail[15:16, 0:1]
    tiles = {place: decode(ref[i * SPAN : (i + 1) * SPAN], exponent) for i, place in enumerate(off)}
    square = decode(ref[at - SPAN : at], exponent)
    line = decode(tail[0:1], exponent)
    tiles[0, 0] = jnp.where(upper, square, 0.0)
    tiles[1, 1] = jnp.where(equal, line, jnp.where(upper, square.T, 0.0))
    return tiles


def split(value):
    high = value.astype(BF16)
    return high, (value - high.astype(F32)).astype(BF16)


def cut_kernel(meta, *refs, targets, given):
    outs = refs[-targets:]
    for number, out in enumerate(outs):
        at = 0
        for ref in refs[number * given : (number + 1) * given]:
            out[:, at : at + ref.shape[1]] = ref[...]
            at += ref.shape[1]


def attention_kernel(meta, *refs, chips, spans, all_spans, documents, most, sets):
    sources = 2 * chips
    near = sources + 4
    query_refs, near_refs = refs[:sources], refs[sources:near]
    far_refs = refs[near : near + sets * (sources - 2)]
    top, bottom, queries, keys, values, slots, limits, left, total = refs[near + sets * (sources - 2) :]
    own = meta[0]
    chip, core = own // 2, lax.rem(own, 2)
    lengths = 4
    order = lengths + documents

    for r in range(all_spans):
        device = r // spans
        distance = lax.rem(chip - device // 2 + chips, chips)
        cross = lax.rem(core + device % 2, 2)
        slots[meta[order + r]] = (distance * 2 + cross) * spans + r % spans

    def place_kv(source, key_part, value_part):
        for t in range(spans):
            rows = slice(t * SPAN, (t + 1) * SPAN)
            keys[source * spans + t] = key_part[rows]
            values[source * spans + t] = value_part[rows].astype(F32).T.astype(BF16)

    place_kv(0, near_refs[0], near_refs[1])
    place_kv(1, near_refs[2], near_refs[3])
    for which in range(sets):

        @pl.when(meta[3] == which)
        def _(which=which):
            for source in range(2, sources):
                ref = far_refs[which * (sources - 2) + source - 2]
                place_kv(source, ref[:, :HEAD_SIZE], ref[:, HEAD_SIZE:])

    for source in range(sources):
        for t in range(spans):
            for h in range(BLOCK_HEADS):
                queries[source * spans + t, h * SPAN : (h + 1) * SPAN] = query_refs[source][
                    t * SPAN : (t + 1) * SPAN, h * HEAD_SIZE : (h + 1) * HEAD_SIZE
                ]

    factor = HEAD_SIZE ** (-0.5) / math.log(2.0)

    def place_of(q):
        source = q // spans
        distance, cross = source // 2, lax.rem(source, 2)
        device = lax.rem(chip - distance + chips, chips) * 2 + lax.rem(core + cross, 2)
        position = meta[order + device * spans + lax.rem(q, spans)]
        first_row = position * SPAN
        begin = jnp.int32(0)
        at = jnp.int32(0)
        query_pos = lax.broadcasted_iota(jnp.int32, (1, SPAN), 1) + first_row
        query_begin = jnp.zeros((1, SPAN), jnp.int32)
        for d in range(documents):
            begin = jnp.where(at <= first_row, at, begin)
            query_begin = jnp.where(query_pos >= at, at, query_begin)
            at = at + meta[lengths + d]
        return position, query_pos, query_begin, position - begin // SPAN + 1

    def one_pair(p, carry):
        pair = [(which, 2 * p + which, place_of(2 * p + which)) for which in range(2)]
        count = jnp.maximum(pair[0][2][3], pair[1][2][3])

        for n in range(1, most + 1):

            @pl.when(count == n)
            def _(n=n):
                for which, q, (position, query_pos, query_begin, _) in pair:
                    lanes = pl.ds(pl.multiple_of(q * SPAN, SPAN), SPAN)
                    held = [slots[jnp.maximum(position - n + 1 + i, 0)] for i in range(n)]
                    for i in range(n):
                        key_pos = lax.broadcasted_iota(jnp.int32, (SPAN, SPAN), 0) + (position - n + 1 + i) * SPAN
                        seen = (key_pos <= query_pos) & (key_pos >= query_begin)
                        limits[which, i * SPAN : (i + 1) * SPAN] = jnp.where(seen, 3e38, -1e30)
                    key_part = jnp.concatenate([keys[slot] for slot in held], axis=0)
                    value_part = jnp.concatenate([values[slot] for slot in held], axis=1)
                    scores = lax.dot_general(key_part, queries[q], NT, preferred_element_type=F32)
                    limit = limits[which, : n * SPAN]
                    scores = jnp.minimum(scores, jnp.concatenate([limit] * BLOCK_HEADS, axis=1))
                    largest = jnp.max(scores, axis=0, keepdims=True)
                    lifted = jnp.exp2((scores - largest) * factor)
                    summed = jnp.sum(lifted, axis=0, keepdims=True)
                    weights = (lifted * (1.0 / summed)).astype(BF16)
                    mixed = jnp.dot(value_part, weights, preferred_element_type=F32)
                    for h in range(BLOCK_HEADS):
                        one_head = mixed[:, h * SPAN : (h + 1) * SPAN]
                        columns = slice(h * HEAD_SIZE, (h + 1) * HEAD_SIZE)
                        high, low = split(one_head)
                        left[0, columns, lanes] = high
                        left[1, columns, lanes] = low

        return carry

    lax.fori_loop(0, all_spans // 2, one_pair, 0)

    half = BLOCK_W // 2
    total[...] = jnp.zeros_like(total)

    def one_pass(i, carry):
        a, b = lax.rem(i, 2), i // 2
        total[:half] += lax.dot_general(left[a, :half], left[b], NT, preferred_element_type=F32)
        total[half:, half:] += lax.dot_general(left[a, half:], left[b, half:], NT, preferred_element_type=F32)
        return carry

    lax.fori_loop(0, 3, one_pass, 0)
    for out, where in zip((top, bottom), sum_tiles()):
        off, pair = where
        (line,) = fold(Tiles(total, PANELS, PANELS, False), out, where=(off, [pair]))
        out[SUM_ROWS - 8 :] = jnp.broadcast_to(line, (8, SPAN))


def diagonal_masks():
    rows = lax.broadcasted_iota(jnp.int32, (SPAN, SPAN), 0)
    columns = lax.broadcasted_iota(jnp.int32, (SPAN, SPAN), 1)
    return rows <= columns, rows == columns


def tile_order(rows, columns):
    off = [(i, j) for i in range(rows) for j in range(i + 1, columns)]
    return off, [(i, i + 1) for i in range(0, rows, 2)]


def sum_tiles():
    off, pairs = tile_order(PANELS, PANELS)
    half = len(off) // 2
    return [(off[:half], pairs[0]), (off[half:], pairs[1])]


def fold(tiles, out, change=lambda value: value, where=None):
    upper, equal = diagonal_masks()
    off, pairs = tile_order(tiles.rows, tiles.columns) if where is None else where
    for i, place in enumerate(off):
        out[i * SPAN : (i + 1) * SPAN] = change(tiles(*place)).astype(out.dtype)
    lines = []
    for i, (a, b) in enumerate(pairs):
        second = tiles(b, b)
        at = (len(off) + i) * SPAN
        lower = second.T if tiles.turn else second
        out[at : at + SPAN] = change(jnp.where(upper, tiles(a, a), lower)).astype(out.dtype)
        lines.append(change(jnp.sum(jnp.where(equal, second, 0.0), axis=0, keepdims=True)))
    return lines


class Tiles:
    def __init__(self, ref, rows, columns, turn):
        self.ref, self.rows, self.columns, self.turn = ref, rows, columns, turn

    def __call__(self, i, j):
        return self.ref[i * SPAN : (i + 1) * SPAN, j * SPAN : (j + 1) * SPAN]


def unfold(halves, work):
    upper, equal = diagonal_masks()
    trace = jnp.zeros((1, 1), F32)
    squares = []
    for total, (off, (a, b)) in zip(halves, sum_tiles()):
        for i, (row, column) in enumerate(off):
            work[row * SPAN : (row + 1) * SPAN, column * SPAN : (column + 1) * SPAN] = total[i * SPAN : (i + 1) * SPAN]
        at = len(off) * SPAN
        square = total[at : at + SPAN]
        turned = square.T
        line = jnp.broadcast_to(total[at + SPAN : at + SPAN + 1], (SPAN, SPAN))
        squares.append((a, jnp.where(upper, square, turned)))
        squares.append((b, jnp.where(equal, line, jnp.where(upper, turned, square))))
    for _, square in squares:
        trace = trace + jnp.sum(jnp.where(equal, square, 0.0), axis=(0, 1), keepdims=True)
    damping = trace * (0.1 / BLOCK_W)
    for a, square in squares:
        work[a * SPAN : (a + 1) * SPAN, a * SPAN : (a + 1) * SPAN] = jnp.where(equal, square + damping, square)


def factor_kernel(*refs, start, stop, received):
    width = BLOCK_W - start
    panels = width // SPAN
    step = 32
    groups = step // 8
    per_tile = SPAN // step
    last = stop == BLOCK_W
    given, refs = (refs[:received], refs[received:])
    out, refs = refs[0], refs[1:]
    if not last:
        rest, refs = refs[0], refs[1:]
    work, previous, upper = refs
    if start == 0:
        work[...] = jnp.zeros_like(work)
        halves = [ref[...] for ref in given[:2]]
        if received == 4:
            halves = [mine + ref[...] for mine, ref in zip(halves, given[2:])]
        unfold(halves, work)
    else:
        work[...] = given[0][...]
    previous[...] = jnp.zeros_like(previous)

    def triple(value, first):
        high, low = split(value)
        return jnp.concatenate((high, low, high) if first else (high, high, low), axis=0)

    def superpanel(g, carry):
        row = pl.multiple_of(g * step, step)
        tile_index = g // per_tile
        tile = pl.ds(pl.multiple_of(tile_index * SPAN, SPAN), SPAN)
        turn = lax.rem(SPAN - lax.rem(g, per_tile) * step, SPAN)
        before = previous[...]
        right = triple(before, False)
        near = pltpu.roll(previous[:, tile], turn, 1)
        fresh = lax.dot_general(triple(near, True), right, TN, preferred_element_type=F32)[:step]
        current = work[pl.ds(row, step), :] - fresh
        work[...] = work[...] - lax.dot_general(triple(before, True), right, TN, preferred_element_type=F32)

        square = current[:, :SPAN]
        for k in range(1, panels):
            square = jnp.where(tile_index == k, current[:, k * SPAN : (k + 1) * SPAN], square)
        square = pltpu.roll(square, turn, 1)
        line = lax.broadcasted_iota(jnp.int32, (8, SPAN), 0)
        held = [
            {q: jnp.broadcast_to(square[8 * q : 8 * q + 8, j : j + 1], (8, SPAN)) for q in range(j // 8, groups)}
            for j in range(step)
        ]
        body = [[current[8 * q : 8 * q + 8, k * SPAN : (k + 1) * SPAN] for k in range(panels)] for q in range(groups)]
        scales = [jnp.zeros((8, SPAN), F32) for _ in range(groups)]

        def spread(value, i):
            return jnp.broadcast_to(value[i % 8 : i % 8 + 1], (8, SPAN))

        for i in range(step):
            at = i // 8
            root = lax.rsqrt(spread(held[i][at], i))
            inverse = root * root
            scales[at] = jnp.where(line == i % 8, root, scales[at])
            ratio = {q: held[i][q] * inverse for q in range(at, groups)}
            ratio[at] = jnp.where(line > i % 8, ratio[at], 0.0)
            for j in range(i + 1, step):
                entry = spread(held[i][j // 8], j)
                for q in range(j // 8, groups):
                    held[j][q] = held[j][q] - ratio[q] * entry
            for k in range(panels):
                pivot_row = spread(body[at][k], i)
                for q in range(at, groups):
                    body[q][k] = body[q][k] - ratio[q] * pivot_row
        result = jnp.concatenate(
            [jnp.concatenate([body[q][k] * scales[q] for k in range(panels)], axis=1) for q in range(groups)], axis=0
        )
        across = lax.broadcasted_iota(jnp.int32, (step, width), 1)
        down = lax.broadcasted_iota(jnp.int32, (step, width), 0)
        result = jnp.where(across >= down + row, result, 0.0)
        previous[...] = result
        upper[pl.ds(row, step), :] = result
        return carry

    lax.fori_loop(0, (stop - start) // step, superpanel, 0)
    if not last:
        done = stop - start
        before = previous[...]
        final = lax.dot_general(
            triple(before[:, done:], True), triple(before[:, done:], False), TN, preferred_element_type=F32
        )
        rest[...] = work[done:, done:] - final
    write_coded(Tiles(upper, (stop - start) // SPAN, panels, True), out)


def whiten_kernel(order, *refs, blocks, starts, first, chunks, aliased):
    count = len(starts)
    u_refs, refs = refs[: blocks * count], refs[blocks * count :]
    w_refs, refs = refs[:chunks], refs[chunks + aliased :]
    lowest = starts[0]
    out, left, ready, sems = refs
    half = BLOCK_W // 2
    chunk = ready.shape[2] // chunks
    step = pl.program_id(0)

    def copy(number, which, c):
        slot = lax.rem(number * count + which, 2)
        columns = pl.ds(c * chunk, chunk)
        return pltpu.make_async_copy(
            ready.at[slot, :, columns],
            out.at[order[first + number], pl.ds(starts[which], half), columns],
            sems.at[slot, c],
        )

    for which, start in enumerate(starts):
        width = BLOCK_W - start
        for b in range(blocks):

            @pl.when(step == b)
            def _(b=b):
                tiles = read_coded(u_refs[b * count + which], width // SPAN)
                for row in range(half // SPAN):
                    rows = slice(row * SPAN, (row + 1) * SPAN)
                    for column in range(width // SPAN):
                        value = tiles[row, column] if column >= row else jnp.zeros((SPAN, SPAN), F32)
                        high, low = split(value)
                        columns = slice(column * SPAN, (column + 1) * SPAN)
                        left[rows, columns] = high
                        left[half + row * SPAN : half + (row + 1) * SPAN, columns] = low

        for c in range(chunks):
            if count == 1:

                @pl.when(step >= 2)
                def _(c=c):
                    copy(step - 2, which, c).wait()

            elif blocks > 1:

                @pl.when(step >= 1)
                def _(c=c):
                    copy(step - 1, which, c).wait()

            weight = w_refs[c][:, start - lowest :]
            product = lax.dot_general(left[:, :width], weight, NT, preferred_element_type=F32)
            ready[lax.rem(step * count + which, 2), :, c * chunk : (c + 1) * chunk] = product[:half] + product[half:]
            copy(step, which, c).start()

    @pl.when(step == blocks - 1)
    def _():
        for c in range(chunks):
            if count > 1:
                copy(step, 0, c).wait()
            elif blocks > 1:
                copy(step - 1, 0, c).wait()
            copy(step, count - 1, c).wait()


def shards(query_rows, key_rows, placed_value_rows, doc_lengths, span_order, out_weight):
    tokens = query_rows.shape[1]
    features = out_weight.shape[0]
    seq = lax.axis_size("seq")
    ring = lax.axis_size("dp")
    chips = seq // 2
    spans = tokens // SPAN
    all_spans = spans * seq
    documents = doc_lengths.shape[1]
    per = KEY_VALUE_HEADS // seq
    blocks = NB // seq
    own = lax.axis_index("seq").astype(jnp.int32)
    place = lax.axis_index("dp").astype(jnp.int32)
    query, key, value = query_rows[0], key_rows[0], placed_value_rows[0]
    vmem = pl.BlockSpec(memory_space=pltpu.VMEM)
    anywhere = pl.BlockSpec(memory_space=pl.ANY)
    in_ring = blocks == ring

    if in_ring:
        turns = [lax.rem(place + 2 * ring - 1 - t, ring) for t in range(blocks)]
    else:
        turns = [jnp.int32(t) for t in range(blocks)]
    first_kv = turns[0] // KV_BLOCKS

    def moved(distance, cross):
        return [
            (x * 2 + c, (x + distance) % chips * 2 + (1 - c if cross else c)) for x in range(chips) for c in range(2)
        ]

    def cut(targets, columns, scalars, name, after=(), limit=OTHER_VMEM):
        specs, arrays = [], []
        for target in targets:
            for array, size, index in columns:
                specs.append(
                    pl.BlockSpec((tokens, size), lambda i, meta, target=target, index=index: (0, index(target(meta), meta)))
                )
                arrays.append(array)
        width = sum(size for _, size, _ in columns)
        return pl.pallas_call(
            functools.partial(cut_kernel, targets=len(targets), given=len(columns)),
            out_shape=[jax.ShapeDtypeStruct((tokens, width), BF16)] * len(targets),
            grid_spec=pltpu.PrefetchScalarGridSpec(
                num_scalar_prefetch=1,
                grid=(1,),
                in_specs=specs + [anywhere] * len(after),
                out_specs=[pl.BlockSpec((tokens, width), lambda i, meta: (0, 0))] * len(targets),
            ),
            compiler_params=params(limit),
            cost_estimate=cost(0, 2**21),
            name=name,
        )(scalars, *arrays, *after)

    tile = 512

    def target_at(distance, cross):
        return lambda meta: lax.rem(meta[0] // 2 + distance, chips) * 2 + lax.rem(lax.rem(meta[0], 2) + cross, 2)

    far = [(distance, cross) for distance in range(1, chips) for cross in range(2)]
    pieces = []

    most = all_spans // 2 + 1

    def grams_of(t):
        kv = turns[t] // KV_BLOCKS
        carriers = pieces[: min(t + 1, per)]
        which = jnp.where(kv == first_kv, 0, 1).astype(jnp.int32)
        meta = jnp.concatenate([jnp.stack([own, turns[t], kv, which]), doc_lengths[0], span_order[0]])
        folded = jax.ShapeDtypeStruct((SUM_ROWS, SPAN), F32)
        peer_kv = blocks * BLOCK_W // HEAD_SIZE
        return pl.pallas_call(
            functools.partial(
                attention_kernel,
                chips=chips, spans=spans, all_spans=all_spans, documents=documents, most=most, sets=len(carriers),
            ),
            out_shape=[folded] * 2,
            grid_spec=pltpu.PrefetchScalarGridSpec(
                num_scalar_prefetch=1,
                grid=(1,),
                in_specs=[
                    pl.BlockSpec((tokens, BLOCK_W), lambda i, meta: (0, meta[0] * blocks + meta[1])),
                    pl.BlockSpec((tokens, BLOCK_W), lambda i, meta: (0, meta[1])),
                ]
                + [pl.BlockSpec((tokens, BLOCK_W), lambda i, meta: (0, 0))] * len(far)
                + [pl.BlockSpec((tokens, HEAD_SIZE), lambda i, meta: (0, meta[0] * per + meta[2]))] * 2
                + [
                    pl.BlockSpec((tokens, HEAD_SIZE), lambda i, meta: (0, peer_kv + meta[2])),
                    pl.BlockSpec((tokens, HEAD_SIZE), lambda i, meta: (0, peer_kv + per + meta[2])),
                ]
                + [pl.BlockSpec((tokens, 2 * HEAD_SIZE), lambda i, meta: (0, BLOCK_W // (2 * HEAD_SIZE)))]
                * (len(carriers) * len(far)),
                out_specs=[pl.BlockSpec((SUM_ROWS, SPAN), lambda i, meta: (0, 0))] * 2,
                scratch_shapes=[
                    pltpu.VMEM((all_spans, BLOCK_HEADS * SPAN, HEAD_SIZE), BF16),
                    pltpu.VMEM((all_spans, SPAN, HEAD_SIZE), BF16),
                    pltpu.VMEM((all_spans, HEAD_SIZE, SPAN), BF16),
                    pltpu.SMEM((all_spans,), jnp.int32),
                    pltpu.VMEM((2, most * SPAN, SPAN), F32),
                    pltpu.VMEM((2, BLOCK_W, all_spans * SPAN), BF16),
                    pltpu.VMEM((BLOCK_W, BLOCK_W), F32),
                ],
            ),
            compiler_params=params(ATTENTION_VMEM),
            cost_estimate=cost(1.4e10, 2**20),
            name="attention_outer_products",
        )(meta, query, peer, *pieces[t], key, value, peer, peer, *[a for carrier in carriers for a in carrier])

    grams = []
    held = []
    swapped = [lax.ppermute(array, "seq", moved(0, 1)) for array in (query, key, value)]
    widths = (blocks * BLOCK_W, per * HEAD_SIZE, per * HEAD_SIZE)
    columns = [(array, width, lambda target, meta: target) for array, width in zip(swapped, widths)]
    peer = cut([lambda meta: meta[0]], columns, own[None], "cut_peer")[0]
    for t in range(blocks + 1):
        if t < blocks:
            kv = first_kv if t == 0 else per - 1 - first_kv
            columns = [(query, BLOCK_W, lambda target, meta: target * blocks + meta[1])]
            if t < per:
                columns += [(array, HEAD_SIZE, lambda target, meta: target * per + meta[2]) for array in (key, value)]
            scalars = jnp.stack([own, turns[t], kv])
            after = [] if t == 0 else swapped[1:2]
            parts = cut(
                [target_at(*where) for where in far], columns, scalars, "cut_piece", after,
                OTHER_VMEM if t else FULL_VMEM,
            )
            if t > 1:
                *parts, held[t - 2] = lax.optimization_barrier((*parts, held[t - 2]))
            pieces.append([lax.ppermute(part, "seq", moved(*where)) for part, where in zip(parts, far)])
        if t == 0:
            continue
        done = t - 1
        grams.append(grams_of(done))
        if done == 0 or not in_ring:
            held.append(grams[done])
        else:
            held.append([mine + theirs for mine, theirs in zip(grams[done], carried)] if done < ring - 1 else None)
        if in_ring and done < ring - 1:
            carried = [lax.ppermute(part, "dp", [(z, (z + 1) % ring) for z in range(ring)]) for part in held[done]]

    half = BLOCK_W // 2
    top_rows, bottom_rows = [
        SPAN * (sum(len(part) for part in tile_order(2, columns))) + 16 for columns in (PANELS, PANELS // 2)
    ]
    scratch = lambda width: [pltpu.VMEM((width, width), F32), pltpu.VMEM((32, width), F32), pltpu.VMEM((half, width), F32)]

    def factor_top(*given):
        return pl.pallas_call(
            functools.partial(factor_kernel, start=0, stop=half, received=len(given)),
            out_shape=[
                jax.ShapeDtypeStruct((top_rows, SPAN), BF16),
                jax.ShapeDtypeStruct((half, half), F32),
            ],
            in_specs=[vmem] * len(given),
            out_specs=[vmem] * 2,
            scratch_shapes=scratch(BLOCK_W),
            compiler_params=params(OTHER_VMEM),
            cost_estimate=cost(1.0e10, 2**20),
            name="factor_top",
        )(*given)

    def factor_bottom(rest):
        return pl.pallas_call(
            functools.partial(factor_kernel, start=half, stop=BLOCK_W, received=1),
            out_shape=jax.ShapeDtypeStruct((bottom_rows, SPAN), BF16),
            in_specs=[vmem],
            out_specs=vmem,
            scratch_shapes=scratch(half),
            compiler_params=params(OTHER_VMEM),
            cost_estimate=cost(0.9e10, 2**20),
            name="factor_bottom",
        )(rest)

    if in_ring:
        top, rest = factor_top(*grams[ring - 1], *carried)

        def shared(array):
            return [array] + [
                lax.ppermute(array, "dp", [(z, (z + d) % ring) for z in range(ring)]) for d in range(1, ring)
            ]

        tops = shared(top)
        bottom = factor_bottom(rest)
        bottoms = shared(bottom)
        order = jnp.stack([lax.rem(place - d + ring, ring) for d in range(ring)])
    else:
        halves = [factor_top(*[lax.psum(part, "dp") for part in grams[t]]) for t in range(blocks)]
        tops = [top for top, _ in halves]
        bottoms = [factor_bottom(rest) for _, rest in halves]
        order = jnp.arange(blocks, dtype=jnp.int32)


    def whiten(uppers, first, starts, result):
        more = [] if result is None else [result]
        depth = BLOCK_W - starts[0]
        chunks = features // tile
        weights = [
            pl.BlockSpec(
                (tile, depth),
                lambda b, order, c=c: (c, order[first + b] * (BLOCK_W // depth) + starts[0] // depth),
            )
            for c in range(chunks)
        ]
        count = len(uppers) // len(starts)
        return pl.pallas_call(
            functools.partial(
                whiten_kernel, blocks=count, starts=starts, first=first, chunks=chunks, aliased=len(more)
            ),
            out_shape=jax.ShapeDtypeStruct((blocks, BLOCK_W, features), F32),
            grid_spec=pltpu.PrefetchScalarGridSpec(
                num_scalar_prefetch=1,
                grid=(count,),
                in_specs=[vmem] * len(uppers) + weights + [anywhere] * len(more),
                out_specs=anywhere,
                scratch_shapes=[
                    pltpu.VMEM((2 * half, depth), BF16),
                    pltpu.VMEM((2, half, features), F32),
                    pltpu.SemaphoreType.DMA((2, chunks)),
                ],
            ),
            input_output_aliases={1 + len(uppers) + chunks: 0} if more else {},
            compiler_params=params(WHITEN_VMEM),
            cost_estimate=cost(2.0e9 * len(uppers), 2**20),
            name="whiten_bottom" if starts[0] else "whiten_top",
        )(order, *uppers, *[out_weight] * chunks, *more)

    result = whiten([tops[0], bottoms[0]], 0, (0, half), None)
    result = whiten(tops[1:2], 1, (0,), result)
    if blocks > 2:
        result = whiten(tops[2:], 2, (0,), result)
    return whiten(bottoms[1:], 1, (half,), result)


def solution(mesh):
    in_specs = (
        P(("groups", "dp"), "seq", None),
        P(("groups", "dp"), "seq", None),
        P(("groups", "dp"), "seq", None),
        P(("groups", "dp"), None),
        P(("groups", "dp"), None),
        P("dp", "seq"),
    )
    out_specs = P(("groups", "seq"), None, "dp")
    return jax.shard_map(shards, mesh=mesh, in_specs=in_specs, out_specs=out_specs, check_vma=False)
```

```python
import functools
import math

import jax
import jax.numpy as jnp
from jax import lax
from jax.experimental import pallas as pl
from jax.experimental.pallas import tpu as pltpu
from jax.sharding import PartitionSpec as P

QUERY_HEADS = 64
KEY_VALUE_HEADS = 8
HEAD_SIZE = 128
BLOCK_W = 512
NB = 16
SPAN = 128
GROUP = QUERY_HEADS // KEY_VALUE_HEADS
BLOCK_HEADS = BLOCK_W // HEAD_SIZE
KV_BLOCKS = GROUP // BLOCK_HEADS
PANELS = BLOCK_W // SPAN
SUM_ROWS = SPAN * PANELS + 8
VMEM_BYTES = 50 * 2**20
FULL_VMEM = 63 * 2**20
ATTENTION_VMEM = 44 * 2**20
WHITEN_VMEM = 44 * 2**20
OTHER_VMEM = 44 * 2**20
F32 = jnp.float32
BF16 = jnp.bfloat16
NT = (((1,), (1,)), ((), ()))
TN = (((0,), (0,)), ((), ()))


def params(limit=OTHER_VMEM):
    return pltpu.CompilerParams(vmem_limit_bytes=limit)


def cost(flops, moved, trans=0):
    return pl.CostEstimate(flops=int(flops), bytes_accessed=int(moved), transcendentals=int(trans))


def encode(value, exponent):
    scaled = value * jnp.exp2(15.0 - exponent)
    power = scaled * scaled
    power = power * power
    power = power * power
    return jnp.where(scaled < 0.0, -power, power)


def decode(code, exponent):
    code = code.astype(F32)
    quarter = lax.rsqrt(lax.rsqrt(jnp.maximum(jnp.abs(code), 1e-37)))
    root = quarter * lax.rsqrt(quarter) * jnp.exp2(exponent - 15.0)
    return jnp.where(code < 0.0, -root, root)


def exponent_of(largest):
    return jnp.ceil(jnp.log(jnp.maximum(largest, 1e-30)) * (1.0 / math.log(2.0)) + 0.001)


def write_coded(tiles, out):
    off, pairs = tile_order(tiles.rows, tiles.columns)
    places = off + [(i, i) for i in range(tiles.rows)]
    largest = functools.reduce(jnp.maximum, [jnp.max(jnp.abs(tiles(*p)), axis=(0, 1), keepdims=True) for p in places])
    exponent = exponent_of(largest)
    (line,) = fold(tiles, out, lambda value: encode(value, exponent))
    row = lax.broadcasted_iota(jnp.int32, (16, SPAN), 0)
    out[(len(off) + len(pairs)) * SPAN :] = jnp.where(row < 8, line, exponent).astype(BF16)


def read_coded(ref, columns):
    upper, equal = diagonal_masks()
    off, pairs = tile_order(2, columns)
    at = (len(off) + len(pairs)) * SPAN
    tail = ref[at:].astype(F32)
    exponent = tail[15:16, 0:1]
    tiles = {place: decode(ref[i * SPAN : (i + 1) * SPAN], exponent) for i, place in enumerate(off)}
    square = decode(ref[at - SPAN : at], exponent)
    line = decode(tail[0:1], exponent)
    tiles[0, 0] = jnp.where(upper, square, 0.0)
    tiles[1, 1] = jnp.where(equal, line, jnp.where(upper, square.T, 0.0))
    return tiles


def split(value):
    high = value.astype(BF16)
    return high, (value - high.astype(F32)).astype(BF16)


def cut_kernel(meta, *refs, targets, given):
    outs = refs[-targets:]
    for number, out in enumerate(outs):
        at = 0
        for ref in refs[number * given : (number + 1) * given]:
            out[:, at : at + ref.shape[1]] = ref[...]
            at += ref.shape[1]


def attention_kernel(meta, *refs, chips, spans, all_spans, documents, most, sets):
    sources = 2 * chips
    near = sources + 4
    query_refs, near_refs = refs[:sources], refs[sources:near]
    far_refs = refs[near : near + sets * (sources - 2)]
    top, bottom, queries, keys, values, slots, limits, left, total = refs[near + sets * (sources - 2) :]
    own = meta[0]
    chip, core = own // 2, lax.rem(own, 2)
    lengths = 4
    order = lengths + documents

    for r in range(all_spans):
        device = r // spans
        distance = lax.rem(chip - device // 2 + chips, chips)
        cross = lax.rem(core + device % 2, 2)
        slots[meta[order + r]] = (distance * 2 + cross) * spans + r % spans

    def place_kv(source, key_part, value_part):
        for t in range(spans):
            rows = slice(t * SPAN, (t + 1) * SPAN)
            keys[source * spans + t] = key_part[rows]
            values[source * spans + t] = value_part[rows].astype(F32).T.astype(BF16)

    place_kv(0, near_refs[0], near_refs[1])
    place_kv(1, near_refs[2], near_refs[3])
    for which in range(sets):

        @pl.when(meta[3] == which)
        def _(which=which):
            for source in range(2, sources):
                ref = far_refs[which * (sources - 2) + source - 2]
                place_kv(source, ref[:, :HEAD_SIZE], ref[:, HEAD_SIZE:])

    for source in range(sources):
        for t in range(spans):
            for h in range(BLOCK_HEADS):
                queries[source * spans + t, h * SPAN : (h + 1) * SPAN] = query_refs[source][
                    t * SPAN : (t + 1) * SPAN, h * HEAD_SIZE : (h + 1) * HEAD_SIZE
                ]

    factor = HEAD_SIZE ** (-0.5) / math.log(2.0)

    def place_of(q):
        source = q // spans
        distance, cross = source // 2, lax.rem(source, 2)
        device = lax.rem(chip - distance + chips, chips) * 2 + lax.rem(core + cross, 2)
        position = meta[order + device * spans + lax.rem(q, spans)]
        first_row = position * SPAN
        begin = jnp.int32(0)
        at = jnp.int32(0)
        query_pos = lax.broadcasted_iota(jnp.int32, (1, SPAN), 1) + first_row
        query_begin = jnp.zeros((1, SPAN), jnp.int32)
        for d in range(documents):
            begin = jnp.where(at <= first_row, at, begin)
            query_begin = jnp.where(query_pos >= at, at, query_begin)
            at = at + meta[lengths + d]
        return position, query_pos, query_begin, position - begin // SPAN + 1

    def one_pair(p, carry):
        pair = [(which, 2 * p + which, place_of(2 * p + which)) for which in range(2)]
        count = jnp.maximum(pair[0][2][3], pair[1][2][3])

        for n in range(1, most + 1):

            @pl.when(count == n)
            def _(n=n):
                for which, q, (position, query_pos, query_begin, _) in pair:
                    lanes = pl.ds(pl.multiple_of(q * SPAN, SPAN), SPAN)
                    held = [slots[jnp.maximum(position - n + 1 + i, 0)] for i in range(n)]
                    for i in range(n):
                        key_pos = lax.broadcasted_iota(jnp.int32, (SPAN, SPAN), 0) + (position - n + 1 + i) * SPAN
                        seen = (key_pos <= query_pos) & (key_pos >= query_begin)
                        limits[which, i * SPAN : (i + 1) * SPAN] = jnp.where(seen, 3e38, -1e30)
                    key_part = jnp.concatenate([keys[slot] for slot in held], axis=0)
                    value_part = jnp.concatenate([values[slot] for slot in held], axis=1)
                    scores = lax.dot_general(key_part, queries[q], NT, preferred_element_type=F32)
                    limit = limits[which, : n * SPAN]
                    scores = jnp.minimum(scores, jnp.concatenate([limit] * BLOCK_HEADS, axis=1))
                    largest = jnp.max(scores, axis=0, keepdims=True)
                    lifted = jnp.exp2((scores - largest) * factor)
                    summed = jnp.sum(lifted, axis=0, keepdims=True)
                    weights = (lifted * (1.0 / summed)).astype(BF16)
                    mixed = jnp.dot(value_part, weights, preferred_element_type=F32)
                    for h in range(BLOCK_HEADS):
                        one_head = mixed[:, h * SPAN : (h + 1) * SPAN]
                        columns = slice(h * HEAD_SIZE, (h + 1) * HEAD_SIZE)
                        high, low = split(one_head)
                        left[0, columns, lanes] = high
                        left[1, columns, lanes] = low

        return carry

    lax.fori_loop(0, all_spans // 2, one_pair, 0)

    half = BLOCK_W // 2
    total[...] = jnp.zeros_like(total)

    def one_pass(i, carry):
        a, b = lax.rem(i, 2), i // 2
        total[:half] += lax.dot_general(left[a, :half], left[b], NT, preferred_element_type=F32)
        total[half:, half:] += lax.dot_general(left[a, half:], left[b, half:], NT, preferred_element_type=F32)
        return carry

    lax.fori_loop(0, 3, one_pass, 0)
    for out, where in zip((top, bottom), sum_tiles()):
        off, pair = where
        (line,) = fold(Tiles(total, PANELS, PANELS, False), out, where=(off, [pair]))
        out[SUM_ROWS - 8 :] = jnp.broadcast_to(line, (8, SPAN))


def diagonal_masks():
    rows = lax.broadcasted_iota(jnp.int32, (SPAN, SPAN), 0)
    columns = lax.broadcasted_iota(jnp.int32, (SPAN, SPAN), 1)
    return rows <= columns, rows == columns


def tile_order(rows, columns):
    off = [(i, j) for i in range(rows) for j in range(i + 1, columns)]
    return off, [(i, i + 1) for i in range(0, rows, 2)]


def sum_tiles():
    off, pairs = tile_order(PANELS, PANELS)
    half = len(off) // 2
    return [(off[:half], pairs[0]), (off[half:], pairs[1])]


def fold(tiles, out, change=lambda value: value, where=None):
    upper, equal = diagonal_masks()
    off, pairs = tile_order(tiles.rows, tiles.columns) if where is None else where
    for i, place in enumerate(off):
        out[i * SPAN : (i + 1) * SPAN] = change(tiles(*place)).astype(out.dtype)
    lines = []
    for i, (a, b) in enumerate(pairs):
        second = tiles(b, b)
        at = (len(off) + i) * SPAN
        lower = second.T if tiles.turn else second
        out[at : at + SPAN] = change(jnp.where(upper, tiles(a, a), lower)).astype(out.dtype)
        lines.append(change(jnp.sum(jnp.where(equal, second, 0.0), axis=0, keepdims=True)))
    return lines


class Tiles:
    def __init__(self, ref, rows, columns, turn):
        self.ref, self.rows, self.columns, self.turn = ref, rows, columns, turn

    def __call__(self, i, j):
        return self.ref[i * SPAN : (i + 1) * SPAN, j * SPAN : (j + 1) * SPAN]


def unfold(halves, work):
    upper, equal = diagonal_masks()
    trace = jnp.zeros((1, 1), F32)
    squares = []
    for total, (off, (a, b)) in zip(halves, sum_tiles()):
        for i, (row, column) in enumerate(off):
            work[row * SPAN : (row + 1) * SPAN, column * SPAN : (column + 1) * SPAN] = total[i * SPAN : (i + 1) * SPAN]
        at = len(off) * SPAN
        square = total[at : at + SPAN]
        turned = square.T
        line = jnp.broadcast_to(total[at + SPAN : at + SPAN + 1], (SPAN, SPAN))
        squares.append((a, jnp.where(upper, square, turned)))
        squares.append((b, jnp.where(equal, line, jnp.where(upper, turned, square))))
    for _, square in squares:
        trace = trace + jnp.sum(jnp.where(equal, square, 0.0), axis=(0, 1), keepdims=True)
    damping = trace * (0.1 / BLOCK_W)
    for a, square in squares:
        work[a * SPAN : (a + 1) * SPAN, a * SPAN : (a + 1) * SPAN] = jnp.where(equal, square + damping, square)


def factor_kernel(*refs, start, stop, received):
    width = BLOCK_W - start
    panels = width // SPAN
    step = 32
    groups = step // 8
    per_tile = SPAN // step
    last = stop == BLOCK_W
    given, refs = (refs[:received], refs[received:])
    out, refs = refs[0], refs[1:]
    if not last:
        rest, refs = refs[0], refs[1:]
    work, previous, upper = refs
    if start == 0:
        work[...] = jnp.zeros_like(work)
        halves = [ref[...] for ref in given[:2]]
        if received == 4:
            halves = [mine + ref[...] for mine, ref in zip(halves, given[2:])]
        unfold(halves, work)
    else:
        work[...] = given[0][...]
    previous[...] = jnp.zeros_like(previous)

    def triple(value, first):
        high, low = split(value)
        return jnp.concatenate((high, low, high) if first else (high, high, low), axis=0)

    def superpanel(g, carry):
        row = pl.multiple_of(g * step, step)
        tile_index = g // per_tile
        tile = pl.ds(pl.multiple_of(tile_index * SPAN, SPAN), SPAN)
        turn = lax.rem(SPAN - lax.rem(g, per_tile) * step, SPAN)
        before = previous[...]
        right = triple(before, False)
        near = pltpu.roll(previous[:, tile], turn, 1)
        fresh = lax.dot_general(triple(near, True), right, TN, preferred_element_type=F32)[:step]
        current = work[pl.ds(row, step), :] - fresh
        work[...] = work[...] - lax.dot_general(triple(before, True), right, TN, preferred_element_type=F32)

        square = current[:, :SPAN]
        for k in range(1, panels):
            square = jnp.where(tile_index == k, current[:, k * SPAN : (k + 1) * SPAN], square)
        square = pltpu.roll(square, turn, 1)
        line = lax.broadcasted_iota(jnp.int32, (8, SPAN), 0)
        held = [
            {q: jnp.broadcast_to(square[8 * q : 8 * q + 8, j : j + 1], (8, SPAN)) for q in range(j // 8, groups)}
            for j in range(step)
        ]
        body = [[current[8 * q : 8 * q + 8, k * SPAN : (k + 1) * SPAN] for k in range(panels)] for q in range(groups)]
        scales = [jnp.zeros((8, SPAN), F32) for _ in range(groups)]

        def spread(value, i):
            return jnp.broadcast_to(value[i % 8 : i % 8 + 1], (8, SPAN))

        for i in range(step):
            at = i // 8
            root = lax.rsqrt(spread(held[i][at], i))
            inverse = root * root
            scales[at] = jnp.where(line == i % 8, root, scales[at])
            ratio = {q: held[i][q] * inverse for q in range(at, groups)}
            ratio[at] = jnp.where(line > i % 8, ratio[at], 0.0)
            for j in range(i + 1, step):
                entry = spread(held[i][j // 8], j)
                for q in range(j // 8, groups):
                    held[j][q] = held[j][q] - ratio[q] * entry
            for k in range(panels):
                pivot_row = spread(body[at][k], i)
                for q in range(at, groups):
                    body[q][k] = body[q][k] - ratio[q] * pivot_row
        result = jnp.concatenate(
            [jnp.concatenate([body[q][k] * scales[q] for k in range(panels)], axis=1) for q in range(groups)], axis=0
        )
        across = lax.broadcasted_iota(jnp.int32, (step, width), 1)
        down = lax.broadcasted_iota(jnp.int32, (step, width), 0)
        result = jnp.where(across >= down + row, result, 0.0)
        previous[...] = result
        upper[pl.ds(row, step), :] = result
        return carry

    lax.fori_loop(0, (stop - start) // step, superpanel, 0)
    if not last:
        done = stop - start
        before = previous[...]
        final = lax.dot_general(
            triple(before[:, done:], True), triple(before[:, done:], False), TN, preferred_element_type=F32
        )
        rest[...] = work[done:, done:] - final
    write_coded(Tiles(upper, (stop - start) // SPAN, panels, True), out)


def whiten_kernel(order, *refs, blocks, starts, first, chunks, aliased):
    count = len(starts)
    u_refs, refs = refs[: blocks * count], refs[blocks * count :]
    w_refs, refs = refs[:chunks], refs[chunks + aliased :]
    lowest = starts[0]
    out, left, ready, sems = refs
    half = BLOCK_W // 2
    chunk = ready.shape[2] // chunks
    step = pl.program_id(0)

    def copy(number, which, c):
        slot = lax.rem(number * count + which, 2)
        columns = pl.ds(c * chunk, chunk)
        return pltpu.make_async_copy(
            ready.at[slot, :, columns],
            out.at[order[first + number], pl.ds(starts[which], half), columns],
            sems.at[slot, c],
        )

    for which, start in enumerate(starts):
        width = BLOCK_W - start
        for b in range(blocks):

            @pl.when(step == b)
            def _(b=b):
                tiles = read_coded(u_refs[b * count + which], width // SPAN)
                for row in range(half // SPAN):
                    rows = slice(row * SPAN, (row + 1) * SPAN)
                    for column in range(width // SPAN):
                        value = tiles[row, column] if column >= row else jnp.zeros((SPAN, SPAN), F32)
                        high, low = split(value)
                        columns = slice(column * SPAN, (column + 1) * SPAN)
                        left[rows, columns] = high
                        left[half + row * SPAN : half + (row + 1) * SPAN, columns] = low

        for c in range(chunks):
            if count == 1:

                @pl.when(step >= 2)
                def _(c=c):
                    copy(step - 2, which, c).wait()

            elif blocks > 1:

                @pl.when(step >= 1)
                def _(c=c):
                    copy(step - 1, which, c).wait()

            weight = w_refs[c][:, start - lowest :]
            product = lax.dot_general(left[:, :width], weight, NT, preferred_element_type=F32)
            ready[lax.rem(step * count + which, 2), :, c * chunk : (c + 1) * chunk] = product[:half] + product[half:]
            copy(step, which, c).start()

    @pl.when(step == blocks - 1)
    def _():
        for c in range(chunks):
            if count > 1:
                copy(step, 0, c).wait()
            elif blocks > 1:
                copy(step - 1, 0, c).wait()
            copy(step, count - 1, c).wait()


def shards(query_rows, key_rows, placed_value_rows, doc_lengths, span_order, out_weight):
    tokens = query_rows.shape[1]
    features = out_weight.shape[0]
    seq = lax.axis_size("seq")
    ring = lax.axis_size("dp")
    chips = seq // 2
    spans = tokens // SPAN
    all_spans = spans * seq
    documents = doc_lengths.shape[1]
    per = KEY_VALUE_HEADS // seq
    blocks = NB // seq
    own = lax.axis_index("seq").astype(jnp.int32)
    place = lax.axis_index("dp").astype(jnp.int32)
    query, key, value = query_rows[0], key_rows[0], placed_value_rows[0]
    vmem = pl.BlockSpec(memory_space=pltpu.VMEM)
    anywhere = pl.BlockSpec(memory_space=pl.ANY)
    in_ring = blocks == ring

    if in_ring:
        turns = [lax.rem(place + 2 * ring - 1 - t, ring) for t in range(blocks)]
    else:
        turns = [jnp.int32(t) for t in range(blocks)]
    first_kv = turns[0] // KV_BLOCKS

    def moved(distance, cross):
        return [
            (x * 2 + c, (x + distance) % chips * 2 + (1 - c if cross else c)) for x in range(chips) for c in range(2)
        ]

    def cut(targets, columns, scalars, name, after=(), limit=OTHER_VMEM):
        specs, arrays = [], []
        for target in targets:
            for array, size, index in columns:
                specs.append(
                    pl.BlockSpec((tokens, size), lambda i, meta, target=target, index=index: (0, index(target(meta), meta)))
                )
                arrays.append(array)
        width = sum(size for _, size, _ in columns)
        return pl.pallas_call(
            functools.partial(cut_kernel, targets=len(targets), given=len(columns)),
            out_shape=[jax.ShapeDtypeStruct((tokens, width), BF16)] * len(targets),
            grid_spec=pltpu.PrefetchScalarGridSpec(
                num_scalar_prefetch=1,
                grid=(1,),
                in_specs=specs + [anywhere] * len(after),
                out_specs=[pl.BlockSpec((tokens, width), lambda i, meta: (0, 0))] * len(targets),
            ),
            compiler_params=params(limit),
            cost_estimate=cost(0, 2**21),
            name=name,
        )(scalars, *arrays, *after)

    tile = 512

    def target_at(distance, cross):
        return lambda meta: lax.rem(meta[0] // 2 + distance, chips) * 2 + lax.rem(lax.rem(meta[0], 2) + cross, 2)

    far = [(distance, cross) for distance in range(1, chips) for cross in range(2)]
    pieces = []

    most = all_spans // 2 + 1

    def grams_of(t):
        kv = turns[t] // KV_BLOCKS
        carriers = pieces[: min(t + 1, per)]
        which = jnp.where(kv == first_kv, 0, 1).astype(jnp.int32)
        meta = jnp.concatenate([jnp.stack([own, turns[t], kv, which]), doc_lengths[0], span_order[0]])
        folded = jax.ShapeDtypeStruct((SUM_ROWS, SPAN), F32)
        peer_kv = blocks * BLOCK_W // HEAD_SIZE
        return pl.pallas_call(
            functools.partial(
                attention_kernel,
                chips=chips, spans=spans, all_spans=all_spans, documents=documents, most=most, sets=len(carriers),
            ),
            out_shape=[folded] * 2,
            grid_spec=pltpu.PrefetchScalarGridSpec(
                num_scalar_prefetch=1,
                grid=(1,),
                in_specs=[
                    pl.BlockSpec((tokens, BLOCK_W), lambda i, meta: (0, meta[0] * blocks + meta[1])),
                    pl.BlockSpec((tokens, BLOCK_W), lambda i, meta: (0, meta[1])),
                ]
                + [pl.BlockSpec((tokens, BLOCK_W), lambda i, meta: (0, 0))] * len(far)
                + [pl.BlockSpec((tokens, HEAD_SIZE), lambda i, meta: (0, meta[0] * per + meta[2]))] * 2
                + [
                    pl.BlockSpec((tokens, HEAD_SIZE), lambda i, meta: (0, peer_kv + meta[2])),
                    pl.BlockSpec((tokens, HEAD_SIZE), lambda i, meta: (0, peer_kv + per + meta[2])),
                ]
                + [pl.BlockSpec((tokens, 2 * HEAD_SIZE), lambda i, meta: (0, BLOCK_W // (2 * HEAD_SIZE)))]
                * (len(carriers) * len(far)),
                out_specs=[pl.BlockSpec((SUM_ROWS, SPAN), lambda i, meta: (0, 0))] * 2,
                scratch_shapes=[
                    pltpu.VMEM((all_spans, BLOCK_HEADS * SPAN, HEAD_SIZE), BF16),
                    pltpu.VMEM((all_spans, SPAN, HEAD_SIZE), BF16),
                    pltpu.VMEM((all_spans, HEAD_SIZE, SPAN), BF16),
                    pltpu.SMEM((all_spans,), jnp.int32),
                    pltpu.VMEM((2, most * SPAN, SPAN), F32),
                    pltpu.VMEM((2, BLOCK_W, all_spans * SPAN), BF16),
                    pltpu.VMEM((BLOCK_W, BLOCK_W), F32),
                ],
            ),
            compiler_params=params(ATTENTION_VMEM),
            cost_estimate=cost(1.4e10, 2**20),
            name="attention_outer_products",
        )(meta, query, peer, *pieces[t], key, value, peer, peer, *[a for carrier in carriers for a in carrier])

    grams = []
    held = []
    swapped = [lax.ppermute(array, "seq", moved(0, 1)) for array in (query, key, value)]
    widths = (blocks * BLOCK_W, per * HEAD_SIZE, per * HEAD_SIZE)
    columns = [(array, width, lambda target, meta: target) for array, width in zip(swapped, widths)]
    peer = cut([lambda meta: meta[0]], columns, own[None], "cut_peer")[0]
    for t in range(blocks + 1):
        if t < blocks:
            kv = first_kv if t == 0 else per - 1 - first_kv
            columns = [(query, BLOCK_W, lambda target, meta: target * blocks + meta[1])]
            if t < per:
                columns += [(array, HEAD_SIZE, lambda target, meta: target * per + meta[2]) for array in (key, value)]
            scalars = jnp.stack([own, turns[t], kv])
            after = [] if t == 0 else swapped[1:2]
            parts = cut(
                [target_at(*where) for where in far], columns, scalars, "cut_piece", after,
                OTHER_VMEM if t else FULL_VMEM,
            )
            if t > 1:
                *parts, held[t - 2] = lax.optimization_barrier((*parts, held[t - 2]))
            pieces.append([lax.ppermute(part, "seq", moved(*where)) for part, where in zip(parts, far)])
        if t == 0:
            continue
        done = t - 1
        grams.append(grams_of(done))
        if done == 0 or not in_ring:
            held.append(grams[done])
        else:
            held.append([mine + theirs for mine, theirs in zip(grams[done], carried)] if done < ring - 1 else None)
        if in_ring and done < ring - 1:
            carried = [lax.ppermute(part, "dp", [(z, (z + 1) % ring) for z in range(ring)]) for part in held[done]]

    half = BLOCK_W // 2
    top_rows, bottom_rows = [
        SPAN * (sum(len(part) for part in tile_order(2, columns))) + 16 for columns in (PANELS, PANELS // 2)
    ]
    scratch = lambda width: [pltpu.VMEM((width, width), F32), pltpu.VMEM((32, width), F32), pltpu.VMEM((half, width), F32)]

    def factor_top(*given):
        return pl.pallas_call(
            functools.partial(factor_kernel, start=0, stop=half, received=len(given)),
            out_shape=[
                jax.ShapeDtypeStruct((top_rows, SPAN), BF16),
                jax.ShapeDtypeStruct((half, half), F32),
            ],
            in_specs=[vmem] * len(given),
            out_specs=[vmem] * 2,
            scratch_shapes=scratch(BLOCK_W),
            compiler_params=params(OTHER_VMEM),
            cost_estimate=cost(1.0e10, 2**20),
            name="factor_top",
        )(*given)

    def factor_bottom(rest):
        return pl.pallas_call(
            functools.partial(factor_kernel, start=half, stop=BLOCK_W, received=1),
            out_shape=jax.ShapeDtypeStruct((bottom_rows, SPAN), BF16),
            in_specs=[vmem],
            out_specs=vmem,
            scratch_shapes=scratch(half),
            compiler_params=params(OTHER_VMEM),
            cost_estimate=cost(0.9e10, 2**20),
            name="factor_bottom",
        )(rest)

    if in_ring:
        top, rest = factor_top(*grams[ring - 1], *carried)

        def shared(array):
            return [array] + [
                lax.ppermute(array, "dp", [(z, (z + d) % ring) for z in range(ring)]) for d in range(1, ring)
            ]

        tops = shared(top)
        bottom = factor_bottom(rest)
        bottoms = shared(bottom)
        order = jnp.stack([lax.rem(place - d + ring, ring) for d in range(ring)])
    else:
        halves = [factor_top(*[lax.psum(part, "dp") for part in grams[t]]) for t in range(blocks)]
        tops = [top for top, _ in halves]
        bottoms = [factor_bottom(rest) for _, rest in halves]
        order = jnp.arange(blocks, dtype=jnp.int32)


    def whiten(uppers, first, starts, result):
        more = [] if result is None else [result]
        depth = BLOCK_W - starts[0]
        chunks = features // tile
        weights = [
            pl.BlockSpec(
                (tile, depth),
                lambda b, order, c=c: (c, order[first + b] * (BLOCK_W // depth) + starts[0] // depth),
            )
            for c in range(chunks)
        ]
        count = len(uppers) // len(starts)
        return pl.pallas_call(
            functools.partial(
                whiten_kernel, blocks=count, starts=starts, first=first, chunks=chunks, aliased=len(more)
            ),
            out_shape=jax.ShapeDtypeStruct((blocks, BLOCK_W, features), F32),
            grid_spec=pltpu.PrefetchScalarGridSpec(
                num_scalar_prefetch=1,
                grid=(count,),
                in_specs=[vmem] * len(uppers) + weights + [anywhere] * len(more),
                out_specs=anywhere,
                scratch_shapes=[
                    pltpu.VMEM((2 * half, depth), BF16),
                    pltpu.VMEM((2, half, features), F32),
                    pltpu.SemaphoreType.DMA((2, chunks)),
                ],
            ),
            input_output_aliases={1 + len(uppers) + chunks: 0} if more else {},
            compiler_params=params(WHITEN_VMEM),
            cost_estimate=cost(2.0e9 * len(uppers), 2**20),
            name="whiten_bottom" if starts[0] else "whiten_top",
        )(order, *uppers, *[out_weight] * chunks, *more)

    result = whiten([tops[0], bottoms[0]], 0, (0, half), None)
    result = whiten(tops[1:2], 1, (0,), result)
    result = whiten(bottoms[1:2], 1, (half,), result)
    if blocks > 2:
        rest = [half_block for pair in zip(tops[2:], bottoms[2:]) for half_block in pair]
        result = whiten(rest, 2, (0, half), result)
    return result


def solution(mesh):
    in_specs = (
        P(("groups", "dp"), "seq", None),
        P(("groups", "dp"), "seq", None),
        P(("groups", "dp"), "seq", None),
        P(("groups", "dp"), None),
        P(("groups", "dp"), None),
        P("dp", "seq"),
    )
    out_specs = P(("groups", "seq"), None, "dp")
    return jax.shard_map(shards, mesh=mesh, in_specs=in_specs, out_specs=out_specs, check_vma=False)
```

```python
import functools
import math

import jax
import jax.numpy as jnp
from jax import lax
from jax.experimental import pallas as pl
from jax.experimental.pallas import tpu as pltpu
from jax.sharding import PartitionSpec as P

QUERY_HEADS = 64
KEY_VALUE_HEADS = 8
HEAD_SIZE = 128
BLOCK_W = 512
NB = 16
SPAN = 128
GROUP = QUERY_HEADS // KEY_VALUE_HEADS
BLOCK_HEADS = BLOCK_W // HEAD_SIZE
KV_BLOCKS = GROUP // BLOCK_HEADS
PANELS = BLOCK_W // SPAN
SUM_ROWS = SPAN * PANELS + 8
VMEM_BYTES = 50 * 2**20
FULL_VMEM = 63 * 2**20
ATTENTION_VMEM = 44 * 2**20
WHITEN_VMEM = 44 * 2**20
OTHER_VMEM = 44 * 2**20
F32 = jnp.float32
BF16 = jnp.bfloat16
NT = (((1,), (1,)), ((), ()))
TN = (((0,), (0,)), ((), ()))


def params(limit=OTHER_VMEM):
    return pltpu.CompilerParams(vmem_limit_bytes=limit)


def cost(flops, moved, trans=0):
    return pl.CostEstimate(flops=int(flops), bytes_accessed=int(moved), transcendentals=int(trans))


def encode(value, exponent):
    scaled = value * jnp.exp2(15.0 - exponent)
    power = scaled * scaled
    power = power * power
    power = power * power
    return jnp.where(scaled < 0.0, -power, power)


def decode(code, exponent):
    code = code.astype(F32)
    quarter = lax.rsqrt(lax.rsqrt(jnp.maximum(jnp.abs(code), 1e-37)))
    root = quarter * lax.rsqrt(quarter) * jnp.exp2(exponent - 15.0)
    return jnp.where(code < 0.0, -root, root)


def exponent_of(largest):
    return jnp.ceil(jnp.log(jnp.maximum(largest, 1e-30)) * (1.0 / math.log(2.0)) + 0.001)


def write_coded(tiles, out):
    off, pairs = tile_order(tiles.rows, tiles.columns)
    places = off + [(i, i) for i in range(tiles.rows)]
    largest = functools.reduce(jnp.maximum, [jnp.max(jnp.abs(tiles(*p)), axis=(0, 1), keepdims=True) for p in places])
    exponent = exponent_of(largest)
    (line,) = fold(tiles, out, lambda value: encode(value, exponent))
    row = lax.broadcasted_iota(jnp.int32, (16, SPAN), 0)
    out[(len(off) + len(pairs)) * SPAN :] = jnp.where(row < 8, line, exponent).astype(BF16)


def read_coded(ref, columns):
    upper, equal = diagonal_masks()
    off, pairs = tile_order(2, columns)
    at = (len(off) + len(pairs)) * SPAN
    tail = ref[at:].astype(F32)
    exponent = tail[15:16, 0:1]
    tiles = {place: decode(ref[i * SPAN : (i + 1) * SPAN], exponent) for i, place in enumerate(off)}
    square = decode(ref[at - SPAN : at], exponent)
    line = decode(tail[0:1], exponent)
    tiles[0, 0] = jnp.where(upper, square, 0.0)
    tiles[1, 1] = jnp.where(equal, line, jnp.where(upper, square.T, 0.0))
    return tiles


def split(value):
    high = value.astype(BF16)
    return high, (value - high.astype(F32)).astype(BF16)


def cut_kernel(meta, *refs, targets, given):
    outs = refs[-targets:]
    for number, out in enumerate(outs):
        at = 0
        for ref in refs[number * given : (number + 1) * given]:
            out[:, at : at + ref.shape[1]] = ref[...]
            at += ref.shape[1]


def attention_kernel(meta, *refs, chips, spans, all_spans, documents, most, sets):
    sources = 2 * chips
    near = sources + 4
    query_refs, near_refs = refs[:sources], refs[sources:near]
    far_refs = refs[near : near + sets * (sources - 2)]
    top, bottom, queries, keys, values, slots, limits, left, total = refs[near + sets * (sources - 2) :]
    own = meta[0]
    chip, core = own // 2, lax.rem(own, 2)
    lengths = 4
    order = lengths + documents

    for r in range(all_spans):
        device = r // spans
        distance = lax.rem(chip - device // 2 + chips, chips)
        cross = lax.rem(core + device % 2, 2)
        slots[meta[order + r]] = (distance * 2 + cross) * spans + r % spans

    def place_kv(source, key_part, value_part):
        for t in range(spans):
            rows = slice(t * SPAN, (t + 1) * SPAN)
            keys[source * spans + t] = key_part[rows]
            values[source * spans + t] = value_part[rows].astype(F32).T.astype(BF16)

    place_kv(0, near_refs[0], near_refs[1])
    place_kv(1, near_refs[2], near_refs[3])
    for which in range(sets):

        @pl.when(meta[3] == which)
        def _(which=which):
            for source in range(2, sources):
                ref = far_refs[which * (sources - 2) + source - 2]
                place_kv(source, ref[:, :HEAD_SIZE], ref[:, HEAD_SIZE:])

    for source in range(sources):
        for t in range(spans):
            for h in range(BLOCK_HEADS):
                queries[source * spans + t, h * SPAN : (h + 1) * SPAN] = query_refs[source][
                    t * SPAN : (t + 1) * SPAN, h * HEAD_SIZE : (h + 1) * HEAD_SIZE
                ]

    factor = HEAD_SIZE ** (-0.5) / math.log(2.0)

    def place_of(q):
        source = q // spans
        distance, cross = source // 2, lax.rem(source, 2)
        device = lax.rem(chip - distance + chips, chips) * 2 + lax.rem(core + cross, 2)
        position = meta[order + device * spans + lax.rem(q, spans)]
        first_row = position * SPAN
        begin = jnp.int32(0)
        at = jnp.int32(0)
        query_pos = lax.broadcasted_iota(jnp.int32, (1, SPAN), 1) + first_row
        query_begin = jnp.zeros((1, SPAN), jnp.int32)
        for d in range(documents):
            begin = jnp.where(at <= first_row, at, begin)
            query_begin = jnp.where(query_pos >= at, at, query_begin)
            at = at + meta[lengths + d]
        return position, query_pos, query_begin, position - begin // SPAN + 1

    def one_pair(p, carry):
        pair = [(which, 2 * p + which, place_of(2 * p + which)) for which in range(2)]
        count = jnp.maximum(pair[0][2][3], pair[1][2][3])

        for n in range(1, most + 1):

            @pl.when(count == n)
            def _(n=n):
                for which, q, (position, query_pos, query_begin, _) in pair:
                    lanes = pl.ds(pl.multiple_of(q * SPAN, SPAN), SPAN)
                    held = [slots[jnp.maximum(position - n + 1 + i, 0)] for i in range(n)]
                    for i in range(n):
                        key_pos = lax.broadcasted_iota(jnp.int32, (SPAN, SPAN), 0) + (position - n + 1 + i) * SPAN
                        seen = (key_pos <= query_pos) & (key_pos >= query_begin)
                        limits[which, i * SPAN : (i + 1) * SPAN] = jnp.where(seen, 3e38, -1e30)
                    key_part = jnp.concatenate([keys[slot] for slot in held], axis=0)
                    value_part = jnp.concatenate([values[slot] for slot in held], axis=1)
                    scores = lax.dot_general(key_part, queries[q], NT, preferred_element_type=F32)
                    limit = limits[which, : n * SPAN]
                    scores = jnp.minimum(scores, jnp.concatenate([limit] * BLOCK_HEADS, axis=1))
                    largest = jnp.max(scores, axis=0, keepdims=True)
                    lifted = jnp.exp2((scores - largest) * factor)
                    summed = jnp.sum(lifted, axis=0, keepdims=True)
                    weights = (lifted * (1.0 / summed)).astype(BF16)
                    mixed = jnp.dot(value_part, weights, preferred_element_type=F32)
                    for h in range(BLOCK_HEADS):
                        one_head = mixed[:, h * SPAN : (h + 1) * SPAN]
                        columns = slice(h * HEAD_SIZE, (h + 1) * HEAD_SIZE)
                        high, low = split(one_head)
                        left[0, columns, lanes] = high
                        left[1, columns, lanes] = low

        return carry

    lax.fori_loop(0, all_spans // 2, one_pair, 0)

    half = BLOCK_W // 2
    total[...] = jnp.zeros_like(total)

    def one_pass(i, carry):
        a, b = lax.rem(i, 2), i // 2
        total[:half] += lax.dot_general(left[a, :half], left[b], NT, preferred_element_type=F32)
        total[half:, half:] += lax.dot_general(left[a, half:], left[b, half:], NT, preferred_element_type=F32)
        return carry

    lax.fori_loop(0, 3, one_pass, 0)
    for out, where in zip((top, bottom), sum_tiles()):
        off, pair = where
        (line,) = fold(Tiles(total, PANELS, PANELS, False), out, where=(off, [pair]))
        out[SUM_ROWS - 8 :] = jnp.broadcast_to(line, (8, SPAN))


def diagonal_masks():
    rows = lax.broadcasted_iota(jnp.int32, (SPAN, SPAN), 0)
    columns = lax.broadcasted_iota(jnp.int32, (SPAN, SPAN), 1)
    return rows <= columns, rows == columns


def tile_order(rows, columns):
    off = [(i, j) for i in range(rows) for j in range(i + 1, columns)]
    return off, [(i, i + 1) for i in range(0, rows, 2)]


def sum_tiles():
    off, pairs = tile_order(PANELS, PANELS)
    half = len(off) // 2
    return [(off[:half], pairs[0]), (off[half:], pairs[1])]


def fold(tiles, out, change=lambda value: value, where=None):
    upper, equal = diagonal_masks()
    off, pairs = tile_order(tiles.rows, tiles.columns) if where is None else where
    for i, place in enumerate(off):
        out[i * SPAN : (i + 1) * SPAN] = change(tiles(*place)).astype(out.dtype)
    lines = []
    for i, (a, b) in enumerate(pairs):
        second = tiles(b, b)
        at = (len(off) + i) * SPAN
        lower = second.T if tiles.turn else second
        out[at : at + SPAN] = change(jnp.where(upper, tiles(a, a), lower)).astype(out.dtype)
        lines.append(change(jnp.sum(jnp.where(equal, second, 0.0), axis=0, keepdims=True)))
    return lines


class Tiles:
    def __init__(self, ref, rows, columns, turn):
        self.ref, self.rows, self.columns, self.turn = ref, rows, columns, turn

    def __call__(self, i, j):
        return self.ref[i * SPAN : (i + 1) * SPAN, j * SPAN : (j + 1) * SPAN]


def unfold(halves, work):
    upper, equal = diagonal_masks()
    trace = jnp.zeros((1, 1), F32)
    squares = []
    for total, (off, (a, b)) in zip(halves, sum_tiles()):
        for i, (row, column) in enumerate(off):
            work[row * SPAN : (row + 1) * SPAN, column * SPAN : (column + 1) * SPAN] = total[i * SPAN : (i + 1) * SPAN]
        at = len(off) * SPAN
        square = total[at : at + SPAN]
        turned = square.T
        line = jnp.broadcast_to(total[at + SPAN : at + SPAN + 1], (SPAN, SPAN))
        squares.append((a, jnp.where(upper, square, turned)))
        squares.append((b, jnp.where(equal, line, jnp.where(upper, turned, square))))
    for _, square in squares:
        trace = trace + jnp.sum(jnp.where(equal, square, 0.0), axis=(0, 1), keepdims=True)
    damping = trace * (0.1 / BLOCK_W)
    for a, square in squares:
        work[a * SPAN : (a + 1) * SPAN, a * SPAN : (a + 1) * SPAN] = jnp.where(equal, square + damping, square)


def factor_kernel(*refs, start, stop, received):
    width = BLOCK_W - start
    panels = width // SPAN
    step = 32
    groups = step // 8
    per_tile = SPAN // step
    last = stop == BLOCK_W
    given, refs = (refs[:received], refs[received:])
    out, refs = refs[0], refs[1:]
    if not last:
        rest, refs = refs[0], refs[1:]
    work, previous, upper = refs
    if start == 0:
        work[...] = jnp.zeros_like(work)
        halves = [ref[...] for ref in given[:2]]
        if received == 4:
            halves = [mine + ref[...] for mine, ref in zip(halves, given[2:])]
        unfold(halves, work)
    else:
        work[...] = given[0][...]
    previous[...] = jnp.zeros_like(previous)

    def triple(value, first):
        high, low = split(value)
        return jnp.concatenate((high, low, high) if first else (high, high, low), axis=0)

    def superpanel(g, carry):
        row = pl.multiple_of(g * step, step)
        tile_index = g // per_tile
        tile = pl.ds(pl.multiple_of(tile_index * SPAN, SPAN), SPAN)
        turn = lax.rem(SPAN - lax.rem(g, per_tile) * step, SPAN)
        before = previous[...]
        right = triple(before, False)
        near = pltpu.roll(previous[:, tile], turn, 1)
        fresh = lax.dot_general(triple(near, True), right, TN, preferred_element_type=F32)[:step]
        current = work[pl.ds(row, step), :] - fresh
        work[...] = work[...] - lax.dot_general(triple(before, True), right, TN, preferred_element_type=F32)

        square = current[:, :SPAN]
        for k in range(1, panels):
            square = jnp.where(tile_index == k, current[:, k * SPAN : (k + 1) * SPAN], square)
        square = pltpu.roll(square, turn, 1)
        line = lax.broadcasted_iota(jnp.int32, (8, SPAN), 0)
        held = [
            {q: jnp.broadcast_to(square[8 * q : 8 * q + 8, j : j + 1], (8, SPAN)) for q in range(j // 8, groups)}
            for j in range(step)
        ]
        body = [[current[8 * q : 8 * q + 8, k * SPAN : (k + 1) * SPAN] for k in range(panels)] for q in range(groups)]
        scales = [jnp.zeros((8, SPAN), F32) for _ in range(groups)]

        def spread(value, i):
            return jnp.broadcast_to(value[i % 8 : i % 8 + 1], (8, SPAN))

        for i in range(step):
            at = i // 8
            root = lax.rsqrt(spread(held[i][at], i))
            inverse = root * root
            scales[at] = jnp.where(line == i % 8, root, scales[at])
            ratio = {q: held[i][q] * inverse for q in range(at, groups)}
            ratio[at] = jnp.where(line > i % 8, ratio[at], 0.0)
            for j in range(i + 1, step):
                entry = spread(held[i][j // 8], j)
                for q in range(j // 8, groups):
                    held[j][q] = held[j][q] - ratio[q] * entry
            for k in range(panels):
                pivot_row = spread(body[at][k], i)
                for q in range(at, groups):
                    body[q][k] = body[q][k] - ratio[q] * pivot_row
        result = jnp.concatenate(
            [jnp.concatenate([body[q][k] * scales[q] for k in range(panels)], axis=1) for q in range(groups)], axis=0
        )
        across = lax.broadcasted_iota(jnp.int32, (step, width), 1)
        down = lax.broadcasted_iota(jnp.int32, (step, width), 0)
        result = jnp.where(across >= down + row, result, 0.0)
        previous[...] = result
        upper[pl.ds(row, step), :] = result
        return carry

    lax.fori_loop(0, (stop - start) // step, superpanel, 0)
    if not last:
        done = stop - start
        before = previous[...]
        final = lax.dot_general(
            triple(before[:, done:], True), triple(before[:, done:], False), TN, preferred_element_type=F32
        )
        rest[...] = work[done:, done:] - final
    write_coded(Tiles(upper, (stop - start) // SPAN, panels, True), out)


def whiten_kernel(order, *refs, blocks, starts, first, chunks, aliased):
    count = len(starts)
    u_refs, refs = refs[: blocks * count], refs[blocks * count :]
    w_refs, refs = refs[:chunks], refs[chunks + aliased :]
    lowest = starts[0]
    out, left, ready, sems = refs
    half = BLOCK_W // 2
    chunk = ready.shape[2] // chunks
    step = pl.program_id(0)

    def copy(number, which, c):
        slot = lax.rem(number * count + which, 2)
        columns = pl.ds(c * chunk, chunk)
        return pltpu.make_async_copy(
            ready.at[slot, :, columns],
            out.at[order[first + number], pl.ds(starts[which], half), columns],
            sems.at[slot, c],
        )

    for which, start in enumerate(starts):
        width = BLOCK_W - start
        for b in range(blocks):

            @pl.when(step == b)
            def _(b=b):
                tiles = read_coded(u_refs[b * count + which], width // SPAN)
                for row in range(half // SPAN):
                    rows = slice(row * SPAN, (row + 1) * SPAN)
                    for column in range(width // SPAN):
                        value = tiles[row, column] if column >= row else jnp.zeros((SPAN, SPAN), F32)
                        high, low = split(value)
                        columns = slice(column * SPAN, (column + 1) * SPAN)
                        left[rows, columns] = high
                        left[half + row * SPAN : half + (row + 1) * SPAN, columns] = low

        for c in range(chunks):
            if count == 1:

                @pl.when(step >= 2)
                def _(c=c):
                    copy(step - 2, which, c).wait()

            elif blocks > 1:

                @pl.when(step >= 1)
                def _(c=c):
                    copy(step - 1, which, c).wait()

            weight = w_refs[c][:, start - lowest :]
            product = lax.dot_general(left[:, :width], weight, NT, preferred_element_type=F32)
            ready[lax.rem(step * count + which, 2), :, c * chunk : (c + 1) * chunk] = product[:half] + product[half:]
            copy(step, which, c).start()

    @pl.when(step == blocks - 1)
    def _():
        for c in range(chunks):
            if count > 1:
                copy(step, 0, c).wait()
            elif blocks > 1:
                copy(step - 1, 0, c).wait()
            copy(step, count - 1, c).wait()


def shards(query_rows, key_rows, placed_value_rows, doc_lengths, span_order, out_weight):
    tokens = query_rows.shape[1]
    features = out_weight.shape[0]
    seq = lax.axis_size("seq")
    ring = lax.axis_size("dp")
    chips = seq // 2
    spans = tokens // SPAN
    all_spans = spans * seq
    documents = doc_lengths.shape[1]
    per = KEY_VALUE_HEADS // seq
    blocks = NB // seq
    own = lax.axis_index("seq").astype(jnp.int32)
    place = lax.axis_index("dp").astype(jnp.int32)
    query, key, value = query_rows[0], key_rows[0], placed_value_rows[0]
    vmem = pl.BlockSpec(memory_space=pltpu.VMEM)
    anywhere = pl.BlockSpec(memory_space=pl.ANY)
    in_ring = blocks == ring

    if in_ring:
        turns = [lax.rem(place + 2 * ring - 1 - t, ring) for t in range(blocks)]
    else:
        turns = [jnp.int32(t) for t in range(blocks)]
    first_kv = turns[0] // KV_BLOCKS

    def moved(distance, cross):
        return [
            (x * 2 + c, (x + distance) % chips * 2 + (1 - c if cross else c)) for x in range(chips) for c in range(2)
        ]

    def cut(targets, columns, scalars, name, after=(), limit=OTHER_VMEM):
        specs, arrays = [], []
        for target in targets:
            for array, size, index in columns:
                specs.append(
                    pl.BlockSpec((tokens, size), lambda i, meta, target=target, index=index: (0, index(target(meta), meta)))
                )
                arrays.append(array)
        width = sum(size for _, size, _ in columns)
        return pl.pallas_call(
            functools.partial(cut_kernel, targets=len(targets), given=len(columns)),
            out_shape=[jax.ShapeDtypeStruct((tokens, width), BF16)] * len(targets),
            grid_spec=pltpu.PrefetchScalarGridSpec(
                num_scalar_prefetch=1,
                grid=(1,),
                in_specs=specs + [anywhere] * len(after),
                out_specs=[pl.BlockSpec((tokens, width), lambda i, meta: (0, 0))] * len(targets),
            ),
            compiler_params=params(limit),
            cost_estimate=cost(0, 2**21),
            name=name,
        )(scalars, *arrays, *after)

    tile = 512

    def target_at(distance, cross):
        return lambda meta: lax.rem(meta[0] // 2 + distance, chips) * 2 + lax.rem(lax.rem(meta[0], 2) + cross, 2)

    far = [(distance, cross) for distance in range(1, chips) for cross in range(2)]
    pieces = []

    most = all_spans // 2 + 1

    def grams_of(t):
        kv = turns[t] // KV_BLOCKS
        carriers = pieces[: min(t + 1, per)]
        which = jnp.where(kv == first_kv, 0, 1).astype(jnp.int32)
        meta = jnp.concatenate([jnp.stack([own, turns[t], kv, which]), doc_lengths[0], span_order[0]])
        folded = jax.ShapeDtypeStruct((SUM_ROWS, SPAN), F32)
        peer_kv = blocks * BLOCK_W // HEAD_SIZE
        return pl.pallas_call(
            functools.partial(
                attention_kernel,
                chips=chips, spans=spans, all_spans=all_spans, documents=documents, most=most, sets=len(carriers),
            ),
            out_shape=[folded] * 2,
            grid_spec=pltpu.PrefetchScalarGridSpec(
                num_scalar_prefetch=1,
                grid=(1,),
                in_specs=[
                    pl.BlockSpec((tokens, BLOCK_W), lambda i, meta: (0, meta[0] * blocks + meta[1])),
                    pl.BlockSpec((tokens, BLOCK_W), lambda i, meta: (0, meta[1])),
                ]
                + [pl.BlockSpec((tokens, BLOCK_W), lambda i, meta: (0, 0))] * len(far)
                + [pl.BlockSpec((tokens, HEAD_SIZE), lambda i, meta: (0, meta[0] * per + meta[2]))] * 2
                + [
                    pl.BlockSpec((tokens, HEAD_SIZE), lambda i, meta: (0, peer_kv + meta[2])),
                    pl.BlockSpec((tokens, HEAD_SIZE), lambda i, meta: (0, peer_kv + per + meta[2])),
                ]
                + [pl.BlockSpec((tokens, 2 * HEAD_SIZE), lambda i, meta: (0, BLOCK_W // (2 * HEAD_SIZE)))]
                * (len(carriers) * len(far)),
                out_specs=[pl.BlockSpec((SUM_ROWS, SPAN), lambda i, meta: (0, 0))] * 2,
                scratch_shapes=[
                    pltpu.VMEM((all_spans, BLOCK_HEADS * SPAN, HEAD_SIZE), BF16),
                    pltpu.VMEM((all_spans, SPAN, HEAD_SIZE), BF16),
                    pltpu.VMEM((all_spans, HEAD_SIZE, SPAN), BF16),
                    pltpu.SMEM((all_spans,), jnp.int32),
                    pltpu.VMEM((2, most * SPAN, SPAN), F32),
                    pltpu.VMEM((2, BLOCK_W, all_spans * SPAN), BF16),
                    pltpu.VMEM((BLOCK_W, BLOCK_W), F32),
                ],
            ),
            compiler_params=params(ATTENTION_VMEM),
            cost_estimate=cost(1.4e10, 2**20),
            name="attention_outer_products",
        )(meta, query, peer, *pieces[t], key, value, peer, peer, *[a for carrier in carriers for a in carrier])

    grams = []
    held = []
    swapped = [lax.ppermute(array, "seq", moved(0, 1)) for array in (query, key, value)]
    widths = (blocks * BLOCK_W, per * HEAD_SIZE, per * HEAD_SIZE)
    columns = [(array, width, lambda target, meta: target) for array, width in zip(swapped, widths)]
    peer = cut([lambda meta: meta[0]], columns, own[None], "cut_peer")[0]
    for t in range(blocks + 1):
        if t < blocks:
            kv = first_kv if t == 0 else per - 1 - first_kv
            columns = [(query, BLOCK_W, lambda target, meta: target * blocks + meta[1])]
            if t < per:
                columns += [(array, HEAD_SIZE, lambda target, meta: target * per + meta[2]) for array in (key, value)]
            scalars = jnp.stack([own, turns[t], kv])
            after = [] if t == 0 else swapped[1:2]
            parts = cut(
                [target_at(*where) for where in far], columns, scalars, "cut_piece", after,
                OTHER_VMEM if t else FULL_VMEM,
            )
            if t > 1:
                *parts, held[t - 2] = lax.optimization_barrier((*parts, held[t - 2]))
            pieces.append([lax.ppermute(part, "seq", moved(*where)) for part, where in zip(parts, far)])
        if t == 0:
            continue
        done = t - 1
        grams.append(grams_of(done))
        if done == 0 or not in_ring:
            held.append(grams[done])
        else:
            held.append([mine + theirs for mine, theirs in zip(grams[done], carried)] if done < ring - 1 else None)
        if in_ring and done < ring - 1:
            carried = [lax.ppermute(part, "dp", [(z, (z + 1) % ring) for z in range(ring)]) for part in held[done]]

    half = BLOCK_W // 2
    top_rows, bottom_rows = [
        SPAN * (sum(len(part) for part in tile_order(2, columns))) + 16 for columns in (PANELS, PANELS // 2)
    ]
    scratch = lambda width: [pltpu.VMEM((width, width), F32), pltpu.VMEM((32, width), F32), pltpu.VMEM((half, width), F32)]

    def factor_top(*given):
        return pl.pallas_call(
            functools.partial(factor_kernel, start=0, stop=half, received=len(given)),
            out_shape=[
                jax.ShapeDtypeStruct((top_rows, SPAN), BF16),
                jax.ShapeDtypeStruct((half, half), F32),
            ],
            in_specs=[vmem] * len(given),
            out_specs=[vmem] * 2,
            scratch_shapes=scratch(BLOCK_W),
            compiler_params=params(OTHER_VMEM),
            cost_estimate=cost(1.0e10, 2**20),
            name="factor_top",
        )(*given)

    def factor_bottom(rest):
        return pl.pallas_call(
            functools.partial(factor_kernel, start=half, stop=BLOCK_W, received=1),
            out_shape=jax.ShapeDtypeStruct((bottom_rows, SPAN), BF16),
            in_specs=[vmem],
            out_specs=vmem,
            scratch_shapes=scratch(half),
            compiler_params=params(OTHER_VMEM),
            cost_estimate=cost(0.9e10, 2**20),
            name="factor_bottom",
        )(rest)

    if in_ring:
        top, rest = factor_top(*grams[ring - 1], *carried)

        paired = ring & (ring - 1) == 0
        distances = [1] + list(range(ring - 1, 1, -1)) if paired else list(range(1, ring))

        def partner(z, d):
            return z ^ d if paired else (z + d) % ring

        def shared(array):
            return [array] + [
                lax.ppermute(array, "dp", [(z, partner(z, d)) for z in range(ring)]) for d in distances
            ]

        tops = shared(top)
        bottom = factor_bottom(rest)
        bottoms = shared(bottom)
        order = jnp.stack([place] + [place ^ d if paired else lax.rem(place - d + ring, ring) for d in distances])
    else:
        halves = [factor_top(*[lax.psum(part, "dp") for part in grams[t]]) for t in range(blocks)]
        tops = [top for top, _ in halves]
        bottoms = [factor_bottom(rest) for _, rest in halves]
        order = jnp.arange(blocks, dtype=jnp.int32)


    def whiten(uppers, first, starts, result):
        more = [] if result is None else [result]
        depth = BLOCK_W - starts[0]
        chunks = features // tile
        weights = [
            pl.BlockSpec(
                (tile, depth),
                lambda b, order, c=c: (c, order[first + b] * (BLOCK_W // depth) + starts[0] // depth),
            )
            for c in range(chunks)
        ]
        count = len(uppers) // len(starts)
        return pl.pallas_call(
            functools.partial(
                whiten_kernel, blocks=count, starts=starts, first=first, chunks=chunks, aliased=len(more)
            ),
            out_shape=jax.ShapeDtypeStruct((blocks, BLOCK_W, features), F32),
            grid_spec=pltpu.PrefetchScalarGridSpec(
                num_scalar_prefetch=1,
                grid=(count,),
                in_specs=[vmem] * len(uppers) + weights + [anywhere] * len(more),
                out_specs=anywhere,
                scratch_shapes=[
                    pltpu.VMEM((2 * half, depth), BF16),
                    pltpu.VMEM((2, half, features), F32),
                    pltpu.SemaphoreType.DMA((2, chunks)),
                ],
            ),
            input_output_aliases={1 + len(uppers) + chunks: 0} if more else {},
            compiler_params=params(WHITEN_VMEM),
            cost_estimate=cost(2.0e9 * len(uppers), 2**20),
            name="whiten_bottom" if starts[0] else "whiten_top",
        )(order, *uppers, *[out_weight] * chunks, *more)

    result = whiten([tops[0], bottoms[0]], 0, (0, half), None)
    result = whiten(tops[1:2], 1, (0,), result)
    result = whiten(bottoms[1:2], 1, (half,), result)
    if blocks > 2:
        rest = [half_block for pair in zip(tops[2:], bottoms[2:]) for half_block in pair]
        result = whiten(rest, 2, (0, half), result)
    return result


def solution(mesh):
    in_specs = (
        P(("groups", "dp"), "seq", None),
        P(("groups", "dp"), "seq", None),
        P(("groups", "dp"), "seq", None),
        P(("groups", "dp"), None),
        P(("groups", "dp"), None),
        P("dp", "seq"),
    )
    out_specs = P(("groups", "seq"), None, "dp")
    return jax.shard_map(shards, mesh=mesh, in_specs=in_specs, out_specs=out_specs, check_vma=False)
```

```python
import functools
import math

import jax
import jax.numpy as jnp
from jax import lax
from jax.experimental import pallas as pl
from jax.experimental.pallas import tpu as pltpu
from jax.sharding import PartitionSpec as P

QUERY_HEADS = 64
KEY_VALUE_HEADS = 8
HEAD_SIZE = 128
BLOCK_W = 512
NB = 16
SPAN = 128
GROUP = QUERY_HEADS // KEY_VALUE_HEADS
BLOCK_HEADS = BLOCK_W // HEAD_SIZE
KV_BLOCKS = GROUP // BLOCK_HEADS
PANELS = BLOCK_W // SPAN
SUM_ROWS = SPAN * PANELS + 8
VMEM_BYTES = 50 * 2**20
FULL_VMEM = 63 * 2**20
ATTENTION_VMEM = 44 * 2**20
WHITEN_VMEM = 44 * 2**20
OTHER_VMEM = 44 * 2**20
F32 = jnp.float32
BF16 = jnp.bfloat16
NT = (((1,), (1,)), ((), ()))
TN = (((0,), (0,)), ((), ()))


def params(limit=OTHER_VMEM):
    return pltpu.CompilerParams(vmem_limit_bytes=limit)


def cost(flops, moved, trans=0):
    return pl.CostEstimate(flops=int(flops), bytes_accessed=int(moved), transcendentals=int(trans))


def encode(value, exponent):
    scaled = value * jnp.exp2(15.0 - exponent)
    power = scaled * scaled
    power = power * power
    power = power * power
    return jnp.where(scaled < 0.0, -power, power)


def decode(code, exponent):
    code = code.astype(F32)
    quarter = lax.rsqrt(lax.rsqrt(jnp.maximum(jnp.abs(code), 1e-37)))
    root = quarter * lax.rsqrt(quarter) * jnp.exp2(exponent - 15.0)
    return jnp.where(code < 0.0, -root, root)


def exponent_of(largest):
    return jnp.ceil(jnp.log(jnp.maximum(largest, 1e-30)) * (1.0 / math.log(2.0)) + 0.001)


def write_coded(tiles, out):
    off, pairs = tile_order(tiles.rows, tiles.columns)
    places = off + [(i, i) for i in range(tiles.rows)]
    largest = functools.reduce(jnp.maximum, [jnp.max(jnp.abs(tiles(*p)), axis=(0, 1), keepdims=True) for p in places])
    exponent = exponent_of(largest)
    (line,) = fold(tiles, out, lambda value: encode(value, exponent))
    row = lax.broadcasted_iota(jnp.int32, (16, SPAN), 0)
    out[(len(off) + len(pairs)) * SPAN :] = jnp.where(row < 8, line, exponent).astype(BF16)


def read_coded(ref, columns):
    upper, equal = diagonal_masks()
    off, pairs = tile_order(2, columns)
    at = (len(off) + len(pairs)) * SPAN
    tail = ref[at:].astype(F32)
    exponent = tail[15:16, 0:1]
    tiles = {place: decode(ref[i * SPAN : (i + 1) * SPAN], exponent) for i, place in enumerate(off)}
    square = decode(ref[at - SPAN : at], exponent)
    line = decode(tail[0:1], exponent)
    tiles[0, 0] = jnp.where(upper, square, 0.0)
    tiles[1, 1] = jnp.where(equal, line, jnp.where(upper, square.T, 0.0))
    return tiles


def split(value):
    high = value.astype(BF16)
    return high, (value - high.astype(F32)).astype(BF16)


def cut_kernel(meta, *refs, targets, given):
    outs = refs[-targets:]
    for number, out in enumerate(outs):
        at = 0
        for ref in refs[number * given : (number + 1) * given]:
            out[:, at : at + ref.shape[1]] = ref[...]
            at += ref.shape[1]


def attention_kernel(meta, *refs, chips, spans, all_spans, documents, most, sets):
    sources = 2 * chips
    near = sources + 4
    query_refs, near_refs = refs[:sources], refs[sources:near]
    far_refs = refs[near : near + sets * (sources - 2)]
    top, bottom, queries, keys, values, slots, limits, left, total = refs[near + sets * (sources - 2) :]
    own = meta[0]
    chip, core = own // 2, lax.rem(own, 2)
    lengths = 4
    order = lengths + documents

    for r in range(all_spans):
        device = r // spans
        distance = lax.rem(chip - device // 2 + chips, chips)
        cross = lax.rem(core + device % 2, 2)
        slots[meta[order + r]] = (distance * 2 + cross) * spans + r % spans

    def place_kv(source, key_part, value_part):
        for t in range(spans):
            rows = slice(t * SPAN, (t + 1) * SPAN)
            keys[source * spans + t] = key_part[rows]
            values[source * spans + t] = value_part[rows].astype(F32).T.astype(BF16)

    place_kv(0, near_refs[0], near_refs[1])
    place_kv(1, near_refs[2], near_refs[3])
    for which in range(sets):

        @pl.when(meta[3] == which)
        def _(which=which):
            for source in range(2, sources):
                ref = far_refs[which * (sources - 2) + source - 2]
                place_kv(source, ref[:, :HEAD_SIZE], ref[:, HEAD_SIZE:])

    for source in range(sources):
        for t in range(spans):
            for h in range(BLOCK_HEADS):
                queries[source * spans + t, h * SPAN : (h + 1) * SPAN] = query_refs[source][
                    t * SPAN : (t + 1) * SPAN, h * HEAD_SIZE : (h + 1) * HEAD_SIZE
                ]

    factor = HEAD_SIZE ** (-0.5) / math.log(2.0)

    def place_of(q):
        source = q // spans
        distance, cross = source // 2, lax.rem(source, 2)
        device = lax.rem(chip - distance + chips, chips) * 2 + lax.rem(core + cross, 2)
        position = meta[order + device * spans + lax.rem(q, spans)]
        first_row = position * SPAN
        begin = jnp.int32(0)
        at = jnp.int32(0)
        query_pos = lax.broadcasted_iota(jnp.int32, (1, SPAN), 1) + first_row
        query_begin = jnp.zeros((1, SPAN), jnp.int32)
        for d in range(documents):
            begin = jnp.where(at <= first_row, at, begin)
            query_begin = jnp.where(query_pos >= at, at, query_begin)
            at = at + meta[lengths + d]
        return position, query_pos, query_begin, position - begin // SPAN + 1

    def one_pair(p, carry):
        pair = [(which, 2 * p + which, place_of(2 * p + which)) for which in range(2)]
        count = jnp.maximum(pair[0][2][3], pair[1][2][3])

        for n in range(1, most + 1):

            @pl.when(count == n)
            def _(n=n):
                for which, q, (position, query_pos, query_begin, _) in pair:
                    lanes = pl.ds(pl.multiple_of(q * SPAN, SPAN), SPAN)
                    held = [slots[jnp.maximum(position - n + 1 + i, 0)] for i in range(n)]
                    for i in range(n):
                        key_pos = lax.broadcasted_iota(jnp.int32, (SPAN, SPAN), 0) + (position - n + 1 + i) * SPAN
                        seen = (key_pos <= query_pos) & (key_pos >= query_begin)
                        limits[which, i * SPAN : (i + 1) * SPAN] = jnp.where(seen, 3e38, -1e30)
                    key_part = jnp.concatenate([keys[slot] for slot in held], axis=0)
                    value_part = jnp.concatenate([values[slot] for slot in held], axis=1)
                    scores = lax.dot_general(key_part, queries[q], NT, preferred_element_type=F32)
                    limit = limits[which, : n * SPAN]
                    scores = jnp.minimum(scores, jnp.concatenate([limit] * BLOCK_HEADS, axis=1))
                    largest = jnp.max(scores, axis=0, keepdims=True)
                    lifted = jnp.exp2((scores - largest) * factor)
                    summed = jnp.sum(lifted, axis=0, keepdims=True)
                    weights = (lifted * (1.0 / summed)).astype(BF16)
                    mixed = jnp.dot(value_part, weights, preferred_element_type=F32)
                    for h in range(BLOCK_HEADS):
                        one_head = mixed[:, h * SPAN : (h + 1) * SPAN]
                        columns = slice(h * HEAD_SIZE, (h + 1) * HEAD_SIZE)
                        high, low = split(one_head)
                        left[0, columns, lanes] = high
                        left[1, columns, lanes] = low

        return carry

    lax.fori_loop(0, all_spans // 2, one_pair, 0)

    half = BLOCK_W // 2
    total[...] = jnp.zeros_like(total)

    def one_pass(i, carry):
        a, b = lax.rem(i, 2), i // 2
        total[:half] += lax.dot_general(left[a, :half], left[b], NT, preferred_element_type=F32)
        total[half:, half:] += lax.dot_general(left[a, half:], left[b, half:], NT, preferred_element_type=F32)
        return carry

    lax.fori_loop(0, 3, one_pass, 0)
    for out, where in zip((top, bottom), sum_tiles()):
        off, pair = where
        (line,) = fold(Tiles(total, PANELS, PANELS, False), out, where=(off, [pair]))
        out[SUM_ROWS - 8 :] = jnp.broadcast_to(line, (8, SPAN))


def diagonal_masks():
    rows = lax.broadcasted_iota(jnp.int32, (SPAN, SPAN), 0)
    columns = lax.broadcasted_iota(jnp.int32, (SPAN, SPAN), 1)
    return rows <= columns, rows == columns


def tile_order(rows, columns):
    off = [(i, j) for i in range(rows) for j in range(i + 1, columns)]
    return off, [(i, i + 1) for i in range(0, rows, 2)]


def sum_tiles():
    off, pairs = tile_order(PANELS, PANELS)
    half = len(off) // 2
    return [(off[:half], pairs[0]), (off[half:], pairs[1])]


def fold(tiles, out, change=lambda value: value, where=None):
    upper, equal = diagonal_masks()
    off, pairs = tile_order(tiles.rows, tiles.columns) if where is None else where
    for i, place in enumerate(off):
        out[i * SPAN : (i + 1) * SPAN] = change(tiles(*place)).astype(out.dtype)
    lines = []
    for i, (a, b) in enumerate(pairs):
        second = tiles(b, b)
        at = (len(off) + i) * SPAN
        lower = second.T if tiles.turn else second
        out[at : at + SPAN] = change(jnp.where(upper, tiles(a, a), lower)).astype(out.dtype)
        lines.append(change(jnp.sum(jnp.where(equal, second, 0.0), axis=0, keepdims=True)))
    return lines


class Tiles:
    def __init__(self, ref, rows, columns, turn):
        self.ref, self.rows, self.columns, self.turn = ref, rows, columns, turn

    def __call__(self, i, j):
        return self.ref[i * SPAN : (i + 1) * SPAN, j * SPAN : (j + 1) * SPAN]


def unfold(halves, work):
    upper, equal = diagonal_masks()
    trace = jnp.zeros((1, 1), F32)
    squares = []
    for total, (off, (a, b)) in zip(halves, sum_tiles()):
        for i, (row, column) in enumerate(off):
            work[row * SPAN : (row + 1) * SPAN, column * SPAN : (column + 1) * SPAN] = total[i * SPAN : (i + 1) * SPAN]
        at = len(off) * SPAN
        square = total[at : at + SPAN]
        turned = square.T
        line = jnp.broadcast_to(total[at + SPAN : at + SPAN + 1], (SPAN, SPAN))
        squares.append((a, jnp.where(upper, square, turned)))
        squares.append((b, jnp.where(equal, line, jnp.where(upper, turned, square))))
    for _, square in squares:
        trace = trace + jnp.sum(jnp.where(equal, square, 0.0), axis=(0, 1), keepdims=True)
    damping = trace * (0.1 / BLOCK_W)
    for a, square in squares:
        work[a * SPAN : (a + 1) * SPAN, a * SPAN : (a + 1) * SPAN] = jnp.where(equal, square + damping, square)


def factor_kernel(*refs, start, stop, received):
    width = BLOCK_W - start
    panels = width // SPAN
    step = 32
    groups = step // 8
    per_tile = SPAN // step
    last = stop == BLOCK_W
    given, refs = (refs[:received], refs[received:])
    out, refs = refs[0], refs[1:]
    if not last:
        rest, refs = refs[0], refs[1:]
    work, previous, upper = refs
    if start == 0:
        work[...] = jnp.zeros_like(work)
        halves = [ref[...] for ref in given[:2]]
        if received == 4:
            halves = [mine + ref[...] for mine, ref in zip(halves, given[2:])]
        unfold(halves, work)
    else:
        work[...] = given[0][...]
    previous[...] = jnp.zeros_like(previous)

    def triple(value, first):
        high, low = split(value)
        return jnp.concatenate((high, low, high) if first else (high, high, low), axis=0)

    def superpanel(g, carry):
        row = pl.multiple_of(g * step, step)
        tile_index = g // per_tile
        tile = pl.ds(pl.multiple_of(tile_index * SPAN, SPAN), SPAN)
        turn = lax.rem(SPAN - lax.rem(g, per_tile) * step, SPAN)
        before = previous[...]
        right = triple(before, False)
        near = pltpu.roll(previous[:, tile], turn, 1)
        fresh = lax.dot_general(triple(near, True), right, TN, preferred_element_type=F32)[:step]
        current = work[pl.ds(row, step), :] - fresh
        work[...] = work[...] - lax.dot_general(triple(before, True), right, TN, preferred_element_type=F32)

        square = current[:, :SPAN]
        for k in range(1, panels):
            square = jnp.where(tile_index == k, current[:, k * SPAN : (k + 1) * SPAN], square)
        square = pltpu.roll(square, turn, 1)
        line = lax.broadcasted_iota(jnp.int32, (8, SPAN), 0)
        held = [
            {q: jnp.broadcast_to(square[8 * q : 8 * q + 8, j : j + 1], (8, SPAN)) for q in range(j // 8, groups)}
            for j in range(step)
        ]
        body = [[current[8 * q : 8 * q + 8, k * SPAN : (k + 1) * SPAN] for k in range(panels)] for q in range(groups)]
        scales = [jnp.zeros((8, SPAN), F32) for _ in range(groups)]

        def spread(value, i):
            return jnp.broadcast_to(value[i % 8 : i % 8 + 1], (8, SPAN))

        for i in range(step):
            at = i // 8
            root = lax.rsqrt(spread(held[i][at], i))
            inverse = root * root
            scales[at] = jnp.where(line == i % 8, root, scales[at])
            ratio = {q: held[i][q] * inverse for q in range(at, groups)}
            ratio[at] = jnp.where(line > i % 8, ratio[at], 0.0)
            for j in range(i + 1, step):
                entry = spread(held[i][j // 8], j)
                for q in range(j // 8, groups):
                    held[j][q] = held[j][q] - ratio[q] * entry
            for k in range(panels):
                pivot_row = spread(body[at][k], i)
                for q in range(at, groups):
                    body[q][k] = body[q][k] - ratio[q] * pivot_row
        result = jnp.concatenate(
            [jnp.concatenate([body[q][k] * scales[q] for k in range(panels)], axis=1) for q in range(groups)], axis=0
        )
        across = lax.broadcasted_iota(jnp.int32, (step, width), 1)
        down = lax.broadcasted_iota(jnp.int32, (step, width), 0)
        result = jnp.where(across >= down + row, result, 0.0)
        previous[...] = result
        upper[pl.ds(row, step), :] = result
        return carry

    lax.fori_loop(0, (stop - start) // step, superpanel, 0)
    if not last:
        done = stop - start
        before = previous[...]
        final = lax.dot_general(
            triple(before[:, done:], True), triple(before[:, done:], False), TN, preferred_element_type=F32
        )
        rest[...] = work[done:, done:] - final
    write_coded(Tiles(upper, (stop - start) // SPAN, panels, True), out)


def whiten_kernel(order, *refs, blocks, starts, first, chunks, aliased):
    count = len(starts)
    u_refs, refs = refs[: blocks * count], refs[blocks * count :]
    w_refs, refs = refs[:chunks], refs[chunks + aliased :]
    lowest = starts[0]
    out, left, ready, sems = refs
    half = BLOCK_W // 2
    chunk = ready.shape[2] // chunks
    step = pl.program_id(0)

    def copy(number, which, c):
        slot = lax.rem(number * count + which, 2)
        columns = pl.ds(c * chunk, chunk)
        return pltpu.make_async_copy(
            ready.at[slot, :, columns],
            out.at[order[first + number], pl.ds(starts[which], half), columns],
            sems.at[slot, c],
        )

    for which, start in enumerate(starts):
        width = BLOCK_W - start
        for b in range(blocks):

            @pl.when(step == b)
            def _(b=b):
                tiles = read_coded(u_refs[b * count + which], width // SPAN)
                for row in range(half // SPAN):
                    rows = slice(row * SPAN, (row + 1) * SPAN)
                    for column in range(width // SPAN):
                        value = tiles[row, column] if column >= row else jnp.zeros((SPAN, SPAN), F32)
                        high, low = split(value)
                        columns = slice(column * SPAN, (column + 1) * SPAN)
                        left[rows, columns] = high
                        left[half + row * SPAN : half + (row + 1) * SPAN, columns] = low

        for c in range(chunks):
            if count == 1:

                @pl.when(step >= 2)
                def _(c=c):
                    copy(step - 2, which, c).wait()

            elif blocks > 1:

                @pl.when(step >= 1)
                def _(c=c):
                    copy(step - 1, which, c).wait()

            weight = w_refs[c][:, start - lowest :]
            product = lax.dot_general(left[:, :width], weight, NT, preferred_element_type=F32)
            ready[lax.rem(step * count + which, 2), :, c * chunk : (c + 1) * chunk] = product[:half] + product[half:]
            copy(step, which, c).start()

    @pl.when(step == blocks - 1)
    def _():
        for c in range(chunks):
            if count > 1:
                copy(step, 0, c).wait()
            elif blocks > 1:
                copy(step - 1, 0, c).wait()
            copy(step, count - 1, c).wait()


def shards(query_rows, key_rows, placed_value_rows, doc_lengths, span_order, out_weight):
    tokens = query_rows.shape[1]
    features = out_weight.shape[0]
    seq = lax.axis_size("seq")
    ring = lax.axis_size("dp")
    chips = seq // 2
    spans = tokens // SPAN
    all_spans = spans * seq
    documents = doc_lengths.shape[1]
    per = KEY_VALUE_HEADS // seq
    blocks = NB // seq
    own = lax.axis_index("seq").astype(jnp.int32)
    place = lax.axis_index("dp").astype(jnp.int32)
    query, key, value = query_rows[0], key_rows[0], placed_value_rows[0]
    vmem = pl.BlockSpec(memory_space=pltpu.VMEM)
    anywhere = pl.BlockSpec(memory_space=pl.ANY)
    in_ring = blocks == ring

    if in_ring:
        turns = [lax.rem(place + 2 * ring - 1 - t, ring) for t in range(blocks)]
    else:
        turns = [jnp.int32(t) for t in range(blocks)]
    first_kv = turns[0] // KV_BLOCKS

    def moved(distance, cross):
        return [
            (x * 2 + c, (x + distance) % chips * 2 + (1 - c if cross else c)) for x in range(chips) for c in range(2)
        ]

    def cut(targets, columns, scalars, name, after=(), limit=OTHER_VMEM):
        specs, arrays = [], []
        for target in targets:
            for array, size, index in columns:
                specs.append(
                    pl.BlockSpec((tokens, size), lambda i, meta, target=target, index=index: (0, index(target(meta), meta)))
                )
                arrays.append(array)
        width = sum(size for _, size, _ in columns)
        return pl.pallas_call(
            functools.partial(cut_kernel, targets=len(targets), given=len(columns)),
            out_shape=[jax.ShapeDtypeStruct((tokens, width), BF16)] * len(targets),
            grid_spec=pltpu.PrefetchScalarGridSpec(
                num_scalar_prefetch=1,
                grid=(1,),
                in_specs=specs + [anywhere] * len(after),
                out_specs=[pl.BlockSpec((tokens, width), lambda i, meta: (0, 0))] * len(targets),
            ),
            compiler_params=params(limit),
            cost_estimate=cost(0, 2**21),
            name=name,
        )(scalars, *arrays, *after)

    tile = 512

    def target_at(distance, cross):
        return lambda meta: lax.rem(meta[0] // 2 + distance, chips) * 2 + lax.rem(lax.rem(meta[0], 2) + cross, 2)

    far = [(distance, cross) for distance in range(1, chips) for cross in range(2)]
    pieces = []

    most = all_spans // 2 + 1

    def grams_of(t):
        kv = turns[t] // KV_BLOCKS
        carriers = pieces[: min(t + 1, per)]
        which = jnp.where(kv == first_kv, 0, 1).astype(jnp.int32)
        meta = jnp.concatenate([jnp.stack([own, turns[t], kv, which]), doc_lengths[0], span_order[0]])
        folded = jax.ShapeDtypeStruct((SUM_ROWS, SPAN), F32)
        peer_kv = blocks * BLOCK_W // HEAD_SIZE
        return pl.pallas_call(
            functools.partial(
                attention_kernel,
                chips=chips, spans=spans, all_spans=all_spans, documents=documents, most=most, sets=len(carriers),
            ),
            out_shape=[folded] * 2,
            grid_spec=pltpu.PrefetchScalarGridSpec(
                num_scalar_prefetch=1,
                grid=(1,),
                in_specs=[
                    pl.BlockSpec((tokens, BLOCK_W), lambda i, meta: (0, meta[0] * blocks + meta[1])),
                    pl.BlockSpec((tokens, BLOCK_W), lambda i, meta: (0, meta[1])),
                ]
                + [pl.BlockSpec((tokens, BLOCK_W), lambda i, meta: (0, 0))] * len(far)
                + [pl.BlockSpec((tokens, HEAD_SIZE), lambda i, meta: (0, meta[0] * per + meta[2]))] * 2
                + [
                    pl.BlockSpec((tokens, HEAD_SIZE), lambda i, meta: (0, peer_kv + meta[2])),
                    pl.BlockSpec((tokens, HEAD_SIZE), lambda i, meta: (0, peer_kv + per + meta[2])),
                ]
                + [pl.BlockSpec((tokens, 2 * HEAD_SIZE), lambda i, meta: (0, BLOCK_W // (2 * HEAD_SIZE)))]
                * (len(carriers) * len(far)),
                out_specs=[pl.BlockSpec((SUM_ROWS, SPAN), lambda i, meta: (0, 0))] * 2,
                scratch_shapes=[
                    pltpu.VMEM((all_spans, BLOCK_HEADS * SPAN, HEAD_SIZE), BF16),
                    pltpu.VMEM((all_spans, SPAN, HEAD_SIZE), BF16),
                    pltpu.VMEM((all_spans, HEAD_SIZE, SPAN), BF16),
                    pltpu.SMEM((all_spans,), jnp.int32),
                    pltpu.VMEM((2, most * SPAN, SPAN), F32),
                    pltpu.VMEM((2, BLOCK_W, all_spans * SPAN), BF16),
                    pltpu.VMEM((BLOCK_W, BLOCK_W), F32),
                ],
            ),
            compiler_params=params(ATTENTION_VMEM),
            cost_estimate=cost(1.4e10, 2**20),
            name="attention_outer_products",
        )(meta, query, peer, *pieces[t], key, value, peer, peer, *[a for carrier in carriers for a in carrier])

    grams = []
    held = []
    swapped = [lax.ppermute(array, "seq", moved(0, 1)) for array in (query, key, value)]
    widths = (blocks * BLOCK_W, per * HEAD_SIZE, per * HEAD_SIZE)
    columns = [(array, width, lambda target, meta: target) for array, width in zip(swapped, widths)]
    peer = cut([lambda meta: meta[0]], columns, own[None], "cut_peer")[0]
    for t in range(blocks + 1):
        if t < blocks:
            kv = first_kv if t == 0 else per - 1 - first_kv
            columns = [(query, BLOCK_W, lambda target, meta: target * blocks + meta[1])]
            if t < per:
                columns += [(array, HEAD_SIZE, lambda target, meta: target * per + meta[2]) for array in (key, value)]
            scalars = jnp.stack([own, turns[t], kv])
            after = [] if t == 0 else swapped[1:2]
            parts = cut(
                [target_at(*where) for where in far], columns, scalars, "cut_piece", after,
                OTHER_VMEM if t else FULL_VMEM,
            )
            if t > 1:
                *parts, held[t - 2] = lax.optimization_barrier((*parts, held[t - 2]))
            pieces.append([lax.ppermute(part, "seq", moved(*where)) for part, where in zip(parts, far)])
        if t == 0:
            continue
        done = t - 1
        grams.append(grams_of(done))
        if done == 0 or not in_ring:
            held.append(grams[done])
        else:
            held.append([mine + theirs for mine, theirs in zip(grams[done], carried)] if done < ring - 1 else None)
        if in_ring and done < ring - 1:
            carried = [lax.ppermute(part, "dp", [(z, (z + 1) % ring) for z in range(ring)]) for part in held[done]]

    half = BLOCK_W // 2
    top_rows, bottom_rows = [
        SPAN * (sum(len(part) for part in tile_order(2, columns))) + 16 for columns in (PANELS, PANELS // 2)
    ]
    scratch = lambda width: [pltpu.VMEM((width, width), F32), pltpu.VMEM((32, width), F32), pltpu.VMEM((half, width), F32)]

    def factor_top(*given):
        return pl.pallas_call(
            functools.partial(factor_kernel, start=0, stop=half, received=len(given)),
            out_shape=[
                jax.ShapeDtypeStruct((top_rows, SPAN), BF16),
                jax.ShapeDtypeStruct((half, half), F32),
            ],
            in_specs=[vmem] * len(given),
            out_specs=[vmem] * 2,
            scratch_shapes=scratch(BLOCK_W),
            compiler_params=params(OTHER_VMEM),
            cost_estimate=cost(1.0e10, 2**20),
            name="factor_top",
        )(*given)

    def factor_bottom(rest):
        return pl.pallas_call(
            functools.partial(factor_kernel, start=half, stop=BLOCK_W, received=1),
            out_shape=jax.ShapeDtypeStruct((bottom_rows, SPAN), BF16),
            in_specs=[vmem],
            out_specs=vmem,
            scratch_shapes=scratch(half),
            compiler_params=params(OTHER_VMEM),
            cost_estimate=cost(0.9e10, 2**20),
            name="factor_bottom",
        )(rest)

    if in_ring:
        top, rest = factor_top(*grams[ring - 1], *carried)

        paired = ring & (ring - 1) == 0
        distances = [1] + list(range(ring - 1, 1, -1)) if paired else list(range(1, ring))

        def partner(z, d):
            return z ^ d if paired else (z + d) % ring

        def shared(array):
            return [array] + [
                lax.ppermute(array, "dp", [(z, partner(z, d)) for z in range(ring)]) for d in distances
            ]

        tops = shared(top)
        bottom = factor_bottom(rest)
        bottoms = shared(bottom)
        order = jnp.stack([place] + [place ^ d if paired else lax.rem(place - d + ring, ring) for d in distances])
    else:
        halves = [factor_top(*[lax.psum(part, "dp") for part in grams[t]]) for t in range(blocks)]
        tops = [top for top, _ in halves]
        bottoms = [factor_bottom(rest) for _, rest in halves]
        order = jnp.arange(blocks, dtype=jnp.int32)


    def whiten(uppers, first, starts, result):
        more = [] if result is None else [result]
        depth = BLOCK_W - starts[0]
        chunks = features // tile
        weights = [
            pl.BlockSpec(
                (tile, depth),
                lambda b, order, c=c: (c, order[first + b] * (BLOCK_W // depth) + starts[0] // depth),
            )
            for c in range(chunks)
        ]
        count = len(uppers) // len(starts)
        return pl.pallas_call(
            functools.partial(
                whiten_kernel, blocks=count, starts=starts, first=first, chunks=chunks, aliased=len(more)
            ),
            out_shape=jax.ShapeDtypeStruct((blocks, BLOCK_W, features), F32),
            grid_spec=pltpu.PrefetchScalarGridSpec(
                num_scalar_prefetch=1,
                grid=(count,),
                in_specs=[vmem] * len(uppers) + weights + [anywhere] * len(more),
                out_specs=anywhere,
                scratch_shapes=[
                    pltpu.VMEM((2 * half, depth), BF16),
                    pltpu.VMEM((2, half, features), F32),
                    pltpu.SemaphoreType.DMA((2, chunks)),
                ],
            ),
            input_output_aliases={1 + len(uppers) + chunks: 0} if more else {},
            compiler_params=params(WHITEN_VMEM),
            cost_estimate=cost(2.0e9 * len(uppers), 2**20),
            name="whiten_bottom" if starts[0] else "whiten_top",
        )(order, *uppers, *[out_weight] * chunks, *more)

    result = whiten([tops[0], bottoms[0]], 0, (0, half), None)
    result = whiten(tops[1:2], 1, (0,), result)
    result = whiten(bottoms[1:2], 1, (half,), result)
    for i in range(2, blocks):
        result = whiten([tops[i], bottoms[i]], i, (0, half), result)
    return result


def solution(mesh):
    in_specs = (
        P(("groups", "dp"), "seq", None),
        P(("groups", "dp"), "seq", None),
        P(("groups", "dp"), "seq", None),
        P(("groups", "dp"), None),
        P(("groups", "dp"), None),
        P("dp", "seq"),
    )
    out_specs = P(("groups", "seq"), None, "dp")
    return jax.shard_map(shards, mesh=mesh, in_specs=in_specs, out_specs=out_specs, check_vma=False)
```
